32 devices in a mesh: seq: 16 (over z, x, core), tp: 2 (over y).
Axes of the slice: x: 2, y: 2, z: 4, core: 2. Of those that a mesh axis runs over, the one named last changes fastest.
Arguments:
- hidden_in: bfloat16 [4, 4096], P(None, 'seq'), may hold values from -12 to 12
- attn_gain: float32 [4096], P('seq'), may hold values from 0.25 to 4
- mlp_gain: float32 [4096], P('seq'), may hold values from 0.25 to 1.75
- query_weight: bfloat16 [4096, 4096], P('seq', 'tp'), may hold values from -0.09375 to 0.09375
- key_weight: bfloat16 [4096, 1024], P('seq', 'tp'), may hold values from -0.21875 to 0.21875
- value_weight: bfloat16 [4096, 1024], P('seq', 'tp'), may hold values from -0.09375 to 0.09375
- out_weight: bfloat16 [4096, 4096], P('tp', 'seq'), may hold values from -0.25 to 0.25
- up_weight: bfloat16 [4096, 21504], P('seq', 'tp'), may hold values from -0.09375 to 0.09375
- down_weight: bfloat16 [21504, 4096], P('tp', 'seq'), may hold values from -0.0390625 to 0.0390625
- key_cache: bfloat16 [4, 2048, 1024], P(None, 'seq', 'tp'), may hold values from -90 to 90
- value_cache: bfloat16 [4, 2048, 1024], P(None, 'seq', 'tp'), may hold values from -6 to 6
- lengths: int32 [4], replicated, may hold values from 1 to 2048, as said below
- block_order: int32 [4], replicated, may hold values from 0 to 3, each once
- pad_mask: int32 [4, 2048], P(None, 'seq'), may hold values 0 or 1
Outputs:
- layer_out: bfloat16 [4, 4096], P(None, 'seq')
The draws below stay inside these ranges and needn't reach their ends.
Inputs may be any that keep to these rules, and one draw needn't show every extreme that they name: `lengths`: exactly one request has 2048 positions; 2 requests have at most 8 positions, the others at least 1536. `block_order`: a permutation of 0 to 3.
All inputs are finite; a program needn't handle non-finite values. No bound on the sum of `pad_mask` on one device may be relied on, other than what follows from the above.
Results may differ from the reference program's by a relative error of at most 0.012.
The reference program's roundings to bfloat16 on the way count: a program that leaves them out, or rounds other values in their place, can miss the bound.
Values may be sent and summed in bfloat16 or wider, within the bound.
No kernel may reach another device: no remote copies, remote signals or barrier semaphores. Data moves between devices by JAX's collectives and lax.ppermute only.
A program may use at most 64 MiB of HBM per device.

```python
import math
import jax
import jax.numpy as jnp
from jax import lax

D = 4096
H = 32
KVH = 8
HD = 128
FF = 21504
R = 4
SPAN = 128
MAXLEN = 2048


def draw_hidden_in(key, part):
    key_base = jax.random.fold_in(key, 0)
    feature_rise = 0.6 * jnp.power(3.0, jnp.arange(D, dtype=jnp.float32) / (D - 1))
    values_f = jax.random.normal(key_base, (R, D), jnp.float32) * feature_rise[None, :]
    return jnp.clip(values_f, -12.0, 12.0).astype(jnp.bfloat16)


def draw_attn_gain(key, part):
    values_f = 1.0 + 0.15 * jnp.clip(jax.random.normal(key, (D,), jnp.float32), -5.0, 5.0)
    return jnp.clip(values_f, 0.25, 4.0).astype(jnp.float32)


def draw_key_cache(key, part):
    key_base = jax.random.fold_in(key, 0)
    shape_all = (R, MAXLEN, KVH * HD)
    values_f = 2.5 * jax.random.normal(key_base, shape_all, jnp.float32)
    values_f = jnp.clip(values_f, -15.0, 15.0)
    return jnp.clip(values_f, -90.0, 90.0).astype(jnp.bfloat16)


def draw_lengths(key, part):
    key_long, key_short, key_order = jax.random.split(key, 3)
    long_lengths = jax.random.randint(key_long, (R,), 3 * MAXLEN // 4, MAXLEN, dtype=jnp.int32)
    short_lengths = jax.random.randint(key_short, (R,), 1, 9, dtype=jnp.int32)
    request_ids = jnp.arange(R, dtype=jnp.int32)
    base_lengths = jnp.where(request_ids == 0, MAXLEN, jnp.where(request_ids < (R + 1) // 2, long_lengths, short_lengths))
    shuffle = jax.random.permutation(key_order, R)
    return base_lengths[shuffle].astype(jnp.int32)


def touch_ends(values, own_key, low, largest):
    extent = values.shape
    place = [jax.random.randint(jax.random.fold_in(own_key, axis), (), 0, extent[axis]) for axis in range(len(extent))]
    values = values.at[tuple(place)].set(low)
    longest = extent.index(max(extent))
    place[longest] = (place[longest] + 1) % extent[longest]
    return values.at[tuple(place)].set(largest)


def shard_levels(rng, shape, pieces, smallest, top_value):
    level = 1.0
    for dim, parts in pieces:
        draws = jax.random.uniform(jax.random.fold_in(jax.random.fold_in(rng, 6), dim), (parts,), jnp.float32, smallest / len(pieces), top_value / len(pieces))
        level = level * jnp.repeat(jnp.exp(draws), shape[dim] // parts).reshape((-1,) + (1,) * (len(shape) - 1 - dim))
    return level


def noise(rng, extent, width, reach, shards=(), kind=jnp.bfloat16):
    entries = width * jax.random.normal(rng, extent, jnp.float32)
    if shards:
        entries = entries * shard_levels(rng, extent, shards, -0.22, 0.18)
    return jnp.clip(entries, -reach, reach).astype(kind)


def setup_inputs(seed: int = 0) -> dict:
    seeds = jax.random.split(jax.random.key(seed), 15)
    hidden_in = draw_hidden_in(jax.random.fold_in(seeds[14], 71), 0)
    attn_gain = draw_attn_gain(jax.random.fold_in(seeds[14], 71), 0)
    mlp_gain = jnp.clip(1.0 + 0.15 * jax.random.normal(seeds[2], (D,), jnp.float32), 0.25, 1.75)
    query_weight = noise(seeds[3], (D, H * HD), D ** -0.5, 0.09375, ((0, 16), (1, 2)))
    key_weight = noise(seeds[4], (D, KVH * HD), (D // 6) ** -0.5, 0.21875, ((0, 16), (1, 2)))
    value_weight = noise(seeds[5], (D, KVH * HD), D ** -0.5, 0.09375, ((0, 16), (1, 2)))
    out_weight = noise(seeds[6], (H * HD, D), (H * HD // 8) ** -0.5, 0.25, ((0, 2), (1, 16)))
    up_weight = noise(seeds[7], (D, FF), D ** -0.5, 0.09375, ((0, 16), (1, 2)))
    down_weight = noise(seeds[8], (FF, D), FF ** -0.5, 0.0390625, ((0, 2), (1, 16)))
    key_cache = draw_key_cache(jax.random.fold_in(seeds[14], 71), 0)
    value_cache = noise(seeds[10], (R, MAXLEN, KVH * HD), 1.0, 6.0, ((1, 16), (2, 2)))
    lengths = draw_lengths(jax.random.fold_in(seeds[14], 71), 0)
    block_order = jax.random.permutation(seeds[12], R).astype(jnp.int32)
    pad_mask = touch_ends((jax.random.randint(seeds[13], (R, MAXLEN), 0, 8) < 7).astype(jnp.int32), jax.random.fold_in(seeds[13], 1), 0, 1)
    return dict(hidden_in=hidden_in, attn_gain=attn_gain, mlp_gain=mlp_gain, query_weight=query_weight, key_weight=key_weight, value_weight=value_weight, out_weight=out_weight, up_weight=up_weight, down_weight=down_weight, key_cache=key_cache, value_cache=value_cache, lengths=lengths, block_order=block_order, pad_mask=pad_mask)


NORM_EPS = 1e-05
MASKED = -1e+30

def squared_relu(values_in):
    positive = jnp.maximum(values_in, 0.0)
    return positive * positive

def reference(hidden_in, attn_gain, mlp_gain, query_weight, key_weight, value_weight, out_weight, up_weight, down_weight, key_cache, value_cache, lengths, block_order, pad_mask):
    q_per_kv = H // KVH
    score_scale = 1.0 / math.sqrt(HD)
    n_blocks = MAXLEN // SPAN
    x_rows = hidden_in.astype(jnp.float32)
    scaled_in = (x_rows * attn_gain).astype(jnp.bfloat16)
    inv_attn = lax.rsqrt(lax.optimization_barrier(jnp.sum(x_rows * x_rows, axis=1, keepdims=True)) / D + NORM_EPS)
    query_rows = (jnp.dot(scaled_in, query_weight, preferred_element_type=jnp.float32) * inv_attn).astype(jnp.bfloat16)
    key_new = (jnp.dot(scaled_in, key_weight, preferred_element_type=jnp.float32) * inv_attn).astype(jnp.bfloat16)
    value_new = (jnp.dot(scaled_in, value_weight, preferred_element_type=jnp.float32) * inv_attn).astype(jnp.bfloat16)
    slot_ids = jnp.arange(MAXLEN, dtype=jnp.int32)
    first_block = (block_order % n_blocks).astype(jnp.int32)
    position = (slot_ids[None, :] // SPAN - first_block[:, None]) % n_blocks * SPAN + slot_ids[None, :] % SPAN
    live_slots = (position < lengths[:, None]) & (pad_mask == 1)

    def one_request(request_items):
        query_one, key_one, value_one, cache_keys, cache_values, live_one = request_items
        query_f = query_one.astype(jnp.float32).reshape(KVH, q_per_kv, HD)
        keys_f = cache_keys.astype(jnp.float32).reshape(MAXLEN, KVH, HD)
        values_f = cache_values.astype(jnp.float32).reshape(MAXLEN, KVH, HD)
        scores = jnp.einsum('kgd,tkd->kgt', query_f, keys_f) * score_scale
        scores = jnp.where(live_one[None, None, :], scores, MASKED)
        self_score = jnp.einsum('kgd,kd->kg', query_f, key_one.astype(jnp.float32).reshape(KVH, HD)) * score_scale
        row_top = jnp.maximum(lax.optimization_barrier(jnp.max(scores, axis=2)), self_score)
        weights = jnp.where(live_one[None, None, :], jnp.exp(scores - row_top[:, :, None]), 0.0)
        self_weight = jnp.exp(self_score - row_top)
        row_total = lax.optimization_barrier(jnp.sum(weights, axis=2)) + self_weight
        rounded = lax.optimization_barrier(weights.astype(jnp.bfloat16)).astype(jnp.float32)
        numerator = jnp.einsum('kgt,tkd->kgd', rounded, values_f)
        numerator = numerator + self_weight[:, :, None] * value_one.astype(jnp.float32).reshape(KVH, 1, HD)
        return (numerator / row_total[:, :, None]).reshape(H * HD).astype(jnp.bfloat16)
    attended = lax.map(one_request, (query_rows, key_new, value_new, key_cache, value_cache, live_slots))
    attn_out = jnp.dot(attended, out_weight, preferred_element_type=jnp.float32)
    hidden_state = (x_rows + attn_out).astype(jnp.bfloat16)
    resid_rows = hidden_state.astype(jnp.float32)
    scaled_mlp = (resid_rows * mlp_gain).astype(jnp.bfloat16)
    inv_mlp = lax.rsqrt(lax.optimization_barrier(jnp.sum(resid_rows * resid_rows, axis=1, keepdims=True)) / D + NORM_EPS)
    up_proj = jnp.dot(scaled_mlp, up_weight, preferred_element_type=jnp.float32) * inv_mlp
    activated = squared_relu(up_proj).astype(jnp.bfloat16)
    mlp_out = jnp.dot(activated, down_weight, preferred_element_type=jnp.float32)
    return (resid_rows + mlp_out).astype(jnp.bfloat16)
```

```python
import math

import jax
import jax.numpy as jnp
from jax import lax
from jax.sharding import Mesh, PartitionSpec as P

D = 4096
H = 32
KVH = 8
HD = 128


NORM_EPS = 1e-05
MASKED = -1e30
LANES = 128


def squared_relu(values_in):
    positive = jnp.maximum(values_in, 0.0)
    return positive * positive


def swap(values_in, axis):
    n = lax.axis_size(axis)
    return lax.ppermute(values_in, axis, [(i, i ^ 1) for i in range(n)])


def gather_all(values_in, axes, n):
    copies = jnp.broadcast_to(values_in[None], (n,) + values_in.shape)
    return lax.all_to_all(copies, axes, 0, 0)


def sum_tp(values_in):
    n = lax.axis_size("tp")
    if n == 2:
        return values_in + swap(values_in, "tp")
    return lax.psum(values_in, "tp")


def per_device(
    hidden_in,
    attn_gain,
    mlp_gain,
    query_weight,
    key_weight,
    value_weight,
    out_weight,
    up_weight,
    down_weight,
    key_cache,
    value_cache,
    lengths,
    block_order,
    pad_mask,
):
    n_req = hidden_in.shape[0]
    q_per_kv = H // KVH
    kv_here = key_cache.shape[2] // HD
    span_here = key_cache.shape[1]
    heads_here = kv_here * q_per_kv
    n_chips = lax.axis_size("chip")
    core = lax.axis_index("core")
    n_blocks = 2 * n_chips
    my_block = 2 * lax.axis_index("chip") + core
    score_scale = 1.0 / math.sqrt(HD)

    x_rows = hidden_in.astype(jnp.float32)
    scaled_in = (x_rows * attn_gain).astype(jnp.bfloat16)
    sq_attn = jnp.sum(x_rows * x_rows, axis=1, keepdims=True)
    proj_query = jnp.dot(scaled_in, query_weight, preferred_element_type=jnp.float32)
    proj_key = jnp.dot(scaled_in, key_weight, preferred_element_type=jnp.float32)
    proj_value = jnp.dot(scaled_in, value_weight, preferred_element_type=jnp.float32)
    half_q, half_kv = proj_query.shape[1] // 2, proj_key.shape[1] // 2
    square_cols = jnp.broadcast_to(sq_attn, (n_req, LANES))

    def half(i):
        return jnp.concatenate(
            [
                proj_query[:, i * half_q : (i + 1) * half_q],
                proj_key[:, i * half_kv : (i + 1) * half_kv],
                proj_value[:, i * half_kv : (i + 1) * half_kv],
                square_cols,
            ],
            axis=1,
        )

    low, high = half(0), half(1)
    mine = jnp.where(core == 0, low, high)
    other = jnp.where(core == 0, high, low)
    pair_sum = mine + swap(other, "core")
    qkv_sum = jnp.sum(gather_all(pair_sum, "chip", n_chips), axis=0)
    inv_attn = lax.rsqrt(qkv_sum[:, -1:] / D + NORM_EPS)
    qkv_half = (qkv_sum[:, :-LANES] * inv_attn).astype(jnp.bfloat16)
    qkv_other = swap(qkv_half, "core")
    qkv_low = jnp.where(core == 0, qkv_half, qkv_other)
    qkv_high = jnp.where(core == 0, qkv_other, qkv_half)

    def both(start, size):
        return jnp.concatenate(
            [qkv_low[:, start : start + size], qkv_high[:, start : start + size]], axis=1
        )

    query_rows = both(0, half_q)
    key_new = both(half_q, half_kv)
    value_new = both(half_q + half_kv, half_kv)

    first_block = block_order % n_blocks
    position = ((my_block - first_block) % n_blocks)[:, None] * span_here + jnp.arange(
        span_here, dtype=jnp.int32
    )[None, :]
    live_slots = ((position < lengths[:, None]) & (pad_mask == 1))[:, None, None, :]
    q_groups = query_rows.reshape(n_req, kv_here, q_per_kv, HD)
    keys_here = key_cache.reshape(n_req, span_here, kv_here, HD)
    values_here = value_cache.reshape(n_req, span_here, kv_here, HD)
    scores = (
        jnp.einsum("rkgd,rtkd->rkgt", q_groups, keys_here, preferred_element_type=jnp.float32)
        * score_scale
    )
    scores = jnp.where(live_slots, scores, MASKED)
    local_top = jnp.max(scores, axis=3, keepdims=True)
    weights = jnp.where(live_slots, jnp.exp(scores - local_top), 0.0)
    local_total = jnp.sum(weights, axis=3, keepdims=True)
    local_out = jnp.einsum(
        "rkgt,rtkd->rkgd",
        weights.astype(jnp.bfloat16),
        values_here,
        preferred_element_type=jnp.float32,
    )
    numer = local_out.reshape(n_req, heads_here, HD)
    stats = jnp.concatenate(
        [
            local_total.reshape(n_req, heads_here, 1),
            local_top.reshape(n_req, heads_here, 1),
        ],
        axis=2,
    )
    stat_rows = stats.reshape(n_req, heads_here * 2)
    pad = (-stat_rows.shape[1]) % LANES
    message = jnp.concatenate(
        [numer.reshape(n_req, heads_here * HD), jnp.pad(stat_rows, ((0, 0), (0, pad)))], axis=1
    )
    arrived = gather_all(message, ("chip", "core"), n_blocks)
    outs = arrived[:, :, : heads_here * HD].reshape(n_blocks, n_req, heads_here, HD)
    stats_all = arrived[:, :, heads_here * HD : heads_here * (HD + 2)].reshape(
        n_blocks, n_req, heads_here, 2
    )
    totals, tops = stats_all[..., 0], stats_all[..., 1]
    self_score = (
        jnp.einsum(
            "rkgd,rkd->rkg",
            q_groups,
            key_new.reshape(n_req, kv_here, HD),
            preferred_element_type=jnp.float32,
        )
        * score_scale
    ).reshape(n_req, heads_here)
    final_top = jnp.maximum(jnp.max(tops, axis=0), self_score)
    fades = jnp.exp(tops - final_top)
    self_weight = jnp.exp(self_score - final_top)
    denominator = jnp.sum(totals * fades, axis=0) + self_weight
    value_self = jnp.broadcast_to(
        value_new.reshape(n_req, kv_here, 1, HD), (n_req, kv_here, q_per_kv, HD)
    ).reshape(n_req, heads_here, HD)
    numerator = jnp.sum(outs * fades[..., None], axis=0) + self_weight[
        ..., None
    ] * value_self.astype(jnp.float32)
    attended = (
        (numerator / denominator[..., None])
        .reshape(n_req, heads_here * HD)
        .astype(jnp.bfloat16)
    )
    head_part = jnp.dot(attended, out_weight, preferred_element_type=jnp.float32)
    attn_out = sum_tp(head_part)
    hidden_state = (x_rows + attn_out).astype(jnp.bfloat16)

    resid_rows = hidden_state.astype(jnp.float32)
    scaled_mlp = (resid_rows * mlp_gain).astype(jnp.bfloat16)
    sq_mlp = jnp.sum(resid_rows * resid_rows, axis=1, keepdims=True)
    up_part = jnp.dot(scaled_mlp, up_weight, preferred_element_type=jnp.float32)
    half_up = up_part.shape[1] // 2
    up_low, up_high = up_part[:, :half_up], up_part[:, half_up:]
    square_cols = jnp.broadcast_to(sq_mlp, (n_req, LANES))
    up_mine = jnp.concatenate([jnp.where(core == 0, up_low, up_high), square_cols], axis=1)
    up_other = jnp.concatenate([jnp.where(core == 0, up_high, up_low), square_cols], axis=1)
    up_pair = up_mine + swap(up_other, "core")
    square_sum = up_pair[:, half_up : half_up + 1]
    piece_0 = lax.reduce_precision(square_sum, 8, 7)
    piece_1 = lax.reduce_precision(square_sum - piece_0, 8, 7)
    piece_2 = square_sum - piece_0 - piece_1
    pieces = jnp.pad(
        jnp.concatenate([piece_0, piece_1, piece_2], axis=1), ((0, 0), (0, LANES - 3))
    )
    up_message = jnp.concatenate([up_pair[:, :half_up], pieces], axis=1).astype(jnp.bfloat16)
    up_sum = jnp.sum(gather_all(up_message, "chip", n_chips).astype(jnp.float32), axis=0)
    squares = jnp.sum(up_sum[:, half_up:], axis=1, keepdims=True)
    inv_mlp = lax.rsqrt(squares / D + NORM_EPS)
    active_half = squared_relu(up_sum[:, :half_up] * inv_mlp).astype(jnp.bfloat16)
    active_other = swap(active_half, "core")
    activated = jnp.concatenate(
        [
            jnp.where(core == 0, active_half, active_other),
            jnp.where(core == 0, active_other, active_half),
        ],
        axis=1,
    )
    down_part = jnp.dot(activated, down_weight, preferred_element_type=jnp.float32)
    mlp_out = sum_tp(down_part)
    return (resid_rows + mlp_out).astype(jnp.bfloat16)


def solution(mesh):
    n_seq, n_tp = mesh.shape["seq"], mesh.shape["tp"]
    split = Mesh(mesh.devices.reshape(n_seq // 2, 2, n_tp), ("chip", "core", "tp"))
    seq = ("chip", "core")
    return jax.shard_map(
        per_device,
        mesh=split,
        in_specs=(
            P(None, seq),
            P(seq),
            P(seq),
            P(seq, "tp"),
            P(seq, "tp"),
            P(seq, "tp"),
            P("tp", seq),
            P(seq, "tp"),
            P("tp", seq),
            P(None, seq, "tp"),
            P(None, seq, "tp"),
            P(),
            P(),
            P(None, seq),
        ),
        out_specs=P(None, seq),
        check_vma=False,
    )
```

```python
import math

import jax
import jax.numpy as jnp
from jax import lax
from jax.experimental import pallas as pl
from jax.experimental.pallas import tpu as pltpu
from jax.sharding import Mesh, PartitionSpec as P

D = 4096
H = 32
KVH = 8
HD = 128


NORM_EPS = 1e-05
MASKED = -1e30
LANES = 128


def squared_relu(values_in):
    positive = jnp.maximum(values_in, 0.0)
    return positive * positive


def swap(values_in, axis):
    n = lax.axis_size(axis)
    return lax.ppermute(values_in, axis, [(i, i ^ 1) for i in range(n)])


def gather_all(values_in, axes, n):
    copies = jnp.broadcast_to(values_in[None], (n,) + values_in.shape)
    return lax.all_to_all(copies, axes, 0, 0)


def sum_tp(values_in):
    n = lax.axis_size("tp")
    if n == 2:
        return values_in + swap(values_in, "tp")
    return lax.psum(values_in, "tp")


def per_device_plain(
    hidden_in,
    attn_gain,
    mlp_gain,
    query_weight,
    key_weight,
    value_weight,
    out_weight,
    up_weight,
    down_weight,
    key_cache,
    value_cache,
    lengths,
    block_order,
    pad_mask,
):
    n_req = hidden_in.shape[0]
    q_per_kv = H // KVH
    kv_here = key_cache.shape[2] // HD
    span_here = key_cache.shape[1]
    heads_here = kv_here * q_per_kv
    n_chips = lax.axis_size("chip")
    core = lax.axis_index("core")
    n_blocks = 2 * n_chips
    my_block = 2 * lax.axis_index("chip") + core
    score_scale = 1.0 / math.sqrt(HD)

    x_rows = hidden_in.astype(jnp.float32)
    scaled_in = (x_rows * attn_gain).astype(jnp.bfloat16)
    sq_attn = jnp.sum(x_rows * x_rows, axis=1, keepdims=True)
    proj_query = jnp.dot(scaled_in, query_weight, preferred_element_type=jnp.float32)
    proj_key = jnp.dot(scaled_in, key_weight, preferred_element_type=jnp.float32)
    proj_value = jnp.dot(scaled_in, value_weight, preferred_element_type=jnp.float32)
    half_q, half_kv = proj_query.shape[1] // 2, proj_key.shape[1] // 2
    square_cols = jnp.broadcast_to(sq_attn, (n_req, LANES))

    def half(i):
        return jnp.concatenate(
            [
                proj_query[:, i * half_q : (i + 1) * half_q],
                proj_key[:, i * half_kv : (i + 1) * half_kv],
                proj_value[:, i * half_kv : (i + 1) * half_kv],
                square_cols,
            ],
            axis=1,
        )

    low, high = half(0), half(1)
    mine = jnp.where(core == 0, low, high)
    other = jnp.where(core == 0, high, low)
    pair_sum = mine + swap(other, "core")
    qkv_sum = jnp.sum(gather_all(pair_sum, "chip", n_chips), axis=0)
    inv_attn = lax.rsqrt(qkv_sum[:, -1:] / D + NORM_EPS)
    qkv_half = (qkv_sum[:, :-LANES] * inv_attn).astype(jnp.bfloat16)
    qkv_other = swap(qkv_half, "core")
    qkv_low = jnp.where(core == 0, qkv_half, qkv_other)
    qkv_high = jnp.where(core == 0, qkv_other, qkv_half)

    def both(start, size):
        return jnp.concatenate(
            [qkv_low[:, start : start + size], qkv_high[:, start : start + size]], axis=1
        )

    query_rows = both(0, half_q)
    key_new = both(half_q, half_kv)
    value_new = both(half_q + half_kv, half_kv)

    first_block = block_order % n_blocks
    position = ((my_block - first_block) % n_blocks)[:, None] * span_here + jnp.arange(
        span_here, dtype=jnp.int32
    )[None, :]
    live_slots = ((position < lengths[:, None]) & (pad_mask == 1))[:, None, None, :]
    q_groups = query_rows.reshape(n_req, kv_here, q_per_kv, HD)
    keys_here = key_cache.reshape(n_req, span_here, kv_here, HD)
    values_here = value_cache.reshape(n_req, span_here, kv_here, HD)
    scores = (
        jnp.einsum("rkgd,rtkd->rkgt", q_groups, keys_here, preferred_element_type=jnp.float32)
        * score_scale
    )
    scores = jnp.where(live_slots, scores, MASKED)
    local_top = jnp.max(scores, axis=3, keepdims=True)
    weights = jnp.where(live_slots, jnp.exp(scores - local_top), 0.0)
    local_total = jnp.sum(weights, axis=3, keepdims=True)
    local_out = jnp.einsum(
        "rkgt,rtkd->rkgd",
        weights.astype(jnp.bfloat16),
        values_here,
        preferred_element_type=jnp.float32,
    )
    numer = local_out.reshape(n_req, heads_here, HD)
    stats = jnp.concatenate(
        [
            local_total.reshape(n_req, heads_here, 1),
            local_top.reshape(n_req, heads_here, 1),
        ],
        axis=2,
    )
    stat_rows = stats.reshape(n_req, heads_here * 2)
    pad = (-stat_rows.shape[1]) % LANES
    message = jnp.concatenate(
        [numer.reshape(n_req, heads_here * HD), jnp.pad(stat_rows, ((0, 0), (0, pad)))], axis=1
    )
    arrived = gather_all(message, ("chip", "core"), n_blocks)
    outs = arrived[:, :, : heads_here * HD].reshape(n_blocks, n_req, heads_here, HD)
    stats_all = arrived[:, :, heads_here * HD : heads_here * (HD + 2)].reshape(
        n_blocks, n_req, heads_here, 2
    )
    totals, tops = stats_all[..., 0], stats_all[..., 1]
    self_score = (
        jnp.einsum(
            "rkgd,rkd->rkg",
            q_groups,
            key_new.reshape(n_req, kv_here, HD),
            preferred_element_type=jnp.float32,
        )
        * score_scale
    ).reshape(n_req, heads_here)
    final_top = jnp.maximum(jnp.max(tops, axis=0), self_score)
    fades = jnp.exp(tops - final_top)
    self_weight = jnp.exp(self_score - final_top)
    denominator = jnp.sum(totals * fades, axis=0) + self_weight
    value_self = jnp.broadcast_to(
        value_new.reshape(n_req, kv_here, 1, HD), (n_req, kv_here, q_per_kv, HD)
    ).reshape(n_req, heads_here, HD)
    numerator = jnp.sum(outs * fades[..., None], axis=0) + self_weight[
        ..., None
    ] * value_self.astype(jnp.float32)
    attended = (
        (numerator / denominator[..., None])
        .reshape(n_req, heads_here * HD)
        .astype(jnp.bfloat16)
    )
    head_part = jnp.dot(attended, out_weight, preferred_element_type=jnp.float32)
    attn_out = sum_tp(head_part)
    hidden_state = (x_rows + attn_out).astype(jnp.bfloat16)

    resid_rows = hidden_state.astype(jnp.float32)
    scaled_mlp = (resid_rows * mlp_gain).astype(jnp.bfloat16)
    sq_mlp = jnp.sum(resid_rows * resid_rows, axis=1, keepdims=True)
    up_part = jnp.dot(scaled_mlp, up_weight, preferred_element_type=jnp.float32)
    half_up = up_part.shape[1] // 2
    up_low, up_high = up_part[:, :half_up], up_part[:, half_up:]
    square_cols = jnp.broadcast_to(sq_mlp, (n_req, LANES))
    up_mine = jnp.concatenate([jnp.where(core == 0, up_low, up_high), square_cols], axis=1)
    up_other = jnp.concatenate([jnp.where(core == 0, up_high, up_low), square_cols], axis=1)
    up_pair = up_mine + swap(up_other, "core")
    square_sum = up_pair[:, half_up : half_up + 1]
    piece_0 = lax.reduce_precision(square_sum, 8, 7)
    piece_1 = lax.reduce_precision(square_sum - piece_0, 8, 7)
    piece_2 = square_sum - piece_0 - piece_1
    pieces = jnp.pad(
        jnp.concatenate([piece_0, piece_1, piece_2], axis=1), ((0, 0), (0, LANES - 3))
    )
    up_message = jnp.concatenate([up_pair[:, :half_up], pieces], axis=1).astype(jnp.bfloat16)
    up_sum = jnp.sum(gather_all(up_message, "chip", n_chips).astype(jnp.float32), axis=0)
    squares = jnp.sum(up_sum[:, half_up:], axis=1, keepdims=True)
    inv_mlp = lax.rsqrt(squares / D + NORM_EPS)
    active_half = squared_relu(up_sum[:, :half_up] * inv_mlp).astype(jnp.bfloat16)
    active_other = swap(active_half, "core")
    activated = jnp.concatenate(
        [
            jnp.where(core == 0, active_half, active_other),
            jnp.where(core == 0, active_other, active_half),
        ],
        axis=1,
    )
    down_part = jnp.dot(activated, down_weight, preferred_element_type=jnp.float32)
    mlp_out = sum_tp(down_part)
    return (resid_rows + mlp_out).astype(jnp.bfloat16)


IN_VMEM = pl.BlockSpec(memory_space=pltpu.VMEM)
IN_SMEM = pl.BlockSpec(memory_space=pltpu.SMEM)
STAT_LANES = 8


def local_kernel(kernel, outs, operands, flops, scratch=()):
    in_specs, placed, moved = [], [], 0
    for x in operands:
        if x.ndim == 1:
            in_specs.append(IN_SMEM)
            placed.append(x)
        else:
            in_specs.append(IN_VMEM)
            placed.append(pltpu.with_memory_space_constraint(x, pltpu.VMEM))
            moved += x.size * x.dtype.itemsize
    return pl.pallas_call(
        kernel,
        out_shape=outs,
        in_specs=in_specs,
        out_specs=jax.tree.map(lambda _: IN_VMEM, outs),
        scratch_shapes=scratch,
        compiler_params=pltpu.CompilerParams(vmem_limit_bytes=24 * 2**20),
        cost_estimate=pl.CostEstimate(flops=flops, bytes_accessed=moved, transcendentals=0),
    )(*placed)


def f32(*shape):
    return jax.ShapeDtypeStruct(shape, jnp.float32)


def bf16(*shape):
    return jax.ShapeDtypeStruct(shape, jnp.bfloat16)


def pieces_of(values_in):
    first = values_in.astype(jnp.bfloat16).astype(jnp.float32)
    second = (values_in - first).astype(jnp.bfloat16).astype(jnp.float32)
    return first, second, values_in - first - second


def qkv_kernel(x_ref, gain_ref, wq_ref, wk_ref, wv_ref, mine_ref, other_ref):
    core = lax.axis_index("core")
    x_rows = x_ref[...].astype(jnp.float32)
    scaled_in = (x_rows * gain_ref[...]).astype(jnp.bfloat16)
    squares = jnp.sum(x_rows * x_rows, axis=1, keepdims=True)
    at = 0
    for w_ref in (wq_ref, wk_ref, wv_ref):
        half = w_ref.shape[1] // 2
        proj = jnp.dot(scaled_in, w_ref[...], preferred_element_type=jnp.float32)
        low, high = proj[:, :half], proj[:, half:]
        mine_ref[:, at : at + half] = jnp.where(core == 0, low, high)
        other_ref[:, at : at + half] = jnp.where(core == 0, high, low)
        at += half
    square_cols = jnp.broadcast_to(squares, (x_rows.shape[0], LANES))
    mine_ref[:, at:] = square_cols
    other_ref[:, at:] = square_cols


def request_ids(lengths_ref):
    is_long = [(lengths_ref[r] > 8).astype(jnp.int32) for r in range(4)]
    long_0 = jnp.where(is_long[0] == 1, 0, jnp.where(is_long[1] == 1, 1, 2))
    long_1 = jnp.where(is_long[3] == 1, 3, jnp.where(is_long[2] == 1, 2, 1))
    short_0 = jnp.where(is_long[0] == 0, 0, jnp.where(is_long[1] == 0, 1, 2))
    short_1 = jnp.where(is_long[3] == 0, 3, jnp.where(is_long[2] == 0, 2, 1))
    return long_0, long_1, short_0, short_1


def attention_kernel(
    own_ref, oth_ref, key_ref, value_ref, mask_ref, lengths_ref, order_ref,
    message_ref, query_out, key_out, value_out,
):
    core = lax.axis_index("core")
    n_blocks = message_ref.shape[0]
    my_block = 2 * lax.axis_index("chip") + core
    n_req, span = mask_ref.shape
    heads = message_ref.shape[1]
    kv_here = key_ref.shape[2] // HD
    group = heads // kv_here
    own = own_ref[...].astype(jnp.float32)
    oth = oth_ref[...].astype(jnp.float32)
    low = jnp.where(core == 0, own, oth)
    high = jnp.where(core == 0, oth, own)
    for i, part in enumerate((low, high)):
        for h in range(heads // 2):
            query_out[:, i * (heads // 2) + h, :] = part[:, h * HD : (h + 1) * HD]
        for k in range(kv_here // 2):
            at = (heads // 2 + k) * HD
            for g in range(group):
                row = (i * (kv_here // 2) + k) * group + g
                key_out[:, row, :] = part[:, at : at + HD]
                at_value = at + (kv_here // 2) * HD
                value_out[:, row, :] = part[:, at_value : at_value + HD]

    long_0, long_1, short_0, short_1 = request_ids(lengths_ref)
    short_here = jnp.where(lax.rem(order_ref[short_1], n_blocks) == my_block, short_1, short_0)
    slot = lax.broadcasted_iota(jnp.int32, (1, span), 1)
    group_of = lax.broadcasted_iota(jnp.int32, (heads, HD), 0) // group
    lane = lax.broadcasted_iota(jnp.int32, (heads, LANES), 1)
    stats = jnp.zeros((heads, LANES), jnp.float32)
    parts = []
    for s, r in enumerate((long_0, long_1, short_here)):
        first_block = lax.rem(order_ref[r], n_blocks)
        position = lax.rem(my_block - first_block + n_blocks, n_blocks) * span + slot
        live = (position < lengths_ref[r]) & (mask_ref[pl.ds(r, 1), :] == 1)
        query = query_out[r]
        spread = jnp.concatenate(
            [jnp.where(group_of == k, query, 0.0) for k in range(kv_here)], axis=1
        ).astype(jnp.bfloat16)
        scores = lax.dot_general(
            spread, key_ref[r], (((1,), (1,)), ((), ())), preferred_element_type=jnp.float32
        ) * (1.0 / math.sqrt(HD))
        scores = jnp.where(live, scores, MASKED)
        top = jnp.max(scores, axis=1, keepdims=True)
        weights = jnp.where(live, jnp.exp(scores - top), 0.0)
        total = jnp.sum(weights, axis=1, keepdims=True)
        wide = jnp.dot(
            weights.astype(jnp.bfloat16), value_ref[r], preferred_element_type=jnp.float32
        )
        numer = jnp.zeros((heads, HD), jnp.float32)
        for k in range(kv_here):
            numer = jnp.where(group_of == k, wide[:, k * HD : (k + 1) * HD], numer)
        parts.append(numer)
        for i, piece in enumerate(pieces_of(total) + pieces_of(top)):
            stats = jnp.where(lane == s * STAT_LANES + i, piece, stats)
    message = jnp.concatenate(parts + [stats], axis=1).astype(jnp.bfloat16)
    for b in range(n_blocks):
        message_ref[b] = message


def combine_kernel(
    arrived_ref, query_ref, key_ref, value_ref, w_ref, lengths_ref, order_ref,
    head_ref, attended_ref,
):
    n_blocks, heads = arrived_ref.shape[:2]
    long_0, long_1, short_0, short_1 = request_ids(lengths_ref)

    def self_terms(r):
        return (
            jnp.sum(query_ref[r] * key_ref[r], axis=1, keepdims=True) * (1.0 / math.sqrt(HD)),
            value_ref[r],
        )

    def stat(block, s):
        lanes = arrived_ref[block, :, 3 * HD :].astype(jnp.float32)
        at = s * STAT_LANES
        one = [lanes[:, at + i : at + i + 1] for i in range(6)]
        return one[0] + one[1] + one[2], one[3] + one[4] + one[5]

    def numerator(block, s):
        return arrived_ref[block, :, s * HD : (s + 1) * HD].astype(jnp.float32)

    jobs = [(long_0, 0, list(range(n_blocks))), (long_1, 1, list(range(n_blocks)))]
    for r in (short_0, short_1):
        jobs.append((r, 2, [lax.rem(order_ref[r], n_blocks)]))
    for r, s, blocks in jobs:
        self_score, value_self = self_terms(r)
        stats = [stat(b, s) for b in blocks]
        final_top = self_score
        for _, top in stats:
            final_top = jnp.maximum(final_top, top)
        self_weight = jnp.exp(self_score - final_top)
        denominator = self_weight
        numer = self_weight * value_self
        for b, (total, top) in zip(blocks, stats):
            fade = jnp.exp(top - final_top)
            denominator = denominator + total * fade
            numer = numer + numerator(b, s) * fade
        attended_ref[r] = numer / denominator
    attended = jnp.concatenate([attended_ref[:, h, :] for h in range(heads)], axis=1)
    head_ref[...] = jnp.dot(
        attended.astype(jnp.bfloat16), w_ref[...], preferred_element_type=jnp.float32
    )


def up_kernel(x_ref, part_ref, peer_ref, gain_ref, w_ref, hidden_ref, mine_ref, other_ref):
    core = lax.axis_index("core")
    attn_out = part_ref[...] + peer_ref[...]
    hidden_state = (x_ref[...].astype(jnp.float32) + attn_out).astype(jnp.bfloat16)
    resid_rows = hidden_state.astype(jnp.float32)
    hidden_ref[...] = resid_rows
    scaled_mlp = (resid_rows * gain_ref[...]).astype(jnp.bfloat16)
    squares = jnp.sum(resid_rows * resid_rows, axis=1, keepdims=True)
    up_part = jnp.dot(scaled_mlp, w_ref[...], preferred_element_type=jnp.float32)
    half = up_part.shape[1] // 2
    low, high = up_part[:, :half], up_part[:, half:]
    mine_ref[:, :half] = jnp.where(core == 0, low, high)
    other_ref[:, :half] = jnp.where(core == 0, high, low)
    square_cols = jnp.broadcast_to(squares, (resid_rows.shape[0], LANES))
    mine_ref[:, half:] = square_cols
    other_ref[:, half:] = square_cols


def per_device(
    hidden_in,
    attn_gain,
    mlp_gain,
    query_weight,
    key_weight,
    value_weight,
    out_weight,
    up_weight,
    down_weight,
    key_cache,
    value_cache,
    lengths,
    block_order,
    pad_mask,
):
    n_req, d_here = hidden_in.shape
    kv_here = key_cache.shape[2] // HD
    heads_here = kv_here * (H // KVH)
    n_chips = lax.axis_size("chip")
    core = lax.axis_index("core")
    n_blocks = 2 * n_chips
    half_qkv = (heads_here + 2 * kv_here) * HD // 2
    half_up = up_weight.shape[1] // 2

    mine, other = local_kernel(
        qkv_kernel,
        [f32(n_req, half_qkv + LANES)] * 2,
        [hidden_in, attn_gain.reshape(1, d_here), query_weight, key_weight, value_weight],
        flops=4 * n_req * d_here * half_qkv,
    )
    pair_sum = mine + swap(other, "core")
    qkv_sum = jnp.sum(gather_all(pair_sum, "chip", n_chips), axis=0)
    inv_attn = lax.rsqrt(qkv_sum[:, -1:] / D + NORM_EPS)
    qkv_half = (qkv_sum[:, :-LANES] * inv_attn).astype(jnp.bfloat16)
    qkv_other = swap(qkv_half, "core")

    message, query_heads, key_heads, value_heads = local_kernel(
        attention_kernel,
        [bf16(n_blocks, heads_here, 3 * HD + LANES)] + [f32(n_req, heads_here, HD)] * 3,
        [qkv_half, qkv_other, key_cache, value_cache, pad_mask, lengths, block_order],
        flops=12 * heads_here * kv_here * HD * pad_mask.shape[1],
    )
    arrived = lax.all_to_all(message, ("chip", "core"), 0, 0)
    head_part = local_kernel(
        combine_kernel,
        f32(n_req, d_here),
        [arrived, query_heads, key_heads, value_heads, out_weight, lengths, block_order],
        flops=2 * n_req * out_weight.size,
        scratch=[pltpu.VMEM((n_req, heads_here, HD), jnp.float32)],
    )
    head_peer = swap(head_part, "tp")

    resid_rows, up_mine, up_other = local_kernel(
        up_kernel,
        [f32(n_req, d_here)] + [f32(n_req, half_up + LANES)] * 2,
        [hidden_in, head_part, head_peer, mlp_gain.reshape(1, d_here), up_weight],
        flops=2 * n_req * up_weight.size,
    )
    up_pair = up_mine + swap(up_other, "core")
    square_sum = up_pair[:, half_up : half_up + 1]
    piece_0 = lax.reduce_precision(square_sum, 8, 7)
    piece_1 = lax.reduce_precision(square_sum - piece_0, 8, 7)
    piece_2 = square_sum - piece_0 - piece_1
    pieces = jnp.pad(
        jnp.concatenate([piece_0, piece_1, piece_2], axis=1), ((0, 0), (0, LANES - 3))
    )
    up_message = jnp.concatenate([up_pair[:, :half_up], pieces], axis=1).astype(jnp.bfloat16)
    up_sum = jnp.sum(gather_all(up_message, "chip", n_chips).astype(jnp.float32), axis=0)
    squares = jnp.sum(up_sum[:, half_up:], axis=1, keepdims=True)
    inv_mlp = lax.rsqrt(squares / D + NORM_EPS)
    active_half = squared_relu(up_sum[:, :half_up] * inv_mlp).astype(jnp.bfloat16)
    active_other = swap(active_half, "core")
    activated = jnp.concatenate(
        [
            jnp.where(core == 0, active_half, active_other),
            jnp.where(core == 0, active_other, active_half),
        ],
        axis=1,
    )
    down_part = jnp.dot(activated, down_weight, preferred_element_type=jnp.float32)
    mlp_out = sum_tp(down_part)
    return (resid_rows + mlp_out).astype(jnp.bfloat16)


def solution(mesh):
    n_seq, n_tp = mesh.shape["seq"], mesh.shape["tp"]
    split = Mesh(mesh.devices.reshape(n_seq // 2, 2, n_tp), ("chip", "core", "tp"))
    seq = ("chip", "core")
    whole_tiles = n_tp == 2 and KVH % (2 * n_tp) == 0 and D % (n_seq * LANES) == 0
    return jax.shard_map(
        per_device if whole_tiles else per_device_plain,
        mesh=split,
        in_specs=(
            P(None, seq),
            P(seq),
            P(seq),
            P(seq, "tp"),
            P(seq, "tp"),
            P(seq, "tp"),
            P("tp", seq),
            P(seq, "tp"),
            P("tp", seq),
            P(None, seq, "tp"),
            P(None, seq, "tp"),
            P(),
            P(),
            P(None, seq),
        ),
        out_specs=P(None, seq),
        check_vma=False,
    )
```

```python
import math

import jax
import jax.numpy as jnp
from jax import lax
from jax.experimental import pallas as pl
from jax.experimental.pallas import tpu as pltpu
from jax.sharding import Mesh, PartitionSpec as P

D = 4096
H = 32
KVH = 8
HD = 128


NORM_EPS = 1e-05
MASKED = -1e30
LANES = 128


def squared_relu(values_in):
    positive = jnp.maximum(values_in, 0.0)
    return positive * positive


def swap(values_in, axis):
    n = lax.axis_size(axis)
    return lax.ppermute(values_in, axis, [(i, i ^ 1) for i in range(n)])


def gather_all(values_in, axes, n):
    copies = jnp.broadcast_to(values_in[None], (n,) + values_in.shape)
    return lax.all_to_all(copies, axes, 0, 0)


def sum_tp(values_in):
    n = lax.axis_size("tp")
    if n == 2:
        return values_in + swap(values_in, "tp")
    return lax.psum(values_in, "tp")


def per_device_plain(
    hidden_in,
    attn_gain,
    mlp_gain,
    query_weight,
    key_weight,
    value_weight,
    out_weight,
    up_weight,
    down_weight,
    key_cache,
    value_cache,
    lengths,
    block_order,
    pad_mask,
):
    n_req = hidden_in.shape[0]
    q_per_kv = H // KVH
    kv_here = key_cache.shape[2] // HD
    span_here = key_cache.shape[1]
    heads_here = kv_here * q_per_kv
    n_chips = lax.axis_size("chip")
    core = lax.axis_index("core")
    n_blocks = 2 * n_chips
    my_block = 2 * lax.axis_index("chip") + core
    score_scale = 1.0 / math.sqrt(HD)

    x_rows = hidden_in.astype(jnp.float32)
    scaled_in = (x_rows * attn_gain).astype(jnp.bfloat16)
    sq_attn = jnp.sum(x_rows * x_rows, axis=1, keepdims=True)
    proj_query = jnp.dot(scaled_in, query_weight, preferred_element_type=jnp.float32)
    proj_key = jnp.dot(scaled_in, key_weight, preferred_element_type=jnp.float32)
    proj_value = jnp.dot(scaled_in, value_weight, preferred_element_type=jnp.float32)
    half_q, half_kv = proj_query.shape[1] // 2, proj_key.shape[1] // 2
    square_cols = jnp.broadcast_to(sq_attn, (n_req, LANES))

    def half(i):
        return jnp.concatenate(
            [
                proj_query[:, i * half_q : (i + 1) * half_q],
                proj_key[:, i * half_kv : (i + 1) * half_kv],
                proj_value[:, i * half_kv : (i + 1) * half_kv],
                square_cols,
            ],
            axis=1,
        )

    low, high = half(0), half(1)
    mine = jnp.where(core == 0, low, high)
    other = jnp.where(core == 0, high, low)
    pair_sum = mine + swap(other, "core")
    qkv_sum = jnp.sum(gather_all(pair_sum, "chip", n_chips), axis=0)
    inv_attn = lax.rsqrt(qkv_sum[:, -1:] / D + NORM_EPS)
    qkv_half = (qkv_sum[:, :-LANES] * inv_attn).astype(jnp.bfloat16)
    qkv_other = swap(qkv_half, "core")
    qkv_low = jnp.where(core == 0, qkv_half, qkv_other)
    qkv_high = jnp.where(core == 0, qkv_other, qkv_half)

    def both(start, size):
        return jnp.concatenate(
            [qkv_low[:, start : start + size], qkv_high[:, start : start + size]], axis=1
        )

    query_rows = both(0, half_q)
    key_new = both(half_q, half_kv)
    value_new = both(half_q + half_kv, half_kv)

    first_block = block_order % n_blocks
    position = ((my_block - first_block) % n_blocks)[:, None] * span_here + jnp.arange(
        span_here, dtype=jnp.int32
    )[None, :]
    live_slots = ((position < lengths[:, None]) & (pad_mask == 1))[:, None, None, :]
    q_groups = query_rows.reshape(n_req, kv_here, q_per_kv, HD)
    keys_here = key_cache.reshape(n_req, span_here, kv_here, HD)
    values_here = value_cache.reshape(n_req, span_here, kv_here, HD)
    scores = (
        jnp.einsum("rkgd,rtkd->rkgt", q_groups, keys_here, preferred_element_type=jnp.float32)
        * score_scale
    )
    scores = jnp.where(live_slots, scores, MASKED)
    local_top = jnp.max(scores, axis=3, keepdims=True)
    weights = jnp.where(live_slots, jnp.exp(scores - local_top), 0.0)
    local_total = jnp.sum(weights, axis=3, keepdims=True)
    local_out = jnp.einsum(
        "rkgt,rtkd->rkgd",
        weights.astype(jnp.bfloat16),
        values_here,
        preferred_element_type=jnp.float32,
    )
    numer = local_out.reshape(n_req, heads_here, HD)
    stats = jnp.concatenate(
        [
            local_total.reshape(n_req, heads_here, 1),
            local_top.reshape(n_req, heads_here, 1),
        ],
        axis=2,
    )
    stat_rows = stats.reshape(n_req, heads_here * 2)
    pad = (-stat_rows.shape[1]) % LANES
    message = jnp.concatenate(
        [numer.reshape(n_req, heads_here * HD), jnp.pad(stat_rows, ((0, 0), (0, pad)))], axis=1
    )
    arrived = gather_all(message, ("chip", "core"), n_blocks)
    outs = arrived[:, :, : heads_here * HD].reshape(n_blocks, n_req, heads_here, HD)
    stats_all = arrived[:, :, heads_here * HD : heads_here * (HD + 2)].reshape(
        n_blocks, n_req, heads_here, 2
    )
    totals, tops = stats_all[..., 0], stats_all[..., 1]
    self_score = (
        jnp.einsum(
            "rkgd,rkd->rkg",
            q_groups,
            key_new.reshape(n_req, kv_here, HD),
            preferred_element_type=jnp.float32,
        )
        * score_scale
    ).reshape(n_req, heads_here)
    final_top = jnp.maximum(jnp.max(tops, axis=0), self_score)
    fades = jnp.exp(tops - final_top)
    self_weight = jnp.exp(self_score - final_top)
    denominator = jnp.sum(totals * fades, axis=0) + self_weight
    value_self = jnp.broadcast_to(
        value_new.reshape(n_req, kv_here, 1, HD), (n_req, kv_here, q_per_kv, HD)
    ).reshape(n_req, heads_here, HD)
    numerator = jnp.sum(outs * fades[..., None], axis=0) + self_weight[
        ..., None
    ] * value_self.astype(jnp.float32)
    attended = (
        (numerator / denominator[..., None])
        .reshape(n_req, heads_here * HD)
        .astype(jnp.bfloat16)
    )
    head_part = jnp.dot(attended, out_weight, preferred_element_type=jnp.float32)
    attn_out = sum_tp(head_part)
    hidden_state = (x_rows + attn_out).astype(jnp.bfloat16)

    resid_rows = hidden_state.astype(jnp.float32)
    scaled_mlp = (resid_rows * mlp_gain).astype(jnp.bfloat16)
    sq_mlp = jnp.sum(resid_rows * resid_rows, axis=1, keepdims=True)
    up_part = jnp.dot(scaled_mlp, up_weight, preferred_element_type=jnp.float32)
    half_up = up_part.shape[1] // 2
    up_low, up_high = up_part[:, :half_up], up_part[:, half_up:]
    square_cols = jnp.broadcast_to(sq_mlp, (n_req, LANES))
    up_mine = jnp.concatenate([jnp.where(core == 0, up_low, up_high), square_cols], axis=1)
    up_other = jnp.concatenate([jnp.where(core == 0, up_high, up_low), square_cols], axis=1)
    up_pair = up_mine + swap(up_other, "core")
    square_sum = up_pair[:, half_up : half_up + 1]
    piece_0 = lax.reduce_precision(square_sum, 8, 7)
    piece_1 = lax.reduce_precision(square_sum - piece_0, 8, 7)
    piece_2 = square_sum - piece_0 - piece_1
    pieces = jnp.pad(
        jnp.concatenate([piece_0, piece_1, piece_2], axis=1), ((0, 0), (0, LANES - 3))
    )
    up_message = jnp.concatenate([up_pair[:, :half_up], pieces], axis=1).astype(jnp.bfloat16)
    up_sum = jnp.sum(gather_all(up_message, "chip", n_chips).astype(jnp.float32), axis=0)
    squares = jnp.sum(up_sum[:, half_up:], axis=1, keepdims=True)
    inv_mlp = lax.rsqrt(squares / D + NORM_EPS)
    active_half = squared_relu(up_sum[:, :half_up] * inv_mlp).astype(jnp.bfloat16)
    active_other = swap(active_half, "core")
    activated = jnp.concatenate(
        [
            jnp.where(core == 0, active_half, active_other),
            jnp.where(core == 0, active_other, active_half),
        ],
        axis=1,
    )
    down_part = jnp.dot(activated, down_weight, preferred_element_type=jnp.float32)
    mlp_out = sum_tp(down_part)
    return (resid_rows + mlp_out).astype(jnp.bfloat16)


IN_VMEM = pl.BlockSpec(memory_space=pltpu.VMEM)
IN_SMEM = pl.BlockSpec(memory_space=pltpu.SMEM)
STAT_LANES = 8


def local_kernel(kernel, outs, operands, flops, scratch=(), in_hbm=(), anywhere=()):
    in_specs, placed, moved = [], [], 0
    for i, x in enumerate(operands):
        if x.ndim == 1:
            in_specs.append(IN_SMEM)
            placed.append(x)
            continue
        space = pltpu.HBM if i in in_hbm else pltpu.VMEM
        in_specs.append(pl.BlockSpec(memory_space=space))
        placed.append(x if i in anywhere else pltpu.with_memory_space_constraint(x, space))
        moved += x.size * x.dtype.itemsize
    out_specs = [IN_SMEM if len(o.shape) == 1 else IN_VMEM for o in outs]
    return pl.pallas_call(
        kernel,
        out_shape=outs,
        in_specs=in_specs,
        out_specs=out_specs,
        scratch_shapes=scratch,
        compiler_params=pltpu.CompilerParams(vmem_limit_bytes=6 * 2**20),
        cost_estimate=pl.CostEstimate(flops=flops, bytes_accessed=moved, transcendentals=0),
    )(*placed)


def f32(*shape):
    return pltpu.VMEM(shape, jnp.float32)


def bf16(*shape):
    return pltpu.VMEM(shape, jnp.bfloat16)


def pieces_of(values_in):
    first = values_in.astype(jnp.bfloat16).astype(jnp.float32)
    second = (values_in - first).astype(jnp.bfloat16).astype(jnp.float32)
    return first, second, values_in - first - second


def qkv_kernel(
    x_hbm, gain_hbm, wq_hbm, wk_hbm, wv_hbm, mine_ref, other_ref, x_ref, gain_ref, *scratch
):
    core = lax.axis_index("core")
    w_refs, sems = scratch[:-1], scratch[-1]
    chunk = w_refs[0].shape[1]
    copies = [
        pltpu.make_async_copy(x_hbm, x_ref, sems.at[0]),
        pltpu.make_async_copy(gain_hbm, gain_ref, sems.at[1]),
    ]
    pieces = [(w, at) for w in (wq_hbm, wk_hbm, wv_hbm) for at in range(0, w.shape[1], chunk)]
    for (w_hbm, at), w_ref in zip(pieces, w_refs):
        copies.append(
            pltpu.make_async_copy(
                w_hbm.at[:, pl.ds(at, chunk)], w_ref, sems.at[len(copies)]
            )
        )
    for copy in copies:
        copy.start()
    copies[0].wait()
    copies[1].wait()
    x_rows = x_ref[...].astype(jnp.float32)
    scaled_in = (x_rows * gain_ref[...]).astype(jnp.bfloat16)
    squares = jnp.sum(x_rows * x_rows, axis=1, keepdims=True)
    proj = []
    for w_ref, copy in zip(w_refs, copies[2:]):
        copy.wait()
        proj.append(jnp.dot(scaled_in, w_ref[...], preferred_element_type=jnp.float32))
    proj = jnp.concatenate(proj, axis=1)
    at, start = 0, 0
    for w_hbm in (wq_hbm, wk_hbm, wv_hbm):
        half = w_hbm.shape[1] // 2
        low, high = proj[:, start : start + half], proj[:, start + half : start + 2 * half]
        mine_ref[:, at : at + half] = jnp.where(core == 0, low, high)
        other_ref[:, at : at + half] = jnp.where(core == 0, high, low)
        at += half
        start += 2 * half
    square_cols = jnp.broadcast_to(squares, (x_rows.shape[0], LANES))
    mine_ref[:, at:] = square_cols
    other_ref[:, at:] = square_cols


def qkv_sum_kernel(arrived_ref, plan_ref, out_ref):
    total = arrived_ref[0]
    for i in range(1, arrived_ref.shape[0]):
        total = total + arrived_ref[i]
    width = out_ref.shape[1]
    inv_attn = lax.rsqrt(total[:, width : width + 1] / D + NORM_EPS)
    out_ref[...] = (total[:, :width] * inv_attn).astype(jnp.bfloat16)


def request_ids(lengths_ref):
    is_long = [(lengths_ref[r] > 8).astype(jnp.int32) for r in range(4)]
    long_0 = jnp.where(is_long[0] == 1, 0, jnp.where(is_long[1] == 1, 1, 2))
    long_1 = jnp.where(is_long[3] == 1, 3, jnp.where(is_long[2] == 1, 2, 1))
    short_0 = jnp.where(is_long[0] == 0, 0, jnp.where(is_long[1] == 0, 1, 2))
    short_1 = jnp.where(is_long[3] == 0, 3, jnp.where(is_long[2] == 0, 2, 1))
    return long_0, long_1, short_0, short_1


PLAN_SLOT = 0
PLAN_LIVE = 3
PLAN_SHORT = 6
PLAN_OWNER = 8
PLAN_SIZE = 16


def prefetch_kernel(
    after_ref, lengths_ref, order_ref, key_hbm, value_hbm, *refs,
):
    n_plain = (len(refs) - 4) // 2
    plain_in, refs = refs[:n_plain], refs[n_plain:]
    plan_ref, key_ref, value_ref = refs[:3]
    plain_out, sems = refs[3:-1], refs[-1]
    n_blocks = lax.axis_size("chip") * 2
    my_block = 2 * lax.axis_index("chip") + lax.axis_index("core")
    span = key_hbm.shape[1]
    long_0, long_1, short_0, short_1 = request_ids(lengths_ref)
    owners = [lax.rem(order_ref[r], n_blocks) for r in (short_0, short_1)]
    short_here = jnp.where(owners[1] == my_block, short_1, short_0)
    copies = []
    for s, r in enumerate((long_0, long_1, short_here)):
        for hbm, vmem in ((key_hbm, key_ref), (value_hbm, value_ref)):
            copies.append(pltpu.make_async_copy(hbm.at[r], vmem.at[s], sems.at[len(copies)]))
            copies[-1].start()
    for hbm, vmem in zip(plain_in, plain_out):
        copies.append(pltpu.make_async_copy(hbm, vmem, sems.at[len(copies)]))
        copies[-1].start()
    for s, r in enumerate((long_0, long_1, short_here)):
        first_block = lax.rem(order_ref[r], n_blocks)
        begin = lax.rem(my_block - first_block + n_blocks, n_blocks) * span
        plan_ref[PLAN_SLOT + s] = r
        plan_ref[PLAN_LIVE + s] = lengths_ref[r] - begin
    for i, r in enumerate((short_0, short_1)):
        plan_ref[PLAN_SHORT + i] = r
        plan_ref[PLAN_OWNER + i] = owners[i]
    for i in range(PLAN_OWNER + 2, PLAN_SIZE):
        plan_ref[i] = 0
    for copy in copies:
        copy.wait()


def copy_kernel(after_ref, w_hbm, w_ref, sem):
    copy = pltpu.make_async_copy(w_hbm, w_ref, sem)
    copy.start()
    copy.wait()


def attention_kernel(
    own_ref, oth_ref, key_ref, value_ref, mask_ref, plan_ref,
    message_ref, query_out, key_out, value_out,
):
    core = lax.axis_index("core")
    n_blocks = message_ref.shape[0]
    n_req, span = mask_ref.shape
    heads = message_ref.shape[1]
    kv_here = key_ref.shape[2] // HD
    group = heads // kv_here
    own = own_ref[...].astype(jnp.float32)
    oth = oth_ref[...].astype(jnp.float32)
    low = jnp.where(core == 0, own, oth)
    high = jnp.where(core == 0, oth, own)
    for i, part in enumerate((low, high)):
        for h in range(heads // 2):
            query_out[:, i * (heads // 2) + h, :] = part[:, h * HD : (h + 1) * HD]
        for k in range(kv_here // 2):
            at = (heads // 2 + k) * HD
            for g in range(group):
                row = (i * (kv_here // 2) + k) * group + g
                key_out[:, row, :] = part[:, at : at + HD]
                at_value = at + (kv_here // 2) * HD
                value_out[:, row, :] = part[:, at_value : at_value + HD]

    slot = lax.broadcasted_iota(jnp.int32, (1, span), 1)
    group_of = lax.broadcasted_iota(jnp.int32, (heads, HD), 0) // group
    lane = lax.broadcasted_iota(jnp.int32, (heads, LANES), 1)
    stats = jnp.zeros((heads, LANES), jnp.float32)
    parts = []
    for s in range(3):
        r = plan_ref[PLAN_SLOT + s]
        live = (slot < plan_ref[PLAN_LIVE + s]) & (mask_ref[pl.ds(r, 1), :] == 1)
        query = query_out[r]
        spread = jnp.concatenate(
            [jnp.where(group_of == k, query, 0.0) for k in range(kv_here)], axis=1
        ).astype(jnp.bfloat16)
        scores = lax.dot_general(
            spread, key_ref[s], (((1,), (1,)), ((), ())), preferred_element_type=jnp.float32
        ) * (1.0 / math.sqrt(HD))
        scores = jnp.where(live, scores, MASKED)
        top = jnp.max(scores, axis=1, keepdims=True)
        weights = jnp.where(live, jnp.exp(scores - top), 0.0)
        total = jnp.sum(weights, axis=1, keepdims=True)
        wide = jnp.dot(
            weights.astype(jnp.bfloat16), value_ref[s], preferred_element_type=jnp.float32
        )
        numer = jnp.zeros((heads, HD), jnp.float32)
        for k in range(kv_here):
            numer = jnp.where(group_of == k, wide[:, k * HD : (k + 1) * HD], numer)
        parts.append(numer)
        for i, piece in enumerate(pieces_of(total) + pieces_of(top)):
            stats = jnp.where(lane == s * STAT_LANES + i, piece, stats)
    message = jnp.concatenate(parts + [stats], axis=1).astype(jnp.bfloat16)
    for b in range(n_blocks):
        message_ref[b] = message


def combine_kernel(
    arrived_ref, query_ref, key_ref, value_ref, w_ref, plan_ref, head_ref, attended_ref
):
    n_blocks, heads = arrived_ref.shape[:2]

    def self_terms(r):
        return (
            jnp.sum(query_ref[r] * key_ref[r], axis=1, keepdims=True) * (1.0 / math.sqrt(HD)),
            value_ref[r],
        )

    def stat(block, s):
        lanes = arrived_ref[block, :, 3 * HD :].astype(jnp.float32)
        at = s * STAT_LANES
        one = [lanes[:, at + i : at + i + 1] for i in range(6)]
        return one[0] + one[1] + one[2], one[3] + one[4] + one[5]

    def numerator(block, s):
        return arrived_ref[block, :, s * HD : (s + 1) * HD].astype(jnp.float32)

    jobs = [(plan_ref[PLAN_SLOT + s], s, list(range(n_blocks))) for s in range(2)]
    for i in range(2):
        jobs.append((plan_ref[PLAN_SHORT + i], 2, [plan_ref[PLAN_OWNER + i]]))
    for r, s, blocks in jobs:
        self_score, value_self = self_terms(r)
        stats = [stat(b, s) for b in blocks]
        final_top = self_score
        for _, top in stats:
            final_top = jnp.maximum(final_top, top)
        self_weight = jnp.exp(self_score - final_top)
        denominator = self_weight
        numer = self_weight * value_self
        for b, (total, top) in zip(blocks, stats):
            fade = jnp.exp(top - final_top)
            denominator = denominator + total * fade
            numer = numer + numerator(b, s) * fade
        attended_ref[r] = numer / denominator
    attended = jnp.concatenate([attended_ref[:, h, :] for h in range(heads)], axis=1)
    head_ref[...] = jnp.dot(
        attended.astype(jnp.bfloat16), w_ref[...], preferred_element_type=jnp.float32
    )


def up_kernel(x_ref, part_ref, peer_ref, gain_ref, w_ref, hidden_ref, mine_ref, other_ref):
    core = lax.axis_index("core")
    attn_out = part_ref[...] + peer_ref[...]
    hidden_state = (x_ref[...].astype(jnp.float32) + attn_out).astype(jnp.bfloat16)
    resid_rows = hidden_state.astype(jnp.float32)
    hidden_ref[...] = resid_rows
    scaled_mlp = (resid_rows * gain_ref[...]).astype(jnp.bfloat16)
    squares = jnp.sum(resid_rows * resid_rows, axis=1, keepdims=True)
    up_part = jnp.dot(scaled_mlp, w_ref[...], preferred_element_type=jnp.float32)
    half = up_part.shape[1] // 2
    low, high = up_part[:, :half], up_part[:, half:]
    mine_ref[:, :half] = jnp.where(core == 0, low, high)
    other_ref[:, :half] = jnp.where(core == 0, high, low)
    square_cols = jnp.broadcast_to(squares, (resid_rows.shape[0], LANES))
    mine_ref[:, half:] = square_cols
    other_ref[:, half:] = square_cols


def down_kernel(own_ref, oth_ref, w_ref, out_ref):
    core = lax.axis_index("core")
    own, oth = own_ref[...], oth_ref[...]
    half = own.shape[1]
    low = jnp.where(core == 0, own, oth)
    high = jnp.where(core == 0, oth, own)
    out_ref[...] = jnp.dot(
        low, w_ref[:half, :], preferred_element_type=jnp.float32
    ) + jnp.dot(high, w_ref[half:, :], preferred_element_type=jnp.float32)


def per_device(
    hidden_in,
    attn_gain,
    mlp_gain,
    query_weight,
    key_weight,
    value_weight,
    out_weight,
    up_weight,
    down_weight,
    key_cache,
    value_cache,
    lengths,
    block_order,
    pad_mask,
):
    n_req, d_here = hidden_in.shape
    kv_here = key_cache.shape[2] // HD
    heads_here = kv_here * (H // KVH)
    n_chips = lax.axis_size("chip")
    core = lax.axis_index("core")
    n_blocks = 2 * n_chips
    half_qkv = (heads_here + 2 * kv_here) * HD // 2
    half_up = up_weight.shape[1] // 2

    chunk = key_weight.shape[1]
    n_chunks = 2 * half_qkv // chunk
    mine, other = local_kernel(
        qkv_kernel,
        [f32(n_req, half_qkv + LANES)] * 2,
        [hidden_in, attn_gain.reshape(1, d_here), query_weight, key_weight, value_weight],
        flops=4 * n_req * d_here * half_qkv,
        scratch=[
            pltpu.VMEM(hidden_in.shape, hidden_in.dtype),
            pltpu.VMEM((1, d_here), jnp.float32),
        ]
        + [pltpu.VMEM((d_here, chunk), jnp.bfloat16)] * n_chunks
        + [pltpu.SemaphoreType.DMA((2 + n_chunks,))],
        in_hbm=range(5),
    )
    pair_sum = mine + swap(other, "core")
    plain = [out_weight, pad_mask, hidden_in, mlp_gain.reshape(1, d_here)]
    span_here = pad_mask.shape[1]
    slots = bf16(3, span_here, key_cache.shape[2])
    plan, keys, values, out_w, mask, x_rows, gain = local_kernel(
        prefetch_kernel,
        [pltpu.SMEM((PLAN_SIZE,), jnp.int32), slots, slots]
        + [pltpu.VMEM(x.shape, x.dtype) for x in plain],
        [pair_sum, lengths, block_order, key_cache, value_cache] + plain,
        flops=0,
        scratch=[pltpu.SemaphoreType.DMA((6 + len(plain),))],
        in_hbm=range(3, 5 + len(plain)),
    )
    (qkv_half,) = local_kernel(
        qkv_sum_kernel,
        [bf16(n_req, half_qkv)],
        [gather_all(pair_sum, "chip", n_chips), plan],
        flops=n_chips * n_req * half_qkv,
    )
    qkv_other = swap(qkv_half, "core")

    message, query_heads, key_heads, value_heads = local_kernel(
        attention_kernel,
        [bf16(n_blocks, heads_here, 3 * HD + LANES)] + [f32(n_req, heads_here, HD)] * 3,
        [qkv_half, qkv_other, keys, values, mask, plan],
        flops=12 * heads_here * kv_here * HD * span_here,
    )
    arrived = lax.all_to_all(message, ("chip", "core"), 0, 0)
    (head_part,) = local_kernel(
        combine_kernel,
        [f32(n_req, d_here)],
        [arrived, query_heads, key_heads, value_heads, out_w, plan],
        flops=2 * n_req * out_weight.size,
        scratch=[pltpu.VMEM((n_req, heads_here, HD), jnp.float32)],
    )
    head_peer = swap(head_part, "tp")
    (up_w,) = local_kernel(
        copy_kernel,
        [bf16(*up_weight.shape)],
        [head_part, up_weight],
        flops=0,
        scratch=[pltpu.SemaphoreType.DMA],
        in_hbm=(1,),
    )

    resid_rows, up_mine, up_other = local_kernel(
        up_kernel,
        [f32(n_req, d_here)] + [f32(n_req, half_up + LANES)] * 2,
        [x_rows, head_part, head_peer, gain, up_w],
        flops=2 * n_req * up_weight.size,
    )
    up_pair = up_mine + swap(up_other, "core")
    square_sum = up_pair[:, half_up : half_up + 1]
    piece_0 = lax.reduce_precision(square_sum, 8, 7)
    piece_1 = lax.reduce_precision(square_sum - piece_0, 8, 7)
    piece_2 = square_sum - piece_0 - piece_1
    pieces = jnp.pad(
        jnp.concatenate([piece_0, piece_1, piece_2], axis=1), ((0, 0), (0, LANES - 3))
    )
    up_message = jnp.concatenate([up_pair[:, :half_up], pieces], axis=1).astype(jnp.bfloat16)
    up_sum = jnp.sum(gather_all(up_message, "chip", n_chips).astype(jnp.float32), axis=0)
    squares = jnp.sum(up_sum[:, half_up:], axis=1, keepdims=True)
    inv_mlp = lax.rsqrt(squares / D + NORM_EPS)
    active_half = squared_relu(up_sum[:, :half_up] * inv_mlp).astype(jnp.bfloat16)
    active_other = swap(active_half, "core")
    (down_part,) = local_kernel(
        down_kernel,
        [f32(n_req, d_here)],
        [active_half, active_other, down_weight],
        flops=2 * n_req * down_weight.size,
        anywhere=(2,),
    )
    mlp_out = sum_tp(down_part)
    return (resid_rows + mlp_out).astype(jnp.bfloat16)


def solution(mesh):
    n_seq, n_tp = mesh.shape["seq"], mesh.shape["tp"]
    split = Mesh(mesh.devices.reshape(n_seq // 2, 2, n_tp), ("chip", "core", "tp"))
    seq = ("chip", "core")
    whole_tiles = n_tp == 2 and KVH % (2 * n_tp) == 0 and D % (n_seq * LANES) == 0
    return jax.shard_map(
        per_device if whole_tiles else per_device_plain,
        mesh=split,
        in_specs=(
            P(None, seq),
            P(seq),
            P(seq),
            P(seq, "tp"),
            P(seq, "tp"),
            P(seq, "tp"),
            P("tp", seq),
            P(seq, "tp"),
            P("tp", seq),
            P(None, seq, "tp"),
            P(None, seq, "tp"),
            P(),
            P(),
            P(None, seq),
        ),
        out_specs=P(None, seq),
        check_vma=False,
    )
```

```python
import math

import jax
import jax.numpy as jnp
from jax import lax
from jax.experimental import pallas as pl
from jax.experimental.pallas import tpu as pltpu
from jax.sharding import Mesh, PartitionSpec as P

D = 4096
H = 32
KVH = 8
HD = 128


NORM_EPS = 1e-05
MASKED = -1e30
LANES = 128


def squared_relu(values_in):
    positive = jnp.maximum(values_in, 0.0)
    return positive * positive


def swap(values_in, axis):
    n = lax.axis_size(axis)
    return lax.ppermute(values_in, axis, [(i, i ^ 1) for i in range(n)])


def gather_all(values_in, axes, n):
    copies = jnp.broadcast_to(values_in[None], (n,) + values_in.shape)
    return lax.all_to_all(copies, axes, 0, 0)


def sum_tp(values_in):
    n = lax.axis_size("tp")
    if n == 2:
        return values_in + swap(values_in, "tp")
    return lax.psum(values_in, "tp")


def per_device_plain(
    hidden_in,
    attn_gain,
    mlp_gain,
    query_weight,
    key_weight,
    value_weight,
    out_weight,
    up_weight,
    down_weight,
    key_cache,
    value_cache,
    lengths,
    block_order,
    pad_mask,
):
    n_req = hidden_in.shape[0]
    q_per_kv = H // KVH
    kv_here = key_cache.shape[2] // HD
    span_here = key_cache.shape[1]
    heads_here = kv_here * q_per_kv
    n_chips = lax.axis_size("chip")
    core = lax.axis_index("core")
    n_blocks = 2 * n_chips
    my_block = 2 * lax.axis_index("chip") + core
    score_scale = 1.0 / math.sqrt(HD)

    x_rows = hidden_in.astype(jnp.float32)
    scaled_in = (x_rows * attn_gain).astype(jnp.bfloat16)
    sq_attn = jnp.sum(x_rows * x_rows, axis=1, keepdims=True)
    proj_query = jnp.dot(scaled_in, query_weight, preferred_element_type=jnp.float32)
    proj_key = jnp.dot(scaled_in, key_weight, preferred_element_type=jnp.float32)
    proj_value = jnp.dot(scaled_in, value_weight, preferred_element_type=jnp.float32)
    half_q, half_kv = proj_query.shape[1] // 2, proj_key.shape[1] // 2
    square_cols = jnp.broadcast_to(sq_attn, (n_req, LANES))

    def half(i):
        return jnp.concatenate(
            [
                proj_query[:, i * half_q : (i + 1) * half_q],
                proj_key[:, i * half_kv : (i + 1) * half_kv],
                proj_value[:, i * half_kv : (i + 1) * half_kv],
                square_cols,
            ],
            axis=1,
        )

    low, high = half(0), half(1)
    mine = jnp.where(core == 0, low, high)
    other = jnp.where(core == 0, high, low)
    pair_sum = mine + swap(other, "core")
    qkv_sum = jnp.sum(gather_all(pair_sum, "chip", n_chips), axis=0)
    inv_attn = lax.rsqrt(qkv_sum[:, -1:] / D + NORM_EPS)
    qkv_half = (qkv_sum[:, :-LANES] * inv_attn).astype(jnp.bfloat16)
    qkv_other = swap(qkv_half, "core")
    qkv_low = jnp.where(core == 0, qkv_half, qkv_other)
    qkv_high = jnp.where(core == 0, qkv_other, qkv_half)

    def both(start, size):
        return jnp.concatenate(
            [qkv_low[:, start : start + size], qkv_high[:, start : start + size]], axis=1
        )

    query_rows = both(0, half_q)
    key_new = both(half_q, half_kv)
    value_new = both(half_q + half_kv, half_kv)

    first_block = block_order % n_blocks
    position = ((my_block - first_block) % n_blocks)[:, None] * span_here + jnp.arange(
        span_here, dtype=jnp.int32
    )[None, :]
    live_slots = ((position < lengths[:, None]) & (pad_mask == 1))[:, None, None, :]
    q_groups = query_rows.reshape(n_req, kv_here, q_per_kv, HD)
    keys_here = key_cache.reshape(n_req, span_here, kv_here, HD)
    values_here = value_cache.reshape(n_req, span_here, kv_here, HD)
    scores = (
        jnp.einsum("rkgd,rtkd->rkgt", q_groups, keys_here, preferred_element_type=jnp.float32)
        * score_scale
    )
    scores = jnp.where(live_slots, scores, MASKED)
    local_top = jnp.max(scores, axis=3, keepdims=True)
    weights = jnp.where(live_slots, jnp.exp(scores - local_top), 0.0)
    local_total = jnp.sum(weights, axis=3, keepdims=True)
    local_out = jnp.einsum(
        "rkgt,rtkd->rkgd",
        weights.astype(jnp.bfloat16),
        values_here,
        preferred_element_type=jnp.float32,
    )
    numer = local_out.reshape(n_req, heads_here, HD)
    stats = jnp.concatenate(
        [
            local_total.reshape(n_req, heads_here, 1),
            local_top.reshape(n_req, heads_here, 1),
        ],
        axis=2,
    )
    stat_rows = stats.reshape(n_req, heads_here * 2)
    pad = (-stat_rows.shape[1]) % LANES
    message = jnp.concatenate(
        [numer.reshape(n_req, heads_here * HD), jnp.pad(stat_rows, ((0, 0), (0, pad)))], axis=1
    )
    arrived = gather_all(message, ("chip", "core"), n_blocks)
    outs = arrived[:, :, : heads_here * HD].reshape(n_blocks, n_req, heads_here, HD)
    stats_all = arrived[:, :, heads_here * HD : heads_here * (HD + 2)].reshape(
        n_blocks, n_req, heads_here, 2
    )
    totals, tops = stats_all[..., 0], stats_all[..., 1]
    self_score = (
        jnp.einsum(
            "rkgd,rkd->rkg",
            q_groups,
            key_new.reshape(n_req, kv_here, HD),
            preferred_element_type=jnp.float32,
        )
        * score_scale
    ).reshape(n_req, heads_here)
    final_top = jnp.maximum(jnp.max(tops, axis=0), self_score)
    fades = jnp.exp(tops - final_top)
    self_weight = jnp.exp(self_score - final_top)
    denominator = jnp.sum(totals * fades, axis=0) + self_weight
    value_self = jnp.broadcast_to(
        value_new.reshape(n_req, kv_here, 1, HD), (n_req, kv_here, q_per_kv, HD)
    ).reshape(n_req, heads_here, HD)
    numerator = jnp.sum(outs * fades[..., None], axis=0) + self_weight[
        ..., None
    ] * value_self.astype(jnp.float32)
    attended = (
        (numerator / denominator[..., None])
        .reshape(n_req, heads_here * HD)
        .astype(jnp.bfloat16)
    )
    head_part = jnp.dot(attended, out_weight, preferred_element_type=jnp.float32)
    attn_out = sum_tp(head_part)
    hidden_state = (x_rows + attn_out).astype(jnp.bfloat16)

    resid_rows = hidden_state.astype(jnp.float32)
    scaled_mlp = (resid_rows * mlp_gain).astype(jnp.bfloat16)
    sq_mlp = jnp.sum(resid_rows * resid_rows, axis=1, keepdims=True)
    up_part = jnp.dot(scaled_mlp, up_weight, preferred_element_type=jnp.float32)
    half_up = up_part.shape[1] // 2
    up_low, up_high = up_part[:, :half_up], up_part[:, half_up:]
    square_cols = jnp.broadcast_to(sq_mlp, (n_req, LANES))
    up_mine = jnp.concatenate([jnp.where(core == 0, up_low, up_high), square_cols], axis=1)
    up_other = jnp.concatenate([jnp.where(core == 0, up_high, up_low), square_cols], axis=1)
    up_pair = up_mine + swap(up_other, "core")
    square_sum = up_pair[:, half_up : half_up + 1]
    piece_0 = lax.reduce_precision(square_sum, 8, 7)
    piece_1 = lax.reduce_precision(square_sum - piece_0, 8, 7)
    piece_2 = square_sum - piece_0 - piece_1
    pieces = jnp.pad(
        jnp.concatenate([piece_0, piece_1, piece_2], axis=1), ((0, 0), (0, LANES - 3))
    )
    up_message = jnp.concatenate([up_pair[:, :half_up], pieces], axis=1).astype(jnp.bfloat16)
    up_sum = jnp.sum(gather_all(up_message, "chip", n_chips).astype(jnp.float32), axis=0)
    squares = jnp.sum(up_sum[:, half_up:], axis=1, keepdims=True)
    inv_mlp = lax.rsqrt(squares / D + NORM_EPS)
    active_half = squared_relu(up_sum[:, :half_up] * inv_mlp).astype(jnp.bfloat16)
    active_other = swap(active_half, "core")
    activated = jnp.concatenate(
        [
            jnp.where(core == 0, active_half, active_other),
            jnp.where(core == 0, active_other, active_half),
        ],
        axis=1,
    )
    down_part = jnp.dot(activated, down_weight, preferred_element_type=jnp.float32)
    mlp_out = sum_tp(down_part)
    return (resid_rows + mlp_out).astype(jnp.bfloat16)


IN_VMEM = pl.BlockSpec(memory_space=pltpu.VMEM)


def local_kernel(kernel, outs, operands, flops, scratch=(), in_hbm=(), anywhere=()):
    in_specs, placed, moved = [], [], 0
    for i, x in enumerate(operands):
        space = pltpu.HBM if i in in_hbm else pltpu.VMEM
        in_specs.append(pl.BlockSpec(memory_space=space))
        placed.append(x if i in anywhere else pltpu.with_memory_space_constraint(x, space))
        moved += x.size * x.dtype.itemsize
    return pl.pallas_call(
        kernel,
        out_shape=outs,
        in_specs=in_specs,
        out_specs=[IN_VMEM] * len(outs),
        scratch_shapes=scratch,
        compiler_params=pltpu.CompilerParams(vmem_limit_bytes=6 * 2**20),
        cost_estimate=pl.CostEstimate(flops=flops, bytes_accessed=moved, transcendentals=0),
    )(*placed)


def f32(*shape):
    return pltpu.VMEM(shape, jnp.float32)


def bf16(*shape):
    return pltpu.VMEM(shape, jnp.bfloat16)


def pieces_of(values_in):
    first = values_in.astype(jnp.bfloat16).astype(jnp.float32)
    second = (values_in - first).astype(jnp.bfloat16).astype(jnp.float32)
    return first, second, values_in - first - second


def qkv_kernel(
    x_hbm, gain_hbm, wq_hbm, wk_hbm, wv_hbm, mine_ref, other_ref, x_ref, gain_ref, *scratch
):
    core = lax.axis_index("core")
    w_refs, sems = scratch[:-1], scratch[-1]
    chunk = w_refs[0].shape[1]
    copies = [
        pltpu.make_async_copy(x_hbm, x_ref, sems.at[0]),
        pltpu.make_async_copy(gain_hbm, gain_ref, sems.at[1]),
    ]
    pieces = [(w, at) for w in (wq_hbm, wk_hbm, wv_hbm) for at in range(0, w.shape[1], chunk)]
    for (w_hbm, at), w_ref in zip(pieces, w_refs):
        copies.append(
            pltpu.make_async_copy(
                w_hbm.at[:, pl.ds(at, chunk)], w_ref, sems.at[len(copies)]
            )
        )
    for copy in copies:
        copy.start()
    copies[0].wait()
    copies[1].wait()
    x_rows = x_ref[...].astype(jnp.float32)
    scaled_in = (x_rows * gain_ref[...]).astype(jnp.bfloat16)
    squares = jnp.sum(x_rows * x_rows, axis=1, keepdims=True)
    proj = []
    for w_ref, copy in zip(w_refs, copies[2:]):
        copy.wait()
        proj.append(jnp.dot(scaled_in, w_ref[...], preferred_element_type=jnp.float32))
    proj = jnp.concatenate(proj, axis=1)
    at, start = 0, 0
    for w_hbm in (wq_hbm, wk_hbm, wv_hbm):
        half = w_hbm.shape[1] // 2
        low, high = proj[:, start : start + half], proj[:, start + half : start + 2 * half]
        mine_ref[:, at : at + half] = jnp.where(core == 0, low, high)
        other_ref[:, at : at + half] = jnp.where(core == 0, high, low)
        at += half
        start += 2 * half
    square_cols = jnp.broadcast_to(squares, (x_rows.shape[0], LANES))
    mine_ref[:, at:] = square_cols
    other_ref[:, at:] = square_cols


def qkv_sum_kernel(arrived_ref, live_ref, out_ref):
    total = arrived_ref[0]
    for i in range(1, arrived_ref.shape[0]):
        total = total + arrived_ref[i]
    width = out_ref.shape[1]
    inv_attn = lax.rsqrt(total[:, width : width + 1] / D + NORM_EPS)
    out_ref[...] = (total[:, :width] * inv_attn).astype(jnp.bfloat16)


def prefetch_kernel(
    after_ref, key_hbm, key_peer, value_hbm, value_peer, mask_hbm, mask_peer, lengths_hbm,
    order_hbm, *refs,
):
    n_plain = (len(refs) - 7) // 2
    plain_in, refs = refs[:n_plain], refs[n_plain:]
    key_ref, value_ref, live_ref = refs[:3]
    plain_out, (mask_ref, lengths_ref, order_ref, sems) = refs[3:-4], refs[-4:]
    core = lax.axis_index("core")
    n_blocks = lax.axis_size("chip") * 2
    my_block = 2 * lax.axis_index("chip") + core
    span = key_hbm.shape[1]
    half = key_ref.shape[2]
    heads = pl.ds(pl.multiple_of(core * half, LANES), half)
    pairs = [(lengths_hbm, lengths_ref), (order_hbm, order_ref)]
    for i, mask in enumerate((mask_hbm, mask_peer)):
        pairs.append((mask, mask_ref.at[i]))
    for i, (key, value) in enumerate(((key_hbm, value_hbm), (key_peer, value_peer))):
        slots = pl.ds(i * span, span)
        pairs.append((key.at[:, :, heads], key_ref.at[:, slots, :]))
        pairs.append((value.at[:, :, heads], value_ref.at[:, slots, :]))
    pairs += list(zip(plain_in, plain_out))
    copies = [pltpu.make_async_copy(src, dst, sems.at[i]) for i, (src, dst) in enumerate(pairs)]
    for copy in copies:
        copy.start()
    for copy in copies[:4]:
        copy.wait()
    slot = lax.broadcasted_iota(jnp.int32, (1, span), 1)
    for i, block in enumerate((my_block, my_block + 1 - 2 * core)):
        for r in range(live_ref.shape[0]):
            first_block = lax.rem(order_ref[r], n_blocks)
            begin = lax.rem(block - first_block + n_blocks, n_blocks) * span
            live = (begin + slot < lengths_ref[r]) & (mask_ref[i, r : r + 1, :] == 1)
            live_ref[r : r + 1, i * span : (i + 1) * span] = live.astype(jnp.int32)
    for copy in copies[4:]:
        copy.wait()


PIECE = 16
TOP_AT = 3 * PIECE


def attention_kernel(
    qkv_ref, key_ref, value_ref, live_ref, message_ref, query_ref, key_new_ref, value_new_ref
):
    n_copies, heads, _ = message_ref.shape
    n_req = live_ref.shape[0]
    kv_half = key_ref.shape[2] // HD
    group = heads // kv_half
    is_first = lax.axis_index("chip") == 0
    qkv = qkv_ref[...].astype(jnp.float32)
    for h in range(heads):
        query_ref[:, h, :] = qkv[:, h * HD : (h + 1) * HD]
        at = (heads + h // group) * HD
        key_new_ref[:, h, :] = qkv[:, at : at + HD]
        at += kv_half * HD
        value_new_ref[:, h, :] = qkv[:, at : at + HD]

    group_of = lax.broadcasted_iota(jnp.int32, (heads, HD), 0) // group
    lane = lax.broadcasted_iota(jnp.int32, (heads, LANES), 1)
    stats = jnp.zeros((heads, LANES), jnp.float32)
    parts = []
    for r in range(n_req):
        live = live_ref[r : r + 1, :] == 1
        query = query_ref[r]
        spread = jnp.concatenate(
            [jnp.where(group_of == k, query, 0.0) for k in range(kv_half)], axis=1
        ).astype(jnp.bfloat16)
        scores = lax.dot_general(
            spread, key_ref[r], (((1,), (1,)), ((), ())), preferred_element_type=jnp.float32
        ) * (1.0 / math.sqrt(HD))
        scores = jnp.where(live, scores, MASKED)
        self_score = jnp.sum(query * key_new_ref[r], axis=1, keepdims=True) * (
            1.0 / math.sqrt(HD)
        )
        top = jnp.max(scores, axis=1, keepdims=True)
        top = jnp.where(is_first, jnp.maximum(top, self_score), top)
        weights = jnp.where(live, jnp.exp(scores - top), 0.0)
        self_weight = jnp.where(is_first, jnp.exp(jnp.minimum(self_score - top, 0.0)), 0.0)
        total = jnp.sum(weights, axis=1, keepdims=True) + self_weight
        wide = jnp.dot(
            weights.astype(jnp.bfloat16), value_ref[r], preferred_element_type=jnp.float32
        )
        numer = self_weight * value_new_ref[r]
        for k in range(kv_half):
            numer = numer + jnp.where(group_of == k, wide[:, k * HD : (k + 1) * HD], 0.0)
        parts.append(numer)
        for p, piece in enumerate(pieces_of(total)):
            stats = jnp.where(lane == p * PIECE + r, piece, stats)
        for p, piece in enumerate(pieces_of(top)):
            stats = jnp.where(lane == TOP_AT + p * PIECE + r, piece, stats)
    message = jnp.concatenate(parts + [stats], axis=1).astype(jnp.bfloat16)
    for i in range(n_copies):
        message_ref[i] = message


def combine_kernel(arrived_ref, w_ref, head_ref, attended_ref):
    n_blocks, heads, width = arrived_ref.shape
    n_req = head_ref.shape[0]
    for c in range(2):
        blocks = range(c, n_blocks, 2)
        totals, tops = [], []
        for b in blocks:
            tile = arrived_ref[b, :, width - LANES :].astype(jnp.float32)
            tile = (
                tile
                + pltpu.roll(tile, LANES - PIECE, 1)
                + pltpu.roll(tile, LANES - 2 * PIECE, 1)
            )
            totals.append(tile)
            tops.append(pltpu.roll(tile, LANES - TOP_AT, 1))
        final_top = tops[0]
        for top in tops[1:]:
            final_top = jnp.maximum(final_top, top)
        fades = [jnp.exp(top - final_top) for top in tops]
        denominator = totals[0] * fades[0]
        for total, fade in zip(totals[1:], fades[1:]):
            denominator = denominator + total * fade
        for r in range(n_req):
            numer = jnp.zeros((heads, HD), jnp.float32)
            for b, fade in zip(blocks, fades):
                part = arrived_ref[b, :, r * HD : (r + 1) * HD].astype(jnp.float32)
                numer = numer + part * fade[:, r : r + 1]
            attended_ref[r, c * heads : (c + 1) * heads, :] = numer / denominator[:, r : r + 1]
    attended = jnp.concatenate([attended_ref[:, h, :] for h in range(2 * heads)], axis=1)
    head_ref[...] = jnp.dot(
        attended.astype(jnp.bfloat16), w_ref[...], preferred_element_type=jnp.float32
    )


def copy_kernel(after_ref, w_hbm, w_ref, sem):
    copy = pltpu.make_async_copy(w_hbm, w_ref, sem)
    copy.start()
    copy.wait()


def up_kernel(x_ref, part_ref, peer_ref, gain_ref, w_ref, hidden_ref, mine_ref, other_ref):
    core = lax.axis_index("core")
    attn_out = part_ref[...] + peer_ref[...]
    hidden_state = (x_ref[...].astype(jnp.float32) + attn_out).astype(jnp.bfloat16)
    resid_rows = hidden_state.astype(jnp.float32)
    hidden_ref[...] = resid_rows
    scaled_mlp = (resid_rows * gain_ref[...]).astype(jnp.bfloat16)
    squares = jnp.sum(resid_rows * resid_rows, axis=1, keepdims=True)
    up_part = jnp.dot(scaled_mlp, w_ref[...], preferred_element_type=jnp.float32)
    half = up_part.shape[1] // 2
    low, high = up_part[:, :half], up_part[:, half:]
    mine_ref[:, :half] = jnp.where(core == 0, low, high)
    other_ref[:, :half] = jnp.where(core == 0, high, low)
    square_cols = jnp.broadcast_to(squares, (resid_rows.shape[0], LANES))
    mine_ref[:, half:] = square_cols
    other_ref[:, half:] = square_cols


def down_kernel(own_ref, oth_ref, w_ref, out_ref):
    core = lax.axis_index("core")
    own, oth = own_ref[...], oth_ref[...]
    half = own.shape[1]
    low = jnp.where(core == 0, own, oth)
    high = jnp.where(core == 0, oth, own)
    out_ref[...] = jnp.dot(
        low, w_ref[:half, :], preferred_element_type=jnp.float32
    ) + jnp.dot(high, w_ref[half:, :], preferred_element_type=jnp.float32)


def per_device(
    hidden_in,
    attn_gain,
    mlp_gain,
    query_weight,
    key_weight,
    value_weight,
    out_weight,
    up_weight,
    down_weight,
    key_cache,
    value_cache,
    lengths,
    block_order,
    pad_mask,
):
    n_req, d_here = hidden_in.shape
    kv_here = key_cache.shape[2] // HD
    heads_here = kv_here * (H // KVH)
    n_chips = lax.axis_size("chip")
    core = lax.axis_index("core")
    n_blocks = 2 * n_chips
    half_qkv = (heads_here + 2 * kv_here) * HD // 2
    half_up = up_weight.shape[1] // 2

    chunk = key_weight.shape[1]
    n_chunks = 2 * half_qkv // chunk
    mine, other = local_kernel(
        qkv_kernel,
        [f32(n_req, half_qkv + LANES)] * 2,
        [hidden_in, attn_gain.reshape(1, d_here), query_weight, key_weight, value_weight],
        flops=4 * n_req * d_here * half_qkv,
        scratch=[
            pltpu.VMEM(hidden_in.shape, hidden_in.dtype),
            pltpu.VMEM((1, d_here), jnp.float32),
        ]
        + [pltpu.VMEM((d_here, chunk), jnp.bfloat16)] * n_chunks
        + [pltpu.SemaphoreType.DMA((2 + n_chunks,))],
        in_hbm=range(5),
    )
    pair_sum, key_own, value_own, mask_own = lax.optimization_barrier(
        (mine + swap(other, "core"), key_cache, value_cache, pad_mask)
    )
    key_peer, value_peer, mask_peer = (swap(x, "core") for x in (key_own, value_own, mask_own))
    plain = [out_weight, hidden_in, mlp_gain.reshape(1, d_here)]
    span_here = pad_mask.shape[1]
    slots = bf16(n_req, 2 * span_here, key_cache.shape[2] // 2)
    caches = [key_cache, key_peer, value_cache, value_peer, pad_mask, mask_peer]
    caches += [lengths, block_order]
    keys, values, live, out_w, x_rows, gain = local_kernel(
        prefetch_kernel,
        [slots, slots, pltpu.VMEM((n_req, 2 * span_here), jnp.int32)]
        + [pltpu.VMEM(x.shape, x.dtype) for x in plain],
        [pair_sum] + caches + plain,
        flops=0,
        scratch=[
            pltpu.VMEM((2, n_req, span_here), jnp.int32),
            pltpu.SMEM(lengths.shape, jnp.int32),
            pltpu.SMEM(block_order.shape, jnp.int32),
            pltpu.SemaphoreType.DMA((len(caches) + len(plain),)),
        ],
        in_hbm=range(1, 1 + len(caches) + len(plain)),
    )
    (qkv_half,) = local_kernel(
        qkv_sum_kernel,
        [bf16(n_req, half_qkv)],
        [gather_all(pair_sum, "chip", n_chips), live],
        flops=n_chips * n_req * half_qkv,
    )
    half_heads = heads_here // 2
    (message,) = local_kernel(
        attention_kernel,
        [bf16(n_blocks, half_heads, n_req * HD + LANES)],
        [qkv_half, keys, values, live],
        flops=4 * n_req * half_heads * kv_here * HD * span_here,
        scratch=[pltpu.VMEM((n_req, half_heads, HD), jnp.float32)] * 3,
    )
    arrived = lax.all_to_all(message, ("chip", "core"), 0, 0)
    (head_part,) = local_kernel(
        combine_kernel,
        [f32(n_req, d_here)],
        [arrived, out_w],
        flops=2 * n_req * out_weight.size,
        scratch=[pltpu.VMEM((n_req, heads_here, HD), jnp.float32)],
    )
    head_peer = swap(head_part, "tp")
    (up_w,) = local_kernel(
        copy_kernel,
        [bf16(*up_weight.shape)],
        [head_part, up_weight],
        flops=0,
        scratch=[pltpu.SemaphoreType.DMA],
        in_hbm=(1,),
    )

    resid_rows, up_mine, up_other = local_kernel(
        up_kernel,
        [f32(n_req, d_here)] + [f32(n_req, half_up + LANES)] * 2,
        [x_rows, head_part, head_peer, gain, up_w],
        flops=2 * n_req * up_weight.size,
    )
    up_pair = up_mine + swap(up_other, "core")
    square_sum = up_pair[:, half_up : half_up + 1]
    piece_0 = lax.reduce_precision(square_sum, 8, 7)
    piece_1 = lax.reduce_precision(square_sum - piece_0, 8, 7)
    piece_2 = square_sum - piece_0 - piece_1
    pieces = jnp.pad(
        jnp.concatenate([piece_0, piece_1, piece_2], axis=1), ((0, 0), (0, LANES - 3))
    )
    up_message = jnp.concatenate([up_pair[:, :half_up], pieces], axis=1).astype(jnp.bfloat16)
    up_sum = jnp.sum(gather_all(up_message, "chip", n_chips).astype(jnp.float32), axis=0)
    squares = jnp.sum(up_sum[:, half_up:], axis=1, keepdims=True)
    inv_mlp = lax.rsqrt(squares / D + NORM_EPS)
    active_half = squared_relu(up_sum[:, :half_up] * inv_mlp).astype(jnp.bfloat16)
    active_other = swap(active_half, "core")
    (down_part,) = local_kernel(
        down_kernel,
        [f32(n_req, d_here)],
        [active_half, active_other, down_weight],
        flops=2 * n_req * down_weight.size,
        anywhere=(2,),
    )
    mlp_out = sum_tp(down_part)
    return (resid_rows + mlp_out).astype(jnp.bfloat16)


def solution(mesh):
    n_seq, n_tp = mesh.shape["seq"], mesh.shape["tp"]
    split = Mesh(mesh.devices.reshape(n_seq // 2, 2, n_tp), ("chip", "core", "tp"))
    seq = ("chip", "core")
    whole_tiles = n_tp == 2 and KVH % (2 * n_tp) == 0 and D % (n_seq * LANES) == 0
    return jax.shard_map(
        per_device if whole_tiles else per_device_plain,
        mesh=split,
        in_specs=(
            P(None, seq),
            P(seq),
            P(seq),
            P(seq, "tp"),
            P(seq, "tp"),
            P(seq, "tp"),
            P("tp", seq),
            P(seq, "tp"),
            P("tp", seq),
            P(None, seq, "tp"),
            P(None, seq, "tp"),
            P(),
            P(),
            P(None, seq),
        ),
        out_specs=P(None, seq),
        check_vma=False,
    )
```

```python
import math

import jax
import jax.numpy as jnp
from jax import lax
from jax.experimental import pallas as pl
from jax.experimental.pallas import tpu as pltpu
from jax.sharding import Mesh, PartitionSpec as P

D = 4096
H = 32
KVH = 8
HD = 128


NORM_EPS = 1e-05
MASKED = -1e30
LANES = 128


def squared_relu(values_in):
    positive = jnp.maximum(values_in, 0.0)
    return positive * positive


def swap(values_in, axis):
    n = lax.axis_size(axis)
    return lax.ppermute(values_in, axis, [(i, i ^ 1) for i in range(n)])


def gather_all(values_in, axes, n):
    copies = jnp.broadcast_to(values_in[None], (n,) + values_in.shape)
    return lax.all_to_all(copies, axes, 0, 0)


def sum_tp(values_in):
    n = lax.axis_size("tp")
    if n == 2:
        return values_in + swap(values_in, "tp")
    return lax.psum(values_in, "tp")


def per_device_plain(
    hidden_in,
    attn_gain,
    mlp_gain,
    query_weight,
    key_weight,
    value_weight,
    out_weight,
    up_weight,
    down_weight,
    key_cache,
    value_cache,
    lengths,
    block_order,
    pad_mask,
):
    n_req = hidden_in.shape[0]
    q_per_kv = H // KVH
    kv_here = key_cache.shape[2] // HD
    span_here = key_cache.shape[1]
    heads_here = kv_here * q_per_kv
    n_chips = lax.axis_size("chip")
    core = lax.axis_index("core")
    n_blocks = 2 * n_chips
    my_block = 2 * lax.axis_index("chip") + core
    score_scale = 1.0 / math.sqrt(HD)

    x_rows = hidden_in.astype(jnp.float32)
    scaled_in = (x_rows * attn_gain).astype(jnp.bfloat16)
    sq_attn = jnp.sum(x_rows * x_rows, axis=1, keepdims=True)
    proj_query = jnp.dot(scaled_in, query_weight, preferred_element_type=jnp.float32)
    proj_key = jnp.dot(scaled_in, key_weight, preferred_element_type=jnp.float32)
    proj_value = jnp.dot(scaled_in, value_weight, preferred_element_type=jnp.float32)
    half_q, half_kv = proj_query.shape[1] // 2, proj_key.shape[1] // 2
    square_cols = jnp.broadcast_to(sq_attn, (n_req, LANES))

    def half(i):
        return jnp.concatenate(
            [
                proj_query[:, i * half_q : (i + 1) * half_q],
                proj_key[:, i * half_kv : (i + 1) * half_kv],
                proj_value[:, i * half_kv : (i + 1) * half_kv],
                square_cols,
            ],
            axis=1,
        )

    low, high = half(0), half(1)
    mine = jnp.where(core == 0, low, high)
    other = jnp.where(core == 0, high, low)
    pair_sum = mine + swap(other, "core")
    qkv_sum = jnp.sum(gather_all(pair_sum, "chip", n_chips), axis=0)
    inv_attn = lax.rsqrt(qkv_sum[:, -1:] / D + NORM_EPS)
    qkv_half = (qkv_sum[:, :-LANES] * inv_attn).astype(jnp.bfloat16)
    qkv_other = swap(qkv_half, "core")
    qkv_low = jnp.where(core == 0, qkv_half, qkv_other)
    qkv_high = jnp.where(core == 0, qkv_other, qkv_half)

    def both(start, size):
        return jnp.concatenate(
            [qkv_low[:, start : start + size], qkv_high[:, start : start + size]], axis=1
        )

    query_rows = both(0, half_q)
    key_new = both(half_q, half_kv)
    value_new = both(half_q + half_kv, half_kv)

    first_block = block_order % n_blocks
    position = ((my_block - first_block) % n_blocks)[:, None] * span_here + jnp.arange(
        span_here, dtype=jnp.int32
    )[None, :]
    live_slots = ((position < lengths[:, None]) & (pad_mask == 1))[:, None, None, :]
    q_groups = query_rows.reshape(n_req, kv_here, q_per_kv, HD)
    keys_here = key_cache.reshape(n_req, span_here, kv_here, HD)
    values_here = value_cache.reshape(n_req, span_here, kv_here, HD)
    scores = (
        jnp.einsum("rkgd,rtkd->rkgt", q_groups, keys_here, preferred_element_type=jnp.float32)
        * score_scale
    )
    scores = jnp.where(live_slots, scores, MASKED)
    local_top = jnp.max(scores, axis=3, keepdims=True)
    weights = jnp.where(live_slots, jnp.exp(scores - local_top), 0.0)
    local_total = jnp.sum(weights, axis=3, keepdims=True)
    local_out = jnp.einsum(
        "rkgt,rtkd->rkgd",
        weights.astype(jnp.bfloat16),
        values_here,
        preferred_element_type=jnp.float32,
    )
    numer = local_out.reshape(n_req, heads_here, HD)
    stats = jnp.concatenate(
        [
            local_total.reshape(n_req, heads_here, 1),
            local_top.reshape(n_req, heads_here, 1),
        ],
        axis=2,
    )
    stat_rows = stats.reshape(n_req, heads_here * 2)
    pad = (-stat_rows.shape[1]) % LANES
    message = jnp.concatenate(
        [numer.reshape(n_req, heads_here * HD), jnp.pad(stat_rows, ((0, 0), (0, pad)))], axis=1
    )
    arrived = gather_all(message, ("chip", "core"), n_blocks)
    outs = arrived[:, :, : heads_here * HD].reshape(n_blocks, n_req, heads_here, HD)
    stats_all = arrived[:, :, heads_here * HD : heads_here * (HD + 2)].reshape(
        n_blocks, n_req, heads_here, 2
    )
    totals, tops = stats_all[..., 0], stats_all[..., 1]
    self_score = (
        jnp.einsum(
            "rkgd,rkd->rkg",
            q_groups,
            key_new.reshape(n_req, kv_here, HD),
            preferred_element_type=jnp.float32,
        )
        * score_scale
    ).reshape(n_req, heads_here)
    final_top = jnp.maximum(jnp.max(tops, axis=0), self_score)
    fades = jnp.exp(tops - final_top)
    self_weight = jnp.exp(self_score - final_top)
    denominator = jnp.sum(totals * fades, axis=0) + self_weight
    value_self = jnp.broadcast_to(
        value_new.reshape(n_req, kv_here, 1, HD), (n_req, kv_here, q_per_kv, HD)
    ).reshape(n_req, heads_here, HD)
    numerator = jnp.sum(outs * fades[..., None], axis=0) + self_weight[
        ..., None
    ] * value_self.astype(jnp.float32)
    attended = (
        (numerator / denominator[..., None])
        .reshape(n_req, heads_here * HD)
        .astype(jnp.bfloat16)
    )
    head_part = jnp.dot(attended, out_weight, preferred_element_type=jnp.float32)
    attn_out = sum_tp(head_part)
    hidden_state = (x_rows + attn_out).astype(jnp.bfloat16)

    resid_rows = hidden_state.astype(jnp.float32)
    scaled_mlp = (resid_rows * mlp_gain).astype(jnp.bfloat16)
    sq_mlp = jnp.sum(resid_rows * resid_rows, axis=1, keepdims=True)
    up_part = jnp.dot(scaled_mlp, up_weight, preferred_element_type=jnp.float32)
    half_up = up_part.shape[1] // 2
    up_low, up_high = up_part[:, :half_up], up_part[:, half_up:]
    square_cols = jnp.broadcast_to(sq_mlp, (n_req, LANES))
    up_mine = jnp.concatenate([jnp.where(core == 0, up_low, up_high), square_cols], axis=1)
    up_other = jnp.concatenate([jnp.where(core == 0, up_high, up_low), square_cols], axis=1)
    up_pair = up_mine + swap(up_other, "core")
    square_sum = up_pair[:, half_up : half_up + 1]
    piece_0 = lax.reduce_precision(square_sum, 8, 7)
    piece_1 = lax.reduce_precision(square_sum - piece_0, 8, 7)
    piece_2 = square_sum - piece_0 - piece_1
    pieces = jnp.pad(
        jnp.concatenate([piece_0, piece_1, piece_2], axis=1), ((0, 0), (0, LANES - 3))
    )
    up_message = jnp.concatenate([up_pair[:, :half_up], pieces], axis=1).astype(jnp.bfloat16)
    up_sum = jnp.sum(gather_all(up_message, "chip", n_chips).astype(jnp.float32), axis=0)
    squares = jnp.sum(up_sum[:, half_up:], axis=1, keepdims=True)
    inv_mlp = lax.rsqrt(squares / D + NORM_EPS)
    active_half = squared_relu(up_sum[:, :half_up] * inv_mlp).astype(jnp.bfloat16)
    active_other = swap(active_half, "core")
    activated = jnp.concatenate(
        [
            jnp.where(core == 0, active_half, active_other),
            jnp.where(core == 0, active_other, active_half),
        ],
        axis=1,
    )
    down_part = jnp.dot(activated, down_weight, preferred_element_type=jnp.float32)
    mlp_out = sum_tp(down_part)
    return (resid_rows + mlp_out).astype(jnp.bfloat16)


IN_VMEM = pl.BlockSpec(memory_space=pltpu.VMEM)


def local_kernel(kernel, outs, operands, flops, scratch=(), in_hbm=(), anywhere=()):
    in_specs, placed, moved = [], [], 0
    for i, x in enumerate(operands):
        space = pltpu.HBM if i in in_hbm else pltpu.VMEM
        in_specs.append(pl.BlockSpec(memory_space=space))
        placed.append(x if i in anywhere else pltpu.with_memory_space_constraint(x, space))
        moved += x.size * x.dtype.itemsize
    return pl.pallas_call(
        kernel,
        out_shape=outs,
        in_specs=in_specs,
        out_specs=[IN_VMEM] * len(outs),
        scratch_shapes=scratch,
        compiler_params=pltpu.CompilerParams(vmem_limit_bytes=6 * 2**20),
        cost_estimate=pl.CostEstimate(flops=flops, bytes_accessed=moved, transcendentals=0),
    )(*placed)


def f32(*shape):
    return pltpu.VMEM(shape, jnp.float32)


def bf16(*shape):
    return pltpu.VMEM(shape, jnp.bfloat16)


def pieces_of(values_in):
    first = values_in.astype(jnp.bfloat16).astype(jnp.float32)
    second = (values_in - first).astype(jnp.bfloat16).astype(jnp.float32)
    return first, second, values_in - first - second


def qkv_kernel(
    x_hbm, gain_hbm, mlp_gain_hbm, mask_hbm, lengths_hbm, order_hbm, wq_hbm, wk_hbm, wv_hbm,
    mine_ref, other_ref, x_ref, mlp_gain_ref, live_ref,
    gain_ref, mask_ref, lengths_ref, order_ref, *scratch,
):
    core = lax.axis_index("core")
    n_blocks = lax.axis_size("chip") * 2
    my_block = 2 * lax.axis_index("chip") + core
    w_refs, sems = scratch[:-1], scratch[-1]
    small = [
        (x_hbm, x_ref), (gain_hbm, gain_ref), (mask_hbm, mask_ref), (lengths_hbm, lengths_ref),
        (order_hbm, order_ref), (mlp_gain_hbm, mlp_gain_ref),
    ]
    copies = [pltpu.make_async_copy(src, dst, sems.at[i]) for i, (src, dst) in enumerate(small)]
    for w_hbm, w_ref in zip((wk_hbm, wv_hbm, wq_hbm), w_refs):
        copies.append(pltpu.make_async_copy(w_hbm, w_ref, sems.at[len(copies)]))
    for copy in copies:
        copy.start()
    for copy in copies[: len(small)]:
        copy.wait()
    n_req, span = live_ref.shape
    slot = lax.broadcasted_iota(jnp.int32, (1, span), 1)
    for r in range(n_req):
        first_block = lax.rem(order_ref[r], n_blocks)
        begin = lax.rem(my_block - first_block + n_blocks, n_blocks) * span
        live = (begin + slot < lengths_ref[r]) & (mask_ref[r : r + 1, :] == 1)
        live_ref[r : r + 1, :] = live.astype(jnp.float32)
    x_rows = x_ref[...].astype(jnp.float32)
    scaled_in = (x_rows * gain_ref[...]).astype(jnp.bfloat16)
    squares = jnp.sum(x_rows * x_rows, axis=1, keepdims=True)
    proj = []
    for w_ref, copy in zip(w_refs, copies[len(small) :]):
        copy.wait()
        proj.append(jnp.dot(scaled_in, w_ref[...], preferred_element_type=jnp.float32))
    proj = jnp.concatenate([proj[2], proj[0], proj[1]], axis=1)
    at, start = 0, 0
    for w_hbm in (wq_hbm, wk_hbm, wv_hbm):
        half = w_hbm.shape[1] // 2
        low, high = proj[:, start : start + half], proj[:, start + half : start + 2 * half]
        mine_ref[:, at : at + half] = jnp.where(core == 0, low, high)
        other_ref[:, at : at + half] = jnp.where(core == 0, high, low)
        at += half
        start += 2 * half
    square_cols = jnp.broadcast_to(squares, (x_rows.shape[0], LANES))
    mine_ref[:, at:] = square_cols
    other_ref[:, at : at + LANES] = square_cols
    other_ref[:, at + LANES :] = live_ref[...]


def qkv_sum_kernel(arrived_ref, out_ref):
    total = arrived_ref[0]
    for i in range(1, arrived_ref.shape[0]):
        total = total + arrived_ref[i]
    width = out_ref.shape[1]
    inv_attn = lax.rsqrt(total[:, width : width + 1] / D + NORM_EPS)
    out_ref[...] = (total[:, :width] * inv_attn).astype(jnp.bfloat16)


PIECE = 16
TOP_AT = 3 * PIECE


def attention_kernel(
    qkv_ref, key_own, key_peer, value_own, value_peer, live_own, live_peer,
    message_ref, query_ref, key_new_ref, value_new_ref,
):
    n_copies, heads, _ = message_ref.shape
    n_req, span = live_own.shape
    half = key_own.shape[2] // 2
    mine = pl.ds(pl.multiple_of(lax.axis_index("core") * half, LANES), half)
    kv_half = half // HD
    group = heads // kv_half
    is_first = lax.axis_index("chip") == 0
    qkv = qkv_ref[...].astype(jnp.float32)
    for h in range(heads):
        query_ref[:, h, :] = qkv[:, h * HD : (h + 1) * HD]
        at = (heads + h // group) * HD
        key_new_ref[:, h, :] = qkv[:, at : at + HD]
        at += kv_half * HD
        value_new_ref[:, h, :] = qkv[:, at : at + HD]

    rows = n_req * heads
    query = query_ref[...].reshape(rows, HD)
    group_of = lax.broadcasted_iota(jnp.int32, (rows, HD), 0) % heads // group
    spread = jnp.concatenate(
        [jnp.where(group_of == k, query, 0.0) for k in range(kv_half)], axis=1
    ).astype(jnp.bfloat16)
    scores, live = [], []
    for r in range(n_req):
        blocks = []
        for keys in (key_own, key_peer):
            blocks.append(
                lax.dot_general(
                    spread[r * heads : (r + 1) * heads, :], keys[r, :, mine],
                    (((1,), (1,)), ((), ())), preferred_element_type=jnp.float32,
                )
            )
        scores.append(jnp.concatenate(blocks, axis=1))
        live_row = jnp.concatenate([live_own[r : r + 1, :], live_peer[r : r + 1, :]], axis=1)
        live.append(jnp.broadcast_to(live_row, (heads, 2 * span)))
    live = jnp.concatenate(live, axis=0) > 0.0
    scale = 1.0 / math.sqrt(HD)
    scores = jnp.where(live, jnp.concatenate(scores, axis=0) * scale, MASKED)
    key_new = key_new_ref[...].reshape(rows, HD)
    self_score = jnp.sum(query * key_new, axis=1, keepdims=True) * scale
    self_score = jnp.where(is_first, self_score, MASKED)
    top = jnp.maximum(jnp.max(scores, axis=1, keepdims=True), self_score)
    weights = jnp.where(live, jnp.exp(scores - top), 0.0)
    self_weight = jnp.where(is_first, jnp.exp(self_score - top), 0.0)
    total = jnp.sum(weights, axis=1, keepdims=True) + self_weight
    rounded = weights.astype(jnp.bfloat16)
    self_part = self_weight * value_new_ref[...].reshape(rows, HD)
    pieces = pieces_of(total) + pieces_of(top)
    lane = lax.broadcasted_iota(jnp.int32, (heads, LANES), 1)
    stats = jnp.zeros((heads, LANES), jnp.float32)
    parts = []
    for r in range(n_req):
        at = slice(r * heads, (r + 1) * heads)
        wide = jnp.dot(
            rounded[at, :span], value_own[r, :, mine], preferred_element_type=jnp.float32
        ) + jnp.dot(
            rounded[at, span:], value_peer[r, :, mine], preferred_element_type=jnp.float32
        )
        numer = self_part[at, :]
        for k in range(kv_half):
            numer = numer + jnp.where(group_of[at, :] == k, wide[:, k * HD : (k + 1) * HD], 0.0)
        parts.append(numer)
        for p, piece in enumerate(pieces):
            stats = jnp.where(lane == p * PIECE + r, piece[at, :], stats)
    message = jnp.concatenate(parts + [stats], axis=1).astype(jnp.bfloat16)
    for i in range(n_copies):
        message_ref[i] = message


def combine_kernel(arrived_ref, w_ref, head_ref, attended_ref):
    n_blocks, heads, width = arrived_ref.shape
    n_req = head_ref.shape[0]
    for c in range(2):
        blocks = range(c, n_blocks, 2)
        totals, tops = [], []
        for b in blocks:
            tile = arrived_ref[b, :, width - LANES :].astype(jnp.float32)
            tile = (
                tile
                + pltpu.roll(tile, LANES - PIECE, 1)
                + pltpu.roll(tile, LANES - 2 * PIECE, 1)
            )
            totals.append(tile)
            tops.append(pltpu.roll(tile, LANES - TOP_AT, 1))
        final_top = tops[0]
        for top in tops[1:]:
            final_top = jnp.maximum(final_top, top)
        fades = [jnp.exp(top - final_top) for top in tops]
        denominator = totals[0] * fades[0]
        for total, fade in zip(totals[1:], fades[1:]):
            denominator = denominator + total * fade
        for r in range(n_req):
            numer = jnp.zeros((heads, HD), jnp.float32)
            for b, fade in zip(blocks, fades):
                part = arrived_ref[b, :, r * HD : (r + 1) * HD].astype(jnp.float32)
                numer = numer + part * fade[:, r : r + 1]
            attended_ref[r, c * heads : (c + 1) * heads, :] = numer / denominator[:, r : r + 1]
    attended = jnp.concatenate([attended_ref[:, h, :] for h in range(2 * heads)], axis=1)
    head_ref[...] = jnp.dot(
        attended.astype(jnp.bfloat16), w_ref[...], preferred_element_type=jnp.float32
    )


def up_kernel(x_ref, part_ref, peer_ref, gain_ref, w_ref, hidden_ref, mine_ref, other_ref):
    core = lax.axis_index("core")
    attn_out = part_ref[...] + peer_ref[...]
    hidden_state = (x_ref[...].astype(jnp.float32) + attn_out).astype(jnp.bfloat16)
    resid_rows = hidden_state.astype(jnp.float32)
    hidden_ref[...] = resid_rows
    scaled_mlp = (resid_rows * gain_ref[...]).astype(jnp.bfloat16)
    squares = jnp.sum(resid_rows * resid_rows, axis=1, keepdims=True)
    up_part = jnp.dot(scaled_mlp, w_ref[...], preferred_element_type=jnp.float32)
    half = up_part.shape[1] // 2
    low, high = up_part[:, :half], up_part[:, half:]
    mine_ref[:, :half] = jnp.where(core == 0, low, high)
    other_ref[:, :half] = jnp.where(core == 0, high, low)
    square_cols = jnp.broadcast_to(squares, (resid_rows.shape[0], LANES))
    mine_ref[:, half:] = square_cols
    other_ref[:, half:] = square_cols


def up_message_kernel(mine_ref, arrived_ref, message_ref):
    half = mine_ref.shape[1] - LANES
    message = (mine_ref[:, :half] + arrived_ref[:, :half]).astype(jnp.bfloat16)
    squares = mine_ref[:, half:] + arrived_ref[:, half:]
    lane = lax.broadcasted_iota(jnp.int32, squares.shape, 1)
    tile = jnp.zeros_like(squares)
    for p, piece in enumerate(pieces_of(squares)):
        tile = jnp.where(lane == p, piece, tile)
    for i in range(message_ref.shape[0]):
        message_ref[i, :, :half] = message
        message_ref[i, :, half:] = tile.astype(jnp.bfloat16)


def activate_kernel(arrived_ref, out_ref):
    half = out_ref.shape[1]
    total = arrived_ref[0].astype(jnp.float32)
    for i in range(1, arrived_ref.shape[0]):
        total = total + arrived_ref[i].astype(jnp.float32)
    squares = jnp.sum(total[:, half:], axis=1, keepdims=True)
    inv_mlp = lax.rsqrt(squares / D + NORM_EPS)
    out_ref[...] = squared_relu(total[:, :half] * inv_mlp).astype(jnp.bfloat16)


def down_kernel(own_ref, oth_ref, w_ref, out_ref):
    core = lax.axis_index("core")
    own, oth = own_ref[...], oth_ref[...]
    half = own.shape[1]
    low = jnp.where(core == 0, own, oth)
    high = jnp.where(core == 0, oth, own)
    out_ref[...] = jnp.dot(
        low, w_ref[:half, :], preferred_element_type=jnp.float32
    ) + jnp.dot(high, w_ref[half:, :], preferred_element_type=jnp.float32)


def per_device(
    hidden_in,
    attn_gain,
    mlp_gain,
    query_weight,
    key_weight,
    value_weight,
    out_weight,
    up_weight,
    down_weight,
    key_cache,
    value_cache,
    lengths,
    block_order,
    pad_mask,
):
    n_req, d_here = hidden_in.shape
    kv_here = key_cache.shape[2] // HD
    heads_here = kv_here * (H // KVH)
    n_chips = lax.axis_size("chip")
    core = lax.axis_index("core")
    n_blocks = 2 * n_chips
    half_qkv = (heads_here + 2 * kv_here) * HD // 2
    half_up = up_weight.shape[1] // 2

    key_peer, value_peer = swap(key_cache, "core"), swap(value_cache, "core")
    row = (1, d_here)
    small = [hidden_in, attn_gain.reshape(row), mlp_gain.reshape(row), pad_mask]
    small += [lengths, block_order]
    mine, other, x_rows, gain, live = local_kernel(
        qkv_kernel,
        [
            f32(n_req, half_qkv + LANES),
            f32(n_req, half_qkv + LANES + pad_mask.shape[1]),
            bf16(*hidden_in.shape),
            f32(*row),
            f32(*pad_mask.shape),
        ],
        small + [query_weight, key_weight, value_weight],
        flops=4 * 10**9,
        scratch=[
            pltpu.VMEM(row, jnp.float32),
            pltpu.VMEM(pad_mask.shape, jnp.int32),
            pltpu.SMEM(lengths.shape, jnp.int32),
            pltpu.SMEM(block_order.shape, jnp.int32),
        ]
        + [pltpu.VMEM(w.shape, w.dtype) for w in (key_weight, value_weight, query_weight)]
        + [pltpu.SemaphoreType.DMA((len(small) + 3,))],
        in_hbm=range(len(small) + 3),
    )
    arrived = swap(other, "core")
    width = mine.shape[1]
    pair_sum, live_peer, key_peer, value_peer = lax.optimization_barrier(
        (mine + arrived[:, :width], arrived[:, width:], key_peer, value_peer)
    )
    (qkv_half,) = local_kernel(
        qkv_sum_kernel,
        [bf16(n_req, half_qkv)],
        [gather_all(pair_sum, "chip", n_chips)],
        flops=n_chips * n_req * half_qkv,
    )
    half_heads = heads_here // 2
    (message,) = local_kernel(
        attention_kernel,
        [bf16(n_blocks, half_heads, n_req * HD + LANES)],
        [qkv_half, key_cache, key_peer, value_cache, value_peer, live, live_peer],
        anywhere=(1, 2, 3, 4),
        flops=4 * 10**9,
        scratch=[pltpu.VMEM((n_req, half_heads, HD), jnp.float32)] * 3,
    )
    arrived = lax.all_to_all(message, ("chip", "core"), 0, 0)
    (head_part,) = local_kernel(
        combine_kernel,
        [f32(n_req, d_here)],
        [arrived, out_weight],
        anywhere=(1,),
        flops=2 * n_req * out_weight.size,
        scratch=[pltpu.VMEM((n_req, heads_here, HD), jnp.float32)],
    )
    head_peer = swap(head_part, "tp")
    resid_rows, up_mine, up_other = local_kernel(
        up_kernel,
        [f32(n_req, d_here)] + [f32(n_req, half_up + LANES)] * 2,
        [x_rows, head_part, head_peer, gain, up_weight],
        flops=2 * n_req * up_weight.size,
        anywhere=(4,),
    )
    (up_message,) = local_kernel(
        up_message_kernel,
        [bf16(n_chips, n_req, half_up + LANES)],
        [up_mine, swap(up_other, "core")],
        flops=n_chips * n_req * half_up,
    )
    (active_half,) = local_kernel(
        activate_kernel,
        [bf16(n_req, half_up)],
        [lax.all_to_all(up_message, "chip", 0, 0)],
        flops=n_chips * n_req * half_up,
    )
    active_other = swap(active_half, "core")
    (down_part,) = local_kernel(
        down_kernel,
        [f32(n_req, d_here)],
        [active_half, active_other, down_weight],
        flops=2 * n_req * down_weight.size,
        anywhere=(2,),
    )
    mlp_out = sum_tp(down_part)
    return (resid_rows + mlp_out).astype(jnp.bfloat16)


def solution(mesh):
    n_seq, n_tp = mesh.shape["seq"], mesh.shape["tp"]
    split = Mesh(mesh.devices.reshape(n_seq // 2, 2, n_tp), ("chip", "core", "tp"))
    seq = ("chip", "core")
    whole_tiles = n_tp == 2 and KVH % (2 * n_tp) == 0 and D % (n_seq * LANES) == 0
    return jax.shard_map(
        per_device if whole_tiles else per_device_plain,
        mesh=split,
        in_specs=(
            P(None, seq),
            P(seq),
            P(seq),
            P(seq, "tp"),
            P(seq, "tp"),
            P(seq, "tp"),
            P("tp", seq),
            P(seq, "tp"),
            P("tp", seq),
            P(None, seq, "tp"),
            P(None, seq, "tp"),
            P(),
            P(),
            P(None, seq),
        ),
        out_specs=P(None, seq),
        check_vma=False,
    )
```

```python
import math

import jax
import jax.numpy as jnp
from jax import lax
from jax.experimental import pallas as pl
from jax.experimental.pallas import tpu as pltpu
from jax.sharding import Mesh, PartitionSpec as P

D = 4096
H = 32
KVH = 8
HD = 128


NORM_EPS = 1e-05
MASKED = -1e30
LANES = 128


def squared_relu(values_in):
    positive = jnp.maximum(values_in, 0.0)
    return positive * positive


def swap(values_in, axis):
    n = lax.axis_size(axis)
    return lax.ppermute(values_in, axis, [(i, i ^ 1) for i in range(n)])


def gather_all(values_in, axes, n):
    copies = jnp.broadcast_to(values_in[None], (n,) + values_in.shape)
    return lax.all_to_all(copies, axes, 0, 0)


def sum_tp(values_in):
    n = lax.axis_size("tp")
    if n == 2:
        return values_in + swap(values_in, "tp")
    return lax.psum(values_in, "tp")


def per_device_plain(
    hidden_in,
    attn_gain,
    mlp_gain,
    query_weight,
    key_weight,
    value_weight,
    out_weight,
    up_weight,
    down_weight,
    key_cache,
    value_cache,
    lengths,
    block_order,
    pad_mask,
):
    n_req = hidden_in.shape[0]
    q_per_kv = H // KVH
    kv_here = key_cache.shape[2] // HD
    span_here = key_cache.shape[1]
    heads_here = kv_here * q_per_kv
    n_chips = lax.axis_size("chip")
    core = lax.axis_index("core")
    n_blocks = 2 * n_chips
    my_block = 2 * lax.axis_index("chip") + core
    score_scale = 1.0 / math.sqrt(HD)

    x_rows = hidden_in.astype(jnp.float32)
    scaled_in = (x_rows * attn_gain).astype(jnp.bfloat16)
    sq_attn = jnp.sum(x_rows * x_rows, axis=1, keepdims=True)
    proj_query = jnp.dot(scaled_in, query_weight, preferred_element_type=jnp.float32)
    proj_key = jnp.dot(scaled_in, key_weight, preferred_element_type=jnp.float32)
    proj_value = jnp.dot(scaled_in, value_weight, preferred_element_type=jnp.float32)
    half_q, half_kv = proj_query.shape[1] // 2, proj_key.shape[1] // 2
    square_cols = jnp.broadcast_to(sq_attn, (n_req, LANES))

    def half(i):
        return jnp.concatenate(
            [
                proj_query[:, i * half_q : (i + 1) * half_q],
                proj_key[:, i * half_kv : (i + 1) * half_kv],
                proj_value[:, i * half_kv : (i + 1) * half_kv],
                square_cols,
            ],
            axis=1,
        )

    low, high = half(0), half(1)
    mine = jnp.where(core == 0, low, high)
    other = jnp.where(core == 0, high, low)
    pair_sum = mine + swap(other, "core")
    qkv_sum = jnp.sum(gather_all(pair_sum, "chip", n_chips), axis=0)
    inv_attn = lax.rsqrt(qkv_sum[:, -1:] / D + NORM_EPS)
    qkv_half = (qkv_sum[:, :-LANES] * inv_attn).astype(jnp.bfloat16)
    qkv_other = swap(qkv_half, "core")
    qkv_low = jnp.where(core == 0, qkv_half, qkv_other)
    qkv_high = jnp.where(core == 0, qkv_other, qkv_half)

    def both(start, size):
        return jnp.concatenate(
            [qkv_low[:, start : start + size], qkv_high[:, start : start + size]], axis=1
        )

    query_rows = both(0, half_q)
    key_new = both(half_q, half_kv)
    value_new = both(half_q + half_kv, half_kv)

    first_block = block_order % n_blocks
    position = ((my_block - first_block) % n_blocks)[:, None] * span_here + jnp.arange(
        span_here, dtype=jnp.int32
    )[None, :]
    live_slots = ((position < lengths[:, None]) & (pad_mask == 1))[:, None, None, :]
    q_groups = query_rows.reshape(n_req, kv_here, q_per_kv, HD)
    keys_here = key_cache.reshape(n_req, span_here, kv_here, HD)
    values_here = value_cache.reshape(n_req, span_here, kv_here, HD)
    scores = (
        jnp.einsum("rkgd,rtkd->rkgt", q_groups, keys_here, preferred_element_type=jnp.float32)
        * score_scale
    )
    scores = jnp.where(live_slots, scores, MASKED)
    local_top = jnp.max(scores, axis=3, keepdims=True)
    weights = jnp.where(live_slots, jnp.exp(scores - local_top), 0.0)
    local_total = jnp.sum(weights, axis=3, keepdims=True)
    local_out = jnp.einsum(
        "rkgt,rtkd->rkgd",
        weights.astype(jnp.bfloat16),
        values_here,
        preferred_element_type=jnp.float32,
    )
    numer = local_out.reshape(n_req, heads_here, HD)
    stats = jnp.concatenate(
        [
            local_total.reshape(n_req, heads_here, 1),
            local_top.reshape(n_req, heads_here, 1),
        ],
        axis=2,
    )
    stat_rows = stats.reshape(n_req, heads_here * 2)
    pad = (-stat_rows.shape[1]) % LANES
    message = jnp.concatenate(
        [numer.reshape(n_req, heads_here * HD), jnp.pad(stat_rows, ((0, 0), (0, pad)))], axis=1
    )
    arrived = gather_all(message, ("chip", "core"), n_blocks)
    outs = arrived[:, :, : heads_here * HD].reshape(n_blocks, n_req, heads_here, HD)
    stats_all = arrived[:, :, heads_here * HD : heads_here * (HD + 2)].reshape(
        n_blocks, n_req, heads_here, 2
    )
    totals, tops = stats_all[..., 0], stats_all[..., 1]
    self_score = (
        jnp.einsum(
            "rkgd,rkd->rkg",
            q_groups,
            key_new.reshape(n_req, kv_here, HD),
            preferred_element_type=jnp.float32,
        )
        * score_scale
    ).reshape(n_req, heads_here)
    final_top = jnp.maximum(jnp.max(tops, axis=0), self_score)
    fades = jnp.exp(tops - final_top)
    self_weight = jnp.exp(self_score - final_top)
    denominator = jnp.sum(totals * fades, axis=0) + self_weight
    value_self = jnp.broadcast_to(
        value_new.reshape(n_req, kv_here, 1, HD), (n_req, kv_here, q_per_kv, HD)
    ).reshape(n_req, heads_here, HD)
    numerator = jnp.sum(outs * fades[..., None], axis=0) + self_weight[
        ..., None
    ] * value_self.astype(jnp.float32)
    attended = (
        (numerator / denominator[..., None])
        .reshape(n_req, heads_here * HD)
        .astype(jnp.bfloat16)
    )
    head_part = jnp.dot(attended, out_weight, preferred_element_type=jnp.float32)
    attn_out = sum_tp(head_part)
    hidden_state = (x_rows + attn_out).astype(jnp.bfloat16)

    resid_rows = hidden_state.astype(jnp.float32)
    scaled_mlp = (resid_rows * mlp_gain).astype(jnp.bfloat16)
    sq_mlp = jnp.sum(resid_rows * resid_rows, axis=1, keepdims=True)
    up_part = jnp.dot(scaled_mlp, up_weight, preferred_element_type=jnp.float32)
    half_up = up_part.shape[1] // 2
    up_low, up_high = up_part[:, :half_up], up_part[:, half_up:]
    square_cols = jnp.broadcast_to(sq_mlp, (n_req, LANES))
    up_mine = jnp.concatenate([jnp.where(core == 0, up_low, up_high), square_cols], axis=1)
    up_other = jnp.concatenate([jnp.where(core == 0, up_high, up_low), square_cols], axis=1)
    up_pair = up_mine + swap(up_other, "core")
    square_sum = up_pair[:, half_up : half_up + 1]
    piece_0 = lax.reduce_precision(square_sum, 8, 7)
    piece_1 = lax.reduce_precision(square_sum - piece_0, 8, 7)
    piece_2 = square_sum - piece_0 - piece_1
    pieces = jnp.pad(
        jnp.concatenate([piece_0, piece_1, piece_2], axis=1), ((0, 0), (0, LANES - 3))
    )
    up_message = jnp.concatenate([up_pair[:, :half_up], pieces], axis=1).astype(jnp.bfloat16)
    up_sum = jnp.sum(gather_all(up_message, "chip", n_chips).astype(jnp.float32), axis=0)
    squares = jnp.sum(up_sum[:, half_up:], axis=1, keepdims=True)
    inv_mlp = lax.rsqrt(squares / D + NORM_EPS)
    active_half = squared_relu(up_sum[:, :half_up] * inv_mlp).astype(jnp.bfloat16)
    active_other = swap(active_half, "core")
    activated = jnp.concatenate(
        [
            jnp.where(core == 0, active_half, active_other),
            jnp.where(core == 0, active_other, active_half),
        ],
        axis=1,
    )
    down_part = jnp.dot(activated, down_weight, preferred_element_type=jnp.float32)
    mlp_out = sum_tp(down_part)
    return (resid_rows + mlp_out).astype(jnp.bfloat16)


IN_VMEM = pl.BlockSpec(memory_space=pltpu.VMEM)


def local_kernel(kernel, outs, operands, flops, scratch=(), in_hbm=(), anywhere=()):
    in_specs, placed, moved = [], [], 0
    for i, x in enumerate(operands):
        space = pltpu.HBM if i in in_hbm else pltpu.VMEM
        in_specs.append(pl.BlockSpec(memory_space=space))
        placed.append(x if i in anywhere else pltpu.with_memory_space_constraint(x, space))
        moved += x.size * x.dtype.itemsize
    return pl.pallas_call(
        kernel,
        out_shape=outs,
        in_specs=in_specs,
        out_specs=[IN_VMEM] * len(outs),
        scratch_shapes=scratch,
        compiler_params=pltpu.CompilerParams(vmem_limit_bytes=6 * 2**20),
        cost_estimate=pl.CostEstimate(flops=flops, bytes_accessed=moved, transcendentals=0),
    )(*placed)


def f32(*shape):
    return pltpu.VMEM(shape, jnp.float32)


def bf16(*shape):
    return pltpu.VMEM(shape, jnp.bfloat16)


def pieces_of(values_in):
    first = values_in.astype(jnp.bfloat16).astype(jnp.float32)
    second = (values_in - first).astype(jnp.bfloat16).astype(jnp.float32)
    return first, second, values_in - first - second


def qkv_kernel(
    x_hbm, gain_hbm, mlp_gain_hbm, mask_hbm, lengths_hbm, order_hbm, wq_hbm, wk_hbm, wv_hbm,
    mine_ref, other_ref, x_ref, mlp_gain_ref, live_ref,
    gain_ref, mask_ref, lengths_ref, order_ref, *scratch,
):
    core = lax.axis_index("core")
    n_blocks = lax.axis_size("chip") * 2
    my_block = 2 * lax.axis_index("chip") + core
    w_refs, sems = scratch[:-1], scratch[-1]
    small = [
        (x_hbm, x_ref), (gain_hbm, gain_ref), (mask_hbm, mask_ref), (lengths_hbm, lengths_ref),
        (order_hbm, order_ref), (mlp_gain_hbm, mlp_gain_ref),
    ]
    copies = [pltpu.make_async_copy(src, dst, sems.at[i]) for i, (src, dst) in enumerate(small)]
    for w_hbm, w_ref in zip((wk_hbm, wv_hbm, wq_hbm), w_refs):
        copies.append(pltpu.make_async_copy(w_hbm, w_ref, sems.at[len(copies)]))
    for copy in copies:
        copy.start()
    for copy in copies[: len(small)]:
        copy.wait()
    n_req, span = live_ref.shape
    slot = lax.broadcasted_iota(jnp.int32, (1, span), 1)
    for r in range(n_req):
        first_block = lax.rem(order_ref[r], n_blocks)
        begin = lax.rem(my_block - first_block + n_blocks, n_blocks) * span
        live = (begin + slot < lengths_ref[r]) & (mask_ref[r : r + 1, :] == 1)
        live_ref[r : r + 1, :] = live.astype(jnp.float32)
    x_rows = x_ref[...].astype(jnp.float32)
    scaled_in = (x_rows * gain_ref[...]).astype(jnp.bfloat16)
    squares = jnp.sum(x_rows * x_rows, axis=1, keepdims=True)
    proj = []
    for w_ref, copy in zip(w_refs, copies[len(small) :]):
        copy.wait()
        proj.append(jnp.dot(scaled_in, w_ref[...], preferred_element_type=jnp.float32))
    proj = jnp.concatenate([proj[2], proj[0], proj[1]], axis=1)
    at, start = 0, 0
    for w_hbm in (wq_hbm, wk_hbm, wv_hbm):
        half = w_hbm.shape[1] // 2
        low, high = proj[:, start : start + half], proj[:, start + half : start + 2 * half]
        mine_ref[:, at : at + half] = jnp.where(core == 0, low, high)
        other_ref[:, at : at + half] = jnp.where(core == 0, high, low)
        at += half
        start += 2 * half
    square_cols = jnp.broadcast_to(squares, (x_rows.shape[0], LANES))
    mine_ref[:, at:] = square_cols
    other_ref[:, at : at + LANES] = square_cols
    other_ref[:, at + LANES :] = live_ref[...]


SCALE_UNIT = 1024.0


def qkv_message_kernel(mine_ref, arrived_ref, out_ref):
    width = mine_ref.shape[1] - LANES
    features = D / lax.axis_size("chip")
    total = mine_ref[...] + arrived_ref[:, : width + LANES]
    squares = total[:, width:]
    scale = jnp.sqrt(jnp.maximum(squares * (1.0 / features), 2.0**-40))
    scale = scale.astype(jnp.bfloat16).astype(jnp.float32)
    inverse = 1.0 / scale
    out_ref[:, :width] = total[:, :width] * inverse[:, :1]
    lane = lax.broadcasted_iota(jnp.int32, squares.shape, 1)
    tile = jnp.where(lane == 0, scale * SCALE_UNIT, 0.0)
    for p, piece in enumerate(pieces_of(squares * inverse * inverse * (1.0 / features))):
        tile = jnp.where(lane == 1 + p, piece, tile)
    out_ref[:, width:] = tile


def qkv_sum_kernel(arrived_ref, out_ref):
    width = out_ref.shape[1]
    features = D / arrived_ref.shape[0]
    total, squares = 0.0, 0.0
    for i in range(arrived_ref.shape[0]):
        tile = arrived_ref[i, :, width:]
        scale = tile[:, :1] * (1.0 / SCALE_UNIT)
        total = total + arrived_ref[i, :, :width] * scale
        mean = tile[:, 1:2] + tile[:, 2:3] + tile[:, 3:4]
        squares = squares + mean * scale * scale * features
    inv_attn = lax.rsqrt(squares / D + NORM_EPS)
    out_ref[...] = (total * inv_attn).astype(jnp.bfloat16)


PIECE = 16
TOP_AT = 3 * PIECE


def attention_kernel(
    qkv_ref, key_own, key_peer, value_own, value_peer, live_own, live_peer,
    message_ref, query_ref, key_new_ref, value_new_ref,
):
    n_copies, heads, _ = message_ref.shape
    n_req, span = live_own.shape
    half = key_own.shape[2] // 2
    mine = pl.ds(pl.multiple_of(lax.axis_index("core") * half, LANES), half)
    kv_half = half // HD
    group = heads // kv_half
    is_first = lax.axis_index("chip") == 0
    qkv = qkv_ref[...].astype(jnp.float32)
    for h in range(heads):
        query_ref[:, h, :] = qkv[:, h * HD : (h + 1) * HD]
        at = (heads + h // group) * HD
        key_new_ref[:, h, :] = qkv[:, at : at + HD]
        at += kv_half * HD
        value_new_ref[:, h, :] = qkv[:, at : at + HD]

    rows = n_req * heads
    query = query_ref[...].reshape(rows, HD)
    group_of = lax.broadcasted_iota(jnp.int32, (rows, HD), 0) % heads // group
    spread = jnp.concatenate(
        [jnp.where(group_of == k, query, 0.0) for k in range(kv_half)], axis=1
    ).astype(jnp.bfloat16)
    scores, live = [], []
    for r in range(n_req):
        blocks = []
        for keys in (key_own, key_peer):
            blocks.append(
                lax.dot_general(
                    spread[r * heads : (r + 1) * heads, :], keys[r, :, mine],
                    (((1,), (1,)), ((), ())), preferred_element_type=jnp.float32,
                )
            )
        scores.append(jnp.concatenate(blocks, axis=1))
        live_row = jnp.concatenate([live_own[r : r + 1, :], live_peer[r : r + 1, :]], axis=1)
        live.append(jnp.broadcast_to(live_row, (heads, 2 * span)))
    live = jnp.concatenate(live, axis=0) > 0.0
    scale = 1.0 / math.sqrt(HD)
    scores = jnp.where(live, jnp.concatenate(scores, axis=0) * scale, MASKED)
    key_new = key_new_ref[...].reshape(rows, HD)
    self_score = jnp.sum(query * key_new, axis=1, keepdims=True) * scale
    self_score = jnp.where(is_first, self_score, MASKED)
    top = jnp.maximum(jnp.max(scores, axis=1, keepdims=True), self_score)
    weights = jnp.where(live, jnp.exp(scores - top), 0.0)
    self_weight = jnp.where(is_first, jnp.exp(self_score - top), 0.0)
    total = jnp.sum(weights, axis=1, keepdims=True) + self_weight
    rounded = weights.astype(jnp.bfloat16)
    self_part = self_weight * value_new_ref[...].reshape(rows, HD)
    pieces = pieces_of(total) + pieces_of(top)
    lane = lax.broadcasted_iota(jnp.int32, (heads, LANES), 1)
    stats = jnp.zeros((heads, LANES), jnp.float32)
    parts = []
    for r in range(n_req):
        at = slice(r * heads, (r + 1) * heads)
        wide = jnp.dot(
            rounded[at, :span], value_own[r, :, mine], preferred_element_type=jnp.float32
        ) + jnp.dot(
            rounded[at, span:], value_peer[r, :, mine], preferred_element_type=jnp.float32
        )
        numer = self_part[at, :]
        for k in range(kv_half):
            numer = numer + jnp.where(group_of[at, :] == k, wide[:, k * HD : (k + 1) * HD], 0.0)
        parts.append(numer)
        for p, piece in enumerate(pieces):
            stats = jnp.where(lane == p * PIECE + r, piece[at, :], stats)
    message = jnp.concatenate(parts + [stats], axis=1).astype(jnp.bfloat16)
    for i in range(n_copies):
        message_ref[i] = message


def combine_kernel(arrived_ref, w_ref, head_ref, attended_ref):
    n_blocks, heads, width = arrived_ref.shape
    n_req = head_ref.shape[0]
    for c in range(2):
        blocks = range(c, n_blocks, 2)
        totals, tops = [], []
        for b in blocks:
            tile = arrived_ref[b, :, width - LANES :].astype(jnp.float32)
            tile = (
                tile
                + pltpu.roll(tile, LANES - PIECE, 1)
                + pltpu.roll(tile, LANES - 2 * PIECE, 1)
            )
            totals.append(tile)
            tops.append(pltpu.roll(tile, LANES - TOP_AT, 1))
        final_top = tops[0]
        for top in tops[1:]:
            final_top = jnp.maximum(final_top, top)
        fades = [jnp.exp(top - final_top) for top in tops]
        denominator = totals[0] * fades[0]
        for total, fade in zip(totals[1:], fades[1:]):
            denominator = denominator + total * fade
        for r in range(n_req):
            numer = jnp.zeros((heads, HD), jnp.float32)
            for b, fade in zip(blocks, fades):
                part = arrived_ref[b, :, r * HD : (r + 1) * HD].astype(jnp.float32)
                numer = numer + part * fade[:, r : r + 1]
            attended_ref[r, c * heads : (c + 1) * heads, :] = numer / denominator[:, r : r + 1]
    attended = jnp.concatenate([attended_ref[:, h, :] for h in range(2 * heads)], axis=1)
    head_ref[...] = jnp.dot(
        attended.astype(jnp.bfloat16), w_ref[...], preferred_element_type=jnp.float32
    )


def up_kernel(x_ref, part_ref, peer_ref, gain_ref, w_ref, hidden_ref, mine_ref, other_ref):
    core = lax.axis_index("core")
    attn_out = part_ref[...] + peer_ref[...]
    hidden_state = (x_ref[...].astype(jnp.float32) + attn_out).astype(jnp.bfloat16)
    resid_rows = hidden_state.astype(jnp.float32)
    hidden_ref[...] = resid_rows
    scaled_mlp = (resid_rows * gain_ref[...]).astype(jnp.bfloat16)
    squares = jnp.sum(resid_rows * resid_rows, axis=1, keepdims=True)
    up_part = jnp.dot(scaled_mlp, w_ref[...], preferred_element_type=jnp.float32)
    half = up_part.shape[1] // 2
    low, high = up_part[:, :half], up_part[:, half:]
    mine_ref[:, :half] = jnp.where(core == 0, low, high)
    other_ref[:, :half] = jnp.where(core == 0, high, low)
    square_cols = jnp.broadcast_to(squares, (resid_rows.shape[0], LANES))
    mine_ref[:, half:] = square_cols
    other_ref[:, half:] = square_cols


def up_message_kernel(mine_ref, arrived_ref, message_ref):
    half = mine_ref.shape[1] - LANES
    message = (mine_ref[:, :half] + arrived_ref[:, :half]).astype(jnp.bfloat16)
    squares = mine_ref[:, half:] + arrived_ref[:, half:]
    lane = lax.broadcasted_iota(jnp.int32, squares.shape, 1)
    tile = jnp.zeros_like(squares)
    for p, piece in enumerate(pieces_of(squares)):
        tile = jnp.where(lane == p, piece, tile)
    for i in range(message_ref.shape[0]):
        message_ref[i, :, :half] = message
        message_ref[i, :, half:] = tile.astype(jnp.bfloat16)


def activate_kernel(arrived_ref, out_ref):
    half = out_ref.shape[1]
    total = arrived_ref[0].astype(jnp.float32)
    for i in range(1, arrived_ref.shape[0]):
        total = total + arrived_ref[i].astype(jnp.float32)
    squares = jnp.sum(total[:, half:], axis=1, keepdims=True)
    inv_mlp = lax.rsqrt(squares / D + NORM_EPS)
    out_ref[...] = squared_relu(total[:, :half] * inv_mlp).astype(jnp.bfloat16)


def down_kernel(own_ref, oth_ref, w_ref, out_ref):
    core = lax.axis_index("core")
    own, oth = own_ref[...], oth_ref[...]
    half = own.shape[1]
    low = jnp.where(core == 0, own, oth)
    high = jnp.where(core == 0, oth, own)
    out_ref[...] = jnp.dot(
        low, w_ref[:half, :], preferred_element_type=jnp.float32
    ) + jnp.dot(high, w_ref[half:, :], preferred_element_type=jnp.float32)


def per_device(
    hidden_in,
    attn_gain,
    mlp_gain,
    query_weight,
    key_weight,
    value_weight,
    out_weight,
    up_weight,
    down_weight,
    key_cache,
    value_cache,
    lengths,
    block_order,
    pad_mask,
):
    n_req, d_here = hidden_in.shape
    kv_here = key_cache.shape[2] // HD
    heads_here = kv_here * (H // KVH)
    n_chips = lax.axis_size("chip")
    core = lax.axis_index("core")
    n_blocks = 2 * n_chips
    half_qkv = (heads_here + 2 * kv_here) * HD // 2
    half_up = up_weight.shape[1] // 2

    key_peer, value_peer = swap(key_cache, "core"), swap(value_cache, "core")
    row = (1, d_here)
    small = [hidden_in, attn_gain.reshape(row), mlp_gain.reshape(row), pad_mask]
    small += [lengths, block_order]
    mine, other, x_rows, gain, live = local_kernel(
        qkv_kernel,
        [
            f32(n_req, half_qkv + LANES),
            f32(n_req, half_qkv + LANES + pad_mask.shape[1]),
            bf16(*hidden_in.shape),
            f32(*row),
            f32(*pad_mask.shape),
        ],
        small + [query_weight, key_weight, value_weight],
        flops=4 * 10**9,
        scratch=[
            pltpu.VMEM(row, jnp.float32),
            pltpu.VMEM(pad_mask.shape, jnp.int32),
            pltpu.SMEM(lengths.shape, jnp.int32),
            pltpu.SMEM(block_order.shape, jnp.int32),
        ]
        + [pltpu.VMEM(w.shape, w.dtype) for w in (key_weight, value_weight, query_weight)]
        + [pltpu.SemaphoreType.DMA((len(small) + 3,))],
        in_hbm=range(len(small) + 3),
    )
    arrived = swap(other, "core")
    width = mine.shape[1]
    (qkv_message,) = local_kernel(
        qkv_message_kernel, [f32(*mine.shape)], [mine, arrived], flops=2 * mine.size
    )
    qkv_message, live_peer, key_peer, value_peer = lax.optimization_barrier(
        (qkv_message.astype(jnp.float16), arrived[:, width:], key_peer, value_peer)
    )
    (qkv_half,) = local_kernel(
        qkv_sum_kernel,
        [bf16(n_req, half_qkv)],
        [gather_all(qkv_message, "chip", n_chips).astype(jnp.float32)],
        flops=n_chips * n_req * half_qkv,
    )
    half_heads = heads_here // 2
    (message,) = local_kernel(
        attention_kernel,
        [bf16(n_blocks, half_heads, n_req * HD + LANES)],
        [qkv_half, key_cache, key_peer, value_cache, value_peer, live, live_peer],
        anywhere=(1, 2, 3, 4),
        flops=4 * 10**9,
        scratch=[pltpu.VMEM((n_req, half_heads, HD), jnp.float32)] * 3,
    )
    arrived = lax.all_to_all(message, ("chip", "core"), 0, 0)
    (head_part,) = local_kernel(
        combine_kernel,
        [f32(n_req, d_here)],
        [arrived, out_weight],
        anywhere=(1,),
        flops=2 * n_req * out_weight.size,
        scratch=[pltpu.VMEM((n_req, heads_here, HD), jnp.float32)],
    )
    head_peer = swap(head_part, "tp")
    resid_rows, up_mine, up_other = local_kernel(
        up_kernel,
        [f32(n_req, d_here)] + [f32(n_req, half_up + LANES)] * 2,
        [x_rows, head_part, head_peer, gain, up_weight],
        flops=2 * n_req * up_weight.size,
        anywhere=(4,),
    )
    (up_message,) = local_kernel(
        up_message_kernel,
        [bf16(n_chips, n_req, half_up + LANES)],
        [up_mine, swap(up_other, "core")],
        flops=n_chips * n_req * half_up,
    )
    (active_half,) = local_kernel(
        activate_kernel,
        [bf16(n_req, half_up)],
        [lax.all_to_all(up_message, "chip", 0, 0)],
        flops=n_chips * n_req * half_up,
    )
    active_other = swap(active_half, "core")
    (down_part,) = local_kernel(
        down_kernel,
        [f32(n_req, d_here)],
        [active_half, active_other, down_weight],
        flops=2 * n_req * down_weight.size,
        anywhere=(2,),
    )
    mlp_out = sum_tp(down_part)
    return (resid_rows + mlp_out).astype(jnp.bfloat16)


def solution(mesh):
    n_seq, n_tp = mesh.shape["seq"], mesh.shape["tp"]
    split = Mesh(mesh.devices.reshape(n_seq // 2, 2, n_tp), ("chip", "core", "tp"))
    seq = ("chip", "core")
    whole_tiles = n_tp == 2 and KVH % (2 * n_tp) == 0 and D % (n_seq * LANES) == 0
    return jax.shard_map(
        per_device if whole_tiles else per_device_plain,
        mesh=split,
        in_specs=(
            P(None, seq),
            P(seq),
            P(seq),
            P(seq, "tp"),
            P(seq, "tp"),
            P(seq, "tp"),
            P("tp", seq),
            P(seq, "tp"),
            P("tp", seq),
            P(None, seq, "tp"),
            P(None, seq, "tp"),
            P(),
            P(),
            P(None, seq),
        ),
        out_specs=P(None, seq),
        check_vma=False,
    )
```

```python
import math

import jax
import jax.numpy as jnp
from jax import lax
from jax.experimental import pallas as pl
from jax.experimental.pallas import tpu as pltpu
from jax.sharding import Mesh, PartitionSpec as P

D = 4096
H = 32
KVH = 8
HD = 128


NORM_EPS = 1e-05
MASKED = -1e30
LANES = 128


def squared_relu(values_in):
    positive = jnp.maximum(values_in, 0.0)
    return positive * positive


def swap(values_in, axis):
    n = lax.axis_size(axis)
    return lax.ppermute(values_in, axis, [(i, i ^ 1) for i in range(n)])


def gather_all(values_in, axes, n):
    copies = jnp.broadcast_to(values_in[None], (n,) + values_in.shape)
    return lax.all_to_all(copies, axes, 0, 0)


def sum_tp(values_in):
    n = lax.axis_size("tp")
    if n == 2:
        return values_in + swap(values_in, "tp")
    return lax.psum(values_in, "tp")


def per_device_plain(
    hidden_in,
    attn_gain,
    mlp_gain,
    query_weight,
    key_weight,
    value_weight,
    out_weight,
    up_weight,
    down_weight,
    key_cache,
    value_cache,
    lengths,
    block_order,
    pad_mask,
):
    n_req = hidden_in.shape[0]
    q_per_kv = H // KVH
    kv_here = key_cache.shape[2] // HD
    span_here = key_cache.shape[1]
    heads_here = kv_here * q_per_kv
    n_chips = lax.axis_size("chip")
    core = lax.axis_index("core")
    n_blocks = 2 * n_chips
    my_block = 2 * lax.axis_index("chip") + core
    score_scale = 1.0 / math.sqrt(HD)

    x_rows = hidden_in.astype(jnp.float32)
    scaled_in = (x_rows * attn_gain).astype(jnp.bfloat16)
    sq_attn = jnp.sum(x_rows * x_rows, axis=1, keepdims=True)
    proj_query = jnp.dot(scaled_in, query_weight, preferred_element_type=jnp.float32)
    proj_key = jnp.dot(scaled_in, key_weight, preferred_element_type=jnp.float32)
    proj_value = jnp.dot(scaled_in, value_weight, preferred_element_type=jnp.float32)
    half_q, half_kv = proj_query.shape[1] // 2, proj_key.shape[1] // 2
    square_cols = jnp.broadcast_to(sq_attn, (n_req, LANES))

    def half(i):
        return jnp.concatenate(
            [
                proj_query[:, i * half_q : (i + 1) * half_q],
                proj_key[:, i * half_kv : (i + 1) * half_kv],
                proj_value[:, i * half_kv : (i + 1) * half_kv],
                square_cols,
            ],
            axis=1,
        )

    low, high = half(0), half(1)
    mine = jnp.where(core == 0, low, high)
    other = jnp.where(core == 0, high, low)
    pair_sum = mine + swap(other, "core")
    qkv_sum = jnp.sum(gather_all(pair_sum, "chip", n_chips), axis=0)
    inv_attn = lax.rsqrt(qkv_sum[:, -1:] / D + NORM_EPS)
    qkv_half = (qkv_sum[:, :-LANES] * inv_attn).astype(jnp.bfloat16)
    qkv_other = swap(qkv_half, "core")
    qkv_low = jnp.where(core == 0, qkv_half, qkv_other)
    qkv_high = jnp.where(core == 0, qkv_other, qkv_half)

    def both(start, size):
        return jnp.concatenate(
            [qkv_low[:, start : start + size], qkv_high[:, start : start + size]], axis=1
        )

    query_rows = both(0, half_q)
    key_new = both(half_q, half_kv)
    value_new = both(half_q + half_kv, half_kv)

    first_block = block_order % n_blocks
    position = ((my_block - first_block) % n_blocks)[:, None] * span_here + jnp.arange(
        span_here, dtype=jnp.int32
    )[None, :]
    live_slots = ((position < lengths[:, None]) & (pad_mask == 1))[:, None, None, :]
    q_groups = query_rows.reshape(n_req, kv_here, q_per_kv, HD)
    keys_here = key_cache.reshape(n_req, span_here, kv_here, HD)
    values_here = value_cache.reshape(n_req, span_here, kv_here, HD)
    scores = (
        jnp.einsum("rkgd,rtkd->rkgt", q_groups, keys_here, preferred_element_type=jnp.float32)
        * score_scale
    )
    scores = jnp.where(live_slots, scores, MASKED)
    local_top = jnp.max(scores, axis=3, keepdims=True)
    weights = jnp.where(live_slots, jnp.exp(scores - local_top), 0.0)
    local_total = jnp.sum(weights, axis=3, keepdims=True)
    local_out = jnp.einsum(
        "rkgt,rtkd->rkgd",
        weights.astype(jnp.bfloat16),
        values_here,
        preferred_element_type=jnp.float32,
    )
    numer = local_out.reshape(n_req, heads_here, HD)
    stats = jnp.concatenate(
        [
            local_total.reshape(n_req, heads_here, 1),
            local_top.reshape(n_req, heads_here, 1),
        ],
        axis=2,
    )
    stat_rows = stats.reshape(n_req, heads_here * 2)
    pad = (-stat_rows.shape[1]) % LANES
    message = jnp.concatenate(
        [numer.reshape(n_req, heads_here * HD), jnp.pad(stat_rows, ((0, 0), (0, pad)))], axis=1
    )
    arrived = gather_all(message, ("chip", "core"), n_blocks)
    outs = arrived[:, :, : heads_here * HD].reshape(n_blocks, n_req, heads_here, HD)
    stats_all = arrived[:, :, heads_here * HD : heads_here * (HD + 2)].reshape(
        n_blocks, n_req, heads_here, 2
    )
    totals, tops = stats_all[..., 0], stats_all[..., 1]
    self_score = (
        jnp.einsum(
            "rkgd,rkd->rkg",
            q_groups,
            key_new.reshape(n_req, kv_here, HD),
            preferred_element_type=jnp.float32,
        )
        * score_scale
    ).reshape(n_req, heads_here)
    final_top = jnp.maximum(jnp.max(tops, axis=0), self_score)
    fades = jnp.exp(tops - final_top)
    self_weight = jnp.exp(self_score - final_top)
    denominator = jnp.sum(totals * fades, axis=0) + self_weight
    value_self = jnp.broadcast_to(
        value_new.reshape(n_req, kv_here, 1, HD), (n_req, kv_here, q_per_kv, HD)
    ).reshape(n_req, heads_here, HD)
    numerator = jnp.sum(outs * fades[..., None], axis=0) + self_weight[
        ..., None
    ] * value_self.astype(jnp.float32)
    attended = (
        (numerator / denominator[..., None])
        .reshape(n_req, heads_here * HD)
        .astype(jnp.bfloat16)
    )
    head_part = jnp.dot(attended, out_weight, preferred_element_type=jnp.float32)
    attn_out = sum_tp(head_part)
    hidden_state = (x_rows + attn_out).astype(jnp.bfloat16)

    resid_rows = hidden_state.astype(jnp.float32)
    scaled_mlp = (resid_rows * mlp_gain).astype(jnp.bfloat16)
    sq_mlp = jnp.sum(resid_rows * resid_rows, axis=1, keepdims=True)
    up_part = jnp.dot(scaled_mlp, up_weight, preferred_element_type=jnp.float32)
    half_up = up_part.shape[1] // 2
    up_low, up_high = up_part[:, :half_up], up_part[:, half_up:]
    square_cols = jnp.broadcast_to(sq_mlp, (n_req, LANES))
    up_mine = jnp.concatenate([jnp.where(core == 0, up_low, up_high), square_cols], axis=1)
    up_other = jnp.concatenate([jnp.where(core == 0, up_high, up_low), square_cols], axis=1)
    up_pair = up_mine + swap(up_other, "core")
    square_sum = up_pair[:, half_up : half_up + 1]
    piece_0 = lax.reduce_precision(square_sum, 8, 7)
    piece_1 = lax.reduce_precision(square_sum - piece_0, 8, 7)
    piece_2 = square_sum - piece_0 - piece_1
    pieces = jnp.pad(
        jnp.concatenate([piece_0, piece_1, piece_2], axis=1), ((0, 0), (0, LANES - 3))
    )
    up_message = jnp.concatenate([up_pair[:, :half_up], pieces], axis=1).astype(jnp.bfloat16)
    up_sum = jnp.sum(gather_all(up_message, "chip", n_chips).astype(jnp.float32), axis=0)
    squares = jnp.sum(up_sum[:, half_up:], axis=1, keepdims=True)
    inv_mlp = lax.rsqrt(squares / D + NORM_EPS)
    active_half = squared_relu(up_sum[:, :half_up] * inv_mlp).astype(jnp.bfloat16)
    active_other = swap(active_half, "core")
    activated = jnp.concatenate(
        [
            jnp.where(core == 0, active_half, active_other),
            jnp.where(core == 0, active_other, active_half),
        ],
        axis=1,
    )
    down_part = jnp.dot(activated, down_weight, preferred_element_type=jnp.float32)
    mlp_out = sum_tp(down_part)
    return (resid_rows + mlp_out).astype(jnp.bfloat16)


IN_VMEM = pl.BlockSpec(memory_space=pltpu.VMEM)


def local_kernel(kernel, outs, operands, flops, scratch=(), in_hbm=(), anywhere=()):
    in_specs, placed, moved = [], [], 0
    for i, x in enumerate(operands):
        space = pltpu.HBM if i in in_hbm else pltpu.VMEM
        in_specs.append(pl.BlockSpec(memory_space=space))
        placed.append(x if i in anywhere else pltpu.with_memory_space_constraint(x, space))
        moved += x.size * x.dtype.itemsize
    return pl.pallas_call(
        kernel,
        out_shape=outs,
        in_specs=in_specs,
        out_specs=[IN_VMEM] * len(outs),
        scratch_shapes=scratch,
        compiler_params=pltpu.CompilerParams(vmem_limit_bytes=6 * 2**20),
        cost_estimate=pl.CostEstimate(flops=flops, bytes_accessed=moved, transcendentals=0),
    )(*placed)


def f32(*shape):
    return pltpu.VMEM(shape, jnp.float32)


def bf16(*shape):
    return pltpu.VMEM(shape, jnp.bfloat16)


def pieces_of(values_in):
    first = values_in.astype(jnp.bfloat16).astype(jnp.float32)
    second = (values_in - first).astype(jnp.bfloat16).astype(jnp.float32)
    return first, second, values_in - first - second


def prepare_kernel(
    x_hbm, gain_hbm, mlp_gain_hbm, mask_hbm, lengths_hbm, order_hbm, key_hbm, value_hbm,
    scaled_ref, squares_ref, live_ref, x_ref, mlp_gain_ref, key_ref, value_ref,
    gain_ref, mask_ref, lengths_ref, order_ref, sems,
):
    core = lax.axis_index("core")
    n_blocks = lax.axis_size("chip") * 2
    my_block = 2 * lax.axis_index("chip") + core
    half = key_ref.shape[2]
    heads = pl.ds(pl.multiple_of((1 - core) * half, LANES), half)
    pairs = [
        (x_hbm, x_ref), (gain_hbm, gain_ref), (mask_hbm, mask_ref), (lengths_hbm, lengths_ref),
        (order_hbm, order_ref), (mlp_gain_hbm, mlp_gain_ref),
        (key_hbm.at[:, :, heads], key_ref), (value_hbm.at[:, :, heads], value_ref),
    ]
    copies = [pltpu.make_async_copy(src, dst, sems.at[i]) for i, (src, dst) in enumerate(pairs)]
    for copy in copies:
        copy.start()
    for copy in copies[:-2]:
        copy.wait()
    n_req, span = live_ref.shape
    slot = lax.broadcasted_iota(jnp.int32, (1, span), 1)
    for r in range(n_req):
        first_block = lax.rem(order_ref[r], n_blocks)
        begin = lax.rem(my_block - first_block + n_blocks, n_blocks) * span
        live = (begin + slot < lengths_ref[r]) & (mask_ref[r : r + 1, :] == 1)
        live_ref[r : r + 1, :] = live.astype(jnp.float32)
    x_rows = x_ref[...].astype(jnp.float32)
    scaled_ref[...] = (x_rows * gain_ref[...]).astype(jnp.bfloat16)
    squares = jnp.sum(x_rows * x_rows, axis=1, keepdims=True)
    squares_ref[...] = jnp.broadcast_to(squares, squares_ref.shape)
    for copy in copies[-2:]:
        copy.wait()


def qkv_columns(scaled_ref, w_refs, core, out_ref):
    at = 0
    for w_ref in w_refs:
        half = w_ref.shape[1] // 2
        mine = pl.ds(pl.multiple_of(core * half, LANES), half)
        out_ref[:, at : at + half] = jnp.dot(
            scaled_ref[...], w_ref[:, mine], preferred_element_type=jnp.float32
        )
        at += half
    return at


def qkv_other_kernel(scaled_ref, squares_ref, live_ref, wq_ref, wk_ref, wv_ref, other_ref):
    other = 1 - lax.axis_index("core")
    at = qkv_columns(scaled_ref, (wq_ref, wk_ref, wv_ref), other, other_ref)
    other_ref[:, at : at + LANES] = squares_ref[...]
    other_ref[:, at + LANES :] = live_ref[...]


def qkv_mine_kernel(scaled_ref, squares_ref, wq_ref, wk_ref, wv_ref, mine_ref):
    core = lax.axis_index("core")
    at = qkv_columns(scaled_ref, (wq_ref, wk_ref, wv_ref), core, mine_ref)
    mine_ref[:, at:] = squares_ref[...]


SCALE_UNIT = 1024.0


def qkv_message_kernel(mine_ref, arrived_ref, out_ref):
    width = mine_ref.shape[1] - LANES
    features = D / lax.axis_size("chip")
    total = mine_ref[...] + arrived_ref[:, : width + LANES]
    squares = total[:, width:]
    scale = jnp.sqrt(jnp.maximum(squares * (1.0 / features), 2.0**-40))
    scale = scale.astype(jnp.bfloat16).astype(jnp.float32)
    inverse = 1.0 / scale
    out_ref[:, :width] = total[:, :width] * inverse[:, :1]
    lane = lax.broadcasted_iota(jnp.int32, squares.shape, 1)
    tile = jnp.where(lane == 0, scale * SCALE_UNIT, 0.0)
    for p, piece in enumerate(pieces_of(squares * inverse * inverse * (1.0 / features))):
        tile = jnp.where(lane == 1 + p, piece, tile)
    out_ref[:, width:] = tile


def qkv_sum_kernel(arrived_ref, out_ref):
    width = out_ref.shape[1]
    features = D / arrived_ref.shape[0]
    total, squares = 0.0, 0.0
    for i in range(arrived_ref.shape[0]):
        tile = arrived_ref[i, :, width:]
        scale = tile[:, :1] * (1.0 / SCALE_UNIT)
        total = total + arrived_ref[i, :, :width] * scale
        mean = tile[:, 1:2] + tile[:, 2:3] + tile[:, 3:4]
        squares = squares + mean * scale * scale * features
    inv_attn = lax.rsqrt(squares / D + NORM_EPS)
    out_ref[...] = (total * inv_attn).astype(jnp.bfloat16)


PIECE = 16
TOP_AT = 3 * PIECE


def attention_kernel(
    qkv_ref, key_own, key_peer, value_own, value_peer, live_own, live_peer,
    message_ref, query_ref, key_new_ref, value_new_ref,
):
    n_copies, heads, _ = message_ref.shape
    n_req, span = live_own.shape
    half = key_own.shape[2] // 2
    mine = pl.ds(pl.multiple_of(lax.axis_index("core") * half, LANES), half)
    kv_half = half // HD
    group = heads // kv_half
    is_first = lax.axis_index("chip") == 0
    qkv = qkv_ref[...].astype(jnp.float32)
    for h in range(heads):
        query_ref[:, h, :] = qkv[:, h * HD : (h + 1) * HD]
        at = (heads + h // group) * HD
        key_new_ref[:, h, :] = qkv[:, at : at + HD]
        at += kv_half * HD
        value_new_ref[:, h, :] = qkv[:, at : at + HD]

    rows = n_req * heads
    query = query_ref[...].reshape(rows, HD)
    group_of = lax.broadcasted_iota(jnp.int32, (rows, HD), 0) % heads // group
    spread = jnp.concatenate(
        [jnp.where(group_of == k, query, 0.0) for k in range(kv_half)], axis=1
    ).astype(jnp.bfloat16)
    scores, live = [], []
    for r in range(n_req):
        blocks = []
        for keys in (key_own[r, :, mine], key_peer[r]):
            blocks.append(
                lax.dot_general(
                    spread[r * heads : (r + 1) * heads, :], keys,
                    (((1,), (1,)), ((), ())), preferred_element_type=jnp.float32,
                )
            )
        scores.append(jnp.concatenate(blocks, axis=1))
        live_row = jnp.concatenate([live_own[r : r + 1, :], live_peer[r : r + 1, :]], axis=1)
        live.append(jnp.broadcast_to(live_row, (heads, 2 * span)))
    live = jnp.concatenate(live, axis=0) > 0.0
    scale = 1.0 / math.sqrt(HD)
    scores = jnp.where(live, jnp.concatenate(scores, axis=0) * scale, MASKED)
    key_new = key_new_ref[...].reshape(rows, HD)
    self_score = jnp.sum(query * key_new, axis=1, keepdims=True) * scale
    self_score = jnp.where(is_first, self_score, MASKED)
    top = jnp.maximum(jnp.max(scores, axis=1, keepdims=True), self_score)
    weights = jnp.where(live, jnp.exp(scores - top), 0.0)
    self_weight = jnp.where(is_first, jnp.exp(self_score - top), 0.0)
    total = jnp.sum(weights, axis=1, keepdims=True) + self_weight
    rounded = weights.astype(jnp.bfloat16)
    self_part = self_weight * value_new_ref[...].reshape(rows, HD)
    pieces = pieces_of(total) + pieces_of(top)
    lane = lax.broadcasted_iota(jnp.int32, (heads, LANES), 1)
    stats = jnp.zeros((heads, LANES), jnp.float32)
    parts = []
    for r in range(n_req):
        at = slice(r * heads, (r + 1) * heads)
        wide = jnp.dot(
            rounded[at, :span], value_own[r, :, mine], preferred_element_type=jnp.float32
        ) + jnp.dot(
            rounded[at, span:], value_peer[r], preferred_element_type=jnp.float32
        )
        numer = self_part[at, :]
        for k in range(kv_half):
            numer = numer + jnp.where(group_of[at, :] == k, wide[:, k * HD : (k + 1) * HD], 0.0)
        parts.append(numer)
        for p, piece in enumerate(pieces):
            stats = jnp.where(lane == p * PIECE + r, piece[at, :], stats)
    message = jnp.concatenate(parts + [stats], axis=1).astype(jnp.bfloat16)
    for i in range(n_copies):
        message_ref[i] = message


def combine_kernel(arrived_ref, w_ref, head_ref, attended_ref):
    n_blocks, heads, width = arrived_ref.shape
    n_req = head_ref.shape[0]
    for c in range(2):
        blocks = range(c, n_blocks, 2)
        totals, tops = [], []
        for b in blocks:
            tile = arrived_ref[b, :, width - LANES :].astype(jnp.float32)
            tile = (
                tile
                + pltpu.roll(tile, LANES - PIECE, 1)
                + pltpu.roll(tile, LANES - 2 * PIECE, 1)
            )
            totals.append(tile)
            tops.append(pltpu.roll(tile, LANES - TOP_AT, 1))
        final_top = tops[0]
        for top in tops[1:]:
            final_top = jnp.maximum(final_top, top)
        fades = [jnp.exp(top - final_top) for top in tops]
        denominator = totals[0] * fades[0]
        for total, fade in zip(totals[1:], fades[1:]):
            denominator = denominator + total * fade
        for r in range(n_req):
            numer = jnp.zeros((heads, HD), jnp.float32)
            for b, fade in zip(blocks, fades):
                part = arrived_ref[b, :, r * HD : (r + 1) * HD].astype(jnp.float32)
                numer = numer + part * fade[:, r : r + 1]
            attended_ref[r, c * heads : (c + 1) * heads, :] = numer / denominator[:, r : r + 1]
    attended = jnp.concatenate([attended_ref[:, h, :] for h in range(2 * heads)], axis=1)
    head_ref[...] = jnp.dot(
        attended.astype(jnp.bfloat16), w_ref[...], preferred_element_type=jnp.float32
    )


def up_columns(scaled_mlp, w_ref, core, out_ref):
    half = out_ref.shape[1] - LANES
    mine = pl.ds(pl.multiple_of(core * half, LANES), half)
    out_ref[:, :half] = jnp.dot(scaled_mlp, w_ref[:, mine], preferred_element_type=jnp.float32)


def up_other_kernel(
    x_ref, part_ref, peer_ref, gain_ref, w_ref, hidden_ref, scaled_ref, squares_ref, other_ref
):
    attn_out = part_ref[...] + peer_ref[...]
    hidden_state = (x_ref[...].astype(jnp.float32) + attn_out).astype(jnp.bfloat16)
    resid_rows = hidden_state.astype(jnp.float32)
    hidden_ref[...] = resid_rows
    scaled_mlp = (resid_rows * gain_ref[...]).astype(jnp.bfloat16)
    scaled_ref[...] = scaled_mlp
    squares = jnp.sum(resid_rows * resid_rows, axis=1, keepdims=True)
    squares_ref[...] = jnp.broadcast_to(squares, squares_ref.shape)
    other_ref[:, other_ref.shape[1] - LANES :] = squares_ref[...]
    up_columns(scaled_mlp, w_ref, 1 - lax.axis_index("core"), other_ref)


def up_mine_kernel(scaled_ref, squares_ref, w_ref, mine_ref):
    mine_ref[:, mine_ref.shape[1] - LANES :] = squares_ref[...]
    up_columns(scaled_ref[...], w_ref, lax.axis_index("core"), mine_ref)


def up_message_kernel(mine_ref, arrived_ref, message_ref):
    half = mine_ref.shape[1] - LANES
    message = (mine_ref[:, :half] + arrived_ref[:, :half]).astype(jnp.bfloat16)
    squares = mine_ref[:, half:] + arrived_ref[:, half:]
    lane = lax.broadcasted_iota(jnp.int32, squares.shape, 1)
    tile = jnp.zeros_like(squares)
    for p, piece in enumerate(pieces_of(squares)):
        tile = jnp.where(lane == p, piece, tile)
    for i in range(message_ref.shape[0]):
        message_ref[i, :, :half] = message
        message_ref[i, :, half:] = tile.astype(jnp.bfloat16)


def activate_kernel(arrived_ref, out_ref):
    half = out_ref.shape[1]
    total = arrived_ref[0].astype(jnp.float32)
    for i in range(1, arrived_ref.shape[0]):
        total = total + arrived_ref[i].astype(jnp.float32)
    squares = jnp.sum(total[:, half:], axis=1, keepdims=True)
    inv_mlp = lax.rsqrt(squares / D + NORM_EPS)
    out_ref[...] = squared_relu(total[:, :half] * inv_mlp).astype(jnp.bfloat16)


def down_own_kernel(own_ref, w_ref, out_ref):
    half = own_ref.shape[1]
    rows = pl.ds(pl.multiple_of(lax.axis_index("core") * half, LANES), half)
    out_ref[...] = jnp.dot(own_ref[...], w_ref[rows, :], preferred_element_type=jnp.float32)


def down_peer_kernel(own_part, peer_ref, w_ref, out_ref):
    half = peer_ref.shape[1]
    rows = pl.ds(pl.multiple_of((1 - lax.axis_index("core")) * half, LANES), half)
    out_ref[...] = own_part[...] + jnp.dot(
        peer_ref[...], w_ref[rows, :], preferred_element_type=jnp.float32
    )


def per_device(
    hidden_in,
    attn_gain,
    mlp_gain,
    query_weight,
    key_weight,
    value_weight,
    out_weight,
    up_weight,
    down_weight,
    key_cache,
    value_cache,
    lengths,
    block_order,
    pad_mask,
):
    n_req, d_here = hidden_in.shape
    kv_here = key_cache.shape[2] // HD
    heads_here = kv_here * (H // KVH)
    n_chips = lax.axis_size("chip")
    core = lax.axis_index("core")
    n_blocks = 2 * n_chips
    half_qkv = (heads_here + 2 * kv_here) * HD // 2
    half_up = up_weight.shape[1] // 2

    row = (1, d_here)
    small = [hidden_in, attn_gain.reshape(row), mlp_gain.reshape(row), pad_mask]
    small += [lengths, block_order, key_cache, value_cache]
    peer_heads = bf16(*key_cache.shape[:2], key_cache.shape[2] // 2)
    scaled_in, squares, live, x_rows, gain, key_sent, value_sent = local_kernel(
        prepare_kernel,
        [
            bf16(*hidden_in.shape),
            f32(n_req, LANES),
            f32(*pad_mask.shape),
            bf16(*hidden_in.shape),
            f32(*row),
            peer_heads,
            peer_heads,
        ],
        small,
        flops=4 * 10**9,
        scratch=[
            pltpu.VMEM(row, jnp.float32),
            pltpu.VMEM(pad_mask.shape, jnp.int32),
            pltpu.SMEM(lengths.shape, jnp.int32),
            pltpu.SMEM(block_order.shape, jnp.int32),
            pltpu.SemaphoreType.DMA((len(small),)),
        ],
        in_hbm=range(len(small)),
    )
    key_peer, value_peer = swap(key_sent, "core"), swap(value_sent, "core")
    (other,) = local_kernel(
        qkv_other_kernel,
        [f32(n_req, half_qkv + LANES + pad_mask.shape[1])],
        [scaled_in, squares, live, query_weight, key_weight, value_weight],
        flops=4 * 10**9,
        anywhere=(3, 4, 5),
    )
    (mine,) = local_kernel(
        qkv_mine_kernel,
        [f32(n_req, half_qkv + LANES)],
        [scaled_in, squares, query_weight, key_weight, value_weight],
        flops=2 * n_req * d_here * half_qkv,
        anywhere=(2, 3, 4),
    )
    arrived = swap(other, "core")
    width = mine.shape[1]
    (qkv_message,) = local_kernel(
        qkv_message_kernel, [f32(*mine.shape)], [mine, arrived], flops=2 * mine.size
    )
    qkv_message, live_peer, key_peer, value_peer = lax.optimization_barrier(
        (qkv_message.astype(jnp.float16), arrived[:, width:], key_peer, value_peer)
    )
    (qkv_half,) = local_kernel(
        qkv_sum_kernel,
        [bf16(n_req, half_qkv)],
        [gather_all(qkv_message, "chip", n_chips).astype(jnp.float32)],
        flops=n_chips * n_req * half_qkv,
    )
    half_heads = heads_here // 2
    (message,) = local_kernel(
        attention_kernel,
        [bf16(n_blocks, half_heads, n_req * HD + LANES)],
        [qkv_half, key_cache, key_peer, value_cache, value_peer, live, live_peer],
        anywhere=(1, 2, 3, 4),
        flops=4 * 10**9,
        scratch=[pltpu.VMEM((n_req, half_heads, HD), jnp.float32)] * 3,
    )
    arrived = lax.all_to_all(message, ("chip", "core"), 0, 0)
    (head_part,) = local_kernel(
        combine_kernel,
        [f32(n_req, d_here)],
        [arrived, out_weight],
        anywhere=(1,),
        flops=2 * n_req * out_weight.size,
        scratch=[pltpu.VMEM((n_req, heads_here, HD), jnp.float32)],
    )
    head_peer = swap(head_part, "tp")
    resid_rows, scaled_mlp, squares, up_other = local_kernel(
        up_other_kernel,
        [
            f32(n_req, d_here),
            bf16(n_req, d_here),
            f32(n_req, LANES),
            f32(n_req, half_up + LANES),
        ],
        [x_rows, head_part, head_peer, gain, up_weight],
        flops=n_req * up_weight.size,
        anywhere=(4,),
    )
    (up_mine,) = local_kernel(
        up_mine_kernel,
        [f32(n_req, half_up + LANES)],
        [scaled_mlp, squares, up_weight],
        flops=n_req * up_weight.size,
        anywhere=(2,),
    )
    (up_message,) = local_kernel(
        up_message_kernel,
        [bf16(n_chips, n_req, half_up + LANES)],
        [up_mine, swap(up_other, "core")],
        flops=n_chips * n_req * half_up,
    )
    (active_half,) = local_kernel(
        activate_kernel,
        [bf16(n_req, half_up)],
        [lax.all_to_all(up_message, "chip", 0, 0)],
        flops=n_chips * n_req * half_up,
    )
    active_other = swap(active_half, "core")
    (down_own,) = local_kernel(
        down_own_kernel,
        [f32(n_req, d_here)],
        [active_half, down_weight],
        flops=n_req * down_weight.size,
        anywhere=(1,),
    )
    (down_part,) = local_kernel(
        down_peer_kernel,
        [f32(n_req, d_here)],
        [down_own, active_other, down_weight],
        flops=n_req * down_weight.size,
        anywhere=(2,),
    )
    mlp_out = sum_tp(down_part)
    return (resid_rows + mlp_out).astype(jnp.bfloat16)


def solution(mesh):
    n_seq, n_tp = mesh.shape["seq"], mesh.shape["tp"]
    split = Mesh(mesh.devices.reshape(n_seq // 2, 2, n_tp), ("chip", "core", "tp"))
    seq = ("chip", "core")
    whole_tiles = n_tp == 2 and KVH % (2 * n_tp) == 0 and D % (n_seq * LANES) == 0
    return jax.shard_map(
        per_device if whole_tiles else per_device_plain,
        mesh=split,
        in_specs=(
            P(None, seq),
            P(seq),
            P(seq),
            P(seq, "tp"),
            P(seq, "tp"),
            P(seq, "tp"),
            P("tp", seq),
            P(seq, "tp"),
            P("tp", seq),
            P(None, seq, "tp"),
            P(None, seq, "tp"),
            P(),
            P(),
            P(None, seq),
        ),
        out_specs=P(None, seq),
        check_vma=False,
    )
```

```python
import math

import jax
import jax.numpy as jnp
from jax import lax
from jax.experimental import pallas as pl
from jax.experimental.pallas import tpu as pltpu
from jax.sharding import Mesh, PartitionSpec as P

D = 4096
H = 32
KVH = 8
HD = 128


NORM_EPS = 1e-05
MASKED = -1e30
LANES = 128


def squared_relu(values_in):
    positive = jnp.maximum(values_in, 0.0)
    return positive * positive


def swap(values_in, axis):
    n = lax.axis_size(axis)
    return lax.ppermute(values_in, axis, [(i, i ^ 1) for i in range(n)])


def swap_diagonal(values_in):
    return lax.ppermute(values_in, ("core", "tp"), [(i, 3 - i) for i in range(4)])


def gather_all(values_in, axes, n):
    copies = jnp.broadcast_to(values_in[None], (n,) + values_in.shape)
    return lax.all_to_all(copies, axes, 0, 0)


def sum_tp(values_in):
    n = lax.axis_size("tp")
    if n == 2:
        return values_in + swap(values_in, "tp")
    return lax.psum(values_in, "tp")


def per_device_plain(
    hidden_in,
    attn_gain,
    mlp_gain,
    query_weight,
    key_weight,
    value_weight,
    out_weight,
    up_weight,
    down_weight,
    key_cache,
    value_cache,
    lengths,
    block_order,
    pad_mask,
):
    n_req = hidden_in.shape[0]
    q_per_kv = H // KVH
    kv_here = key_cache.shape[2] // HD
    span_here = key_cache.shape[1]
    heads_here = kv_here * q_per_kv
    n_chips = lax.axis_size("chip")
    core = lax.axis_index("core")
    n_blocks = 2 * n_chips
    my_block = 2 * lax.axis_index("chip") + core
    score_scale = 1.0 / math.sqrt(HD)

    x_rows = hidden_in.astype(jnp.float32)
    scaled_in = (x_rows * attn_gain).astype(jnp.bfloat16)
    sq_attn = jnp.sum(x_rows * x_rows, axis=1, keepdims=True)
    proj_query = jnp.dot(scaled_in, query_weight, preferred_element_type=jnp.float32)
    proj_key = jnp.dot(scaled_in, key_weight, preferred_element_type=jnp.float32)
    proj_value = jnp.dot(scaled_in, value_weight, preferred_element_type=jnp.float32)
    half_q, half_kv = proj_query.shape[1] // 2, proj_key.shape[1] // 2
    square_cols = jnp.broadcast_to(sq_attn, (n_req, LANES))

    def half(i):
        return jnp.concatenate(
            [
                proj_query[:, i * half_q : (i + 1) * half_q],
                proj_key[:, i * half_kv : (i + 1) * half_kv],
                proj_value[:, i * half_kv : (i + 1) * half_kv],
                square_cols,
            ],
            axis=1,
        )

    low, high = half(0), half(1)
    mine = jnp.where(core == 0, low, high)
    other = jnp.where(core == 0, high, low)
    pair_sum = mine + swap(other, "core")
    qkv_sum = jnp.sum(gather_all(pair_sum, "chip", n_chips), axis=0)
    inv_attn = lax.rsqrt(qkv_sum[:, -1:] / D + NORM_EPS)
    qkv_half = (qkv_sum[:, :-LANES] * inv_attn).astype(jnp.bfloat16)
    qkv_other = swap(qkv_half, "core")
    qkv_low = jnp.where(core == 0, qkv_half, qkv_other)
    qkv_high = jnp.where(core == 0, qkv_other, qkv_half)

    def both(start, size):
        return jnp.concatenate(
            [qkv_low[:, start : start + size], qkv_high[:, start : start + size]], axis=1
        )

    query_rows = both(0, half_q)
    key_new = both(half_q, half_kv)
    value_new = both(half_q + half_kv, half_kv)

    first_block = block_order % n_blocks
    position = ((my_block - first_block) % n_blocks)[:, None] * span_here + jnp.arange(
        span_here, dtype=jnp.int32
    )[None, :]
    live_slots = ((position < lengths[:, None]) & (pad_mask == 1))[:, None, None, :]
    q_groups = query_rows.reshape(n_req, kv_here, q_per_kv, HD)
    keys_here = key_cache.reshape(n_req, span_here, kv_here, HD)
    values_here = value_cache.reshape(n_req, span_here, kv_here, HD)
    scores = (
        jnp.einsum("rkgd,rtkd->rkgt", q_groups, keys_here, preferred_element_type=jnp.float32)
        * score_scale
    )
    scores = jnp.where(live_slots, scores, MASKED)
    local_top = jnp.max(scores, axis=3, keepdims=True)
    weights = jnp.where(live_slots, jnp.exp(scores - local_top), 0.0)
    local_total = jnp.sum(weights, axis=3, keepdims=True)
    local_out = jnp.einsum(
        "rkgt,rtkd->rkgd",
        weights.astype(jnp.bfloat16),
        values_here,
        preferred_element_type=jnp.float32,
    )
    numer = local_out.reshape(n_req, heads_here, HD)
    stats = jnp.concatenate(
        [
            local_total.reshape(n_req, heads_here, 1),
            local_top.reshape(n_req, heads_here, 1),
        ],
        axis=2,
    )
    stat_rows = stats.reshape(n_req, heads_here * 2)
    pad = (-stat_rows.shape[1]) % LANES
    message = jnp.concatenate(
        [numer.reshape(n_req, heads_here * HD), jnp.pad(stat_rows, ((0, 0), (0, pad)))], axis=1
    )
    arrived = gather_all(message, ("chip", "core"), n_blocks)
    outs = arrived[:, :, : heads_here * HD].reshape(n_blocks, n_req, heads_here, HD)
    stats_all = arrived[:, :, heads_here * HD : heads_here * (HD + 2)].reshape(
        n_blocks, n_req, heads_here, 2
    )
    totals, tops = stats_all[..., 0], stats_all[..., 1]
    self_score = (
        jnp.einsum(
            "rkgd,rkd->rkg",
            q_groups,
            key_new.reshape(n_req, kv_here, HD),
            preferred_element_type=jnp.float32,
        )
        * score_scale
    ).reshape(n_req, heads_here)
    final_top = jnp.maximum(jnp.max(tops, axis=0), self_score)
    fades = jnp.exp(tops - final_top)
    self_weight = jnp.exp(self_score - final_top)
    denominator = jnp.sum(totals * fades, axis=0) + self_weight
    value_self = jnp.broadcast_to(
        value_new.reshape(n_req, kv_here, 1, HD), (n_req, kv_here, q_per_kv, HD)
    ).reshape(n_req, heads_here, HD)
    numerator = jnp.sum(outs * fades[..., None], axis=0) + self_weight[
        ..., None
    ] * value_self.astype(jnp.float32)
    attended = (
        (numerator / denominator[..., None])
        .reshape(n_req, heads_here * HD)
        .astype(jnp.bfloat16)
    )
    head_part = jnp.dot(attended, out_weight, preferred_element_type=jnp.float32)
    attn_out = sum_tp(head_part)
    hidden_state = (x_rows + attn_out).astype(jnp.bfloat16)

    resid_rows = hidden_state.astype(jnp.float32)
    scaled_mlp = (resid_rows * mlp_gain).astype(jnp.bfloat16)
    sq_mlp = jnp.sum(resid_rows * resid_rows, axis=1, keepdims=True)
    up_part = jnp.dot(scaled_mlp, up_weight, preferred_element_type=jnp.float32)
    half_up = up_part.shape[1] // 2
    up_low, up_high = up_part[:, :half_up], up_part[:, half_up:]
    square_cols = jnp.broadcast_to(sq_mlp, (n_req, LANES))
    up_mine = jnp.concatenate([jnp.where(core == 0, up_low, up_high), square_cols], axis=1)
    up_other = jnp.concatenate([jnp.where(core == 0, up_high, up_low), square_cols], axis=1)
    up_pair = up_mine + swap(up_other, "core")
    square_sum = up_pair[:, half_up : half_up + 1]
    piece_0 = lax.reduce_precision(square_sum, 8, 7)
    piece_1 = lax.reduce_precision(square_sum - piece_0, 8, 7)
    piece_2 = square_sum - piece_0 - piece_1
    pieces = jnp.pad(
        jnp.concatenate([piece_0, piece_1, piece_2], axis=1), ((0, 0), (0, LANES - 3))
    )
    up_message = jnp.concatenate([up_pair[:, :half_up], pieces], axis=1).astype(jnp.bfloat16)
    up_sum = jnp.sum(gather_all(up_message, "chip", n_chips).astype(jnp.float32), axis=0)
    squares = jnp.sum(up_sum[:, half_up:], axis=1, keepdims=True)
    inv_mlp = lax.rsqrt(squares / D + NORM_EPS)
    active_half = squared_relu(up_sum[:, :half_up] * inv_mlp).astype(jnp.bfloat16)
    active_other = swap(active_half, "core")
    activated = jnp.concatenate(
        [
            jnp.where(core == 0, active_half, active_other),
            jnp.where(core == 0, active_other, active_half),
        ],
        axis=1,
    )
    down_part = jnp.dot(activated, down_weight, preferred_element_type=jnp.float32)
    mlp_out = sum_tp(down_part)
    return (resid_rows + mlp_out).astype(jnp.bfloat16)


IN_VMEM = pl.BlockSpec(memory_space=pltpu.VMEM)


def chip_turn(chip):
    return chip // 2 % 2


def head_half():
    return (lax.axis_index("core") + chip_turn(lax.axis_index("chip"))) % 2


def local_kernel(kernel, outs, operands, flops, scratch=(), in_hbm=(), anywhere=()):
    in_specs, placed, moved = [], [], 0
    for i, x in enumerate(operands):
        space = pltpu.HBM if i in in_hbm else pltpu.VMEM
        in_specs.append(pl.BlockSpec(memory_space=space))
        placed.append(x if i in anywhere else pltpu.with_memory_space_constraint(x, space))
        moved += x.size * x.dtype.itemsize
    return pl.pallas_call(
        kernel,
        out_shape=outs,
        in_specs=in_specs,
        out_specs=[IN_VMEM] * len(outs),
        scratch_shapes=scratch,
        compiler_params=pltpu.CompilerParams(vmem_limit_bytes=6 * 2**20),
        cost_estimate=pl.CostEstimate(flops=flops, bytes_accessed=moved, transcendentals=0),
    )(*placed)


def f32(*shape):
    return pltpu.VMEM(shape, jnp.float32)


def bf16(*shape):
    return pltpu.VMEM(shape, jnp.bfloat16)


def pieces_of(values_in):
    first = values_in.astype(jnp.bfloat16).astype(jnp.float32)
    second = (values_in - first).astype(jnp.bfloat16).astype(jnp.float32)
    return first, second, values_in - first - second


def prepare_kernel(
    x_hbm, gain_hbm, mlp_gain_hbm, mask_hbm, lengths_hbm, order_hbm, key_hbm, value_hbm,
    scaled_ref, squares_ref, live_ref, x_ref, mlp_gain_ref, cache_ref,
    gain_ref, mask_ref, lengths_ref, order_ref, sems,
):
    core = lax.axis_index("core")
    n_blocks = lax.axis_size("chip") * 2
    my_block = 2 * lax.axis_index("chip") + core
    half = cache_ref.shape[3]
    heads = pl.ds(pl.multiple_of((1 - head_half()) * half, LANES), half)
    pairs = [
        (x_hbm, x_ref), (gain_hbm, gain_ref), (mask_hbm, mask_ref), (lengths_hbm, lengths_ref),
        (order_hbm, order_ref), (mlp_gain_hbm, mlp_gain_ref),
        (key_hbm.at[:, :, heads], cache_ref.at[0]), (value_hbm.at[:, :, heads], cache_ref.at[1]),
    ]
    copies = [pltpu.make_async_copy(src, dst, sems.at[i]) for i, (src, dst) in enumerate(pairs)]
    for copy in copies:
        copy.start()
    for copy in copies[:-2]:
        copy.wait()
    n_req, span = live_ref.shape
    slot = lax.broadcasted_iota(jnp.int32, (1, span), 1)
    for r in range(n_req):
        first_block = lax.rem(order_ref[r], n_blocks)
        begin = lax.rem(my_block - first_block + n_blocks, n_blocks) * span
        live = (begin + slot < lengths_ref[r]) & (mask_ref[r : r + 1, :] == 1)
        live_ref[r : r + 1, :] = live.astype(jnp.float32)
    x_rows = x_ref[...].astype(jnp.float32)
    scaled_ref[...] = (x_rows * gain_ref[...]).astype(jnp.bfloat16)
    squares = jnp.sum(x_rows * x_rows, axis=1, keepdims=True)
    squares_ref[...] = jnp.broadcast_to(squares, squares_ref.shape)
    for copy in copies[-2:]:
        copy.wait()


def qkv_columns(scaled_ref, w_refs, side, out_ref):
    at = 0
    for w_ref in w_refs:
        half = w_ref.shape[1] // 2
        mine = pl.ds(pl.multiple_of(side * half, LANES), half)
        out_ref[:, at : at + half] = jnp.dot(
            scaled_ref[...], w_ref[:, mine], preferred_element_type=jnp.float32
        )
        at += half
    return at


def qkv_other_kernel(scaled_ref, squares_ref, live_ref, wq_ref, wk_ref, wv_ref, other_ref):
    other = 1 - head_half()
    at = qkv_columns(scaled_ref, (wq_ref, wk_ref, wv_ref), other, other_ref)
    other_ref[:, at : at + LANES] = squares_ref[...]
    other_ref[:, at + LANES :] = live_ref[...]


def qkv_mine_kernel(scaled_ref, squares_ref, wq_ref, wk_ref, wv_ref, mine_ref):
    at = qkv_columns(scaled_ref, (wq_ref, wk_ref, wv_ref), head_half(), mine_ref)
    mine_ref[:, at:] = squares_ref[...]


SCALE_UNIT = 1024.0


def qkv_message_kernel(mine_ref, arrived_ref, out_ref):
    width = mine_ref.shape[1] - LANES
    features = D / lax.axis_size("chip")
    total = mine_ref[...] + arrived_ref[:, : width + LANES]
    squares = total[:, width:]
    scale = jnp.sqrt(jnp.maximum(squares * (1.0 / features), 2.0**-40))
    scale = scale.astype(jnp.bfloat16).astype(jnp.float32)
    inverse = 1.0 / scale
    out_ref[:, :width] = total[:, :width] * inverse[:, :1]
    lane = lax.broadcasted_iota(jnp.int32, squares.shape, 1)
    tile = jnp.where(lane == 0, scale * SCALE_UNIT, 0.0)
    for p, piece in enumerate(pieces_of(squares * inverse * inverse * (1.0 / features))):
        tile = jnp.where(lane == 1 + p, piece, tile)
    out_ref[:, width:] = tile


def qkv_sum_kernel(arrived_ref, out_ref):
    width = out_ref.shape[1]
    features = D / arrived_ref.shape[0]
    total, squares = 0.0, 0.0
    for i in range(arrived_ref.shape[0]):
        tile = arrived_ref[i, :, width:]
        scale = tile[:, :1] * (1.0 / SCALE_UNIT)
        total = total + arrived_ref[i, :, :width] * scale
        mean = tile[:, 1:2] + tile[:, 2:3] + tile[:, 3:4]
        squares = squares + mean * scale * scale * features
    inv_attn = lax.rsqrt(squares / D + NORM_EPS)
    out_ref[...] = (total * inv_attn).astype(jnp.bfloat16)


PIECE = 16
TOP_AT = 3 * PIECE


def attention_kernel(
    qkv_ref, key_own, value_own, cache_peer, live_own, live_peer,
    message_ref, query_ref, key_new_ref, value_new_ref,
):
    n_copies, heads, _ = message_ref.shape
    n_req, span = live_own.shape
    half = key_own.shape[2] // 2
    mine = pl.ds(pl.multiple_of(head_half() * half, LANES), half)
    kv_half = half // HD
    group = heads // kv_half
    is_first = lax.axis_index("chip") == 0
    qkv = qkv_ref[...].astype(jnp.float32)
    for h in range(heads):
        query_ref[:, h, :] = qkv[:, h * HD : (h + 1) * HD]
        at = (heads + h // group) * HD
        key_new_ref[:, h, :] = qkv[:, at : at + HD]
        at += kv_half * HD
        value_new_ref[:, h, :] = qkv[:, at : at + HD]

    rows = n_req * heads
    query = query_ref[...].reshape(rows, HD)
    group_of = lax.broadcasted_iota(jnp.int32, (rows, HD), 0) % heads // group
    spread = jnp.concatenate(
        [jnp.where(group_of == k, query, 0.0) for k in range(kv_half)], axis=1
    ).astype(jnp.bfloat16)
    scores, live = [], []
    for r in range(n_req):
        blocks = []
        for keys in (key_own[r, :, mine], cache_peer[0, r]):
            blocks.append(
                lax.dot_general(
                    spread[r * heads : (r + 1) * heads, :], keys,
                    (((1,), (1,)), ((), ())), preferred_element_type=jnp.float32,
                )
            )
        scores.append(jnp.concatenate(blocks, axis=1))
        live_row = jnp.concatenate([live_own[r : r + 1, :], live_peer[r : r + 1, :]], axis=1)
        live.append(jnp.broadcast_to(live_row, (heads, 2 * span)))
    live = jnp.concatenate(live, axis=0) > 0.0
    scale = 1.0 / math.sqrt(HD)
    scores = jnp.where(live, jnp.concatenate(scores, axis=0) * scale, MASKED)
    key_new = key_new_ref[...].reshape(rows, HD)
    self_score = jnp.sum(query * key_new, axis=1, keepdims=True) * scale
    self_score = jnp.where(is_first, self_score, MASKED)
    top = jnp.maximum(jnp.max(scores, axis=1, keepdims=True), self_score)
    weights = jnp.where(live, jnp.exp(scores - top), 0.0)
    self_weight = jnp.where(is_first, jnp.exp(self_score - top), 0.0)
    total = jnp.sum(weights, axis=1, keepdims=True) + self_weight
    rounded = weights.astype(jnp.bfloat16)
    self_part = self_weight * value_new_ref[...].reshape(rows, HD)
    pieces = pieces_of(total) + pieces_of(top)
    lane = lax.broadcasted_iota(jnp.int32, (heads, LANES), 1)
    stats = jnp.zeros((heads, LANES), jnp.float32)
    parts = []
    for r in range(n_req):
        at = slice(r * heads, (r + 1) * heads)
        wide = jnp.dot(
            rounded[at, :span], value_own[r, :, mine], preferred_element_type=jnp.float32
        ) + jnp.dot(
            rounded[at, span:], cache_peer[1, r], preferred_element_type=jnp.float32
        )
        numer = self_part[at, :]
        for k in range(kv_half):
            numer = numer + jnp.where(group_of[at, :] == k, wide[:, k * HD : (k + 1) * HD], 0.0)
        parts.append(numer)
        for p, piece in enumerate(pieces):
            stats = jnp.where(lane == p * PIECE + r, piece[at, :], stats)
    message = jnp.concatenate(parts + [stats], axis=1).astype(jnp.bfloat16)
    for i in range(n_copies):
        message_ref[i] = message


def combine_kernel(arrived_ref, w_ref, head_ref, rows_ref, attended_ref):
    n_blocks, heads, width = arrived_ref.shape
    n_req = head_ref.shape[0]
    for c in range(2):
        blocks = [2 * chip + (c + chip_turn(chip)) % 2 for chip in range(n_blocks // 2)]
        totals, tops = [], []
        for b in blocks:
            tile = arrived_ref[b, :, width - LANES :].astype(jnp.float32)
            tile = (
                tile
                + pltpu.roll(tile, LANES - PIECE, 1)
                + pltpu.roll(tile, LANES - 2 * PIECE, 1)
            )
            totals.append(tile)
            tops.append(pltpu.roll(tile, LANES - TOP_AT, 1))
        final_top = tops[0]
        for top in tops[1:]:
            final_top = jnp.maximum(final_top, top)
        fades = [jnp.exp(top - final_top) for top in tops]
        denominator = totals[0] * fades[0]
        for total, fade in zip(totals[1:], fades[1:]):
            denominator = denominator + total * fade
        for r in range(n_req):
            numer = jnp.zeros((heads, HD), jnp.float32)
            for b, fade in zip(blocks, fades):
                part = arrived_ref[b, :, r * HD : (r + 1) * HD].astype(jnp.float32)
                numer = numer + part * fade[:, r : r + 1]
            attended_ref[r, c * heads : (c + 1) * heads, :] = numer / denominator[:, r : r + 1]
    attended = jnp.concatenate([attended_ref[:, h, :] for h in range(2 * heads)], axis=1)
    attended = attended.astype(jnp.bfloat16)
    rows_ref[...] = attended
    head_ref[...] = jnp.dot(attended, w_ref[...], preferred_element_type=jnp.float32)


def out_kernel(rows_ref, w_ref, head_ref):
    head_ref[...] = jnp.dot(rows_ref[...], w_ref[...], preferred_element_type=jnp.float32)


def up_columns(scaled_mlp, w_ref, core, out_ref):
    half = out_ref.shape[1] - LANES
    mine = pl.ds(pl.multiple_of(core * half, LANES), half)
    out_ref[:, :half] = jnp.dot(scaled_mlp, w_ref[:, mine], preferred_element_type=jnp.float32)


def up_other_kernel(
    x_ref, part_ref, peer_ref, gain_ref, w_ref, hidden_ref, scaled_ref, squares_ref, other_ref
):
    attn_out = part_ref[...] + peer_ref[...]
    hidden_state = (x_ref[...].astype(jnp.float32) + attn_out).astype(jnp.bfloat16)
    resid_rows = hidden_state.astype(jnp.float32)
    hidden_ref[...] = resid_rows
    scaled_mlp = (resid_rows * gain_ref[...]).astype(jnp.bfloat16)
    scaled_ref[...] = scaled_mlp
    squares = jnp.sum(resid_rows * resid_rows, axis=1, keepdims=True)
    squares_ref[...] = jnp.broadcast_to(squares, squares_ref.shape)
    other_ref[:, other_ref.shape[1] - LANES :] = squares_ref[...]
    up_columns(scaled_mlp, w_ref, 1 - lax.axis_index("core"), other_ref)


def up_mine_kernel(scaled_ref, squares_ref, w_ref, mine_ref):
    mine_ref[:, mine_ref.shape[1] - LANES :] = squares_ref[...]
    up_columns(scaled_ref[...], w_ref, lax.axis_index("core"), mine_ref)


def up_message_kernel(mine_ref, arrived_ref, message_ref):
    half = mine_ref.shape[1] - LANES
    message = (mine_ref[:, :half] + arrived_ref[:, :half]).astype(jnp.bfloat16)
    squares = mine_ref[:, half:] + arrived_ref[:, half:]
    lane = lax.broadcasted_iota(jnp.int32, squares.shape, 1)
    tile = jnp.zeros_like(squares)
    for p, piece in enumerate(pieces_of(squares)):
        tile = jnp.where(lane == p, piece, tile)
    for i in range(message_ref.shape[0]):
        message_ref[i, :, :half] = message
        message_ref[i, :, half:] = tile.astype(jnp.bfloat16)


def activate_kernel(arrived_ref, out_ref):
    half = out_ref.shape[1]
    total = arrived_ref[0].astype(jnp.float32)
    for i in range(1, arrived_ref.shape[0]):
        total = total + arrived_ref[i].astype(jnp.float32)
    squares = jnp.sum(total[:, half:], axis=1, keepdims=True)
    inv_mlp = lax.rsqrt(squares / D + NORM_EPS)
    out_ref[...] = squared_relu(total[:, :half] * inv_mlp).astype(jnp.bfloat16)


def down_rows(rows_ref, w_ref, core):
    half = rows_ref.shape[1]
    mine = pl.ds(pl.multiple_of(core * half, LANES), half)
    return jnp.dot(rows_ref[...], w_ref[mine, :], preferred_element_type=jnp.float32)


def down_own_kernel(own_ref, w_ref, out_ref):
    out_ref[...] = down_rows(own_ref, w_ref, lax.axis_index("core"))


def down_peer_kernel(own_part, peer_ref, w_ref, out_ref):
    out_ref[...] = own_part[...] + down_rows(peer_ref, w_ref, 1 - lax.axis_index("core"))


def per_device(
    hidden_in,
    attn_gain,
    mlp_gain,
    query_weight,
    key_weight,
    value_weight,
    out_weight,
    up_weight,
    down_weight,
    key_cache,
    value_cache,
    lengths,
    block_order,
    pad_mask,
):
    n_req, d_here = hidden_in.shape
    kv_here = key_cache.shape[2] // HD
    heads_here = kv_here * (H // KVH)
    n_chips = lax.axis_size("chip")
    core = lax.axis_index("core")
    n_blocks = 2 * n_chips
    half_qkv = (heads_here + 2 * kv_here) * HD // 2
    half_up = up_weight.shape[1] // 2

    row = (1, d_here)
    small = [hidden_in, attn_gain.reshape(row), mlp_gain.reshape(row), pad_mask]
    small += [lengths, block_order, key_cache, value_cache]
    scaled_in, squares, live, x_rows, gain, cache_sent = local_kernel(
        prepare_kernel,
        [
            bf16(*hidden_in.shape),
            f32(n_req, LANES),
            f32(*pad_mask.shape),
            bf16(*hidden_in.shape),
            f32(*row),
            bf16(2, *key_cache.shape[:2], key_cache.shape[2] // 2),
        ],
        small,
        flops=4 * 10**9,
        scratch=[
            pltpu.VMEM(row, jnp.float32),
            pltpu.VMEM(pad_mask.shape, jnp.int32),
            pltpu.SMEM(lengths.shape, jnp.int32),
            pltpu.SMEM(block_order.shape, jnp.int32),
            pltpu.SemaphoreType.DMA((len(small),)),
        ],
        in_hbm=range(len(small)),
    )
    (other,) = local_kernel(
        qkv_other_kernel,
        [f32(n_req, half_qkv + LANES + pad_mask.shape[1])],
        [scaled_in, squares, live, query_weight, key_weight, value_weight],
        flops=4 * 10**9,
        anywhere=(3, 4, 5),
    )
    (mine,) = local_kernel(
        qkv_mine_kernel,
        [f32(n_req, half_qkv + LANES)],
        [scaled_in, squares, query_weight, key_weight, value_weight],
        flops=2 * n_req * d_here * half_qkv,
        anywhere=(2, 3, 4),
    )
    arrived = swap(other, "core")
    width = mine.shape[1]
    (qkv_message,) = local_kernel(
        qkv_message_kernel, [f32(*mine.shape)], [mine, arrived], flops=2 * mine.size
    )
    qkv_message, live_peer, *moved = lax.optimization_barrier(
        (
            qkv_message.astype(jnp.float16),
            arrived[:, width:],
            cache_sent,
            out_weight,
        )
    )
    cache_peer, out_peer = (swap(x, "core") for x in moved)
    sides = [
        [2 * chip + (side + chip_turn(chip)) % 2 for chip in range(n_chips)] for side in range(2)
    ]
    qkv_all = lax.all_to_all(
        jnp.broadcast_to(qkv_message[None], (n_chips,) + qkv_message.shape),
        ("chip", "core"),
        0,
        0,
        axis_index_groups=sides,
    )
    (qkv_half,) = local_kernel(
        qkv_sum_kernel,
        [bf16(n_req, half_qkv)],
        [qkv_all.astype(jnp.float32)],
        flops=n_chips * n_req * half_qkv,
    )
    half_heads = heads_here // 2
    (message,) = local_kernel(
        attention_kernel,
        [bf16(n_blocks, half_heads, n_req * HD + LANES)],
        [qkv_half, key_cache, value_cache, cache_peer, live, live_peer],
        anywhere=(1, 2, 3),
        flops=4 * 10**9,
        scratch=[pltpu.VMEM((n_req, half_heads, HD), jnp.float32)] * 3,
    )
    message, out_peer = lax.optimization_barrier((message, out_peer))
    arrived = lax.all_to_all(message, ("chip", "core"), 0, 0)
    head_sent, attended = local_kernel(
        combine_kernel,
        [f32(n_req, d_here), bf16(n_req, heads_here * HD)],
        [arrived, out_peer],
        anywhere=(1,),
        flops=2 * n_req * out_weight.size,
        scratch=[pltpu.VMEM((n_req, heads_here, HD), jnp.float32)],
    )
    head_peer = swap_diagonal(head_sent)
    (head_part,) = local_kernel(
        out_kernel,
        [f32(n_req, d_here)],
        [attended, out_weight],
        anywhere=(1,),
        flops=2 * n_req * out_weight.size,
    )

    resid_rows, scaled_mlp, squares, up_other = local_kernel(
        up_other_kernel,
        [
            f32(n_req, d_here),
            bf16(n_req, d_here),
            f32(n_req, LANES),
            f32(n_req, half_up + LANES),
        ],
        [x_rows, head_part, head_peer, gain, up_weight],
        flops=n_req * up_weight.size,
        anywhere=(4,),
    )
    (up_mine,) = local_kernel(
        up_mine_kernel,
        [f32(n_req, half_up + LANES)],
        [scaled_mlp, squares, up_weight],
        flops=n_req * up_weight.size,
        anywhere=(2,),
    )
    (up_message,) = local_kernel(
        up_message_kernel,
        [bf16(n_chips, n_req, half_up + LANES)],
        [up_mine, swap(up_other, "core")],
        flops=n_chips * n_req * half_up,
    )
    (active_half,) = local_kernel(
        activate_kernel,
        [bf16(n_req, half_up)],
        [lax.all_to_all(up_message, "chip", 0, 0)],
        flops=n_chips * n_req * half_up,
    )
    active_other = swap(active_half, "core")
    (down_own,) = local_kernel(
        down_own_kernel,
        [f32(n_req, d_here)],
        [active_half, down_weight],
        flops=n_req * down_weight.size,
        anywhere=(1,),
    )
    (down_part,) = local_kernel(
        down_peer_kernel,
        [f32(n_req, d_here)],
        [down_own, active_other, down_weight],
        flops=n_req * down_weight.size,
        anywhere=(2,),
    )
    mlp_out = sum_tp(down_part)
    return (resid_rows + mlp_out).astype(jnp.bfloat16)


def solution(mesh):
    n_seq, n_tp = mesh.shape["seq"], mesh.shape["tp"]
    split = Mesh(mesh.devices.reshape(n_seq // 2, 2, n_tp), ("chip", "core", "tp"))
    seq = ("chip", "core")
    whole_tiles = n_tp == 2 and KVH % (2 * n_tp) == 0 and D % (n_seq * LANES) == 0
    return jax.shard_map(
        per_device if whole_tiles else per_device_plain,
        mesh=split,
        in_specs=(
            P(None, seq),
            P(seq),
            P(seq),
            P(seq, "tp"),
            P(seq, "tp"),
            P(seq, "tp"),
            P("tp", seq),
            P(seq, "tp"),
            P("tp", seq),
            P(None, seq, "tp"),
            P(None, seq, "tp"),
            P(),
            P(),
            P(None, seq),
        ),
        out_specs=P(None, seq),
        check_vma=False,
    )
```

```python
import math

import jax
import jax.numpy as jnp
from jax import lax
from jax.experimental import pallas as pl
from jax.experimental.pallas import tpu as pltpu
from jax.sharding import Mesh, PartitionSpec as P

D = 4096
H = 32
KVH = 8
HD = 128


NORM_EPS = 1e-05
MASKED = -1e30
LANES = 128


def squared_relu(values_in):
    positive = jnp.maximum(values_in, 0.0)
    return positive * positive


def swap(values_in, axis):
    n = lax.axis_size(axis)
    return lax.ppermute(values_in, axis, [(i, i ^ 1) for i in range(n)])


def swap_diagonal(values_in):
    return lax.ppermute(values_in, ("core", "tp"), [(i, 3 - i) for i in range(4)])


def gather_all(values_in, axes, n):
    copies = jnp.broadcast_to(values_in[None], (n,) + values_in.shape)
    return lax.all_to_all(copies, axes, 0, 0)


def sum_tp(values_in):
    n = lax.axis_size("tp")
    if n == 2:
        return values_in + swap(values_in, "tp")
    return lax.psum(values_in, "tp")


def per_device_plain(
    hidden_in,
    attn_gain,
    mlp_gain,
    query_weight,
    key_weight,
    value_weight,
    out_weight,
    up_weight,
    down_weight,
    key_cache,
    value_cache,
    lengths,
    block_order,
    pad_mask,
):
    n_req = hidden_in.shape[0]
    q_per_kv = H // KVH
    kv_here = key_cache.shape[2] // HD
    span_here = key_cache.shape[1]
    heads_here = kv_here * q_per_kv
    n_chips = lax.axis_size("chip")
    core = lax.axis_index("core")
    n_blocks = 2 * n_chips
    my_block = 2 * lax.axis_index("chip") + core
    score_scale = 1.0 / math.sqrt(HD)

    x_rows = hidden_in.astype(jnp.float32)
    scaled_in = (x_rows * attn_gain).astype(jnp.bfloat16)
    sq_attn = jnp.sum(x_rows * x_rows, axis=1, keepdims=True)
    proj_query = jnp.dot(scaled_in, query_weight, preferred_element_type=jnp.float32)
    proj_key = jnp.dot(scaled_in, key_weight, preferred_element_type=jnp.float32)
    proj_value = jnp.dot(scaled_in, value_weight, preferred_element_type=jnp.float32)
    half_q, half_kv = proj_query.shape[1] // 2, proj_key.shape[1] // 2
    square_cols = jnp.broadcast_to(sq_attn, (n_req, LANES))

    def half(i):
        return jnp.concatenate(
            [
                proj_query[:, i * half_q : (i + 1) * half_q],
                proj_key[:, i * half_kv : (i + 1) * half_kv],
                proj_value[:, i * half_kv : (i + 1) * half_kv],
                square_cols,
            ],
            axis=1,
        )

    low, high = half(0), half(1)
    mine = jnp.where(core == 0, low, high)
    other = jnp.where(core == 0, high, low)
    pair_sum = mine + swap(other, "core")
    qkv_sum = jnp.sum(gather_all(pair_sum, "chip", n_chips), axis=0)
    inv_attn = lax.rsqrt(qkv_sum[:, -1:] / D + NORM_EPS)
    qkv_half = (qkv_sum[:, :-LANES] * inv_attn).astype(jnp.bfloat16)
    qkv_other = swap(qkv_half, "core")
    qkv_low = jnp.where(core == 0, qkv_half, qkv_other)
    qkv_high = jnp.where(core == 0, qkv_other, qkv_half)

    def both(start, size):
        return jnp.concatenate(
            [qkv_low[:, start : start + size], qkv_high[:, start : start + size]], axis=1
        )

    query_rows = both(0, half_q)
    key_new = both(half_q, half_kv)
    value_new = both(half_q + half_kv, half_kv)

    first_block = block_order % n_blocks
    position = ((my_block - first_block) % n_blocks)[:, None] * span_here + jnp.arange(
        span_here, dtype=jnp.int32
    )[None, :]
    live_slots = ((position < lengths[:, None]) & (pad_mask == 1))[:, None, None, :]
    q_groups = query_rows.reshape(n_req, kv_here, q_per_kv, HD)
    keys_here = key_cache.reshape(n_req, span_here, kv_here, HD)
    values_here = value_cache.reshape(n_req, span_here, kv_here, HD)
    scores = (
        jnp.einsum("rkgd,rtkd->rkgt", q_groups, keys_here, preferred_element_type=jnp.float32)
        * score_scale
    )
    scores = jnp.where(live_slots, scores, MASKED)
    local_top = jnp.max(scores, axis=3, keepdims=True)
    weights = jnp.where(live_slots, jnp.exp(scores - local_top), 0.0)
    local_total = jnp.sum(weights, axis=3, keepdims=True)
    local_out = jnp.einsum(
        "rkgt,rtkd->rkgd",
        weights.astype(jnp.bfloat16),
        values_here,
        preferred_element_type=jnp.float32,
    )
    numer = local_out.reshape(n_req, heads_here, HD)
    stats = jnp.concatenate(
        [
            local_total.reshape(n_req, heads_here, 1),
            local_top.reshape(n_req, heads_here, 1),
        ],
        axis=2,
    )
    stat_rows = stats.reshape(n_req, heads_here * 2)
    pad = (-stat_rows.shape[1]) % LANES
    message = jnp.concatenate(
        [numer.reshape(n_req, heads_here * HD), jnp.pad(stat_rows, ((0, 0), (0, pad)))], axis=1
    )
    arrived = gather_all(message, ("chip", "core"), n_blocks)
    outs = arrived[:, :, : heads_here * HD].reshape(n_blocks, n_req, heads_here, HD)
    stats_all = arrived[:, :, heads_here * HD : heads_here * (HD + 2)].reshape(
        n_blocks, n_req, heads_here, 2
    )
    totals, tops = stats_all[..., 0], stats_all[..., 1]
    self_score = (
        jnp.einsum(
            "rkgd,rkd->rkg",
            q_groups,
            key_new.reshape(n_req, kv_here, HD),
            preferred_element_type=jnp.float32,
        )
        * score_scale
    ).reshape(n_req, heads_here)
    final_top = jnp.maximum(jnp.max(tops, axis=0), self_score)
    fades = jnp.exp(tops - final_top)
    self_weight = jnp.exp(self_score - final_top)
    denominator = jnp.sum(totals * fades, axis=0) + self_weight
    value_self = jnp.broadcast_to(
        value_new.reshape(n_req, kv_here, 1, HD), (n_req, kv_here, q_per_kv, HD)
    ).reshape(n_req, heads_here, HD)
    numerator = jnp.sum(outs * fades[..., None], axis=0) + self_weight[
        ..., None
    ] * value_self.astype(jnp.float32)
    attended = (
        (numerator / denominator[..., None])
        .reshape(n_req, heads_here * HD)
        .astype(jnp.bfloat16)
    )
    head_part = jnp.dot(attended, out_weight, preferred_element_type=jnp.float32)
    attn_out = sum_tp(head_part)
    hidden_state = (x_rows + attn_out).astype(jnp.bfloat16)

    resid_rows = hidden_state.astype(jnp.float32)
    scaled_mlp = (resid_rows * mlp_gain).astype(jnp.bfloat16)
    sq_mlp = jnp.sum(resid_rows * resid_rows, axis=1, keepdims=True)
    up_part = jnp.dot(scaled_mlp, up_weight, preferred_element_type=jnp.float32)
    half_up = up_part.shape[1] // 2
    up_low, up_high = up_part[:, :half_up], up_part[:, half_up:]
    square_cols = jnp.broadcast_to(sq_mlp, (n_req, LANES))
    up_mine = jnp.concatenate([jnp.where(core == 0, up_low, up_high), square_cols], axis=1)
    up_other = jnp.concatenate([jnp.where(core == 0, up_high, up_low), square_cols], axis=1)
    up_pair = up_mine + swap(up_other, "core")
    square_sum = up_pair[:, half_up : half_up + 1]
    piece_0 = lax.reduce_precision(square_sum, 8, 7)
    piece_1 = lax.reduce_precision(square_sum - piece_0, 8, 7)
    piece_2 = square_sum - piece_0 - piece_1
    pieces = jnp.pad(
        jnp.concatenate([piece_0, piece_1, piece_2], axis=1), ((0, 0), (0, LANES - 3))
    )
    up_message = jnp.concatenate([up_pair[:, :half_up], pieces], axis=1).astype(jnp.bfloat16)
    up_sum = jnp.sum(gather_all(up_message, "chip", n_chips).astype(jnp.float32), axis=0)
    squares = jnp.sum(up_sum[:, half_up:], axis=1, keepdims=True)
    inv_mlp = lax.rsqrt(squares / D + NORM_EPS)
    active_half = squared_relu(up_sum[:, :half_up] * inv_mlp).astype(jnp.bfloat16)
    active_other = swap(active_half, "core")
    activated = jnp.concatenate(
        [
            jnp.where(core == 0, active_half, active_other),
            jnp.where(core == 0, active_other, active_half),
        ],
        axis=1,
    )
    down_part = jnp.dot(activated, down_weight, preferred_element_type=jnp.float32)
    mlp_out = sum_tp(down_part)
    return (resid_rows + mlp_out).astype(jnp.bfloat16)


IN_VMEM = pl.BlockSpec(memory_space=pltpu.VMEM)


def chip_turn(chip):
    return chip // 2 % 2


def head_half():
    return (lax.axis_index("core") + chip_turn(lax.axis_index("chip"))) % 2


def local_kernel(kernel, outs, operands, flops, scratch=(), in_hbm=(), anywhere=()):
    in_specs, placed, moved = [], [], 0
    for i, x in enumerate(operands):
        space = pltpu.HBM if i in in_hbm else pltpu.VMEM
        in_specs.append(pl.BlockSpec(memory_space=space))
        placed.append(x if i in anywhere else pltpu.with_memory_space_constraint(x, space))
        moved += x.size * x.dtype.itemsize
    return pl.pallas_call(
        kernel,
        out_shape=outs,
        in_specs=in_specs,
        out_specs=[IN_VMEM] * len(outs),
        scratch_shapes=scratch,
        compiler_params=pltpu.CompilerParams(vmem_limit_bytes=6 * 2**20),
        cost_estimate=pl.CostEstimate(flops=flops, bytes_accessed=moved, transcendentals=0),
    )(*placed)


def f32(*shape):
    return pltpu.VMEM(shape, jnp.float32)


def bf16(*shape):
    return pltpu.VMEM(shape, jnp.bfloat16)


def pieces_of(values_in):
    first = values_in.astype(jnp.bfloat16).astype(jnp.float32)
    second = (values_in - first).astype(jnp.bfloat16).astype(jnp.float32)
    return first, second, values_in - first - second


def prepare_kernel(
    x_hbm, gain_hbm, mlp_gain_hbm, mask_hbm, lengths_hbm, order_hbm, key_hbm, value_hbm,
    scaled_ref, squares_ref, live_ref, x_ref, mlp_gain_ref, cache_ref,
    gain_ref, mask_ref, lengths_ref, order_ref, sems,
):
    core = lax.axis_index("core")
    n_blocks = lax.axis_size("chip") * 2
    my_block = 2 * lax.axis_index("chip") + core
    half = cache_ref.shape[3]
    heads = pl.ds(pl.multiple_of((1 - head_half()) * half, LANES), half)
    pairs = [
        (x_hbm, x_ref), (gain_hbm, gain_ref), (mask_hbm, mask_ref), (lengths_hbm, lengths_ref),
        (order_hbm, order_ref), (mlp_gain_hbm, mlp_gain_ref),
        (key_hbm.at[:, :, heads], cache_ref.at[0]), (value_hbm.at[:, :, heads], cache_ref.at[1]),
    ]
    copies = [pltpu.make_async_copy(src, dst, sems.at[i]) for i, (src, dst) in enumerate(pairs)]
    for copy in copies:
        copy.start()
    for copy in copies[:-2]:
        copy.wait()
    n_req, span = live_ref.shape
    slot = lax.broadcasted_iota(jnp.int32, (1, span), 1)
    for r in range(n_req):
        first_block = lax.rem(order_ref[r], n_blocks)
        begin = lax.rem(my_block - first_block + n_blocks, n_blocks) * span
        live = (begin + slot < lengths_ref[r]) & (mask_ref[r : r + 1, :] == 1)
        live_ref[r : r + 1, :] = live.astype(jnp.float32)
    x_rows = x_ref[...].astype(jnp.float32)
    scaled_ref[...] = (x_rows * gain_ref[...]).astype(jnp.bfloat16)
    squares = jnp.sum(x_rows * x_rows, axis=1, keepdims=True)
    squares_ref[...] = jnp.broadcast_to(squares, squares_ref.shape)
    for copy in copies[-2:]:
        copy.wait()


def qkv_columns(scaled_ref, w_refs, side, out_ref):
    at = 0
    for w_ref in w_refs:
        half = w_ref.shape[1] // 2
        mine = pl.ds(pl.multiple_of(side * half, LANES), half)
        out_ref[:, at : at + half] = jnp.dot(
            scaled_ref[...], w_ref[:, mine], preferred_element_type=jnp.float32
        )
        at += half
    return at


def qkv_other_kernel(scaled_ref, squares_ref, live_ref, wq_ref, wk_ref, wv_ref, other_ref):
    other = 1 - head_half()
    at = qkv_columns(scaled_ref, (wq_ref, wk_ref, wv_ref), other, other_ref)
    other_ref[:, at : at + LANES] = squares_ref[...]
    other_ref[:, at + LANES :] = live_ref[...]


def qkv_mine_kernel(scaled_ref, squares_ref, wq_ref, wk_ref, wv_ref, mine_ref):
    at = qkv_columns(scaled_ref, (wq_ref, wk_ref, wv_ref), head_half(), mine_ref)
    mine_ref[:, at:] = squares_ref[...]


SCALE_UNIT = 1024.0


def qkv_message_kernel(mine_ref, arrived_ref, out_ref):
    width = mine_ref.shape[1] - LANES
    features = D / lax.axis_size("chip")
    total = mine_ref[...] + arrived_ref[:, : width + LANES]
    squares = total[:, width:]
    scale = jnp.sqrt(jnp.maximum(squares * (1.0 / features), 2.0**-40))
    scale = scale.astype(jnp.bfloat16).astype(jnp.float32)
    inverse = 1.0 / scale
    out_ref[:, :width] = total[:, :width] * inverse[:, :1]
    lane = lax.broadcasted_iota(jnp.int32, squares.shape, 1)
    tile = jnp.where(lane == 0, scale * SCALE_UNIT, 0.0)
    for p, piece in enumerate(pieces_of(squares * inverse * inverse * (1.0 / features))):
        tile = jnp.where(lane == 1 + p, piece, tile)
    out_ref[:, width:] = tile


def qkv_sum_kernel(arrived_ref, out_ref):
    width = out_ref.shape[1]
    features = D / arrived_ref.shape[0]
    total, squares = 0.0, 0.0
    for i in range(arrived_ref.shape[0]):
        tile = arrived_ref[i, :, width:]
        scale = tile[:, :1] * (1.0 / SCALE_UNIT)
        total = total + arrived_ref[i, :, :width] * scale
        mean = tile[:, 1:2] + tile[:, 2:3] + tile[:, 3:4]
        squares = squares + mean * scale * scale * features
    inv_attn = lax.rsqrt(squares / D + NORM_EPS)
    out_ref[...] = (total * inv_attn).astype(jnp.bfloat16)


PIECE = 16
TOP_AT = 3 * PIECE


def attention_kernel(
    qkv_ref, key_own, value_own, cache_peer, live_own, live_peer,
    message_ref, query_ref, key_new_ref, value_new_ref,
):
    n_copies, heads, _ = message_ref.shape
    n_req, span = live_own.shape
    half = key_own.shape[2] // 2
    mine = pl.ds(pl.multiple_of(head_half() * half, LANES), half)
    kv_half = half // HD
    group = heads // kv_half
    is_first = lax.axis_index("chip") == 0
    qkv = qkv_ref[...].astype(jnp.float32)
    for h in range(heads):
        query_ref[:, h, :] = qkv[:, h * HD : (h + 1) * HD]
        at = (heads + h // group) * HD
        key_new_ref[:, h, :] = qkv[:, at : at + HD]
        at += kv_half * HD
        value_new_ref[:, h, :] = qkv[:, at : at + HD]

    rows = n_req * heads
    query = query_ref[...].reshape(rows, HD)
    group_of = lax.broadcasted_iota(jnp.int32, (rows, HD), 0) % heads // group
    spread = jnp.concatenate(
        [jnp.where(group_of == k, query, 0.0) for k in range(kv_half)], axis=1
    ).astype(jnp.bfloat16)
    scores, live = [], []
    for r in range(n_req):
        blocks = []
        for keys in (key_own[r, :, mine], cache_peer[0, r]):
            blocks.append(
                lax.dot_general(
                    spread[r * heads : (r + 1) * heads, :], keys,
                    (((1,), (1,)), ((), ())), preferred_element_type=jnp.float32,
                )
            )
        scores.append(jnp.concatenate(blocks, axis=1))
        live_row = jnp.concatenate([live_own[r : r + 1, :], live_peer[r : r + 1, :]], axis=1)
        live.append(jnp.broadcast_to(live_row, (heads, 2 * span)))
    live = jnp.concatenate(live, axis=0) > 0.0
    scale = 1.0 / math.sqrt(HD)
    scores = jnp.where(live, jnp.concatenate(scores, axis=0) * scale, MASKED)
    key_new = key_new_ref[...].reshape(rows, HD)
    self_score = jnp.sum(query * key_new, axis=1, keepdims=True) * scale
    self_score = jnp.where(is_first, self_score, MASKED)
    top = jnp.maximum(jnp.max(scores, axis=1, keepdims=True), self_score)
    weights = jnp.where(live, jnp.exp(scores - top), 0.0)
    self_weight = jnp.where(is_first, jnp.exp(self_score - top), 0.0)
    total = jnp.sum(weights, axis=1, keepdims=True) + self_weight
    rounded = weights.astype(jnp.bfloat16)
    self_part = self_weight * value_new_ref[...].reshape(rows, HD)
    pieces = pieces_of(total) + pieces_of(top)
    lane = lax.broadcasted_iota(jnp.int32, (heads, LANES), 1)
    stats = jnp.zeros((heads, LANES), jnp.float32)
    parts = []
    for r in range(n_req):
        at = slice(r * heads, (r + 1) * heads)
        wide = jnp.dot(
            rounded[at, :span], value_own[r, :, mine], preferred_element_type=jnp.float32
        ) + jnp.dot(
            rounded[at, span:], cache_peer[1, r], preferred_element_type=jnp.float32
        )
        numer = self_part[at, :]
        for k in range(kv_half):
            numer = numer + jnp.where(group_of[at, :] == k, wide[:, k * HD : (k + 1) * HD], 0.0)
        parts.append(numer)
        for p, piece in enumerate(pieces):
            stats = jnp.where(lane == p * PIECE + r, piece[at, :], stats)
    message = jnp.concatenate(parts + [stats], axis=1).astype(jnp.bfloat16)
    for i in range(n_copies):
        message_ref[i] = message


def combine_kernel(arrived_ref, rows_ref, attended_ref):
    n_chips, heads, width = arrived_ref.shape
    n_req = rows_ref.shape[0]
    totals, tops = [], []
    for chip in range(n_chips):
        tile = arrived_ref[chip, :, width - LANES :].astype(jnp.float32)
        tile = (
            tile
            + pltpu.roll(tile, LANES - PIECE, 1)
            + pltpu.roll(tile, LANES - 2 * PIECE, 1)
        )
        totals.append(tile)
        tops.append(pltpu.roll(tile, LANES - TOP_AT, 1))
    final_top = tops[0]
    for top in tops[1:]:
        final_top = jnp.maximum(final_top, top)
    fades = [jnp.exp(top - final_top) for top in tops]
    denominator = totals[0] * fades[0]
    for total, fade in zip(totals[1:], fades[1:]):
        denominator = denominator + total * fade
    for r in range(n_req):
        numer = jnp.zeros((heads, HD), jnp.float32)
        for chip, fade in enumerate(fades):
            part = arrived_ref[chip, :, r * HD : (r + 1) * HD].astype(jnp.float32)
            numer = numer + part * fade[:, r : r + 1]
        attended_ref[r] = numer / denominator[:, r : r + 1]
    rows = jnp.concatenate([attended_ref[:, h, :] for h in range(heads)], axis=1)
    rows_ref[...] = rows.astype(jnp.bfloat16)


def half_rows(rows_ref, w_ref, side):
    half = rows_ref.shape[1]
    rows = pl.ds(pl.multiple_of(side * half, LANES), half)
    return jnp.dot(rows_ref[...], w_ref[rows, :], preferred_element_type=jnp.float32)


def out_own_kernel(own_ref, w_ref, out_ref):
    out_ref[...] = half_rows(own_ref, w_ref, head_half())


def out_peer_kernel(own_part, peer_ref, w_ref, out_ref):
    out_ref[...] = own_part[...] + half_rows(peer_ref, w_ref, 1 - head_half())


def out_both_kernel(own_ref, peer_ref, w_ref, out_ref):
    side = head_half()
    out_ref[...] = half_rows(own_ref, w_ref, side) + half_rows(peer_ref, w_ref, 1 - side)


def up_columns(scaled_mlp, w_ref, core, out_ref):
    half = out_ref.shape[1] - LANES
    mine = pl.ds(pl.multiple_of(core * half, LANES), half)
    out_ref[:, :half] = jnp.dot(scaled_mlp, w_ref[:, mine], preferred_element_type=jnp.float32)


def up_other_kernel(
    x_ref, part_ref, peer_ref, gain_ref, w_ref, hidden_ref, scaled_ref, squares_ref, other_ref
):
    attn_out = part_ref[...] + peer_ref[...]
    hidden_state = (x_ref[...].astype(jnp.float32) + attn_out).astype(jnp.bfloat16)
    resid_rows = hidden_state.astype(jnp.float32)
    hidden_ref[...] = resid_rows
    scaled_mlp = (resid_rows * gain_ref[...]).astype(jnp.bfloat16)
    scaled_ref[...] = scaled_mlp
    squares = jnp.sum(resid_rows * resid_rows, axis=1, keepdims=True)
    squares_ref[...] = jnp.broadcast_to(squares, squares_ref.shape)
    other_ref[:, other_ref.shape[1] - LANES :] = squares_ref[...]
    up_columns(scaled_mlp, w_ref, 1 - lax.axis_index("core"), other_ref)


def up_mine_kernel(scaled_ref, squares_ref, w_ref, mine_ref):
    mine_ref[:, mine_ref.shape[1] - LANES :] = squares_ref[...]
    up_columns(scaled_ref[...], w_ref, lax.axis_index("core"), mine_ref)


def up_message_kernel(mine_ref, arrived_ref, message_ref):
    half = mine_ref.shape[1] - LANES
    message = (mine_ref[:, :half] + arrived_ref[:, :half]).astype(jnp.bfloat16)
    squares = mine_ref[:, half:] + arrived_ref[:, half:]
    lane = lax.broadcasted_iota(jnp.int32, squares.shape, 1)
    tile = jnp.zeros_like(squares)
    for p, piece in enumerate(pieces_of(squares)):
        tile = jnp.where(lane == p, piece, tile)
    for i in range(message_ref.shape[0]):
        message_ref[i, :, :half] = message
        message_ref[i, :, half:] = tile.astype(jnp.bfloat16)


def activate_kernel(arrived_ref, out_ref):
    half = out_ref.shape[1]
    total = arrived_ref[0].astype(jnp.float32)
    for i in range(1, arrived_ref.shape[0]):
        total = total + arrived_ref[i].astype(jnp.float32)
    squares = jnp.sum(total[:, half:], axis=1, keepdims=True)
    inv_mlp = lax.rsqrt(squares / D + NORM_EPS)
    out_ref[...] = squared_relu(total[:, :half] * inv_mlp).astype(jnp.bfloat16)


def down_own_kernel(own_ref, w_ref, out_ref):
    out_ref[...] = half_rows(own_ref, w_ref, lax.axis_index("core"))


def down_peer_kernel(own_part, peer_ref, w_ref, out_ref):
    out_ref[...] = own_part[...] + half_rows(peer_ref, w_ref, 1 - lax.axis_index("core"))


def per_device(
    hidden_in,
    attn_gain,
    mlp_gain,
    query_weight,
    key_weight,
    value_weight,
    out_weight,
    up_weight,
    down_weight,
    key_cache,
    value_cache,
    lengths,
    block_order,
    pad_mask,
):
    n_req, d_here = hidden_in.shape
    kv_here = key_cache.shape[2] // HD
    heads_here = kv_here * (H // KVH)
    n_chips = lax.axis_size("chip")
    core = lax.axis_index("core")
    n_blocks = 2 * n_chips
    half_qkv = (heads_here + 2 * kv_here) * HD // 2
    half_up = up_weight.shape[1] // 2

    row = (1, d_here)
    small = [hidden_in, attn_gain.reshape(row), mlp_gain.reshape(row), pad_mask]
    small += [lengths, block_order, key_cache, value_cache]
    scaled_in, squares, live, x_rows, gain, cache_sent = local_kernel(
        prepare_kernel,
        [
            bf16(*hidden_in.shape),
            f32(n_req, LANES),
            f32(*pad_mask.shape),
            bf16(*hidden_in.shape),
            f32(*row),
            bf16(2, *key_cache.shape[:2], key_cache.shape[2] // 2),
        ],
        small,
        flops=4 * 10**9,
        scratch=[
            pltpu.VMEM(row, jnp.float32),
            pltpu.VMEM(pad_mask.shape, jnp.int32),
            pltpu.SMEM(lengths.shape, jnp.int32),
            pltpu.SMEM(block_order.shape, jnp.int32),
            pltpu.SemaphoreType.DMA((len(small),)),
        ],
        in_hbm=range(len(small)),
    )
    (other,) = local_kernel(
        qkv_other_kernel,
        [f32(n_req, half_qkv + LANES + pad_mask.shape[1])],
        [scaled_in, squares, live, query_weight, key_weight, value_weight],
        flops=4 * 10**9,
        anywhere=(3, 4, 5),
    )
    (mine,) = local_kernel(
        qkv_mine_kernel,
        [f32(n_req, half_qkv + LANES)],
        [scaled_in, squares, query_weight, key_weight, value_weight],
        flops=2 * n_req * d_here * half_qkv,
        anywhere=(2, 3, 4),
    )
    arrived = swap(other, "core")
    width = mine.shape[1]
    (qkv_message,) = local_kernel(
        qkv_message_kernel, [f32(*mine.shape)], [mine, arrived], flops=2 * mine.size
    )
    qkv_message, live_peer, *moved = lax.optimization_barrier(
        (
            qkv_message.astype(jnp.float16),
            arrived[:, width:],
            cache_sent,
            out_weight,
        )
    )
    cache_peer, out_peer = (swap(x, "core") for x in moved)
    sides = [
        [2 * chip + (side + chip_turn(chip)) % 2 for chip in range(n_chips)] for side in range(2)
    ]
    qkv_all = lax.all_to_all(
        jnp.broadcast_to(qkv_message[None], (n_chips,) + qkv_message.shape),
        ("chip", "core"),
        0,
        0,
        axis_index_groups=sides,
    )
    (qkv_half,) = local_kernel(
        qkv_sum_kernel,
        [bf16(n_req, half_qkv)],
        [qkv_all.astype(jnp.float32)],
        flops=n_chips * n_req * half_qkv,
    )
    half_heads = heads_here // 2
    (message,) = local_kernel(
        attention_kernel,
        [bf16(n_chips, half_heads, n_req * HD + LANES)],
        [qkv_half, key_cache, value_cache, cache_peer, live, live_peer],
        anywhere=(1, 2, 3),
        flops=4 * 10**9,
        scratch=[pltpu.VMEM((n_req, half_heads, HD), jnp.float32)] * 3,
    )
    message, out_peer = lax.optimization_barrier((message, out_peer))
    (attended,) = local_kernel(
        combine_kernel,
        [bf16(n_req, half_heads * HD)],
        [lax.all_to_all(message, ("chip", "core"), 0, 0, axis_index_groups=sides)],
        flops=n_chips * n_req * half_heads * HD,
        scratch=[pltpu.VMEM((n_req, half_heads, HD), jnp.float32)],
    )
    attended_peer = swap(attended, "core")
    (head_own,) = local_kernel(
        out_own_kernel,
        [f32(n_req, d_here)],
        [attended, out_peer],
        anywhere=(1,),
        flops=n_req * out_weight.size,
    )
    (head_sent,) = local_kernel(
        out_peer_kernel,
        [f32(n_req, d_here)],
        [head_own, attended_peer, out_peer],
        anywhere=(2,),
        flops=n_req * out_weight.size,
    )
    head_peer = swap_diagonal(head_sent)
    (head_part,) = local_kernel(
        out_both_kernel,
        [f32(n_req, d_here)],
        [attended, attended_peer, out_weight],
        anywhere=(2,),
        flops=2 * n_req * out_weight.size,
    )

    resid_rows, scaled_mlp, squares, up_other = local_kernel(
        up_other_kernel,
        [
            f32(n_req, d_here),
            bf16(n_req, d_here),
            f32(n_req, LANES),
            f32(n_req, half_up + LANES),
        ],
        [x_rows, head_part, head_peer, gain, up_weight],
        flops=n_req * up_weight.size,
        anywhere=(4,),
    )
    (up_mine,) = local_kernel(
        up_mine_kernel,
        [f32(n_req, half_up + LANES)],
        [scaled_mlp, squares, up_weight],
        flops=n_req * up_weight.size,
        anywhere=(2,),
    )
    (up_message,) = local_kernel(
        up_message_kernel,
        [bf16(n_chips, n_req, half_up + LANES)],
        [up_mine, swap(up_other, "core")],
        flops=n_chips * n_req * half_up,
    )
    (active_half,) = local_kernel(
        activate_kernel,
        [bf16(n_req, half_up)],
        [lax.all_to_all(up_message, "chip", 0, 0)],
        flops=n_chips * n_req * half_up,
    )
    active_other = swap(active_half, "core")
    (down_own,) = local_kernel(
        down_own_kernel,
        [f32(n_req, d_here)],
        [active_half, down_weight],
        flops=n_req * down_weight.size,
        anywhere=(1,),
    )
    (down_part,) = local_kernel(
        down_peer_kernel,
        [f32(n_req, d_here)],
        [down_own, active_other, down_weight],
        flops=n_req * down_weight.size,
        anywhere=(2,),
    )
    mlp_out = sum_tp(down_part)
    return (resid_rows + mlp_out).astype(jnp.bfloat16)


def solution(mesh):
    n_seq, n_tp = mesh.shape["seq"], mesh.shape["tp"]
    split = Mesh(mesh.devices.reshape(n_seq // 2, 2, n_tp), ("chip", "core", "tp"))
    seq = ("chip", "core")
    whole_tiles = n_tp == 2 and KVH % (2 * n_tp) == 0 and D % (n_seq * LANES) == 0
    return jax.shard_map(
        per_device if whole_tiles else per_device_plain,
        mesh=split,
        in_specs=(
            P(None, seq),
            P(seq),
            P(seq),
            P(seq, "tp"),
            P(seq, "tp"),
            P(seq, "tp"),
            P("tp", seq),
            P(seq, "tp"),
            P("tp", seq),
            P(None, seq, "tp"),
            P(None, seq, "tp"),
            P(),
            P(),
            P(None, seq),
        ),
        out_specs=P(None, seq),
        check_vma=False,
    )
```

```python
import math

import jax
import jax.numpy as jnp
from jax import lax
from jax.experimental import pallas as pl
from jax.experimental.pallas import tpu as pltpu
from jax.sharding import Mesh, PartitionSpec as P

D = 4096
H = 32
KVH = 8
HD = 128


NORM_EPS = 1e-05
MASKED = -1e30
LANES = 128


def squared_relu(values_in):
    positive = jnp.maximum(values_in, 0.0)
    return positive * positive


def swap(values_in, axis):
    n = lax.axis_size(axis)
    return lax.ppermute(values_in, axis, [(i, i ^ 1) for i in range(n)])


def swap_diagonal(values_in):
    return lax.ppermute(values_in, ("core", "tp"), [(i, 3 - i) for i in range(4)])


def swap_next_chip(values_in):
    n = 2 * lax.axis_size("chip")
    return lax.ppermute(values_in, ("chip", "core"), [(i, i ^ 3) for i in range(n)])


def gather_all(values_in, axes, n):
    copies = jnp.broadcast_to(values_in[None], (n,) + values_in.shape)
    return lax.all_to_all(copies, axes, 0, 0)


def sum_tp(values_in):
    n = lax.axis_size("tp")
    if n == 2:
        return values_in + swap(values_in, "tp")
    return lax.psum(values_in, "tp")


def per_device_plain(
    hidden_in,
    attn_gain,
    mlp_gain,
    query_weight,
    key_weight,
    value_weight,
    out_weight,
    up_weight,
    down_weight,
    key_cache,
    value_cache,
    lengths,
    block_order,
    pad_mask,
):
    n_req = hidden_in.shape[0]
    q_per_kv = H // KVH
    kv_here = key_cache.shape[2] // HD
    span_here = key_cache.shape[1]
    heads_here = kv_here * q_per_kv
    n_chips = lax.axis_size("chip")
    core = lax.axis_index("core")
    n_blocks = 2 * n_chips
    my_block = 2 * lax.axis_index("chip") + core
    score_scale = 1.0 / math.sqrt(HD)

    x_rows = hidden_in.astype(jnp.float32)
    scaled_in = (x_rows * attn_gain).astype(jnp.bfloat16)
    sq_attn = jnp.sum(x_rows * x_rows, axis=1, keepdims=True)
    proj_query = jnp.dot(scaled_in, query_weight, preferred_element_type=jnp.float32)
    proj_key = jnp.dot(scaled_in, key_weight, preferred_element_type=jnp.float32)
    proj_value = jnp.dot(scaled_in, value_weight, preferred_element_type=jnp.float32)
    half_q, half_kv = proj_query.shape[1] // 2, proj_key.shape[1] // 2
    square_cols = jnp.broadcast_to(sq_attn, (n_req, LANES))

    def half(i):
        return jnp.concatenate(
            [
                proj_query[:, i * half_q : (i + 1) * half_q],
                proj_key[:, i * half_kv : (i + 1) * half_kv],
                proj_value[:, i * half_kv : (i + 1) * half_kv],
                square_cols,
            ],
            axis=1,
        )

    low, high = half(0), half(1)
    mine = jnp.where(core == 0, low, high)
    other = jnp.where(core == 0, high, low)
    pair_sum = mine + swap(other, "core")
    qkv_sum = jnp.sum(gather_all(pair_sum, "chip", n_chips), axis=0)
    inv_attn = lax.rsqrt(qkv_sum[:, -1:] / D + NORM_EPS)
    qkv_half = (qkv_sum[:, :-LANES] * inv_attn).astype(jnp.bfloat16)
    qkv_other = swap(qkv_half, "core")
    qkv_low = jnp.where(core == 0, qkv_half, qkv_other)
    qkv_high = jnp.where(core == 0, qkv_other, qkv_half)

    def both(start, size):
        return jnp.concatenate(
            [qkv_low[:, start : start + size], qkv_high[:, start : start + size]], axis=1
        )

    query_rows = both(0, half_q)
    key_new = both(half_q, half_kv)
    value_new = both(half_q + half_kv, half_kv)

    first_block = block_order % n_blocks
    position = ((my_block - first_block) % n_blocks)[:, None] * span_here + jnp.arange(
        span_here, dtype=jnp.int32
    )[None, :]
    live_slots = ((position < lengths[:, None]) & (pad_mask == 1))[:, None, None, :]
    q_groups = query_rows.reshape(n_req, kv_here, q_per_kv, HD)
    keys_here = key_cache.reshape(n_req, span_here, kv_here, HD)
    values_here = value_cache.reshape(n_req, span_here, kv_here, HD)
    scores = (
        jnp.einsum("rkgd,rtkd->rkgt", q_groups, keys_here, preferred_element_type=jnp.float32)
        * score_scale
    )
    scores = jnp.where(live_slots, scores, MASKED)
    local_top = jnp.max(scores, axis=3, keepdims=True)
    weights = jnp.where(live_slots, jnp.exp(scores - local_top), 0.0)
    local_total = jnp.sum(weights, axis=3, keepdims=True)
    local_out = jnp.einsum(
        "rkgt,rtkd->rkgd",
        weights.astype(jnp.bfloat16),
        values_here,
        preferred_element_type=jnp.float32,
    )
    numer = local_out.reshape(n_req, heads_here, HD)
    stats = jnp.concatenate(
        [
            local_total.reshape(n_req, heads_here, 1),
            local_top.reshape(n_req, heads_here, 1),
        ],
        axis=2,
    )
    stat_rows = stats.reshape(n_req, heads_here * 2)
    pad = (-stat_rows.shape[1]) % LANES
    message = jnp.concatenate(
        [numer.reshape(n_req, heads_here * HD), jnp.pad(stat_rows, ((0, 0), (0, pad)))], axis=1
    )
    arrived = gather_all(message, ("chip", "core"), n_blocks)
    outs = arrived[:, :, : heads_here * HD].reshape(n_blocks, n_req, heads_here, HD)
    stats_all = arrived[:, :, heads_here * HD : heads_here * (HD + 2)].reshape(
        n_blocks, n_req, heads_here, 2
    )
    totals, tops = stats_all[..., 0], stats_all[..., 1]
    self_score = (
        jnp.einsum(
            "rkgd,rkd->rkg",
            q_groups,
            key_new.reshape(n_req, kv_here, HD),
            preferred_element_type=jnp.float32,
        )
        * score_scale
    ).reshape(n_req, heads_here)
    final_top = jnp.maximum(jnp.max(tops, axis=0), self_score)
    fades = jnp.exp(tops - final_top)
    self_weight = jnp.exp(self_score - final_top)
    denominator = jnp.sum(totals * fades, axis=0) + self_weight
    value_self = jnp.broadcast_to(
        value_new.reshape(n_req, kv_here, 1, HD), (n_req, kv_here, q_per_kv, HD)
    ).reshape(n_req, heads_here, HD)
    numerator = jnp.sum(outs * fades[..., None], axis=0) + self_weight[
        ..., None
    ] * value_self.astype(jnp.float32)
    attended = (
        (numerator / denominator[..., None])
        .reshape(n_req, heads_here * HD)
        .astype(jnp.bfloat16)
    )
    head_part = jnp.dot(attended, out_weight, preferred_element_type=jnp.float32)
    attn_out = sum_tp(head_part)
    hidden_state = (x_rows + attn_out).astype(jnp.bfloat16)

    resid_rows = hidden_state.astype(jnp.float32)
    scaled_mlp = (resid_rows * mlp_gain).astype(jnp.bfloat16)
    sq_mlp = jnp.sum(resid_rows * resid_rows, axis=1, keepdims=True)
    up_part = jnp.dot(scaled_mlp, up_weight, preferred_element_type=jnp.float32)
    half_up = up_part.shape[1] // 2
    up_low, up_high = up_part[:, :half_up], up_part[:, half_up:]
    square_cols = jnp.broadcast_to(sq_mlp, (n_req, LANES))
    up_mine = jnp.concatenate([jnp.where(core == 0, up_low, up_high), square_cols], axis=1)
    up_other = jnp.concatenate([jnp.where(core == 0, up_high, up_low), square_cols], axis=1)
    up_pair = up_mine + swap(up_other, "core")
    square_sum = up_pair[:, half_up : half_up + 1]
    piece_0 = lax.reduce_precision(square_sum, 8, 7)
    piece_1 = lax.reduce_precision(square_sum - piece_0, 8, 7)
    piece_2 = square_sum - piece_0 - piece_1
    pieces = jnp.pad(
        jnp.concatenate([piece_0, piece_1, piece_2], axis=1), ((0, 0), (0, LANES - 3))
    )
    up_message = jnp.concatenate([up_pair[:, :half_up], pieces], axis=1).astype(jnp.bfloat16)
    up_sum = jnp.sum(gather_all(up_message, "chip", n_chips).astype(jnp.float32), axis=0)
    squares = jnp.sum(up_sum[:, half_up:], axis=1, keepdims=True)
    inv_mlp = lax.rsqrt(squares / D + NORM_EPS)
    active_half = squared_relu(up_sum[:, :half_up] * inv_mlp).astype(jnp.bfloat16)
    active_other = swap(active_half, "core")
    activated = jnp.concatenate(
        [
            jnp.where(core == 0, active_half, active_other),
            jnp.where(core == 0, active_other, active_half),
        ],
        axis=1,
    )
    down_part = jnp.dot(activated, down_weight, preferred_element_type=jnp.float32)
    mlp_out = sum_tp(down_part)
    return (resid_rows + mlp_out).astype(jnp.bfloat16)


IN_VMEM = pl.BlockSpec(memory_space=pltpu.VMEM)


def chip_turn(chip):
    return chip // 2 % 2


def head_half():
    return (lax.axis_index("core") + chip_turn(lax.axis_index("chip"))) % 2


def up_half():
    return (lax.axis_index("core") + lax.axis_index("chip")) % 2


def local_kernel(kernel, outs, operands, flops, scratch=(), in_hbm=(), anywhere=()):
    in_specs, placed, moved = [], [], 0
    for i, x in enumerate(operands):
        space = pltpu.HBM if i in in_hbm else pltpu.VMEM
        in_specs.append(pl.BlockSpec(memory_space=space))
        placed.append(x if i in anywhere else pltpu.with_memory_space_constraint(x, space))
        moved += x.size * x.dtype.itemsize
    return pl.pallas_call(
        kernel,
        out_shape=outs,
        in_specs=in_specs,
        out_specs=[IN_VMEM] * len(outs),
        scratch_shapes=scratch,
        compiler_params=pltpu.CompilerParams(vmem_limit_bytes=6 * 2**20),
        cost_estimate=pl.CostEstimate(flops=flops, bytes_accessed=moved, transcendentals=0),
    )(*placed)


def f32(*shape):
    return pltpu.VMEM(shape, jnp.float32)


def bf16(*shape):
    return pltpu.VMEM(shape, jnp.bfloat16)


def pieces_of(values_in):
    first = values_in.astype(jnp.bfloat16).astype(jnp.float32)
    second = (values_in - first).astype(jnp.bfloat16).astype(jnp.float32)
    return first, second, values_in - first - second


def prepare_kernel(
    x_hbm, gain_hbm, mlp_gain_hbm, mask_hbm, lengths_hbm, order_hbm, key_hbm, value_hbm,
    scaled_ref, squares_ref, live_ref, x_ref, mlp_gain_ref, cache_ref,
    gain_ref, mask_ref, lengths_ref, order_ref, sems,
):
    core = lax.axis_index("core")
    n_blocks = lax.axis_size("chip") * 2
    my_block = 2 * lax.axis_index("chip") + core
    half = cache_ref.shape[3]
    heads = pl.ds(pl.multiple_of((1 - head_half()) * half, LANES), half)
    pairs = [
        (x_hbm, x_ref), (gain_hbm, gain_ref), (mask_hbm, mask_ref), (lengths_hbm, lengths_ref),
        (order_hbm, order_ref), (mlp_gain_hbm, mlp_gain_ref),
        (key_hbm.at[:, :, heads], cache_ref.at[0]), (value_hbm.at[:, :, heads], cache_ref.at[1]),
    ]
    copies = [pltpu.make_async_copy(src, dst, sems.at[i]) for i, (src, dst) in enumerate(pairs)]
    for copy in copies:
        copy.start()
    for copy in copies[:-2]:
        copy.wait()
    n_req, span = live_ref.shape
    slot = lax.broadcasted_iota(jnp.int32, (1, span), 1)
    for r in range(n_req):
        first_block = lax.rem(order_ref[r], n_blocks)
        begin = lax.rem(my_block - first_block + n_blocks, n_blocks) * span
        live = (begin + slot < lengths_ref[r]) & (mask_ref[r : r + 1, :] == 1)
        live_ref[r : r + 1, :] = live.astype(jnp.float32)
    x_rows = x_ref[...].astype(jnp.float32)
    scaled_ref[...] = (x_rows * gain_ref[...]).astype(jnp.bfloat16)
    squares = jnp.sum(x_rows * x_rows, axis=1, keepdims=True)
    squares_ref[...] = jnp.broadcast_to(squares, squares_ref.shape)
    for copy in copies[-2:]:
        copy.wait()


def qkv_columns(scaled_ref, w_refs, side, out_ref):
    at = 0
    for w_ref in w_refs:
        half = w_ref.shape[1] // 2
        mine = pl.ds(pl.multiple_of(side * half, LANES), half)
        out_ref[:, at : at + half] = jnp.dot(
            scaled_ref[...], w_ref[:, mine], preferred_element_type=jnp.float32
        )
        at += half
    return at


def qkv_other_kernel(scaled_ref, squares_ref, live_ref, wq_ref, wk_ref, wv_ref, other_ref):
    other = 1 - head_half()
    at = qkv_columns(scaled_ref, (wq_ref, wk_ref, wv_ref), other, other_ref)
    other_ref[:, at : at + LANES] = squares_ref[...]
    other_ref[:, at + LANES :] = live_ref[...]


def qkv_mine_kernel(scaled_ref, squares_ref, wq_ref, wk_ref, wv_ref, mine_ref):
    at = qkv_columns(scaled_ref, (wq_ref, wk_ref, wv_ref), head_half(), mine_ref)
    mine_ref[:, at:] = squares_ref[...]


SCALE_UNIT = 1024.0


def qkv_message_kernel(mine_ref, arrived_ref, out_ref):
    width = mine_ref.shape[1] - LANES
    features = D / lax.axis_size("chip")
    total = mine_ref[...] + arrived_ref[:, : width + LANES]
    squares = total[:, width:]
    scale = jnp.sqrt(jnp.maximum(squares * (1.0 / features), 2.0**-40))
    scale = scale.astype(jnp.bfloat16).astype(jnp.float32)
    inverse = 1.0 / scale
    out_ref[:, :width] = total[:, :width] * inverse[:, :1]
    lane = lax.broadcasted_iota(jnp.int32, squares.shape, 1)
    tile = jnp.where(lane == 0, scale * SCALE_UNIT, 0.0)
    for p, piece in enumerate(pieces_of(squares * inverse * inverse * (1.0 / features))):
        tile = jnp.where(lane == 1 + p, piece, tile)
    out_ref[:, width:] = tile


def qkv_sum_kernel(arrived_ref, out_ref):
    width = out_ref.shape[1]
    features = D / arrived_ref.shape[0]
    total, squares = 0.0, 0.0
    for i in range(arrived_ref.shape[0]):
        tile = arrived_ref[i, :, width:]
        scale = tile[:, :1] * (1.0 / SCALE_UNIT)
        total = total + arrived_ref[i, :, :width] * scale
        mean = tile[:, 1:2] + tile[:, 2:3] + tile[:, 3:4]
        squares = squares + mean * scale * scale * features
    inv_attn = lax.rsqrt(squares / D + NORM_EPS)
    out_ref[...] = (total * inv_attn).astype(jnp.bfloat16)


PIECE = 16
TOP_AT = 3 * PIECE


def attention_kernel(
    qkv_ref, key_own, value_own, cache_peer, live_own, live_peer,
    message_ref, query_ref, key_new_ref, value_new_ref,
):
    n_copies, heads, _ = message_ref.shape
    n_req, span = live_own.shape
    half = key_own.shape[2] // 2
    mine = pl.ds(pl.multiple_of(head_half() * half, LANES), half)
    kv_half = half // HD
    group = heads // kv_half
    is_first = lax.axis_index("chip") == 0
    qkv = qkv_ref[...].astype(jnp.float32)
    for h in range(heads):
        query_ref[:, h, :] = qkv[:, h * HD : (h + 1) * HD]
        at = (heads + h // group) * HD
        key_new_ref[:, h, :] = qkv[:, at : at + HD]
        at += kv_half * HD
        value_new_ref[:, h, :] = qkv[:, at : at + HD]

    rows = n_req * heads
    query = query_ref[...].reshape(rows, HD)
    group_of = lax.broadcasted_iota(jnp.int32, (rows, HD), 0) % heads // group
    spread = jnp.concatenate(
        [jnp.where(group_of == k, query, 0.0) for k in range(kv_half)], axis=1
    ).astype(jnp.bfloat16)
    scores, live = [], []
    for r in range(n_req):
        blocks = []
        for keys in (key_own[r, :, mine], cache_peer[0, r]):
            blocks.append(
                lax.dot_general(
                    spread[r * heads : (r + 1) * heads, :], keys,
                    (((1,), (1,)), ((), ())), preferred_element_type=jnp.float32,
                )
            )
        scores.append(jnp.concatenate(blocks, axis=1))
        live_row = jnp.concatenate([live_own[r : r + 1, :], live_peer[r : r + 1, :]], axis=1)
        live.append(jnp.broadcast_to(live_row, (heads, 2 * span)))
    live = jnp.concatenate(live, axis=0) > 0.0
    scale = 1.0 / math.sqrt(HD)
    scores = jnp.where(live, jnp.concatenate(scores, axis=0) * scale, MASKED)
    key_new = key_new_ref[...].reshape(rows, HD)
    self_score = jnp.sum(query * key_new, axis=1, keepdims=True) * scale
    self_score = jnp.where(is_first, self_score, MASKED)
    top = jnp.maximum(jnp.max(scores, axis=1, keepdims=True), self_score)
    weights = jnp.where(live, jnp.exp(scores - top), 0.0)
    self_weight = jnp.where(is_first, jnp.exp(self_score - top), 0.0)
    total = jnp.sum(weights, axis=1, keepdims=True) + self_weight
    rounded = weights.astype(jnp.bfloat16)
    self_part = self_weight * value_new_ref[...].reshape(rows, HD)
    pieces = pieces_of(total) + pieces_of(top)
    lane = lax.broadcasted_iota(jnp.int32, (heads, LANES), 1)
    stats = jnp.zeros((heads, LANES), jnp.float32)
    parts = []
    for r in range(n_req):
        at = slice(r * heads, (r + 1) * heads)
        wide = jnp.dot(
            rounded[at, :span], value_own[r, :, mine], preferred_element_type=jnp.float32
        ) + jnp.dot(
            rounded[at, span:], cache_peer[1, r], preferred_element_type=jnp.float32
        )
        numer = self_part[at, :]
        for k in range(kv_half):
            numer = numer + jnp.where(group_of[at, :] == k, wide[:, k * HD : (k + 1) * HD], 0.0)
        parts.append(numer)
        for p, piece in enumerate(pieces):
            stats = jnp.where(lane == p * PIECE + r, piece[at, :], stats)
    message = jnp.concatenate(parts + [stats], axis=1).astype(jnp.bfloat16)
    for i in range(n_copies):
        message_ref[i] = message


def combine_kernel(arrived_ref, rows_ref, attended_ref):
    n_chips, heads, width = arrived_ref.shape
    n_req = rows_ref.shape[0]
    totals, tops = [], []
    for chip in range(n_chips):
        tile = arrived_ref[chip, :, width - LANES :].astype(jnp.float32)
        tile = (
            tile
            + pltpu.roll(tile, LANES - PIECE, 1)
            + pltpu.roll(tile, LANES - 2 * PIECE, 1)
        )
        totals.append(tile)
        tops.append(pltpu.roll(tile, LANES - TOP_AT, 1))
    final_top = tops[0]
    for top in tops[1:]:
        final_top = jnp.maximum(final_top, top)
    fades = [jnp.exp(top - final_top) for top in tops]
    denominator = totals[0] * fades[0]
    for total, fade in zip(totals[1:], fades[1:]):
        denominator = denominator + total * fade
    for r in range(n_req):
        numer = jnp.zeros((heads, HD), jnp.float32)
        for chip, fade in enumerate(fades):
            part = arrived_ref[chip, :, r * HD : (r + 1) * HD].astype(jnp.float32)
            numer = numer + part * fade[:, r : r + 1]
        attended_ref[r] = numer / denominator[:, r : r + 1]
    rows = jnp.concatenate([attended_ref[:, h, :] for h in range(heads)], axis=1)
    rows_ref[...] = rows.astype(jnp.bfloat16)


def half_rows(rows_ref, w_ref, side):
    half = rows_ref.shape[1]
    rows = pl.ds(pl.multiple_of(side * half, LANES), half)
    return jnp.dot(rows_ref[...], w_ref[rows, :], preferred_element_type=jnp.float32)


def out_own_kernel(own_ref, w_ref, out_ref):
    out_ref[...] = half_rows(own_ref, w_ref, head_half())


def out_peer_kernel(own_part, peer_ref, w_ref, out_ref):
    out_ref[...] = own_part[...] + half_rows(peer_ref, w_ref, 1 - head_half())


def out_both_kernel(own_ref, peer_ref, w_ref, out_ref):
    side = head_half()
    out_ref[...] = half_rows(own_ref, w_ref, side) + half_rows(peer_ref, w_ref, 1 - side)


def up_columns(scaled_mlp, w_ref, side, out_ref):
    half = out_ref.shape[1] - LANES
    mine = pl.ds(pl.multiple_of(side * half, LANES), half)
    out_ref[:, :half] = jnp.dot(scaled_mlp, w_ref[:, mine], preferred_element_type=jnp.float32)


def up_other_kernel(
    x_ref, part_ref, peer_ref, gain_ref, w_ref, hidden_ref, scaled_ref, squares_ref, other_ref
):
    attn_out = part_ref[...] + peer_ref[...]
    hidden_state = (x_ref[...].astype(jnp.float32) + attn_out).astype(jnp.bfloat16)
    resid_rows = hidden_state.astype(jnp.float32)
    hidden_ref[...] = resid_rows
    scaled_mlp = (resid_rows * gain_ref[...]).astype(jnp.bfloat16)
    scaled_ref[...] = scaled_mlp
    squares = jnp.sum(resid_rows * resid_rows, axis=1, keepdims=True)
    squares_ref[...] = jnp.broadcast_to(squares, squares_ref.shape)
    other_ref[:, other_ref.shape[1] - LANES :] = squares_ref[...]
    up_columns(scaled_mlp, w_ref, 1 - up_half(), other_ref)


def up_mine_kernel(scaled_ref, squares_ref, w_ref, mine_ref):
    mine_ref[:, mine_ref.shape[1] - LANES :] = squares_ref[...]
    up_columns(scaled_ref[...], w_ref, up_half(), mine_ref)


def squares_tile(squares):
    lane = lax.broadcasted_iota(jnp.int32, squares.shape, 1)
    tile = jnp.zeros_like(squares)
    for p, piece in enumerate(pieces_of(squares)):
        tile = jnp.where(lane == p, piece, tile)
    return tile.astype(jnp.bfloat16)


def up_pair_kernel(mine_ref, arrived_ref, pair_ref, sent_ref):
    half = mine_ref.shape[1] - LANES
    total = mine_ref[...] + arrived_ref[...]
    pair_ref[...] = total
    sent_ref[:, :half] = total[:, :half].astype(jnp.bfloat16)
    sent_ref[:, half:] = squares_tile(total[:, half:])


def up_message_kernel(pair_ref, arrived_ref, message_ref):
    half = pair_ref.shape[1] - LANES
    message = pair_ref[:, :half] + arrived_ref[:, :half].astype(jnp.float32)
    message = message.astype(jnp.bfloat16)
    arrived = jnp.sum(arrived_ref[:, half:].astype(jnp.float32), axis=1, keepdims=True)
    tile = squares_tile(pair_ref[:, half:] + arrived)
    for i in range(message_ref.shape[0]):
        message_ref[i, :, :half] = message
        message_ref[i, :, half:] = tile


def activate_kernel(arrived_ref, out_ref):
    half = out_ref.shape[1]
    total = arrived_ref[0].astype(jnp.float32)
    for i in range(1, arrived_ref.shape[0]):
        total = total + arrived_ref[i].astype(jnp.float32)
    squares = jnp.sum(total[:, half:], axis=1, keepdims=True)
    inv_mlp = lax.rsqrt(squares / D + NORM_EPS)
    out_ref[...] = squared_relu(total[:, :half] * inv_mlp).astype(jnp.bfloat16)


def down_own_kernel(own_ref, w_ref, out_ref):
    out_ref[...] = half_rows(own_ref, w_ref, up_half())


def down_peer_kernel(own_part, peer_ref, w_ref, out_ref):
    out_ref[...] = own_part[...] + half_rows(peer_ref, w_ref, 1 - up_half())


def per_device(
    hidden_in,
    attn_gain,
    mlp_gain,
    query_weight,
    key_weight,
    value_weight,
    out_weight,
    up_weight,
    down_weight,
    key_cache,
    value_cache,
    lengths,
    block_order,
    pad_mask,
):
    n_req, d_here = hidden_in.shape
    kv_here = key_cache.shape[2] // HD
    heads_here = kv_here * (H // KVH)
    n_chips = lax.axis_size("chip")
    core = lax.axis_index("core")
    n_blocks = 2 * n_chips
    half_qkv = (heads_here + 2 * kv_here) * HD // 2
    half_up = up_weight.shape[1] // 2

    row = (1, d_here)
    small = [hidden_in, attn_gain.reshape(row), mlp_gain.reshape(row), pad_mask]
    small += [lengths, block_order, key_cache, value_cache]
    scaled_in, squares, live, x_rows, gain, cache_sent = local_kernel(
        prepare_kernel,
        [
            bf16(*hidden_in.shape),
            f32(n_req, LANES),
            f32(*pad_mask.shape),
            bf16(*hidden_in.shape),
            f32(*row),
            bf16(2, *key_cache.shape[:2], key_cache.shape[2] // 2),
        ],
        small,
        flops=4 * 10**9,
        scratch=[
            pltpu.VMEM(row, jnp.float32),
            pltpu.VMEM(pad_mask.shape, jnp.int32),
            pltpu.SMEM(lengths.shape, jnp.int32),
            pltpu.SMEM(block_order.shape, jnp.int32),
            pltpu.SemaphoreType.DMA((len(small),)),
        ],
        in_hbm=range(len(small)),
    )
    (other,) = local_kernel(
        qkv_other_kernel,
        [f32(n_req, half_qkv + LANES + pad_mask.shape[1])],
        [scaled_in, squares, live, query_weight, key_weight, value_weight],
        flops=4 * 10**9,
        anywhere=(3, 4, 5),
    )
    (mine,) = local_kernel(
        qkv_mine_kernel,
        [f32(n_req, half_qkv + LANES)],
        [scaled_in, squares, query_weight, key_weight, value_weight],
        flops=2 * n_req * d_here * half_qkv,
        anywhere=(2, 3, 4),
    )
    arrived = swap(other, "core")
    width = mine.shape[1]
    (qkv_message,) = local_kernel(
        qkv_message_kernel, [f32(*mine.shape)], [mine, arrived], flops=2 * mine.size
    )
    qkv_message, live_peer, *moved = lax.optimization_barrier(
        (
            qkv_message.astype(jnp.float16),
            arrived[:, width:],
            cache_sent,
            out_weight,
        )
    )
    cache_peer, out_peer = (swap(x, "core") for x in moved)
    sides = [
        [2 * chip + (side + chip_turn(chip)) % 2 for chip in range(n_chips)] for side in range(2)
    ]
    qkv_all = lax.all_to_all(
        jnp.broadcast_to(qkv_message[None], (n_chips,) + qkv_message.shape),
        ("chip", "core"),
        0,
        0,
        axis_index_groups=sides,
    )
    (qkv_half,) = local_kernel(
        qkv_sum_kernel,
        [bf16(n_req, half_qkv)],
        [qkv_all.astype(jnp.float32)],
        flops=n_chips * n_req * half_qkv,
    )
    half_heads = heads_here // 2
    (message,) = local_kernel(
        attention_kernel,
        [bf16(n_chips, half_heads, n_req * HD + LANES)],
        [qkv_half, key_cache, value_cache, cache_peer, live, live_peer],
        anywhere=(1, 2, 3),
        flops=4 * 10**9,
        scratch=[pltpu.VMEM((n_req, half_heads, HD), jnp.float32)] * 3,
    )
    message, out_peer = lax.optimization_barrier((message, out_peer))
    (attended,) = local_kernel(
        combine_kernel,
        [bf16(n_req, half_heads * HD)],
        [lax.all_to_all(message, ("chip", "core"), 0, 0, axis_index_groups=sides)],
        flops=n_chips * n_req * half_heads * HD,
        scratch=[pltpu.VMEM((n_req, half_heads, HD), jnp.float32)],
    )
    attended_peer = swap(attended, "core")
    (head_own,) = local_kernel(
        out_own_kernel,
        [f32(n_req, d_here)],
        [attended, out_peer],
        anywhere=(1,),
        flops=n_req * out_weight.size,
    )
    (head_sent,) = local_kernel(
        out_peer_kernel,
        [f32(n_req, d_here)],
        [head_own, attended_peer, out_peer],
        anywhere=(2,),
        flops=n_req * out_weight.size,
    )
    head_peer = swap_diagonal(head_sent)
    (head_part,) = local_kernel(
        out_both_kernel,
        [f32(n_req, d_here)],
        [attended, attended_peer, out_weight],
        anywhere=(2,),
        flops=2 * n_req * out_weight.size,
    )

    resid_rows, scaled_mlp, squares, up_other = local_kernel(
        up_other_kernel,
        [
            f32(n_req, d_here),
            bf16(n_req, d_here),
            f32(n_req, LANES),
            f32(n_req, half_up + LANES),
        ],
        [x_rows, head_part, head_peer, gain, up_weight],
        flops=n_req * up_weight.size,
        anywhere=(4,),
    )
    (up_mine,) = local_kernel(
        up_mine_kernel,
        [f32(n_req, half_up + LANES)],
        [scaled_mlp, squares, up_weight],
        flops=n_req * up_weight.size,
        anywhere=(2,),
    )
    up_pair, up_sent = local_kernel(
        up_pair_kernel,
        [f32(*up_mine.shape), bf16(*up_mine.shape)],
        [up_mine, swap(up_other, "core")],
        flops=up_mine.size,
    )
    (up_message,) = local_kernel(
        up_message_kernel,
        [bf16(n_chips // 2, *up_pair.shape)],
        [up_pair, swap_next_chip(up_sent)],
        flops=up_mine.size,
    )
    columns = [
        [2 * chip + core for chip in range(turn, n_chips, 2)]
        for turn in range(2)
        for core in range(2)
    ]
    (active_half,) = local_kernel(
        activate_kernel,
        [bf16(n_req, half_up)],
        [lax.all_to_all(up_message, ("chip", "core"), 0, 0, axis_index_groups=columns)],
        flops=n_chips * n_req * half_up,
    )
    active_other = swap(active_half, "core")
    (down_own,) = local_kernel(
        down_own_kernel,
        [f32(n_req, d_here)],
        [active_half, down_weight],
        flops=n_req * down_weight.size,
        anywhere=(1,),
    )
    (down_part,) = local_kernel(
        down_peer_kernel,
        [f32(n_req, d_here)],
        [down_own, active_other, down_weight],
        flops=n_req * down_weight.size,
        anywhere=(2,),
    )
    mlp_out = sum_tp(down_part)
    return (resid_rows + mlp_out).astype(jnp.bfloat16)


def solution(mesh):
    n_seq, n_tp = mesh.shape["seq"], mesh.shape["tp"]
    split = Mesh(mesh.devices.reshape(n_seq // 2, 2, n_tp), ("chip", "core", "tp"))
    seq = ("chip", "core")
    whole_tiles = n_tp == 2 and KVH % (2 * n_tp) == 0 and D % (n_seq * LANES) == 0
    return jax.shard_map(
        per_device if whole_tiles else per_device_plain,
        mesh=split,
        in_specs=(
            P(None, seq),
            P(seq),
            P(seq),
            P(seq, "tp"),
            P(seq, "tp"),
            P(seq, "tp"),
            P("tp", seq),
            P(seq, "tp"),
            P("tp", seq),
            P(None, seq, "tp"),
            P(None, seq, "tp"),
            P(),
            P(),
            P(None, seq),
        ),
        out_specs=P(None, seq),
        check_vma=False,
    )
```

```python
import math

import jax
import jax.numpy as jnp
from jax import lax
from jax.experimental import pallas as pl
from jax.experimental.pallas import tpu as pltpu
from jax.sharding import Mesh, PartitionSpec as P

D = 4096
H = 32
KVH = 8
HD = 128


NORM_EPS = 1e-05
MASKED = -1e30
LANES = 128


def squared_relu(values_in):
    positive = jnp.maximum(values_in, 0.0)
    return positive * positive


def swap(values_in, axis):
    n = lax.axis_size(axis)
    return lax.ppermute(values_in, axis, [(i, i ^ 1) for i in range(n)])


def swap_diagonal(values_in):
    return lax.ppermute(values_in, ("core", "tp"), [(i, 3 - i) for i in range(4)])


def swap_chips(values_in, bit):
    n = 2 * lax.axis_size("chip")
    return lax.ppermute(
        values_in, ("chip", "core"), [(i, i ^ (2 << bit) ^ 1) for i in range(n)]
    )


def gather_all(values_in, axes, n):
    copies = jnp.broadcast_to(values_in[None], (n,) + values_in.shape)
    return lax.all_to_all(copies, axes, 0, 0)


def sum_tp(values_in):
    n = lax.axis_size("tp")
    if n == 2:
        return values_in + swap(values_in, "tp")
    return lax.psum(values_in, "tp")


def per_device_plain(
    hidden_in,
    attn_gain,
    mlp_gain,
    query_weight,
    key_weight,
    value_weight,
    out_weight,
    up_weight,
    down_weight,
    key_cache,
    value_cache,
    lengths,
    block_order,
    pad_mask,
):
    n_req = hidden_in.shape[0]
    q_per_kv = H // KVH
    kv_here = key_cache.shape[2] // HD
    span_here = key_cache.shape[1]
    heads_here = kv_here * q_per_kv
    n_chips = lax.axis_size("chip")
    core = lax.axis_index("core")
    n_blocks = 2 * n_chips
    my_block = 2 * lax.axis_index("chip") + core
    score_scale = 1.0 / math.sqrt(HD)

    x_rows = hidden_in.astype(jnp.float32)
    scaled_in = (x_rows * attn_gain).astype(jnp.bfloat16)
    sq_attn = jnp.sum(x_rows * x_rows, axis=1, keepdims=True)
    proj_query = jnp.dot(scaled_in, query_weight, preferred_element_type=jnp.float32)
    proj_key = jnp.dot(scaled_in, key_weight, preferred_element_type=jnp.float32)
    proj_value = jnp.dot(scaled_in, value_weight, preferred_element_type=jnp.float32)
    half_q, half_kv = proj_query.shape[1] // 2, proj_key.shape[1] // 2
    square_cols = jnp.broadcast_to(sq_attn, (n_req, LANES))

    def half(i):
        return jnp.concatenate(
            [
                proj_query[:, i * half_q : (i + 1) * half_q],
                proj_key[:, i * half_kv : (i + 1) * half_kv],
                proj_value[:, i * half_kv : (i + 1) * half_kv],
                square_cols,
            ],
            axis=1,
        )

    low, high = half(0), half(1)
    mine = jnp.where(core == 0, low, high)
    other = jnp.where(core == 0, high, low)
    pair_sum = mine + swap(other, "core")
    qkv_sum = jnp.sum(gather_all(pair_sum, "chip", n_chips), axis=0)
    inv_attn = lax.rsqrt(qkv_sum[:, -1:] / D + NORM_EPS)
    qkv_half = (qkv_sum[:, :-LANES] * inv_attn).astype(jnp.bfloat16)
    qkv_other = swap(qkv_half, "core")
    qkv_low = jnp.where(core == 0, qkv_half, qkv_other)
    qkv_high = jnp.where(core == 0, qkv_other, qkv_half)

    def both(start, size):
        return jnp.concatenate(
            [qkv_low[:, start : start + size], qkv_high[:, start : start + size]], axis=1
        )

    query_rows = both(0, half_q)
    key_new = both(half_q, half_kv)
    value_new = both(half_q + half_kv, half_kv)

    first_block = block_order % n_blocks
    position = ((my_block - first_block) % n_blocks)[:, None] * span_here + jnp.arange(
        span_here, dtype=jnp.int32
    )[None, :]
    live_slots = ((position < lengths[:, None]) & (pad_mask == 1))[:, None, None, :]
    q_groups = query_rows.reshape(n_req, kv_here, q_per_kv, HD)
    keys_here = key_cache.reshape(n_req, span_here, kv_here, HD)
    values_here = value_cache.reshape(n_req, span_here, kv_here, HD)
    scores = (
        jnp.einsum("rkgd,rtkd->rkgt", q_groups, keys_here, preferred_element_type=jnp.float32)
        * score_scale
    )
    scores = jnp.where(live_slots, scores, MASKED)
    local_top = jnp.max(scores, axis=3, keepdims=True)
    weights = jnp.where(live_slots, jnp.exp(scores - local_top), 0.0)
    local_total = jnp.sum(weights, axis=3, keepdims=True)
    local_out = jnp.einsum(
        "rkgt,rtkd->rkgd",
        weights.astype(jnp.bfloat16),
        values_here,
        preferred_element_type=jnp.float32,
    )
    numer = local_out.reshape(n_req, heads_here, HD)
    stats = jnp.concatenate(
        [
            local_total.reshape(n_req, heads_here, 1),
            local_top.reshape(n_req, heads_here, 1),
        ],
        axis=2,
    )
    stat_rows = stats.reshape(n_req, heads_here * 2)
    pad = (-stat_rows.shape[1]) % LANES
    message = jnp.concatenate(
        [numer.reshape(n_req, heads_here * HD), jnp.pad(stat_rows, ((0, 0), (0, pad)))], axis=1
    )
    arrived = gather_all(message, ("chip", "core"), n_blocks)
    outs = arrived[:, :, : heads_here * HD].reshape(n_blocks, n_req, heads_here, HD)
    stats_all = arrived[:, :, heads_here * HD : heads_here * (HD + 2)].reshape(
        n_blocks, n_req, heads_here, 2
    )
    totals, tops = stats_all[..., 0], stats_all[..., 1]
    self_score = (
        jnp.einsum(
            "rkgd,rkd->rkg",
            q_groups,
            key_new.reshape(n_req, kv_here, HD),
            preferred_element_type=jnp.float32,
        )
        * score_scale
    ).reshape(n_req, heads_here)
    final_top = jnp.maximum(jnp.max(tops, axis=0), self_score)
    fades = jnp.exp(tops - final_top)
    self_weight = jnp.exp(self_score - final_top)
    denominator = jnp.sum(totals * fades, axis=0) + self_weight
    value_self = jnp.broadcast_to(
        value_new.reshape(n_req, kv_here, 1, HD), (n_req, kv_here, q_per_kv, HD)
    ).reshape(n_req, heads_here, HD)
    numerator = jnp.sum(outs * fades[..., None], axis=0) + self_weight[
        ..., None
    ] * value_self.astype(jnp.float32)
    attended = (
        (numerator / denominator[..., None])
        .reshape(n_req, heads_here * HD)
        .astype(jnp.bfloat16)
    )
    head_part = jnp.dot(attended, out_weight, preferred_element_type=jnp.float32)
    attn_out = sum_tp(head_part)
    hidden_state = (x_rows + attn_out).astype(jnp.bfloat16)

    resid_rows = hidden_state.astype(jnp.float32)
    scaled_mlp = (resid_rows * mlp_gain).astype(jnp.bfloat16)
    sq_mlp = jnp.sum(resid_rows * resid_rows, axis=1, keepdims=True)
    up_part = jnp.dot(scaled_mlp, up_weight, preferred_element_type=jnp.float32)
    half_up = up_part.shape[1] // 2
    up_low, up_high = up_part[:, :half_up], up_part[:, half_up:]
    square_cols = jnp.broadcast_to(sq_mlp, (n_req, LANES))
    up_mine = jnp.concatenate([jnp.where(core == 0, up_low, up_high), square_cols], axis=1)
    up_other = jnp.concatenate([jnp.where(core == 0, up_high, up_low), square_cols], axis=1)
    up_pair = up_mine + swap(up_other, "core")
    square_sum = up_pair[:, half_up : half_up + 1]
    piece_0 = lax.reduce_precision(square_sum, 8, 7)
    piece_1 = lax.reduce_precision(square_sum - piece_0, 8, 7)
    piece_2 = square_sum - piece_0 - piece_1
    pieces = jnp.pad(
        jnp.concatenate([piece_0, piece_1, piece_2], axis=1), ((0, 0), (0, LANES - 3))
    )
    up_message = jnp.concatenate([up_pair[:, :half_up], pieces], axis=1).astype(jnp.bfloat16)
    up_sum = jnp.sum(gather_all(up_message, "chip", n_chips).astype(jnp.float32), axis=0)
    squares = jnp.sum(up_sum[:, half_up:], axis=1, keepdims=True)
    inv_mlp = lax.rsqrt(squares / D + NORM_EPS)
    active_half = squared_relu(up_sum[:, :half_up] * inv_mlp).astype(jnp.bfloat16)
    active_other = swap(active_half, "core")
    activated = jnp.concatenate(
        [
            jnp.where(core == 0, active_half, active_other),
            jnp.where(core == 0, active_other, active_half),
        ],
        axis=1,
    )
    down_part = jnp.dot(activated, down_weight, preferred_element_type=jnp.float32)
    mlp_out = sum_tp(down_part)
    return (resid_rows + mlp_out).astype(jnp.bfloat16)


IN_VMEM = pl.BlockSpec(memory_space=pltpu.VMEM)


def chip_turn(chip):
    return chip // 2 % 2


def head_half():
    return (lax.axis_index("core") + chip_turn(lax.axis_index("chip"))) % 2


def up_half():
    turns, chip = lax.axis_index("core"), lax.axis_index("chip")
    for bit in range(chip_bits()):
        turns = turns + chip // 2**bit % 2
    return turns % 2


def chip_bits():
    return lax.axis_size("chip").bit_length() - 1


def local_kernel(kernel, outs, operands, flops, scratch=(), in_hbm=(), anywhere=()):
    in_specs, placed, moved = [], [], 0
    for i, x in enumerate(operands):
        space = pltpu.HBM if i in in_hbm else pltpu.VMEM
        in_specs.append(pl.BlockSpec(memory_space=space))
        placed.append(x if i in anywhere else pltpu.with_memory_space_constraint(x, space))
        moved += x.size * x.dtype.itemsize
    return pl.pallas_call(
        kernel,
        out_shape=outs,
        in_specs=in_specs,
        out_specs=[IN_VMEM] * len(outs),
        scratch_shapes=scratch,
        compiler_params=pltpu.CompilerParams(vmem_limit_bytes=6 * 2**20),
        cost_estimate=pl.CostEstimate(flops=flops, bytes_accessed=moved, transcendentals=0),
    )(*placed)


def f32(*shape):
    return pltpu.VMEM(shape, jnp.float32)


def bf16(*shape):
    return pltpu.VMEM(shape, jnp.bfloat16)


def pieces_of(values_in):
    first = values_in.astype(jnp.bfloat16).astype(jnp.float32)
    second = (values_in - first).astype(jnp.bfloat16).astype(jnp.float32)
    return first, second, values_in - first - second


def prepare_kernel(
    x_hbm, gain_hbm, mlp_gain_hbm, mask_hbm, lengths_hbm, order_hbm, key_hbm, value_hbm,
    scaled_ref, squares_ref, live_ref, x_ref, mlp_gain_ref, cache_ref,
    gain_ref, mask_ref, lengths_ref, order_ref, sems,
):
    core = lax.axis_index("core")
    n_blocks = lax.axis_size("chip") * 2
    my_block = 2 * lax.axis_index("chip") + core
    half = cache_ref.shape[3]
    heads = pl.ds(pl.multiple_of((1 - head_half()) * half, LANES), half)
    pairs = [
        (x_hbm, x_ref), (gain_hbm, gain_ref), (mask_hbm, mask_ref), (lengths_hbm, lengths_ref),
        (order_hbm, order_ref), (mlp_gain_hbm, mlp_gain_ref),
        (key_hbm.at[:, :, heads], cache_ref.at[0]), (value_hbm.at[:, :, heads], cache_ref.at[1]),
    ]
    copies = [pltpu.make_async_copy(src, dst, sems.at[i]) for i, (src, dst) in enumerate(pairs)]
    for copy in copies:
        copy.start()
    for copy in copies[:-2]:
        copy.wait()
    n_req, span = live_ref.shape
    slot = lax.broadcasted_iota(jnp.int32, (1, span), 1)
    for r in range(n_req):
        first_block = lax.rem(order_ref[r], n_blocks)
        begin = lax.rem(my_block - first_block + n_blocks, n_blocks) * span
        live = (begin + slot < lengths_ref[r]) & (mask_ref[r : r + 1, :] == 1)
        live_ref[r : r + 1, :] = live.astype(jnp.float32)
    x_rows = x_ref[...].astype(jnp.float32)
    scaled_ref[...] = (x_rows * gain_ref[...]).astype(jnp.bfloat16)
    squares = jnp.sum(x_rows * x_rows, axis=1, keepdims=True)
    squares_ref[...] = jnp.broadcast_to(squares, squares_ref.shape)
    for copy in copies[-2:]:
        copy.wait()


def qkv_columns(scaled_ref, w_refs, side, out_ref):
    at = 0
    for w_ref in w_refs:
        half = w_ref.shape[1] // 2
        mine = pl.ds(pl.multiple_of(side * half, LANES), half)
        out_ref[:, at : at + half] = jnp.dot(
            scaled_ref[...], w_ref[:, mine], preferred_element_type=jnp.float32
        )
        at += half
    return at


def qkv_other_kernel(scaled_ref, squares_ref, live_ref, wq_ref, wk_ref, wv_ref, other_ref):
    other = 1 - head_half()
    at = qkv_columns(scaled_ref, (wq_ref, wk_ref, wv_ref), other, other_ref)
    other_ref[:, at : at + LANES] = squares_ref[...]
    other_ref[:, at + LANES :] = live_ref[...]


def qkv_mine_kernel(scaled_ref, squares_ref, wq_ref, wk_ref, wv_ref, mine_ref):
    at = qkv_columns(scaled_ref, (wq_ref, wk_ref, wv_ref), head_half(), mine_ref)
    mine_ref[:, at:] = squares_ref[...]


SCALE_UNIT = 1024.0


def qkv_message_kernel(mine_ref, arrived_ref, out_ref):
    width = mine_ref.shape[1] - LANES
    features = D / lax.axis_size("chip")
    total = mine_ref[...] + arrived_ref[:, : width + LANES]
    squares = total[:, width:]
    scale = jnp.sqrt(jnp.maximum(squares * (1.0 / features), 2.0**-40))
    scale = scale.astype(jnp.bfloat16).astype(jnp.float32)
    inverse = 1.0 / scale
    out_ref[:, :width] = total[:, :width] * inverse[:, :1]
    lane = lax.broadcasted_iota(jnp.int32, squares.shape, 1)
    tile = jnp.where(lane == 0, scale * SCALE_UNIT, 0.0)
    for p, piece in enumerate(pieces_of(squares * inverse * inverse * (1.0 / features))):
        tile = jnp.where(lane == 1 + p, piece, tile)
    out_ref[:, width:] = tile


def qkv_sum(arrived_ref):
    n_chips, _, width = arrived_ref.shape
    width -= LANES
    features = D / n_chips
    total, squares = 0.0, 0.0
    for i in range(n_chips):
        tile = arrived_ref[i, :, width:]
        scale = tile[:, :1] * (1.0 / SCALE_UNIT)
        total = total + arrived_ref[i, :, :width] * scale
        mean = tile[:, 1:2] + tile[:, 2:3] + tile[:, 3:4]
        squares = squares + mean * scale * scale * features
    inv_attn = lax.rsqrt(squares / D + NORM_EPS)
    return (total * inv_attn).astype(jnp.bfloat16).astype(jnp.float32)


PIECE = 16
TOP_AT = 3 * PIECE


def attention_kernel(
    arrived_ref, key_own, value_own, cache_peer, live_own, live_peer,
    message_ref, query_ref, key_new_ref, value_new_ref,
):
    n_copies, heads, _ = message_ref.shape
    n_req, span = live_own.shape
    half = key_own.shape[2] // 2
    mine = pl.ds(pl.multiple_of(head_half() * half, LANES), half)
    kv_half = half // HD
    group = heads // kv_half
    is_first = lax.axis_index("chip") == 0
    qkv = qkv_sum(arrived_ref)
    for h in range(heads):
        query_ref[:, h, :] = qkv[:, h * HD : (h + 1) * HD]
        at = (heads + h // group) * HD
        key_new_ref[:, h, :] = qkv[:, at : at + HD]
        at += kv_half * HD
        value_new_ref[:, h, :] = qkv[:, at : at + HD]

    rows = n_req * heads
    query = query_ref[...].reshape(rows, HD)
    group_of = lax.broadcasted_iota(jnp.int32, (rows, HD), 0) % heads // group
    spread = jnp.concatenate(
        [jnp.where(group_of == k, query, 0.0) for k in range(kv_half)], axis=1
    ).astype(jnp.bfloat16)
    scores, live = [], []
    for r in range(n_req):
        blocks = []
        for keys in (key_own[r, :, mine], cache_peer[0, r]):
            blocks.append(
                lax.dot_general(
                    spread[r * heads : (r + 1) * heads, :], keys,
                    (((1,), (1,)), ((), ())), preferred_element_type=jnp.float32,
                )
            )
        scores.append(jnp.concatenate(blocks, axis=1))
        live_row = jnp.concatenate([live_own[r : r + 1, :], live_peer[r : r + 1, :]], axis=1)
        live.append(jnp.broadcast_to(live_row, (heads, 2 * span)))
    live = jnp.concatenate(live, axis=0) > 0.0
    scale = 1.0 / math.sqrt(HD)
    scores = jnp.where(live, jnp.concatenate(scores, axis=0) * scale, MASKED)
    key_new = key_new_ref[...].reshape(rows, HD)
    self_score = jnp.sum(query * key_new, axis=1, keepdims=True) * scale
    self_score = jnp.where(is_first, self_score, MASKED)
    top = jnp.maximum(jnp.max(scores, axis=1, keepdims=True), self_score)
    weights = jnp.where(live, jnp.exp(scores - top), 0.0)
    self_weight = jnp.where(is_first, jnp.exp(self_score - top), 0.0)
    total = jnp.sum(weights, axis=1, keepdims=True) + self_weight
    rounded = weights.astype(jnp.bfloat16)
    self_part = self_weight * value_new_ref[...].reshape(rows, HD)
    pieces = pieces_of(total) + pieces_of(top)
    lane = lax.broadcasted_iota(jnp.int32, (heads, LANES), 1)
    stats = jnp.zeros((heads, LANES), jnp.float32)
    parts = []
    for r in range(n_req):
        at = slice(r * heads, (r + 1) * heads)
        wide = jnp.dot(
            rounded[at, :span], value_own[r, :, mine], preferred_element_type=jnp.float32
        ) + jnp.dot(
            rounded[at, span:], cache_peer[1, r], preferred_element_type=jnp.float32
        )
        numer = self_part[at, :]
        for k in range(kv_half):
            numer = numer + jnp.where(group_of[at, :] == k, wide[:, k * HD : (k + 1) * HD], 0.0)
        parts.append(numer)
        for p, piece in enumerate(pieces):
            stats = jnp.where(lane == p * PIECE + r, piece[at, :], stats)
    message = jnp.concatenate(parts + [stats], axis=1).astype(jnp.bfloat16)
    for i in range(n_copies):
        message_ref[i] = message


def combine_kernel(arrived_ref, rows_ref, attended_ref):
    n_chips, heads, width = arrived_ref.shape
    n_req = rows_ref.shape[0]
    totals, tops = [], []
    for chip in range(n_chips):
        tile = arrived_ref[chip, :, width - LANES :].astype(jnp.float32)
        tile = (
            tile
            + pltpu.roll(tile, LANES - PIECE, 1)
            + pltpu.roll(tile, LANES - 2 * PIECE, 1)
        )
        totals.append(tile)
        tops.append(pltpu.roll(tile, LANES - TOP_AT, 1))
    final_top = tops[0]
    for top in tops[1:]:
        final_top = jnp.maximum(final_top, top)
    fades = [jnp.exp(top - final_top) for top in tops]
    denominator = totals[0] * fades[0]
    for total, fade in zip(totals[1:], fades[1:]):
        denominator = denominator + total * fade
    for r in range(n_req):
        numer = jnp.zeros((heads, HD), jnp.float32)
        for chip, fade in enumerate(fades):
            part = arrived_ref[chip, :, r * HD : (r + 1) * HD].astype(jnp.float32)
            numer = numer + part * fade[:, r : r + 1]
        attended_ref[r] = numer / denominator[:, r : r + 1]
    rows = jnp.concatenate([attended_ref[:, h, :] for h in range(heads)], axis=1)
    rows_ref[...] = rows.astype(jnp.bfloat16)


def half_rows(rows_ref, w_ref, side):
    half = rows_ref.shape[1]
    rows = pl.ds(pl.multiple_of(side * half, LANES), half)
    return jnp.dot(rows_ref[...], w_ref[rows, :], preferred_element_type=jnp.float32)


def out_own_kernel(own_ref, w_ref, out_ref):
    out_ref[...] = half_rows(own_ref, w_ref, head_half())


def out_peer_kernel(own_part, peer_ref, w_ref, out_ref):
    out_ref[...] = own_part[...] + half_rows(peer_ref, w_ref, 1 - head_half())


def out_both_kernel(own_ref, peer_ref, w_ref, out_ref):
    side = head_half()
    out_ref[...] = half_rows(own_ref, w_ref, side) + half_rows(peer_ref, w_ref, 1 - side)


def up_columns(scaled_mlp, w_ref, side, out_ref):
    half = out_ref.shape[1] - LANES
    mine = pl.ds(pl.multiple_of(side * half, LANES), half)
    out_ref[:, :half] = jnp.dot(scaled_mlp, w_ref[:, mine], preferred_element_type=jnp.float32)


def up_other_kernel(
    x_ref, part_ref, peer_ref, gain_ref, w_ref, hidden_ref, scaled_ref, squares_ref, other_ref
):
    attn_out = part_ref[...] + peer_ref[...]
    hidden_state = (x_ref[...].astype(jnp.float32) + attn_out).astype(jnp.bfloat16)
    resid_rows = hidden_state.astype(jnp.float32)
    hidden_ref[...] = resid_rows
    scaled_mlp = (resid_rows * gain_ref[...]).astype(jnp.bfloat16)
    scaled_ref[...] = scaled_mlp
    squares = jnp.sum(resid_rows * resid_rows, axis=1, keepdims=True)
    squares_ref[...] = jnp.broadcast_to(squares, squares_ref.shape)
    other_ref[:, other_ref.shape[1] - LANES :] = squares_ref[...]
    up_columns(scaled_mlp, w_ref, 1 - up_half(), other_ref)


def up_mine_kernel(scaled_ref, squares_ref, w_ref, mine_ref):
    mine_ref[:, mine_ref.shape[1] - LANES :] = squares_ref[...]
    up_columns(scaled_ref[...], w_ref, up_half(), mine_ref)


def squares_tile(squares):
    lane = lax.broadcasted_iota(jnp.int32, squares.shape, 1)
    tile = jnp.zeros_like(squares)
    for p, piece in enumerate(pieces_of(squares)):
        tile = jnp.where(lane == p, piece, tile)
    return tile.astype(jnp.bfloat16)


def send_sum(total, sent_ref):
    half = sent_ref.shape[1] - LANES
    sent_ref[:, :half] = total[:, :half].astype(jnp.bfloat16)
    sent_ref[:, half:] = squares_tile(total[:, half:])


def add_arrived(total, arrived):
    half = total.shape[1] - LANES
    arrived = arrived.astype(jnp.float32)
    squares = jnp.sum(arrived[:, half:], axis=1, keepdims=True)
    return total[:, :half] + arrived[:, :half], total[:, half:] + squares


def up_pair_kernel(mine_ref, arrived_ref, total_a, sent_a, total_b, sent_b):
    total = mine_ref[...] + arrived_ref[...]
    width = total_a.shape[1]
    total_a[...] = total[:, :width]
    sent_a[...] = total[:, :width].astype(jnp.bfloat16)
    total_b[...] = total[:, width:]
    send_sum(total[:, width:], sent_b)


def up_add_a_kernel(part_ref, arrived_ref, total_ref, sent_ref):
    total = part_ref[...] + arrived_ref[...].astype(jnp.float32)
    total_ref[...] = total
    sent_ref[...] = total.astype(jnp.bfloat16)


def up_add_b_kernel(part_ref, arrived_ref, total_ref, sent_ref):
    total = jnp.concatenate(add_arrived(part_ref[...], arrived_ref[...]), axis=1)
    total_ref[...] = total
    send_sum(total, sent_ref)


def activate_kernel(part_a, arrived_a, part_b, arrived_b, out_ref):
    width = part_a.shape[1]
    total_a = part_a[...] + arrived_a[...].astype(jnp.float32)
    total_b, squares = add_arrived(part_b[...], arrived_b[...])
    inv_mlp = lax.rsqrt(squares[:, :1] / D + NORM_EPS)
    out_ref[:, :width] = squared_relu(total_a * inv_mlp).astype(jnp.bfloat16)
    out_ref[:, width:] = squared_relu(total_b * inv_mlp).astype(jnp.bfloat16)


def down_own_kernel(own_ref, w_ref, out_ref):
    out_ref[...] = half_rows(own_ref, w_ref, up_half())


def down_peer_kernel(own_part, peer_ref, w_ref, out_ref):
    out_ref[...] = own_part[...] + half_rows(peer_ref, w_ref, 1 - up_half())


def per_device(
    hidden_in,
    attn_gain,
    mlp_gain,
    query_weight,
    key_weight,
    value_weight,
    out_weight,
    up_weight,
    down_weight,
    key_cache,
    value_cache,
    lengths,
    block_order,
    pad_mask,
):
    n_req, d_here = hidden_in.shape
    kv_here = key_cache.shape[2] // HD
    heads_here = kv_here * (H // KVH)
    n_chips = lax.axis_size("chip")
    core = lax.axis_index("core")
    n_blocks = 2 * n_chips
    half_qkv = (heads_here + 2 * kv_here) * HD // 2
    half_up = up_weight.shape[1] // 2

    row = (1, d_here)
    small = [hidden_in, attn_gain.reshape(row), mlp_gain.reshape(row), pad_mask]
    small += [lengths, block_order, key_cache, value_cache]
    scaled_in, squares, live, x_rows, gain, cache_sent = local_kernel(
        prepare_kernel,
        [
            bf16(*hidden_in.shape),
            f32(n_req, LANES),
            f32(*pad_mask.shape),
            bf16(*hidden_in.shape),
            f32(*row),
            bf16(2, *key_cache.shape[:2], key_cache.shape[2] // 2),
        ],
        small,
        flops=4 * 10**9,
        scratch=[
            pltpu.VMEM(row, jnp.float32),
            pltpu.VMEM(pad_mask.shape, jnp.int32),
            pltpu.SMEM(lengths.shape, jnp.int32),
            pltpu.SMEM(block_order.shape, jnp.int32),
            pltpu.SemaphoreType.DMA((len(small),)),
        ],
        in_hbm=range(len(small)),
    )
    (other,) = local_kernel(
        qkv_other_kernel,
        [f32(n_req, half_qkv + LANES + pad_mask.shape[1])],
        [scaled_in, squares, live, query_weight, key_weight, value_weight],
        flops=4 * 10**9,
        anywhere=(3, 4, 5),
    )
    (mine,) = local_kernel(
        qkv_mine_kernel,
        [f32(n_req, half_qkv + LANES)],
        [scaled_in, squares, query_weight, key_weight, value_weight],
        flops=2 * n_req * d_here * half_qkv,
        anywhere=(2, 3, 4),
    )
    arrived = swap(other, "core")
    width = mine.shape[1]
    (qkv_message,) = local_kernel(
        qkv_message_kernel, [f32(*mine.shape)], [mine, arrived], flops=2 * mine.size
    )
    qkv_message, live_peer, *moved = lax.optimization_barrier(
        (
            qkv_message.astype(jnp.float16),
            arrived[:, width:],
            cache_sent,
            out_weight,
        )
    )
    cache_peer, out_peer = (swap(x, "core") for x in moved)
    sides = [
        [2 * chip + (side + chip_turn(chip)) % 2 for chip in range(n_chips)] for side in range(2)
    ]
    qkv_all = lax.all_to_all(
        jnp.broadcast_to(qkv_message[None], (n_chips,) + qkv_message.shape),
        ("chip", "core"),
        0,
        0,
        axis_index_groups=sides,
    )
    half_heads = heads_here // 2
    (message,) = local_kernel(
        attention_kernel,
        [bf16(n_chips, half_heads, n_req * HD + LANES)],
        [qkv_all.astype(jnp.float32), key_cache, value_cache, cache_peer, live, live_peer],
        anywhere=(1, 2, 3),
        flops=4 * 10**9,
        scratch=[pltpu.VMEM((n_req, half_heads, HD), jnp.float32)] * 3,
    )
    message, out_peer = lax.optimization_barrier((message, out_peer))
    (attended,) = local_kernel(
        combine_kernel,
        [bf16(n_req, half_heads * HD)],
        [lax.all_to_all(message, ("chip", "core"), 0, 0, axis_index_groups=sides)],
        flops=n_chips * n_req * half_heads * HD,
        scratch=[pltpu.VMEM((n_req, half_heads, HD), jnp.float32)],
    )
    attended_peer = swap(attended, "core")
    (head_own,) = local_kernel(
        out_own_kernel,
        [f32(n_req, d_here)],
        [attended, out_peer],
        anywhere=(1,),
        flops=n_req * out_weight.size,
    )
    (head_sent,) = local_kernel(
        out_peer_kernel,
        [f32(n_req, d_here)],
        [head_own, attended_peer, out_peer],
        anywhere=(2,),
        flops=n_req * out_weight.size,
    )
    head_peer = swap_diagonal(head_sent)
    (head_part,) = local_kernel(
        out_both_kernel,
        [f32(n_req, d_here)],
        [attended, attended_peer, out_weight],
        anywhere=(2,),
        flops=2 * n_req * out_weight.size,
    )

    resid_rows, scaled_mlp, squares, up_other = local_kernel(
        up_other_kernel,
        [
            f32(n_req, d_here),
            bf16(n_req, d_here),
            f32(n_req, LANES),
            f32(n_req, half_up + LANES),
        ],
        [x_rows, head_part, head_peer, gain, up_weight],
        flops=n_req * up_weight.size,
        anywhere=(4,),
    )
    (up_mine,) = local_kernel(
        up_mine_kernel,
        [f32(n_req, half_up + LANES)],
        [scaled_mlp, squares, up_weight],
        flops=n_req * up_weight.size,
        anywhere=(2,),
    )
    width_a = half_up // (2 * LANES) * LANES
    widths = [width_a, half_up + LANES - width_a]
    sums = [[f32(n_req, width), bf16(n_req, width)] for width in widths]
    pair = local_kernel(
        up_pair_kernel,
        sums[0] + sums[1],
        [up_mine, swap(up_other, "core")],
        flops=up_mine.size,
    )
    parts = [pair[:2], pair[2:]]
    orders = [[2, 1, 0], [1, 0, 2]]
    arrived = [swap_chips(part[1], order[0]) for part, order in zip(parts, orders)]
    for step in range(1, chip_bits()):
        for i, kernel in enumerate((up_add_a_kernel, up_add_b_kernel)):
            parts[i] = local_kernel(
                kernel, sums[i], [parts[i][0], arrived[i]], flops=n_req * widths[i]
            )
            arrived[i] = swap_chips(parts[i][1], orders[i][step])
    (active_half,) = local_kernel(
        activate_kernel,
        [bf16(n_req, half_up)],
        [parts[0][0], arrived[0], parts[1][0], arrived[1]],
        flops=4 * up_mine.size,
    )
    active_other = swap(active_half, "core")
    (down_own,) = local_kernel(
        down_own_kernel,
        [f32(n_req, d_here)],
        [active_half, down_weight],
        flops=n_req * down_weight.size,
        anywhere=(1,),
    )
    (down_part,) = local_kernel(
        down_peer_kernel,
        [f32(n_req, d_here)],
        [down_own, active_other, down_weight],
        flops=n_req * down_weight.size,
        anywhere=(2,),
    )
    mlp_out = sum_tp(down_part)
    return (resid_rows + mlp_out).astype(jnp.bfloat16)


def solution(mesh):
    n_seq, n_tp = mesh.shape["seq"], mesh.shape["tp"]
    split = Mesh(mesh.devices.reshape(n_seq // 2, 2, n_tp), ("chip", "core", "tp"))
    seq = ("chip", "core")
    chips = n_seq // 2
    whole_tiles = chips == 8 and n_tp == 2
    return jax.shard_map(
        per_device if whole_tiles else per_device_plain,
        mesh=split,
        in_specs=(
            P(None, seq),
            P(seq),
            P(seq),
            P(seq, "tp"),
            P(seq, "tp"),
            P(seq, "tp"),
            P("tp", seq),
            P(seq, "tp"),
            P("tp", seq),
            P(None, seq, "tp"),
            P(None, seq, "tp"),
            P(),
            P(),
            P(None, seq),
        ),
        out_specs=P(None, seq),
        check_vma=False,
    )
```

```python
import functools
import math

import jax
import jax.numpy as jnp
from jax import lax
from jax.experimental import pallas as pl
from jax.experimental.pallas import tpu as pltpu
from jax.sharding import Mesh, PartitionSpec as P

D = 4096
H = 32
KVH = 8
HD = 128


NORM_EPS = 1e-05
MASKED = -1e30
LANES = 128


def squared_relu(values_in):
    positive = jnp.maximum(values_in, 0.0)
    return positive * positive


def swap(values_in, axis):
    n = lax.axis_size(axis)
    return lax.ppermute(values_in, axis, [(i, i ^ 1) for i in range(n)])


def swap_diagonal(values_in):
    return lax.ppermute(values_in, ("core", "tp"), [(i, 3 - i) for i in range(4)])


def swap_chips(values_in, bit):
    n = 2 * lax.axis_size("chip")
    return lax.ppermute(
        values_in, ("chip", "core"), [(i, i ^ (2 << bit) ^ 1) for i in range(n)]
    )


def gather_all(values_in, axes, n):
    copies = jnp.broadcast_to(values_in[None], (n,) + values_in.shape)
    return lax.all_to_all(copies, axes, 0, 0)


def sum_tp(values_in):
    n = lax.axis_size("tp")
    if n == 2:
        return values_in + swap(values_in, "tp")
    return lax.psum(values_in, "tp")


def per_device_plain(
    hidden_in,
    attn_gain,
    mlp_gain,
    query_weight,
    key_weight,
    value_weight,
    out_weight,
    up_weight,
    down_weight,
    key_cache,
    value_cache,
    lengths,
    block_order,
    pad_mask,
):
    n_req = hidden_in.shape[0]
    q_per_kv = H // KVH
    kv_here = key_cache.shape[2] // HD
    span_here = key_cache.shape[1]
    heads_here = kv_here * q_per_kv
    n_chips = lax.axis_size("chip")
    core = lax.axis_index("core")
    n_blocks = 2 * n_chips
    my_block = 2 * lax.axis_index("chip") + core
    score_scale = 1.0 / math.sqrt(HD)

    x_rows = hidden_in.astype(jnp.float32)
    scaled_in = (x_rows * attn_gain).astype(jnp.bfloat16)
    sq_attn = jnp.sum(x_rows * x_rows, axis=1, keepdims=True)
    proj_query = jnp.dot(scaled_in, query_weight, preferred_element_type=jnp.float32)
    proj_key = jnp.dot(scaled_in, key_weight, preferred_element_type=jnp.float32)
    proj_value = jnp.dot(scaled_in, value_weight, preferred_element_type=jnp.float32)
    half_q, half_kv = proj_query.shape[1] // 2, proj_key.shape[1] // 2
    square_cols = jnp.broadcast_to(sq_attn, (n_req, LANES))

    def half(i):
        return jnp.concatenate(
            [
                proj_query[:, i * half_q : (i + 1) * half_q],
                proj_key[:, i * half_kv : (i + 1) * half_kv],
                proj_value[:, i * half_kv : (i + 1) * half_kv],
                square_cols,
            ],
            axis=1,
        )

    low, high = half(0), half(1)
    mine = jnp.where(core == 0, low, high)
    other = jnp.where(core == 0, high, low)
    pair_sum = mine + swap(other, "core")
    qkv_sum = jnp.sum(gather_all(pair_sum, "chip", n_chips), axis=0)
    inv_attn = lax.rsqrt(qkv_sum[:, -1:] / D + NORM_EPS)
    qkv_half = (qkv_sum[:, :-LANES] * inv_attn).astype(jnp.bfloat16)
    qkv_other = swap(qkv_half, "core")
    qkv_low = jnp.where(core == 0, qkv_half, qkv_other)
    qkv_high = jnp.where(core == 0, qkv_other, qkv_half)

    def both(start, size):
        return jnp.concatenate(
            [qkv_low[:, start : start + size], qkv_high[:, start : start + size]], axis=1
        )

    query_rows = both(0, half_q)
    key_new = both(half_q, half_kv)
    value_new = both(half_q + half_kv, half_kv)

    first_block = block_order % n_blocks
    position = ((my_block - first_block) % n_blocks)[:, None] * span_here + jnp.arange(
        span_here, dtype=jnp.int32
    )[None, :]
    live_slots = ((position < lengths[:, None]) & (pad_mask == 1))[:, None, None, :]
    q_groups = query_rows.reshape(n_req, kv_here, q_per_kv, HD)
    keys_here = key_cache.reshape(n_req, span_here, kv_here, HD)
    values_here = value_cache.reshape(n_req, span_here, kv_here, HD)
    scores = (
        jnp.einsum("rkgd,rtkd->rkgt", q_groups, keys_here, preferred_element_type=jnp.float32)
        * score_scale
    )
    scores = jnp.where(live_slots, scores, MASKED)
    local_top = jnp.max(scores, axis=3, keepdims=True)
    weights = jnp.where(live_slots, jnp.exp(scores - local_top), 0.0)
    local_total = jnp.sum(weights, axis=3, keepdims=True)
    local_out = jnp.einsum(
        "rkgt,rtkd->rkgd",
        weights.astype(jnp.bfloat16),
        values_here,
        preferred_element_type=jnp.float32,
    )
    numer = local_out.reshape(n_req, heads_here, HD)
    stats = jnp.concatenate(
        [
            local_total.reshape(n_req, heads_here, 1),
            local_top.reshape(n_req, heads_here, 1),
        ],
        axis=2,
    )
    stat_rows = stats.reshape(n_req, heads_here * 2)
    pad = (-stat_rows.shape[1]) % LANES
    message = jnp.concatenate(
        [numer.reshape(n_req, heads_here * HD), jnp.pad(stat_rows, ((0, 0), (0, pad)))], axis=1
    )
    arrived = gather_all(message, ("chip", "core"), n_blocks)
    outs = arrived[:, :, : heads_here * HD].reshape(n_blocks, n_req, heads_here, HD)
    stats_all = arrived[:, :, heads_here * HD : heads_here * (HD + 2)].reshape(
        n_blocks, n_req, heads_here, 2
    )
    totals, tops = stats_all[..., 0], stats_all[..., 1]
    self_score = (
        jnp.einsum(
            "rkgd,rkd->rkg",
            q_groups,
            key_new.reshape(n_req, kv_here, HD),
            preferred_element_type=jnp.float32,
        )
        * score_scale
    ).reshape(n_req, heads_here)
    final_top = jnp.maximum(jnp.max(tops, axis=0), self_score)
    fades = jnp.exp(tops - final_top)
    self_weight = jnp.exp(self_score - final_top)
    denominator = jnp.sum(totals * fades, axis=0) + self_weight
    value_self = jnp.broadcast_to(
        value_new.reshape(n_req, kv_here, 1, HD), (n_req, kv_here, q_per_kv, HD)
    ).reshape(n_req, heads_here, HD)
    numerator = jnp.sum(outs * fades[..., None], axis=0) + self_weight[
        ..., None
    ] * value_self.astype(jnp.float32)
    attended = (
        (numerator / denominator[..., None])
        .reshape(n_req, heads_here * HD)
        .astype(jnp.bfloat16)
    )
    head_part = jnp.dot(attended, out_weight, preferred_element_type=jnp.float32)
    attn_out = sum_tp(head_part)
    hidden_state = (x_rows + attn_out).astype(jnp.bfloat16)

    resid_rows = hidden_state.astype(jnp.float32)
    scaled_mlp = (resid_rows * mlp_gain).astype(jnp.bfloat16)
    sq_mlp = jnp.sum(resid_rows * resid_rows, axis=1, keepdims=True)
    up_part = jnp.dot(scaled_mlp, up_weight, preferred_element_type=jnp.float32)
    half_up = up_part.shape[1] // 2
    up_low, up_high = up_part[:, :half_up], up_part[:, half_up:]
    square_cols = jnp.broadcast_to(sq_mlp, (n_req, LANES))
    up_mine = jnp.concatenate([jnp.where(core == 0, up_low, up_high), square_cols], axis=1)
    up_other = jnp.concatenate([jnp.where(core == 0, up_high, up_low), square_cols], axis=1)
    up_pair = up_mine + swap(up_other, "core")
    square_sum = up_pair[:, half_up : half_up + 1]
    piece_0 = lax.reduce_precision(square_sum, 8, 7)
    piece_1 = lax.reduce_precision(square_sum - piece_0, 8, 7)
    piece_2 = square_sum - piece_0 - piece_1
    pieces = jnp.pad(
        jnp.concatenate([piece_0, piece_1, piece_2], axis=1), ((0, 0), (0, LANES - 3))
    )
    up_message = jnp.concatenate([up_pair[:, :half_up], pieces], axis=1).astype(jnp.bfloat16)
    up_sum = jnp.sum(gather_all(up_message, "chip", n_chips).astype(jnp.float32), axis=0)
    squares = jnp.sum(up_sum[:, half_up:], axis=1, keepdims=True)
    inv_mlp = lax.rsqrt(squares / D + NORM_EPS)
    active_half = squared_relu(up_sum[:, :half_up] * inv_mlp).astype(jnp.bfloat16)
    active_other = swap(active_half, "core")
    activated = jnp.concatenate(
        [
            jnp.where(core == 0, active_half, active_other),
            jnp.where(core == 0, active_other, active_half),
        ],
        axis=1,
    )
    down_part = jnp.dot(activated, down_weight, preferred_element_type=jnp.float32)
    mlp_out = sum_tp(down_part)
    return (resid_rows + mlp_out).astype(jnp.bfloat16)


IN_VMEM = pl.BlockSpec(memory_space=pltpu.VMEM)


def chip_turn(chip):
    return chip // 2 % 2


def head_half():
    return (lax.axis_index("core") + chip_turn(lax.axis_index("chip"))) % 2


def up_half():
    turns, chip = lax.axis_index("core"), lax.axis_index("chip")
    for bit in range(chip_bits()):
        turns = turns + chip // 2**bit % 2
    return turns % 2


def chip_bits():
    return lax.axis_size("chip").bit_length() - 1


def local_kernel(kernel, outs, operands, flops, scratch=(), in_hbm=(), anywhere=()):
    in_specs, placed, moved = [], [], 0
    for i, x in enumerate(operands):
        space = pltpu.HBM if i in in_hbm else pltpu.VMEM
        in_specs.append(pl.BlockSpec(memory_space=space))
        placed.append(x if i in anywhere else pltpu.with_memory_space_constraint(x, space))
        moved += x.size * x.dtype.itemsize
    return pl.pallas_call(
        kernel,
        out_shape=outs,
        in_specs=in_specs,
        out_specs=[IN_VMEM] * len(outs),
        scratch_shapes=scratch,
        compiler_params=pltpu.CompilerParams(vmem_limit_bytes=6 * 2**20),
        cost_estimate=pl.CostEstimate(flops=flops, bytes_accessed=moved, transcendentals=0),
    )(*placed)


def f32(*shape):
    return pltpu.VMEM(shape, jnp.float32)


def bf16(*shape):
    return pltpu.VMEM(shape, jnp.bfloat16)


def pieces_of(values_in):
    first = values_in.astype(jnp.bfloat16).astype(jnp.float32)
    second = (values_in - first).astype(jnp.bfloat16).astype(jnp.float32)
    return first, second, values_in - first - second


def prepare_kernel(
    x_hbm, gain_hbm, mlp_gain_hbm, mask_hbm, lengths_hbm, order_hbm, key_hbm, value_hbm,
    scaled_ref, squares_ref, live_ref, x_ref, mlp_gain_ref, cache_ref,
    gain_ref, mask_ref, lengths_ref, order_ref, sems,
):
    core = lax.axis_index("core")
    n_blocks = lax.axis_size("chip") * 2
    my_block = 2 * lax.axis_index("chip") + core
    half = cache_ref.shape[3]
    heads = pl.ds(pl.multiple_of((1 - head_half()) * half, LANES), half)
    pairs = [
        (x_hbm, x_ref), (gain_hbm, gain_ref), (mask_hbm, mask_ref), (lengths_hbm, lengths_ref),
        (order_hbm, order_ref), (mlp_gain_hbm, mlp_gain_ref),
        (key_hbm.at[:, :, heads], cache_ref.at[0]), (value_hbm.at[:, :, heads], cache_ref.at[1]),
    ]
    copies = [pltpu.make_async_copy(src, dst, sems.at[i]) for i, (src, dst) in enumerate(pairs)]
    for copy in copies:
        copy.start()
    for copy in copies[:-2]:
        copy.wait()
    n_req, span = live_ref.shape
    slot = lax.broadcasted_iota(jnp.int32, (1, span), 1)
    for r in range(n_req):
        first_block = lax.rem(order_ref[r], n_blocks)
        begin = lax.rem(my_block - first_block + n_blocks, n_blocks) * span
        live = (begin + slot < lengths_ref[r]) & (mask_ref[r : r + 1, :] == 1)
        live_ref[r : r + 1, :] = live.astype(jnp.float32)
    x_rows = x_ref[...].astype(jnp.float32)
    scaled_ref[...] = (x_rows * gain_ref[...]).astype(jnp.bfloat16)
    squares = jnp.sum(x_rows * x_rows, axis=1, keepdims=True)
    squares_ref[...] = jnp.broadcast_to(squares, squares_ref.shape)
    for copy in copies[-2:]:
        copy.wait()


def qkv_columns(scaled_ref, w_refs, side, out_ref):
    at = 0
    for w_ref in w_refs:
        half = w_ref.shape[1] // 2
        mine = pl.ds(pl.multiple_of(side * half, LANES), half)
        out_ref[:, at : at + half] = jnp.dot(
            scaled_ref[...], w_ref[:, mine], preferred_element_type=jnp.float32
        )
        at += half
    return at


def qkv_other_kernel(scaled_ref, squares_ref, live_ref, wq_ref, wk_ref, wv_ref, other_ref):
    other = 1 - head_half()
    at = qkv_columns(scaled_ref, (wq_ref, wk_ref, wv_ref), other, other_ref)
    other_ref[:, at : at + LANES] = squares_ref[...]
    other_ref[:, at + LANES :] = live_ref[...]


def qkv_mine_kernel(scaled_ref, squares_ref, wq_ref, wk_ref, wv_ref, mine_ref):
    at = qkv_columns(scaled_ref, (wq_ref, wk_ref, wv_ref), head_half(), mine_ref)
    mine_ref[:, at:] = squares_ref[...]


SCALE_UNIT = 1024.0


def qkv_message_kernel(mine_ref, arrived_ref, out_ref):
    width = mine_ref.shape[1] - LANES
    features = D / lax.axis_size("chip")
    total = mine_ref[...] + arrived_ref[:, : width + LANES]
    squares = total[:, width:]
    scale = jnp.sqrt(jnp.maximum(squares * (1.0 / features), 2.0**-40))
    scale = scale.astype(jnp.bfloat16).astype(jnp.float32)
    inverse = 1.0 / scale
    out_ref[:, :width] = total[:, :width] * inverse[:, :1]
    lane = lax.broadcasted_iota(jnp.int32, squares.shape, 1)
    tile = jnp.where(lane == 0, scale * SCALE_UNIT, 0.0)
    for p, piece in enumerate(pieces_of(squares * inverse * inverse * (1.0 / features))):
        tile = jnp.where(lane == 1 + p, piece, tile)
    out_ref[:, width:] = tile


def qkv_sum(arrived_ref):
    n_chips, _, width = arrived_ref.shape
    width -= LANES
    features = D / n_chips
    total, squares = 0.0, 0.0
    for i in range(n_chips):
        tile = arrived_ref[i, :, width:]
        scale = tile[:, :1] * (1.0 / SCALE_UNIT)
        total = total + arrived_ref[i, :, :width] * scale
        mean = tile[:, 1:2] + tile[:, 2:3] + tile[:, 3:4]
        squares = squares + mean * scale * scale * features
    inv_attn = lax.rsqrt(squares / D + NORM_EPS)
    return (total * inv_attn).astype(jnp.bfloat16).astype(jnp.float32)


PIECE = 16
TOP_AT = 3 * PIECE


def attention_kernel(
    arrived_ref, key_own, value_own, cache_peer, live_own, live_peer,
    message_ref, query_ref, key_new_ref, value_new_ref,
):
    n_copies, heads, _ = message_ref.shape
    n_req, span = live_own.shape
    half = key_own.shape[2] // 2
    mine = pl.ds(pl.multiple_of(head_half() * half, LANES), half)
    kv_half = half // HD
    group = heads // kv_half
    is_first = lax.axis_index("chip") == 0
    qkv = qkv_sum(arrived_ref)
    for h in range(heads):
        query_ref[:, h, :] = qkv[:, h * HD : (h + 1) * HD]
        at = (heads + h // group) * HD
        key_new_ref[:, h, :] = qkv[:, at : at + HD]
        at += kv_half * HD
        value_new_ref[:, h, :] = qkv[:, at : at + HD]

    rows = n_req * heads
    query = query_ref[...].reshape(rows, HD)
    group_of = lax.broadcasted_iota(jnp.int32, (rows, HD), 0) % heads // group
    spread = jnp.concatenate(
        [jnp.where(group_of == k, query, 0.0) for k in range(kv_half)], axis=1
    ).astype(jnp.bfloat16)
    scores, live = [], []
    for r in range(n_req):
        blocks = []
        for keys in (key_own[r, :, mine], cache_peer[0, r]):
            blocks.append(
                lax.dot_general(
                    spread[r * heads : (r + 1) * heads, :], keys,
                    (((1,), (1,)), ((), ())), preferred_element_type=jnp.float32,
                )
            )
        scores.append(jnp.concatenate(blocks, axis=1))
        live_row = jnp.concatenate([live_own[r : r + 1, :], live_peer[r : r + 1, :]], axis=1)
        live.append(jnp.broadcast_to(live_row, (heads, 2 * span)))
    live = jnp.concatenate(live, axis=0) > 0.0
    scale = 1.0 / math.sqrt(HD)
    scores = jnp.where(live, jnp.concatenate(scores, axis=0) * scale, MASKED)
    key_new = key_new_ref[...].reshape(rows, HD)
    self_score = jnp.sum(query * key_new, axis=1, keepdims=True) * scale
    self_score = jnp.where(is_first, self_score, MASKED)
    top = jnp.maximum(jnp.max(scores, axis=1, keepdims=True), self_score)
    weights = jnp.where(live, jnp.exp(scores - top), 0.0)
    self_weight = jnp.where(is_first, jnp.exp(self_score - top), 0.0)
    total = jnp.sum(weights, axis=1, keepdims=True) + self_weight
    rounded = weights.astype(jnp.bfloat16)
    self_part = self_weight * value_new_ref[...].reshape(rows, HD)
    pieces = pieces_of(total) + pieces_of(top)
    lane = lax.broadcasted_iota(jnp.int32, (heads, LANES), 1)
    stats = jnp.zeros((heads, LANES), jnp.float32)
    parts = []
    for r in range(n_req):
        at = slice(r * heads, (r + 1) * heads)
        wide = jnp.dot(
            rounded[at, :span], value_own[r, :, mine], preferred_element_type=jnp.float32
        ) + jnp.dot(
            rounded[at, span:], cache_peer[1, r], preferred_element_type=jnp.float32
        )
        numer = self_part[at, :]
        for k in range(kv_half):
            numer = numer + jnp.where(group_of[at, :] == k, wide[:, k * HD : (k + 1) * HD], 0.0)
        parts.append(numer)
        for p, piece in enumerate(pieces):
            stats = jnp.where(lane == p * PIECE + r, piece[at, :], stats)
    message = jnp.concatenate(parts + [stats], axis=1).astype(jnp.bfloat16)
    for i in range(n_copies):
        message_ref[i] = message


def combine_kernel(arrived_ref, rows_ref, attended_ref):
    n_chips, heads, width = arrived_ref.shape
    n_req = rows_ref.shape[0]
    totals, tops = [], []
    for chip in range(n_chips):
        tile = arrived_ref[chip, :, width - LANES :].astype(jnp.float32)
        tile = (
            tile
            + pltpu.roll(tile, LANES - PIECE, 1)
            + pltpu.roll(tile, LANES - 2 * PIECE, 1)
        )
        totals.append(tile)
        tops.append(pltpu.roll(tile, LANES - TOP_AT, 1))
    final_top = tops[0]
    for top in tops[1:]:
        final_top = jnp.maximum(final_top, top)
    fades = [jnp.exp(top - final_top) for top in tops]
    denominator = totals[0] * fades[0]
    for total, fade in zip(totals[1:], fades[1:]):
        denominator = denominator + total * fade
    for r in range(n_req):
        numer = jnp.zeros((heads, HD), jnp.float32)
        for chip, fade in enumerate(fades):
            part = arrived_ref[chip, :, r * HD : (r + 1) * HD].astype(jnp.float32)
            numer = numer + part * fade[:, r : r + 1]
        attended_ref[r] = numer / denominator[:, r : r + 1]
    rows = jnp.concatenate([attended_ref[:, h, :] for h in range(heads)], axis=1)
    rows_ref[...] = rows.astype(jnp.bfloat16)


def half_rows(rows_ref, w_ref, side):
    half = rows_ref.shape[1]
    rows = pl.ds(pl.multiple_of(side * half, LANES), half)
    return jnp.dot(rows_ref[...], w_ref[rows, :], preferred_element_type=jnp.float32)


def out_own_kernel(own_ref, w_ref, out_ref):
    out_ref[...] = half_rows(own_ref, w_ref, head_half())


def out_peer_kernel(own_part, peer_ref, w_ref, out_ref):
    out_ref[...] = own_part[...] + half_rows(peer_ref, w_ref, 1 - head_half())


def out_both_kernel(own_ref, peer_ref, w_ref, out_ref):
    side = head_half()
    out_ref[...] = half_rows(own_ref, w_ref, side) + half_rows(peer_ref, w_ref, 1 - side)


def up_columns(scaled_mlp, w_ref, side, out_ref):
    half = out_ref.shape[1] - LANES
    mine = pl.ds(pl.multiple_of(side * half, LANES), half)
    out_ref[:, :half] = jnp.dot(scaled_mlp, w_ref[:, mine], preferred_element_type=jnp.float32)


def up_other_kernel(
    x_ref, part_ref, peer_ref, gain_ref, w_ref, hidden_ref, scaled_ref, squares_ref, other_ref
):
    attn_out = part_ref[...] + peer_ref[...]
    hidden_state = (x_ref[...].astype(jnp.float32) + attn_out).astype(jnp.bfloat16)
    resid_rows = hidden_state.astype(jnp.float32)
    hidden_ref[...] = resid_rows
    scaled_mlp = (resid_rows * gain_ref[...]).astype(jnp.bfloat16)
    scaled_ref[...] = scaled_mlp
    squares = jnp.sum(resid_rows * resid_rows, axis=1, keepdims=True)
    squares_ref[...] = jnp.broadcast_to(squares, squares_ref.shape)
    other_ref[:, other_ref.shape[1] - LANES :] = squares_ref[...]
    up_columns(scaled_mlp, w_ref, 1 - up_half(), other_ref)


def up_mine_kernel(scaled_ref, squares_ref, w_ref, mine_ref):
    mine_ref[:, mine_ref.shape[1] - LANES :] = squares_ref[...]
    up_columns(scaled_ref[...], w_ref, up_half(), mine_ref)


def up_pair_kernel(mine_ref, arrived_ref, total_a, sent_a, total_b, sent_b):
    half = mine_ref.shape[1] - LANES
    start = total_a.shape[1]
    total = mine_ref[:, :half] + arrived_ref[:, :half]
    squares = mine_ref[:, half:] + arrived_ref[:, half:]
    lane = lax.broadcasted_iota(jnp.int32, squares.shape, 1)
    tile = jnp.zeros_like(squares)
    for p, piece in enumerate(pieces_of(squares)):
        tile = jnp.where(lane == p, piece, tile)
    total_a[...] = total[:, :start]
    sent_a[...] = total[:, :start].astype(jnp.bfloat16)
    put_b(total[:, start:], tile, total_b, sent_b)


def put_b(total, tile, total_ref, sent_ref):
    width = total.shape[1]
    for at, value in ((slice(0, width), total), (slice(width, None), tile)):
        total_ref[:, at] = value
        sent_ref[:, at] = value.astype(jnp.bfloat16)


def up_add_a_kernel(part_ref, arrived_ref, total_ref, sent_ref):
    total = part_ref[...] + arrived_ref[...].astype(jnp.float32)
    total_ref[...] = total
    sent_ref[...] = total.astype(jnp.bfloat16)


def up_add_b_kernel(shift, part_ref, arrived_ref, total_ref, sent_ref):
    width = part_ref.shape[1] - LANES
    total = part_ref[:, :width] + arrived_ref[:, :width].astype(jnp.float32)
    pieces = pltpu.roll(arrived_ref[:, width:].astype(jnp.float32), shift, 1)
    put_b(total, part_ref[:, width:] + pieces, total_ref, sent_ref)


def activate_kernel(part_a, arrived_a, part_b, arrived_b, out_ref):
    start, width = part_a.shape[1], part_b.shape[1] - LANES
    pieces = part_b[:, width:] + arrived_b[:, width:].astype(jnp.float32)
    squares = jnp.sum(pieces, axis=1, keepdims=True)
    inv_mlp = lax.rsqrt(squares / D + NORM_EPS)
    total_a = part_a[...] + arrived_a[...].astype(jnp.float32)
    out_ref[:, :start] = squared_relu(total_a * inv_mlp).astype(jnp.bfloat16)
    total_b = part_b[:, :width] + arrived_b[:, :width].astype(jnp.float32)
    out_ref[:, start:] = squared_relu(total_b * inv_mlp).astype(jnp.bfloat16)


def down_own_kernel(own_ref, w_ref, out_ref):
    out_ref[...] = half_rows(own_ref, w_ref, up_half())


def down_peer_kernel(own_part, peer_ref, w_ref, out_ref):
    out_ref[...] = own_part[...] + half_rows(peer_ref, w_ref, 1 - up_half())


def per_device(
    hidden_in,
    attn_gain,
    mlp_gain,
    query_weight,
    key_weight,
    value_weight,
    out_weight,
    up_weight,
    down_weight,
    key_cache,
    value_cache,
    lengths,
    block_order,
    pad_mask,
):
    n_req, d_here = hidden_in.shape
    kv_here = key_cache.shape[2] // HD
    heads_here = kv_here * (H // KVH)
    n_chips = lax.axis_size("chip")
    core = lax.axis_index("core")
    n_blocks = 2 * n_chips
    half_qkv = (heads_here + 2 * kv_here) * HD // 2
    half_up = up_weight.shape[1] // 2

    row = (1, d_here)
    small = [hidden_in, attn_gain.reshape(row), mlp_gain.reshape(row), pad_mask]
    small += [lengths, block_order, key_cache, value_cache]
    scaled_in, squares, live, x_rows, gain, cache_sent = local_kernel(
        prepare_kernel,
        [
            bf16(*hidden_in.shape),
            f32(n_req, LANES),
            f32(*pad_mask.shape),
            bf16(*hidden_in.shape),
            f32(*row),
            bf16(2, *key_cache.shape[:2], key_cache.shape[2] // 2),
        ],
        small,
        flops=4 * 10**9,
        scratch=[
            pltpu.VMEM(row, jnp.float32),
            pltpu.VMEM(pad_mask.shape, jnp.int32),
            pltpu.SMEM(lengths.shape, jnp.int32),
            pltpu.SMEM(block_order.shape, jnp.int32),
            pltpu.SemaphoreType.DMA((len(small),)),
        ],
        in_hbm=range(len(small)),
    )
    (other,) = local_kernel(
        qkv_other_kernel,
        [f32(n_req, half_qkv + LANES + pad_mask.shape[1])],
        [scaled_in, squares, live, query_weight, key_weight, value_weight],
        flops=4 * 10**9,
        anywhere=(3, 4, 5),
    )
    (mine,) = local_kernel(
        qkv_mine_kernel,
        [f32(n_req, half_qkv + LANES)],
        [scaled_in, squares, query_weight, key_weight, value_weight],
        flops=2 * n_req * d_here * half_qkv,
        anywhere=(2, 3, 4),
    )
    arrived = swap(other, "core")
    width = mine.shape[1]
    (qkv_message,) = local_kernel(
        qkv_message_kernel, [f32(*mine.shape)], [mine, arrived], flops=2 * mine.size
    )
    qkv_message, live_peer, *moved = lax.optimization_barrier(
        (
            qkv_message.astype(jnp.float16),
            arrived[:, width:],
            cache_sent,
            out_weight,
        )
    )
    cache_peer, out_peer = (swap(x, "core") for x in moved)
    sides = [
        [2 * chip + (side + chip_turn(chip)) % 2 for chip in range(n_chips)] for side in range(2)
    ]
    qkv_all = lax.all_to_all(
        jnp.broadcast_to(qkv_message[None], (n_chips,) + qkv_message.shape),
        ("chip", "core"),
        0,
        0,
        axis_index_groups=sides,
    )
    half_heads = heads_here // 2
    (message,) = local_kernel(
        attention_kernel,
        [bf16(n_chips, half_heads, n_req * HD + LANES)],
        [qkv_all.astype(jnp.float32), key_cache, value_cache, cache_peer, live, live_peer],
        anywhere=(1, 2, 3),
        flops=4 * 10**9,
        scratch=[pltpu.VMEM((n_req, half_heads, HD), jnp.float32)] * 3,
    )
    message, out_peer = lax.optimization_barrier((message, out_peer))
    (attended,) = local_kernel(
        combine_kernel,
        [bf16(n_req, half_heads * HD)],
        [lax.all_to_all(message, ("chip", "core"), 0, 0, axis_index_groups=sides)],
        flops=n_chips * n_req * half_heads * HD,
        scratch=[pltpu.VMEM((n_req, half_heads, HD), jnp.float32)],
    )
    attended_peer = swap(attended, "core")
    (head_own,) = local_kernel(
        out_own_kernel,
        [f32(n_req, d_here)],
        [attended, out_peer],
        anywhere=(1,),
        flops=n_req * out_weight.size,
    )
    (head_sent,) = local_kernel(
        out_peer_kernel,
        [f32(n_req, d_here)],
        [head_own, attended_peer, out_peer],
        anywhere=(2,),
        flops=n_req * out_weight.size,
    )
    head_peer = swap_diagonal(head_sent)
    (head_part,) = local_kernel(
        out_both_kernel,
        [f32(n_req, d_here)],
        [attended, attended_peer, out_weight],
        anywhere=(2,),
        flops=2 * n_req * out_weight.size,
    )

    resid_rows, scaled_mlp, squares, up_other = local_kernel(
        up_other_kernel,
        [
            f32(n_req, d_here),
            bf16(n_req, d_here),
            f32(n_req, LANES),
            f32(n_req, half_up + LANES),
        ],
        [x_rows, head_part, head_peer, gain, up_weight],
        flops=n_req * up_weight.size,
        anywhere=(4,),
    )
    (up_mine,) = local_kernel(
        up_mine_kernel,
        [f32(n_req, half_up + LANES)],
        [scaled_mlp, squares, up_weight],
        flops=n_req * up_weight.size,
        anywhere=(2,),
    )
    width_a = half_up // (2 * LANES) * LANES
    widths = [width_a, half_up + LANES - width_a]
    sums = [[f32(n_req, width), bf16(n_req, width)] for width in widths]
    pair = local_kernel(
        up_pair_kernel,
        sums[0] + sums[1],
        [up_mine, swap(up_other, "core")],
        flops=up_mine.size,
    )
    parts = [pair[:2], pair[2:]]
    orders = [(2, 1, 0), (1, 0, 2)]
    arrived = [swap_chips(part[1], order[0]) for part, order in zip(parts, orders)]
    for step in range(1, chip_bits()):
        add_b = functools.partial(up_add_b_kernel, 3 * 2 ** (step - 1))
        for i, kernel in enumerate((up_add_a_kernel, add_b)):
            parts[i] = local_kernel(
                kernel, sums[i], [parts[i][0], arrived[i]], flops=n_req * widths[i]
            )
            arrived[i] = swap_chips(parts[i][1], orders[i][step])
    (active_half,) = local_kernel(
        activate_kernel,
        [bf16(n_req, half_up)],
        [parts[0][0], arrived[0], parts[1][0], arrived[1]],
        flops=4 * up_mine.size,
    )
    active_other = swap(active_half, "core")
    (down_own,) = local_kernel(
        down_own_kernel,
        [f32(n_req, d_here)],
        [active_half, down_weight],
        flops=n_req * down_weight.size,
        anywhere=(1,),
    )
    (down_part,) = local_kernel(
        down_peer_kernel,
        [f32(n_req, d_here)],
        [down_own, active_other, down_weight],
        flops=n_req * down_weight.size,
        anywhere=(2,),
    )
    mlp_out = sum_tp(down_part)
    return (resid_rows + mlp_out).astype(jnp.bfloat16)


def solution(mesh):
    n_seq, n_tp = mesh.shape["seq"], mesh.shape["tp"]
    split = Mesh(mesh.devices.reshape(n_seq // 2, 2, n_tp), ("chip", "core", "tp"))
    seq = ("chip", "core")
    chips = n_seq // 2
    whole_tiles = chips == 8 and n_tp == 2
    return jax.shard_map(
        per_device if whole_tiles else per_device_plain,
        mesh=split,
        in_specs=(
            P(None, seq),
            P(seq),
            P(seq),
            P(seq, "tp"),
            P(seq, "tp"),
            P(seq, "tp"),
            P("tp", seq),
            P(seq, "tp"),
            P("tp", seq),
            P(None, seq, "tp"),
            P(None, seq, "tp"),
            P(),
            P(),
            P(None, seq),
        ),
        out_specs=P(None, seq),
        check_vma=False,
    )
```

```python
import math

import jax
import jax.numpy as jnp
from jax import lax
from jax.experimental import pallas as pl
from jax.experimental.pallas import tpu as pltpu
from jax.sharding import Mesh, PartitionSpec as P

D = 4096
H = 32
KVH = 8
HD = 128


NORM_EPS = 1e-05
MASKED = -1e30
LANES = 128


def squared_relu(values_in):
    positive = jnp.maximum(values_in, 0.0)
    return positive * positive


def swap(values_in, axis):
    n = lax.axis_size(axis)
    return lax.ppermute(values_in, axis, [(i, i ^ 1) for i in range(n)])


def swap_diagonal(values_in):
    return lax.ppermute(values_in, ("core", "tp"), [(i, 3 - i) for i in range(4)])


def swap_chips(values_in, bit):
    n = 2 * lax.axis_size("chip")
    return lax.ppermute(
        values_in, ("chip", "core"), [(i, i ^ (2 << bit) ^ 1) for i in range(n)]
    )


def gather_all(values_in, axes, n):
    copies = jnp.broadcast_to(values_in[None], (n,) + values_in.shape)
    return lax.all_to_all(copies, axes, 0, 0)


def sum_tp(values_in):
    n = lax.axis_size("tp")
    if n == 2:
        return values_in + swap(values_in, "tp")
    return lax.psum(values_in, "tp")


def per_device_plain(
    hidden_in,
    attn_gain,
    mlp_gain,
    query_weight,
    key_weight,
    value_weight,
    out_weight,
    up_weight,
    down_weight,
    key_cache,
    value_cache,
    lengths,
    block_order,
    pad_mask,
):
    n_req = hidden_in.shape[0]
    q_per_kv = H // KVH
    kv_here = key_cache.shape[2] // HD
    span_here = key_cache.shape[1]
    heads_here = kv_here * q_per_kv
    n_chips = lax.axis_size("chip")
    core = lax.axis_index("core")
    n_blocks = 2 * n_chips
    my_block = 2 * lax.axis_index("chip") + core
    score_scale = 1.0 / math.sqrt(HD)

    x_rows = hidden_in.astype(jnp.float32)
    scaled_in = (x_rows * attn_gain).astype(jnp.bfloat16)
    sq_attn = jnp.sum(x_rows * x_rows, axis=1, keepdims=True)
    proj_query = jnp.dot(scaled_in, query_weight, preferred_element_type=jnp.float32)
    proj_key = jnp.dot(scaled_in, key_weight, preferred_element_type=jnp.float32)
    proj_value = jnp.dot(scaled_in, value_weight, preferred_element_type=jnp.float32)
    half_q, half_kv = proj_query.shape[1] // 2, proj_key.shape[1] // 2
    square_cols = jnp.broadcast_to(sq_attn, (n_req, LANES))

    def half(i):
        return jnp.concatenate(
            [
                proj_query[:, i * half_q : (i + 1) * half_q],
                proj_key[:, i * half_kv : (i + 1) * half_kv],
                proj_value[:, i * half_kv : (i + 1) * half_kv],
                square_cols,
            ],
            axis=1,
        )

    low, high = half(0), half(1)
    mine = jnp.where(core == 0, low, high)
    other = jnp.where(core == 0, high, low)
    pair_sum = mine + swap(other, "core")
    qkv_sum = jnp.sum(gather_all(pair_sum, "chip", n_chips), axis=0)
    inv_attn = lax.rsqrt(qkv_sum[:, -1:] / D + NORM_EPS)
    qkv_half = (qkv_sum[:, :-LANES] * inv_attn).astype(jnp.bfloat16)
    qkv_other = swap(qkv_half, "core")
    qkv_low = jnp.where(core == 0, qkv_half, qkv_other)
    qkv_high = jnp.where(core == 0, qkv_other, qkv_half)

    def both(start, size):
        return jnp.concatenate(
            [qkv_low[:, start : start + size], qkv_high[:, start : start + size]], axis=1
        )

    query_rows = both(0, half_q)
    key_new = both(half_q, half_kv)
    value_new = both(half_q + half_kv, half_kv)

    first_block = block_order % n_blocks
    position = ((my_block - first_block) % n_blocks)[:, None] * span_here + jnp.arange(
        span_here, dtype=jnp.int32
    )[None, :]
    live_slots = ((position < lengths[:, None]) & (pad_mask == 1))[:, None, None, :]
    q_groups = query_rows.reshape(n_req, kv_here, q_per_kv, HD)
    keys_here = key_cache.reshape(n_req, span_here, kv_here, HD)
    values_here = value_cache.reshape(n_req, span_here, kv_here, HD)
    scores = (
        jnp.einsum("rkgd,rtkd->rkgt", q_groups, keys_here, preferred_element_type=jnp.float32)
        * score_scale
    )
    scores = jnp.where(live_slots, scores, MASKED)
    local_top = jnp.max(scores, axis=3, keepdims=True)
    weights = jnp.where(live_slots, jnp.exp(scores - local_top), 0.0)
    local_total = jnp.sum(weights, axis=3, keepdims=True)
    local_out = jnp.einsum(
        "rkgt,rtkd->rkgd",
        weights.astype(jnp.bfloat16),
        values_here,
        preferred_element_type=jnp.float32,
    )
    numer = local_out.reshape(n_req, heads_here, HD)
    stats = jnp.concatenate(
        [
            local_total.reshape(n_req, heads_here, 1),
            local_top.reshape(n_req, heads_here, 1),
        ],
        axis=2,
    )
    stat_rows = stats.reshape(n_req, heads_here * 2)
    pad = (-stat_rows.shape[1]) % LANES
    message = jnp.concatenate(
        [numer.reshape(n_req, heads_here * HD), jnp.pad(stat_rows, ((0, 0), (0, pad)))], axis=1
    )
    arrived = gather_all(message, ("chip", "core"), n_blocks)
    outs = arrived[:, :, : heads_here * HD].reshape(n_blocks, n_req, heads_here, HD)
    stats_all = arrived[:, :, heads_here * HD : heads_here * (HD + 2)].reshape(
        n_blocks, n_req, heads_here, 2
    )
    totals, tops = stats_all[..., 0], stats_all[..., 1]
    self_score = (
        jnp.einsum(
            "rkgd,rkd->rkg",
            q_groups,
            key_new.reshape(n_req, kv_here, HD),
            preferred_element_type=jnp.float32,
        )
        * score_scale
    ).reshape(n_req, heads_here)
    final_top = jnp.maximum(jnp.max(tops, axis=0), self_score)
    fades = jnp.exp(tops - final_top)
    self_weight = jnp.exp(self_score - final_top)
    denominator = jnp.sum(totals * fades, axis=0) + self_weight
    value_self = jnp.broadcast_to(
        value_new.reshape(n_req, kv_here, 1, HD), (n_req, kv_here, q_per_kv, HD)
    ).reshape(n_req, heads_here, HD)
    numerator = jnp.sum(outs * fades[..., None], axis=0) + self_weight[
        ..., None
    ] * value_self.astype(jnp.float32)
    attended = (
        (numerator / denominator[..., None])
        .reshape(n_req, heads_here * HD)
        .astype(jnp.bfloat16)
    )
    head_part = jnp.dot(attended, out_weight, preferred_element_type=jnp.float32)
    attn_out = sum_tp(head_part)
    hidden_state = (x_rows + attn_out).astype(jnp.bfloat16)

    resid_rows = hidden_state.astype(jnp.float32)
    scaled_mlp = (resid_rows * mlp_gain).astype(jnp.bfloat16)
    sq_mlp = jnp.sum(resid_rows * resid_rows, axis=1, keepdims=True)
    up_part = jnp.dot(scaled_mlp, up_weight, preferred_element_type=jnp.float32)
    half_up = up_part.shape[1] // 2
    up_low, up_high = up_part[:, :half_up], up_part[:, half_up:]
    square_cols = jnp.broadcast_to(sq_mlp, (n_req, LANES))
    up_mine = jnp.concatenate([jnp.where(core == 0, up_low, up_high), square_cols], axis=1)
    up_other = jnp.concatenate([jnp.where(core == 0, up_high, up_low), square_cols], axis=1)
    up_pair = up_mine + swap(up_other, "core")
    square_sum = up_pair[:, half_up : half_up + 1]
    piece_0 = lax.reduce_precision(square_sum, 8, 7)
    piece_1 = lax.reduce_precision(square_sum - piece_0, 8, 7)
    piece_2 = square_sum - piece_0 - piece_1
    pieces = jnp.pad(
        jnp.concatenate([piece_0, piece_1, piece_2], axis=1), ((0, 0), (0, LANES - 3))
    )
    up_message = jnp.concatenate([up_pair[:, :half_up], pieces], axis=1).astype(jnp.bfloat16)
    up_sum = jnp.sum(gather_all(up_message, "chip", n_chips).astype(jnp.float32), axis=0)
    squares = jnp.sum(up_sum[:, half_up:], axis=1, keepdims=True)
    inv_mlp = lax.rsqrt(squares / D + NORM_EPS)
    active_half = squared_relu(up_sum[:, :half_up] * inv_mlp).astype(jnp.bfloat16)
    active_other = swap(active_half, "core")
    activated = jnp.concatenate(
        [
            jnp.where(core == 0, active_half, active_other),
            jnp.where(core == 0, active_other, active_half),
        ],
        axis=1,
    )
    down_part = jnp.dot(activated, down_weight, preferred_element_type=jnp.float32)
    mlp_out = sum_tp(down_part)
    return (resid_rows + mlp_out).astype(jnp.bfloat16)


IN_VMEM = pl.BlockSpec(memory_space=pltpu.VMEM)


def chip_turn(chip):
    return chip // 2 % 2


def head_half():
    return (lax.axis_index("core") + chip_turn(lax.axis_index("chip"))) % 2


def up_half():
    turns, chip = lax.axis_index("core"), lax.axis_index("chip")
    for bit in range(chip_bits()):
        turns = turns + chip // 2**bit % 2
    return turns % 2


def chip_bits():
    return lax.axis_size("chip").bit_length() - 1


def local_kernel(kernel, outs, operands, flops, scratch=(), in_hbm=(), anywhere=()):
    in_specs, placed, moved = [], [], 0
    for i, x in enumerate(operands):
        space = pltpu.HBM if i in in_hbm else pltpu.VMEM
        in_specs.append(pl.BlockSpec(memory_space=space))
        placed.append(x if i in anywhere else pltpu.with_memory_space_constraint(x, space))
        moved += x.size * x.dtype.itemsize
    return pl.pallas_call(
        kernel,
        out_shape=outs,
        in_specs=in_specs,
        out_specs=[IN_VMEM] * len(outs),
        scratch_shapes=scratch,
        compiler_params=pltpu.CompilerParams(vmem_limit_bytes=6 * 2**20),
        cost_estimate=pl.CostEstimate(flops=flops, bytes_accessed=moved, transcendentals=0),
    )(*placed)


def f32(*shape):
    return pltpu.VMEM(shape, jnp.float32)


def bf16(*shape):
    return pltpu.VMEM(shape, jnp.bfloat16)


def pieces_of(values_in):
    first = values_in.astype(jnp.bfloat16).astype(jnp.float32)
    second = (values_in - first).astype(jnp.bfloat16).astype(jnp.float32)
    return first, second, values_in - first - second


def prepare_kernel(
    x_hbm, gain_hbm, mlp_gain_hbm, mask_hbm, lengths_hbm, order_hbm, key_hbm, value_hbm,
    scaled_ref, squares_ref, live_ref, x_ref, mlp_gain_ref, cache_ref,
    gain_ref, mask_ref, lengths_ref, order_ref, sems,
):
    core = lax.axis_index("core")
    n_blocks = lax.axis_size("chip") * 2
    my_block = 2 * lax.axis_index("chip") + core
    half = cache_ref.shape[3]
    heads = pl.ds(pl.multiple_of((1 - head_half()) * half, LANES), half)
    pairs = [
        (x_hbm, x_ref), (gain_hbm, gain_ref), (mask_hbm, mask_ref), (lengths_hbm, lengths_ref),
        (order_hbm, order_ref), (mlp_gain_hbm, mlp_gain_ref),
        (key_hbm.at[:, :, heads], cache_ref.at[0]), (value_hbm.at[:, :, heads], cache_ref.at[1]),
    ]
    copies = [pltpu.make_async_copy(src, dst, sems.at[i]) for i, (src, dst) in enumerate(pairs)]
    for copy in copies:
        copy.start()
    for copy in copies[:-2]:
        copy.wait()
    n_req, span = live_ref.shape
    slot = lax.broadcasted_iota(jnp.int32, (1, span), 1)
    for r in range(n_req):
        first_block = lax.rem(order_ref[r], n_blocks)
        begin = lax.rem(my_block - first_block + n_blocks, n_blocks) * span
        live = (begin + slot < lengths_ref[r]) & (mask_ref[r : r + 1, :] == 1)
        live_ref[r : r + 1, :] = live.astype(jnp.float32)
    x_rows = x_ref[...].astype(jnp.float32)
    scaled_ref[...] = (x_rows * gain_ref[...]).astype(jnp.bfloat16)
    squares = jnp.sum(x_rows * x_rows, axis=1, keepdims=True)
    squares_ref[...] = jnp.broadcast_to(squares, squares_ref.shape)
    for copy in copies[-2:]:
        copy.wait()


def qkv_columns(scaled_ref, w_refs, side, out_ref):
    at = 0
    for w_ref in w_refs:
        half = w_ref.shape[1] // 2
        mine = pl.ds(pl.multiple_of(side * half, LANES), half)
        out_ref[:, at : at + half] = jnp.dot(
            scaled_ref[...], w_ref[:, mine], preferred_element_type=jnp.float32
        )
        at += half
    return at


def qkv_other_kernel(scaled_ref, squares_ref, live_ref, wq_ref, wk_ref, wv_ref, other_ref):
    other = 1 - head_half()
    at = qkv_columns(scaled_ref, (wq_ref, wk_ref, wv_ref), other, other_ref)
    other_ref[:, at : at + LANES] = squares_ref[...]
    other_ref[:, at + LANES :] = live_ref[...]


def qkv_mine_kernel(scaled_ref, squares_ref, wq_ref, wk_ref, wv_ref, mine_ref):
    at = qkv_columns(scaled_ref, (wq_ref, wk_ref, wv_ref), head_half(), mine_ref)
    mine_ref[:, at:] = squares_ref[...]


SCALE_UNIT = 1024.0


def qkv_message_kernel(mine_ref, arrived_ref, out_ref):
    width = mine_ref.shape[1] - LANES
    features = D / lax.axis_size("chip")
    total = mine_ref[...] + arrived_ref[:, : width + LANES]
    squares = total[:, width:]
    scale = jnp.sqrt(jnp.maximum(squares * (1.0 / features), 2.0**-40))
    scale = scale.astype(jnp.bfloat16).astype(jnp.float32)
    inverse = 1.0 / scale
    out_ref[:, :width] = total[:, :width] * inverse[:, :1]
    lane = lax.broadcasted_iota(jnp.int32, squares.shape, 1)
    tile = jnp.where(lane == 0, scale * SCALE_UNIT, 0.0)
    for p, piece in enumerate(pieces_of(squares * inverse * inverse * (1.0 / features))):
        tile = jnp.where(lane == 1 + p, piece, tile)
    out_ref[:, width:] = tile


def qkv_sum(arrived_ref):
    n_chips, _, width = arrived_ref.shape
    width -= LANES
    features = D / n_chips
    total, squares = 0.0, 0.0
    for i in range(n_chips):
        tile = arrived_ref[i, :, width:]
        scale = tile[:, :1] * (1.0 / SCALE_UNIT)
        total = total + arrived_ref[i, :, :width] * scale
        mean = tile[:, 1:2] + tile[:, 2:3] + tile[:, 3:4]
        squares = squares + mean * scale * scale * features
    inv_attn = lax.rsqrt(squares / D + NORM_EPS)
    return (total * inv_attn).astype(jnp.bfloat16).astype(jnp.float32)


PIECE = 16
TOP_AT = 3 * PIECE


def attention_kernel(
    arrived_ref, key_own, value_own, cache_peer, live_own, live_peer,
    message_ref, query_ref, key_new_ref, value_new_ref,
):
    n_copies, heads, _ = message_ref.shape
    n_req, span = live_own.shape
    half = key_own.shape[2] // 2
    mine = pl.ds(pl.multiple_of(head_half() * half, LANES), half)
    kv_half = half // HD
    group = heads // kv_half
    is_first = lax.axis_index("chip") == 0
    qkv = qkv_sum(arrived_ref)
    for h in range(heads):
        query_ref[:, h, :] = qkv[:, h * HD : (h + 1) * HD]
        at = (heads + h // group) * HD
        key_new_ref[:, h, :] = qkv[:, at : at + HD]
        at += kv_half * HD
        value_new_ref[:, h, :] = qkv[:, at : at + HD]

    rows = n_req * heads
    query = query_ref[...].reshape(rows, HD)
    group_of = lax.broadcasted_iota(jnp.int32, (rows, HD), 0) % heads // group
    spread = jnp.concatenate(
        [jnp.where(group_of == k, query, 0.0) for k in range(kv_half)], axis=1
    ).astype(jnp.bfloat16)
    scores, live = [], []
    for r in range(n_req):
        blocks = []
        for keys in (key_own[r, :, mine], cache_peer[0, r]):
            blocks.append(
                lax.dot_general(
                    spread[r * heads : (r + 1) * heads, :], keys,
                    (((1,), (1,)), ((), ())), preferred_element_type=jnp.float32,
                )
            )
        scores.append(jnp.concatenate(blocks, axis=1))
        live_row = jnp.concatenate([live_own[r : r + 1, :], live_peer[r : r + 1, :]], axis=1)
        live.append(jnp.broadcast_to(live_row, (heads, 2 * span)))
    live = jnp.concatenate(live, axis=0) > 0.0
    scale = 1.0 / math.sqrt(HD)
    scores = jnp.where(live, jnp.concatenate(scores, axis=0) * scale, MASKED)
    key_new = key_new_ref[...].reshape(rows, HD)
    self_score = jnp.sum(query * key_new, axis=1, keepdims=True) * scale
    self_score = jnp.where(is_first, self_score, MASKED)
    top = jnp.maximum(jnp.max(scores, axis=1, keepdims=True), self_score)
    weights = jnp.where(live, jnp.exp(scores - top), 0.0)
    self_weight = jnp.where(is_first, jnp.exp(self_score - top), 0.0)
    total = jnp.sum(weights, axis=1, keepdims=True) + self_weight
    rounded = weights.astype(jnp.bfloat16)
    self_part = self_weight * value_new_ref[...].reshape(rows, HD)
    pieces = pieces_of(total) + pieces_of(top)
    lane = lax.broadcasted_iota(jnp.int32, (heads, LANES), 1)
    stats = jnp.zeros((heads, LANES), jnp.float32)
    parts = []
    for r in range(n_req):
        at = slice(r * heads, (r + 1) * heads)
        wide = jnp.dot(
            rounded[at, :span], value_own[r, :, mine], preferred_element_type=jnp.float32
        ) + jnp.dot(
            rounded[at, span:], cache_peer[1, r], preferred_element_type=jnp.float32
        )
        numer = self_part[at, :]
        for k in range(kv_half):
            numer = numer + jnp.where(group_of[at, :] == k, wide[:, k * HD : (k + 1) * HD], 0.0)
        parts.append(numer)
        for p, piece in enumerate(pieces):
            stats = jnp.where(lane == p * PIECE + r, piece[at, :], stats)
    message = jnp.concatenate(parts + [stats], axis=1).astype(jnp.bfloat16)
    for i in range(n_copies):
        message_ref[i] = message


def combine_kernel(arrived_ref, rows_ref, attended_ref):
    n_chips, heads, width = arrived_ref.shape
    n_req = rows_ref.shape[0]
    totals, tops = [], []
    for chip in range(n_chips):
        tile = arrived_ref[chip, :, width - LANES :].astype(jnp.float32)
        tile = (
            tile
            + pltpu.roll(tile, LANES - PIECE, 1)
            + pltpu.roll(tile, LANES - 2 * PIECE, 1)
        )
        totals.append(tile)
        tops.append(pltpu.roll(tile, LANES - TOP_AT, 1))
    final_top = tops[0]
    for top in tops[1:]:
        final_top = jnp.maximum(final_top, top)
    fades = [jnp.exp(top - final_top) for top in tops]
    denominator = totals[0] * fades[0]
    for total, fade in zip(totals[1:], fades[1:]):
        denominator = denominator + total * fade
    for r in range(n_req):
        numer = jnp.zeros((heads, HD), jnp.float32)
        for chip, fade in enumerate(fades):
            part = arrived_ref[chip, :, r * HD : (r + 1) * HD].astype(jnp.float32)
            numer = numer + part * fade[:, r : r + 1]
        attended_ref[r] = numer / denominator[:, r : r + 1]
    rows = jnp.concatenate([attended_ref[:, h, :] for h in range(heads)], axis=1)
    rows_ref[...] = rows.astype(jnp.bfloat16)


def half_rows(rows_ref, w_ref, side):
    half = rows_ref.shape[1]
    rows = pl.ds(pl.multiple_of(side * half, LANES), half)
    return jnp.dot(rows_ref[...], w_ref[rows, :], preferred_element_type=jnp.float32)


def out_own_kernel(own_ref, w_ref, out_ref):
    out_ref[...] = half_rows(own_ref, w_ref, head_half())


def out_peer_kernel(own_part, peer_ref, w_ref, out_ref):
    out_ref[...] = own_part[...] + half_rows(peer_ref, w_ref, 1 - head_half())


def out_both_kernel(own_ref, peer_ref, w_ref, out_ref):
    side = head_half()
    out_ref[...] = half_rows(own_ref, w_ref, side) + half_rows(peer_ref, w_ref, 1 - side)


def up_columns(scaled_mlp, w_ref, side, out_ref):
    half = out_ref.shape[1] - LANES
    mine = pl.ds(pl.multiple_of(side * half, LANES), half)
    out_ref[:, :half] = jnp.dot(scaled_mlp, w_ref[:, mine], preferred_element_type=jnp.float32)


def up_other_kernel(
    x_ref, part_ref, peer_ref, gain_ref, w_ref, hidden_ref, scaled_ref, squares_ref, other_ref
):
    attn_out = part_ref[...] + peer_ref[...]
    hidden_state = (x_ref[...].astype(jnp.float32) + attn_out).astype(jnp.bfloat16)
    resid_rows = hidden_state.astype(jnp.float32)
    hidden_ref[...] = resid_rows
    scaled_mlp = (resid_rows * gain_ref[...]).astype(jnp.bfloat16)
    scaled_ref[...] = scaled_mlp
    squares = jnp.sum(resid_rows * resid_rows, axis=1, keepdims=True)
    squares_ref[...] = jnp.broadcast_to(squares, squares_ref.shape)
    other_ref[:, other_ref.shape[1] - LANES :] = squares_ref[...]
    up_columns(scaled_mlp, w_ref, 1 - up_half(), other_ref)


def up_mine_kernel(scaled_ref, squares_ref, w_ref, mine_ref):
    mine_ref[:, mine_ref.shape[1] - LANES :] = squares_ref[...]
    up_columns(scaled_ref[...], w_ref, up_half(), mine_ref)


def up_pair_kernel(mine_ref, arrived_ref, total_a, sent_a, total_b, sent_b):
    half = mine_ref.shape[1] - LANES
    start = total_a.shape[1]
    total = mine_ref[:, :half] + arrived_ref[:, :half]
    squares = mine_ref[:, half:] + arrived_ref[:, half:]
    lane = lax.broadcasted_iota(jnp.int32, squares.shape, 1)
    tile = jnp.zeros_like(squares)
    first = 3 * lax.axis_index("chip")
    for p, piece in enumerate(pieces_of(squares)):
        tile = jnp.where(lane == first + p, piece, tile)
    total_a[...] = total[:, :start]
    sent_a[...] = total[:, :start].astype(jnp.bfloat16)
    put_b(total[:, start:], tile, total_b, sent_b)


def put_b(total, tile, total_ref, sent_ref):
    width = total.shape[1]
    for at, value in ((slice(0, width), total), (slice(width, None), tile)):
        total_ref[:, at] = value
        sent_ref[:, at] = value.astype(jnp.bfloat16)


def up_add_kernel(part_ref, arrived_ref, total_ref, sent_ref):
    total = part_ref[...] + arrived_ref[...].astype(jnp.float32)
    total_ref[...] = total
    sent_ref[...] = total.astype(jnp.bfloat16)


def activate_kernel(part_a, arrived_a, part_b, arrived_b, out_ref):
    start, width = part_a.shape[1], part_b.shape[1] - LANES
    pieces = part_b[:, width:] + arrived_b[:, width:].astype(jnp.float32)
    squares = jnp.sum(pieces, axis=1, keepdims=True)
    inv_mlp = lax.rsqrt(squares / D + NORM_EPS)
    total_a = part_a[...] + arrived_a[...].astype(jnp.float32)
    out_ref[:, :start] = squared_relu(total_a * inv_mlp).astype(jnp.bfloat16)
    total_b = part_b[:, :width] + arrived_b[:, :width].astype(jnp.float32)
    out_ref[:, start:] = squared_relu(total_b * inv_mlp).astype(jnp.bfloat16)


def down_own_kernel(own_ref, w_ref, out_ref):
    out_ref[...] = half_rows(own_ref, w_ref, up_half())


def down_peer_kernel(own_part, peer_ref, w_ref, out_ref):
    out_ref[...] = own_part[...] + half_rows(peer_ref, w_ref, 1 - up_half())


def per_device(
    hidden_in,
    attn_gain,
    mlp_gain,
    query_weight,
    key_weight,
    value_weight,
    out_weight,
    up_weight,
    down_weight,
    key_cache,
    value_cache,
    lengths,
    block_order,
    pad_mask,
):
    n_req, d_here = hidden_in.shape
    kv_here = key_cache.shape[2] // HD
    heads_here = kv_here * (H // KVH)
    n_chips = lax.axis_size("chip")
    core = lax.axis_index("core")
    n_blocks = 2 * n_chips
    half_qkv = (heads_here + 2 * kv_here) * HD // 2
    half_up = up_weight.shape[1] // 2

    row = (1, d_here)
    small = [hidden_in, attn_gain.reshape(row), mlp_gain.reshape(row), pad_mask]
    small += [lengths, block_order, key_cache, value_cache]
    scaled_in, squares, live, x_rows, gain, cache_sent = local_kernel(
        prepare_kernel,
        [
            bf16(*hidden_in.shape),
            f32(n_req, LANES),
            f32(*pad_mask.shape),
            bf16(*hidden_in.shape),
            f32(*row),
            bf16(2, *key_cache.shape[:2], key_cache.shape[2] // 2),
        ],
        small,
        flops=4 * 10**9,
        scratch=[
            pltpu.VMEM(row, jnp.float32),
            pltpu.VMEM(pad_mask.shape, jnp.int32),
            pltpu.SMEM(lengths.shape, jnp.int32),
            pltpu.SMEM(block_order.shape, jnp.int32),
            pltpu.SemaphoreType.DMA((len(small),)),
        ],
        in_hbm=range(len(small)),
    )
    (other,) = local_kernel(
        qkv_other_kernel,
        [f32(n_req, half_qkv + LANES + pad_mask.shape[1])],
        [scaled_in, squares, live, query_weight, key_weight, value_weight],
        flops=4 * 10**9,
        anywhere=(3, 4, 5),
    )
    (mine,) = local_kernel(
        qkv_mine_kernel,
        [f32(n_req, half_qkv + LANES)],
        [scaled_in, squares, query_weight, key_weight, value_weight],
        flops=2 * n_req * d_here * half_qkv,
        anywhere=(2, 3, 4),
    )
    arrived = swap(other, "core")
    width = mine.shape[1]
    (qkv_message,) = local_kernel(
        qkv_message_kernel, [f32(*mine.shape)], [mine, arrived], flops=2 * mine.size
    )
    qkv_message, live_peer, *moved = lax.optimization_barrier(
        (
            qkv_message.astype(jnp.float16),
            arrived[:, width:],
            cache_sent,
            out_weight,
        )
    )
    cache_peer, out_peer = (swap(x, "core") for x in moved)
    sides = [
        [2 * chip + (side + chip_turn(chip)) % 2 for chip in range(n_chips)] for side in range(2)
    ]
    qkv_all = lax.all_to_all(
        jnp.broadcast_to(qkv_message[None], (n_chips,) + qkv_message.shape),
        ("chip", "core"),
        0,
        0,
        axis_index_groups=sides,
    )
    half_heads = heads_here // 2
    (message,) = local_kernel(
        attention_kernel,
        [bf16(n_chips, half_heads, n_req * HD + LANES)],
        [qkv_all.astype(jnp.float32), key_cache, value_cache, cache_peer, live, live_peer],
        anywhere=(1, 2, 3),
        flops=4 * 10**9,
        scratch=[pltpu.VMEM((n_req, half_heads, HD), jnp.float32)] * 3,
    )
    message, out_peer = lax.optimization_barrier((message, out_peer))
    (attended,) = local_kernel(
        combine_kernel,
        [bf16(n_req, half_heads * HD)],
        [lax.all_to_all(message, ("chip", "core"), 0, 0, axis_index_groups=sides)],
        flops=n_chips * n_req * half_heads * HD,
        scratch=[pltpu.VMEM((n_req, half_heads, HD), jnp.float32)],
    )
    attended_peer = swap(attended, "core")
    (head_own,) = local_kernel(
        out_own_kernel,
        [f32(n_req, d_here)],
        [attended, out_peer],
        anywhere=(1,),
        flops=n_req * out_weight.size,
    )
    (head_sent,) = local_kernel(
        out_peer_kernel,
        [f32(n_req, d_here)],
        [head_own, attended_peer, out_peer],
        anywhere=(2,),
        flops=n_req * out_weight.size,
    )
    head_peer = swap_diagonal(head_sent)
    (head_part,) = local_kernel(
        out_both_kernel,
        [f32(n_req, d_here)],
        [attended, attended_peer, out_weight],
        anywhere=(2,),
        flops=2 * n_req * out_weight.size,
    )

    resid_rows, scaled_mlp, squares, up_other = local_kernel(
        up_other_kernel,
        [
            f32(n_req, d_here),
            bf16(n_req, d_here),
            f32(n_req, LANES),
            f32(n_req, half_up + LANES),
        ],
        [x_rows, head_part, head_peer, gain, up_weight],
        flops=n_req * up_weight.size,
        anywhere=(4,),
    )
    (up_mine,) = local_kernel(
        up_mine_kernel,
        [f32(n_req, half_up + LANES)],
        [scaled_mlp, squares, up_weight],
        flops=n_req * up_weight.size,
        anywhere=(2,),
    )
    width_a = half_up // (2 * LANES) * LANES
    widths = [width_a, half_up + LANES - width_a]
    sums = [[f32(n_req, width), bf16(n_req, width)] for width in widths]
    pair = local_kernel(
        up_pair_kernel,
        sums[0] + sums[1],
        [up_mine, swap(up_other, "core")],
        flops=up_mine.size,
    )
    parts = [pair[:2], pair[2:]]
    orders = [(2, 1, 0), (1, 0, 2)]
    arrived = [swap_chips(part[1], order[0]) for part, order in zip(parts, orders)]
    for step in range(1, chip_bits()):
        for i in range(2):
            parts[i] = local_kernel(
                up_add_kernel, sums[i], [parts[i][0], arrived[i]], flops=n_req * widths[i]
            )
            arrived[i] = swap_chips(parts[i][1], orders[i][step])
    (active_half,) = local_kernel(
        activate_kernel,
        [bf16(n_req, half_up)],
        [parts[0][0], arrived[0], parts[1][0], arrived[1]],
        flops=4 * up_mine.size,
    )
    active_other = swap(active_half, "core")
    (down_own,) = local_kernel(
        down_own_kernel,
        [f32(n_req, d_here)],
        [active_half, down_weight],
        flops=n_req * down_weight.size,
        anywhere=(1,),
    )
    (down_part,) = local_kernel(
        down_peer_kernel,
        [f32(n_req, d_here)],
        [down_own, active_other, down_weight],
        flops=n_req * down_weight.size,
        anywhere=(2,),
    )
    mlp_out = sum_tp(down_part)
    return (resid_rows + mlp_out).astype(jnp.bfloat16)


def solution(mesh):
    n_seq, n_tp = mesh.shape["seq"], mesh.shape["tp"]
    split = Mesh(mesh.devices.reshape(n_seq // 2, 2, n_tp), ("chip", "core", "tp"))
    seq = ("chip", "core")
    chips = n_seq // 2
    whole_tiles = chips == 8 and n_tp == 2
    return jax.shard_map(
        per_device if whole_tiles else per_device_plain,
        mesh=split,
        in_specs=(
            P(None, seq),
            P(seq),
            P(seq),
            P(seq, "tp"),
            P(seq, "tp"),
            P(seq, "tp"),
            P("tp", seq),
            P(seq, "tp"),
            P("tp", seq),
            P(None, seq, "tp"),
            P(None, seq, "tp"),
            P(),
            P(),
            P(None, seq),
        ),
        out_specs=P(None, seq),
        check_vma=False,
    )
```

```python
import math

import jax
import jax.numpy as jnp
from jax import lax
from jax.experimental import pallas as pl
from jax.experimental.pallas import tpu as pltpu
from jax.sharding import Mesh, PartitionSpec as P

D = 4096
H = 32
KVH = 8
HD = 128


NORM_EPS = 1e-05
MASKED = -1e30
LANES = 128


def squared_relu(values_in):
    positive = jnp.maximum(values_in, 0.0)
    return positive * positive


def swap(values_in, axis):
    n = lax.axis_size(axis)
    return lax.ppermute(values_in, axis, [(i, i ^ 1) for i in range(n)])


def swap_diagonal(values_in):
    return lax.ppermute(values_in, ("core", "tp"), [(i, 3 - i) for i in range(4)])


def swap_chips(values_in, bit):
    n = 2 * lax.axis_size("chip")
    return lax.ppermute(
        values_in, ("chip", "core"), [(i, i ^ (2 << bit) ^ 1) for i in range(n)]
    )


def gather_all(values_in, axes, n):
    copies = jnp.broadcast_to(values_in[None], (n,) + values_in.shape)
    return lax.all_to_all(copies, axes, 0, 0)


def sum_tp(values_in):
    n = lax.axis_size("tp")
    if n == 2:
        return values_in + swap(values_in, "tp")
    return lax.psum(values_in, "tp")


def per_device_plain(
    hidden_in,
    attn_gain,
    mlp_gain,
    query_weight,
    key_weight,
    value_weight,
    out_weight,
    up_weight,
    down_weight,
    key_cache,
    value_cache,
    lengths,
    block_order,
    pad_mask,
):
    n_req = hidden_in.shape[0]
    q_per_kv = H // KVH
    kv_here = key_cache.shape[2] // HD
    span_here = key_cache.shape[1]
    heads_here = kv_here * q_per_kv
    n_chips = lax.axis_size("chip")
    core = lax.axis_index("core")
    n_blocks = 2 * n_chips
    my_block = 2 * lax.axis_index("chip") + core
    score_scale = 1.0 / math.sqrt(HD)

    x_rows = hidden_in.astype(jnp.float32)
    scaled_in = (x_rows * attn_gain).astype(jnp.bfloat16)
    sq_attn = jnp.sum(x_rows * x_rows, axis=1, keepdims=True)
    proj_query = jnp.dot(scaled_in, query_weight, preferred_element_type=jnp.float32)
    proj_key = jnp.dot(scaled_in, key_weight, preferred_element_type=jnp.float32)
    proj_value = jnp.dot(scaled_in, value_weight, preferred_element_type=jnp.float32)
    half_q, half_kv = proj_query.shape[1] // 2, proj_key.shape[1] // 2
    square_cols = jnp.broadcast_to(sq_attn, (n_req, LANES))

    def half(i):
        return jnp.concatenate(
            [
                proj_query[:, i * half_q : (i + 1) * half_q],
                proj_key[:, i * half_kv : (i + 1) * half_kv],
                proj_value[:, i * half_kv : (i + 1) * half_kv],
                square_cols,
            ],
            axis=1,
        )

    low, high = half(0), half(1)
    mine = jnp.where(core == 0, low, high)
    other = jnp.where(core == 0, high, low)
    pair_sum = mine + swap(other, "core")
    qkv_sum = jnp.sum(gather_all(pair_sum, "chip", n_chips), axis=0)
    inv_attn = lax.rsqrt(qkv_sum[:, -1:] / D + NORM_EPS)
    qkv_half = (qkv_sum[:, :-LANES] * inv_attn).astype(jnp.bfloat16)
    qkv_other = swap(qkv_half, "core")
    qkv_low = jnp.where(core == 0, qkv_half, qkv_other)
    qkv_high = jnp.where(core == 0, qkv_other, qkv_half)

    def both(start, size):
        return jnp.concatenate(
            [qkv_low[:, start : start + size], qkv_high[:, start : start + size]], axis=1
        )

    query_rows = both(0, half_q)
    key_new = both(half_q, half_kv)
    value_new = both(half_q + half_kv, half_kv)

    first_block = block_order % n_blocks
    position = ((my_block - first_block) % n_blocks)[:, None] * span_here + jnp.arange(
        span_here, dtype=jnp.int32
    )[None, :]
    live_slots = ((position < lengths[:, None]) & (pad_mask == 1))[:, None, None, :]
    q_groups = query_rows.reshape(n_req, kv_here, q_per_kv, HD)
    keys_here = key_cache.reshape(n_req, span_here, kv_here, HD)
    values_here = value_cache.reshape(n_req, span_here, kv_here, HD)
    scores = (
        jnp.einsum("rkgd,rtkd->rkgt", q_groups, keys_here, preferred_element_type=jnp.float32)
        * score_scale
    )
    scores = jnp.where(live_slots, scores, MASKED)
    local_top = jnp.max(scores, axis=3, keepdims=True)
    weights = jnp.where(live_slots, jnp.exp(scores - local_top), 0.0)
    local_total = jnp.sum(weights, axis=3, keepdims=True)
    local_out = jnp.einsum(
        "rkgt,rtkd->rkgd",
        weights.astype(jnp.bfloat16),
        values_here,
        preferred_element_type=jnp.float32,
    )
    numer = local_out.reshape(n_req, heads_here, HD)
    stats = jnp.concatenate(
        [
            local_total.reshape(n_req, heads_here, 1),
            local_top.reshape(n_req, heads_here, 1),
        ],
        axis=2,
    )
    stat_rows = stats.reshape(n_req, heads_here * 2)
    pad = (-stat_rows.shape[1]) % LANES
    message = jnp.concatenate(
        [numer.reshape(n_req, heads_here * HD), jnp.pad(stat_rows, ((0, 0), (0, pad)))], axis=1
    )
    arrived = gather_all(message, ("chip", "core"), n_blocks)
    outs = arrived[:, :, : heads_here * HD].reshape(n_blocks, n_req, heads_here, HD)
    stats_all = arrived[:, :, heads_here * HD : heads_here * (HD + 2)].reshape(
        n_blocks, n_req, heads_here, 2
    )
    totals, tops = stats_all[..., 0], stats_all[..., 1]
    self_score = (
        jnp.einsum(
            "rkgd,rkd->rkg",
            q_groups,
            key_new.reshape(n_req, kv_here, HD),
            preferred_element_type=jnp.float32,
        )
        * score_scale
    ).reshape(n_req, heads_here)
    final_top = jnp.maximum(jnp.max(tops, axis=0), self_score)
    fades = jnp.exp(tops - final_top)
    self_weight = jnp.exp(self_score - final_top)
    denominator = jnp.sum(totals * fades, axis=0) + self_weight
    value_self = jnp.broadcast_to(
        value_new.reshape(n_req, kv_here, 1, HD), (n_req, kv_here, q_per_kv, HD)
    ).reshape(n_req, heads_here, HD)
    numerator = jnp.sum(outs * fades[..., None], axis=0) + self_weight[
        ..., None
    ] * value_self.astype(jnp.float32)
    attended = (
        (numerator / denominator[..., None])
        .reshape(n_req, heads_here * HD)
        .astype(jnp.bfloat16)
    )
    head_part = jnp.dot(attended, out_weight, preferred_element_type=jnp.float32)
    attn_out = sum_tp(head_part)
    hidden_state = (x_rows + attn_out).astype(jnp.bfloat16)

    resid_rows = hidden_state.astype(jnp.float32)
    scaled_mlp = (resid_rows * mlp_gain).astype(jnp.bfloat16)
    sq_mlp = jnp.sum(resid_rows * resid_rows, axis=1, keepdims=True)
    up_part = jnp.dot(scaled_mlp, up_weight, preferred_element_type=jnp.float32)
    half_up = up_part.shape[1] // 2
    up_low, up_high = up_part[:, :half_up], up_part[:, half_up:]
    square_cols = jnp.broadcast_to(sq_mlp, (n_req, LANES))
    up_mine = jnp.concatenate([jnp.where(core == 0, up_low, up_high), square_cols], axis=1)
    up_other = jnp.concatenate([jnp.where(core == 0, up_high, up_low), square_cols], axis=1)
    up_pair = up_mine + swap(up_other, "core")
    square_sum = up_pair[:, half_up : half_up + 1]
    piece_0 = lax.reduce_precision(square_sum, 8, 7)
    piece_1 = lax.reduce_precision(square_sum - piece_0, 8, 7)
    piece_2 = square_sum - piece_0 - piece_1
    pieces = jnp.pad(
        jnp.concatenate([piece_0, piece_1, piece_2], axis=1), ((0, 0), (0, LANES - 3))
    )
    up_message = jnp.concatenate([up_pair[:, :half_up], pieces], axis=1).astype(jnp.bfloat16)
    up_sum = jnp.sum(gather_all(up_message, "chip", n_chips).astype(jnp.float32), axis=0)
    squares = jnp.sum(up_sum[:, half_up:], axis=1, keepdims=True)
    inv_mlp = lax.rsqrt(squares / D + NORM_EPS)
    active_half = squared_relu(up_sum[:, :half_up] * inv_mlp).astype(jnp.bfloat16)
    active_other = swap(active_half, "core")
    activated = jnp.concatenate(
        [
            jnp.where(core == 0, active_half, active_other),
            jnp.where(core == 0, active_other, active_half),
        ],
        axis=1,
    )
    down_part = jnp.dot(activated, down_weight, preferred_element_type=jnp.float32)
    mlp_out = sum_tp(down_part)
    return (resid_rows + mlp_out).astype(jnp.bfloat16)


IN_VMEM = pl.BlockSpec(memory_space=pltpu.VMEM)


def chip_turn(chip):
    return chip // 2 % 2


def head_half():
    return (lax.axis_index("core") + chip_turn(lax.axis_index("chip"))) % 2


def up_half():
    turns, chip = lax.axis_index("core"), lax.axis_index("chip")
    for bit in range(chip_bits()):
        turns = turns + chip // 2**bit % 2
    return turns % 2


def chip_bits():
    return lax.axis_size("chip").bit_length() - 1


def local_kernel(kernel, outs, operands, flops, scratch=(), in_hbm=(), anywhere=()):
    in_specs, placed, moved = [], [], 0
    for i, x in enumerate(operands):
        space = pltpu.HBM if i in in_hbm else pltpu.VMEM
        in_specs.append(pl.BlockSpec(memory_space=space))
        placed.append(x if i in anywhere else pltpu.with_memory_space_constraint(x, space))
        moved += x.size * x.dtype.itemsize
    return pl.pallas_call(
        kernel,
        out_shape=outs,
        in_specs=in_specs,
        out_specs=[IN_VMEM] * len(outs),
        scratch_shapes=scratch,
        compiler_params=pltpu.CompilerParams(vmem_limit_bytes=6 * 2**20),
        cost_estimate=pl.CostEstimate(flops=flops, bytes_accessed=moved, transcendentals=0),
    )(*placed)


def f32(*shape):
    return pltpu.VMEM(shape, jnp.float32)


def bf16(*shape):
    return pltpu.VMEM(shape, jnp.bfloat16)


def pieces_of(values_in):
    first = values_in.astype(jnp.bfloat16).astype(jnp.float32)
    second = (values_in - first).astype(jnp.bfloat16).astype(jnp.float32)
    return first, second, values_in - first - second


def prepare_kernel(
    x_hbm, gain_hbm, mlp_gain_hbm, mask_hbm, lengths_hbm, order_hbm, key_hbm, value_hbm,
    scaled_ref, squares_ref, live_ref, x_ref, mlp_gain_ref, cache_ref,
    gain_ref, mask_ref, lengths_ref, order_ref, sems,
):
    core = lax.axis_index("core")
    n_blocks = lax.axis_size("chip") * 2
    my_block = 2 * lax.axis_index("chip") + core
    half = cache_ref.shape[3]
    heads = pl.ds(pl.multiple_of((1 - head_half()) * half, LANES), half)
    pairs = [
        (x_hbm, x_ref), (gain_hbm, gain_ref), (mask_hbm, mask_ref), (lengths_hbm, lengths_ref),
        (order_hbm, order_ref), (mlp_gain_hbm, mlp_gain_ref),
        (key_hbm.at[:, :, heads], cache_ref.at[0]), (value_hbm.at[:, :, heads], cache_ref.at[1]),
    ]
    copies = [pltpu.make_async_copy(src, dst, sems.at[i]) for i, (src, dst) in enumerate(pairs)]
    for copy in copies:
        copy.start()
    for copy in copies[:-2]:
        copy.wait()
    n_req, span = live_ref.shape
    slot = lax.broadcasted_iota(jnp.int32, (1, span), 1)
    for r in range(n_req):
        first_block = lax.rem(order_ref[r], n_blocks)
        begin = lax.rem(my_block - first_block + n_blocks, n_blocks) * span
        live = (begin + slot < lengths_ref[r]) & (mask_ref[r : r + 1, :] == 1)
        live_ref[r : r + 1, :] = live.astype(jnp.float32)
    x_rows = x_ref[...].astype(jnp.float32)
    scaled_ref[...] = (x_rows * gain_ref[...]).astype(jnp.bfloat16)
    squares = jnp.sum(x_rows * x_rows, axis=1, keepdims=True)
    squares_ref[...] = jnp.broadcast_to(squares, squares_ref.shape)
    for copy in copies[-2:]:
        copy.wait()


def qkv_columns(scaled_ref, w_refs, side, out_ref):
    at = 0
    for w_ref in w_refs:
        half = w_ref.shape[1] // 2
        mine = pl.ds(pl.multiple_of(side * half, LANES), half)
        out_ref[:, at : at + half] = jnp.dot(
            scaled_ref[...], w_ref[:, mine], preferred_element_type=jnp.float32
        )
        at += half
    return at


def qkv_other_kernel(scaled_ref, squares_ref, live_ref, wq_ref, wk_ref, wv_ref, other_ref):
    other = 1 - head_half()
    at = qkv_columns(scaled_ref, (wq_ref, wk_ref, wv_ref), other, other_ref)
    other_ref[:, at : at + LANES] = squares_ref[...]
    other_ref[:, at + LANES :] = live_ref[...]


def qkv_mine_kernel(scaled_ref, squares_ref, wq_ref, wk_ref, wv_ref, mine_ref):
    at = qkv_columns(scaled_ref, (wq_ref, wk_ref, wv_ref), head_half(), mine_ref)
    mine_ref[:, at:] = squares_ref[...]


SCALE_UNIT = 1024.0


def qkv_message_kernel(mine_ref, arrived_ref, out_ref):
    width = mine_ref.shape[1] - LANES
    features = D / lax.axis_size("chip")
    total = mine_ref[...] + arrived_ref[:, : width + LANES]
    squares = total[:, width:]
    scale = jnp.sqrt(jnp.maximum(squares * (1.0 / features), 2.0**-40))
    scale = scale.astype(jnp.bfloat16).astype(jnp.float32)
    inverse = 1.0 / scale
    out_ref[:, :width] = total[:, :width] * inverse[:, :1]
    lane = lax.broadcasted_iota(jnp.int32, squares.shape, 1)
    tile = jnp.where(lane == 0, scale * SCALE_UNIT, 0.0)
    for p, piece in enumerate(pieces_of(squares * inverse * inverse * (1.0 / features))):
        tile = jnp.where(lane == 1 + p, piece, tile)
    out_ref[:, width:] = tile


def qkv_sum(arrived_ref):
    n_chips, _, width = arrived_ref.shape
    width -= LANES
    features = D / n_chips
    total, squares = 0.0, 0.0
    for i in range(n_chips):
        tile = arrived_ref[i, :, width:]
        scale = tile[:, :1] * (1.0 / SCALE_UNIT)
        total = total + arrived_ref[i, :, :width] * scale
        mean = tile[:, 1:2] + tile[:, 2:3] + tile[:, 3:4]
        squares = squares + mean * scale * scale * features
    inv_attn = lax.rsqrt(squares / D + NORM_EPS)
    return (total * inv_attn).astype(jnp.bfloat16).astype(jnp.float32)


PIECE = 16
TOP_AT = 3 * PIECE


def attention_kernel(
    arrived_ref, key_own, value_own, cache_peer, live_own, live_peer,
    message_ref, query_ref, key_new_ref, value_new_ref,
):
    n_copies, heads, _ = message_ref.shape
    n_req, span = live_own.shape
    half = key_own.shape[2] // 2
    mine = pl.ds(pl.multiple_of(head_half() * half, LANES), half)
    kv_half = half // HD
    group = heads // kv_half
    is_first = lax.axis_index("chip") == 0
    qkv = qkv_sum(arrived_ref)
    for h in range(heads):
        query_ref[:, h, :] = qkv[:, h * HD : (h + 1) * HD]
        at = (heads + h // group) * HD
        key_new_ref[:, h, :] = qkv[:, at : at + HD]
        at += kv_half * HD
        value_new_ref[:, h, :] = qkv[:, at : at + HD]

    rows = n_req * heads
    query = query_ref[...].reshape(rows, HD)
    group_of = lax.broadcasted_iota(jnp.int32, (rows, HD), 0) % heads // group
    spread = jnp.concatenate(
        [jnp.where(group_of == k, query, 0.0) for k in range(kv_half)], axis=1
    ).astype(jnp.bfloat16)
    scores, live = [], []
    for r in range(n_req):
        blocks = []
        for keys in (key_own[r, :, mine], cache_peer[0, r]):
            blocks.append(
                lax.dot_general(
                    spread[r * heads : (r + 1) * heads, :], keys,
                    (((1,), (1,)), ((), ())), preferred_element_type=jnp.float32,
                )
            )
        scores.append(jnp.concatenate(blocks, axis=1))
        live_row = jnp.concatenate([live_own[r : r + 1, :], live_peer[r : r + 1, :]], axis=1)
        live.append(jnp.broadcast_to(live_row, (heads, 2 * span)))
    live = jnp.concatenate(live, axis=0) > 0.0
    scale = 1.0 / math.sqrt(HD)
    scores = jnp.where(live, jnp.concatenate(scores, axis=0) * scale, MASKED)
    key_new = key_new_ref[...].reshape(rows, HD)
    self_score = jnp.sum(query * key_new, axis=1, keepdims=True) * scale
    self_score = jnp.where(is_first, self_score, MASKED)
    top = jnp.maximum(jnp.max(scores, axis=1, keepdims=True), self_score)
    weights = jnp.where(live, jnp.exp(scores - top), 0.0)
    self_weight = jnp.where(is_first, jnp.exp(self_score - top), 0.0)
    total = jnp.sum(weights, axis=1, keepdims=True) + self_weight
    rounded = weights.astype(jnp.bfloat16)
    self_part = self_weight * value_new_ref[...].reshape(rows, HD)
    pieces = pieces_of(total) + pieces_of(top)
    lane = lax.broadcasted_iota(jnp.int32, (heads, LANES), 1)
    stats = jnp.zeros((heads, LANES), jnp.float32)
    parts = []
    for r in range(n_req):
        at = slice(r * heads, (r + 1) * heads)
        wide = jnp.dot(
            rounded[at, :span], value_own[r, :, mine], preferred_element_type=jnp.float32
        ) + jnp.dot(
            rounded[at, span:], cache_peer[1, r], preferred_element_type=jnp.float32
        )
        numer = self_part[at, :]
        for k in range(kv_half):
            numer = numer + jnp.where(group_of[at, :] == k, wide[:, k * HD : (k + 1) * HD], 0.0)
        parts.append(numer)
        for p, piece in enumerate(pieces):
            stats = jnp.where(lane == p * PIECE + r, piece[at, :], stats)
    message = jnp.concatenate(parts + [stats], axis=1).astype(jnp.bfloat16)
    for i in range(n_copies):
        message_ref[i] = message


def combine_kernel(arrived_ref, rows_ref, attended_ref):
    n_chips, heads, width = arrived_ref.shape
    n_req = rows_ref.shape[0]
    totals, tops = [], []
    for chip in range(n_chips):
        tile = arrived_ref[chip, :, width - LANES :].astype(jnp.float32)
        tile = (
            tile
            + pltpu.roll(tile, LANES - PIECE, 1)
            + pltpu.roll(tile, LANES - 2 * PIECE, 1)
        )
        totals.append(tile)
        tops.append(pltpu.roll(tile, LANES - TOP_AT, 1))
    final_top = tops[0]
    for top in tops[1:]:
        final_top = jnp.maximum(final_top, top)
    fades = [jnp.exp(top - final_top) for top in tops]
    denominator = totals[0] * fades[0]
    for total, fade in zip(totals[1:], fades[1:]):
        denominator = denominator + total * fade
    for r in range(n_req):
        numer = jnp.zeros((heads, HD), jnp.float32)
        for chip, fade in enumerate(fades):
            part = arrived_ref[chip, :, r * HD : (r + 1) * HD].astype(jnp.float32)
            numer = numer + part * fade[:, r : r + 1]
        attended_ref[r] = numer / denominator[:, r : r + 1]
    rows = jnp.concatenate([attended_ref[:, h, :] for h in range(heads)], axis=1)
    rows_ref[...] = rows.astype(jnp.bfloat16)


def half_rows(rows_ref, w_ref, side):
    half = rows_ref.shape[1]
    rows = pl.ds(pl.multiple_of(side * half, LANES), half)
    return jnp.dot(rows_ref[...], w_ref[rows, :], preferred_element_type=jnp.float32)


def out_own_kernel(own_ref, w_ref, out_ref):
    out_ref[...] = half_rows(own_ref, w_ref, head_half())


def out_peer_kernel(own_part, peer_ref, w_ref, out_ref):
    out_ref[...] = own_part[...] + half_rows(peer_ref, w_ref, 1 - head_half())


def out_both_kernel(own_ref, peer_ref, w_ref, out_ref):
    side = head_half()
    out_ref[...] = half_rows(own_ref, w_ref, side) + half_rows(peer_ref, w_ref, 1 - side)


def up_columns(scaled_mlp, w_ref, side, out_ref):
    half = out_ref.shape[1] - LANES
    mine = pl.ds(pl.multiple_of(side * half, LANES), half)
    columns = jnp.dot(scaled_mlp, w_ref[:, mine], preferred_element_type=jnp.float32)
    out_ref[:, :half] = columns.astype(out_ref.dtype)


def up_other_kernel(
    x_ref, part_ref, peer_ref, gain_ref, w_ref, hidden_ref, scaled_ref, tile_ref, other_ref
):
    attn_out = part_ref[...] + peer_ref[...]
    hidden_state = (x_ref[...].astype(jnp.float32) + attn_out).astype(jnp.bfloat16)
    resid_rows = hidden_state.astype(jnp.float32)
    hidden_ref[...] = resid_rows
    scaled_mlp = (resid_rows * gain_ref[...]).astype(jnp.bfloat16)
    scaled_ref[...] = scaled_mlp
    squares = jnp.sum(resid_rows * resid_rows, axis=1, keepdims=True)
    first = 3 * (2 * lax.axis_index("chip") + lax.axis_index("core"))
    lane = lax.broadcasted_iota(jnp.int32, tile_ref.shape, 1)
    tile = jnp.zeros(tile_ref.shape, jnp.float32)
    for p, piece in enumerate(pieces_of(squares)):
        tile = jnp.where(lane == first + p, piece, tile)
    tile_ref[...] = tile
    other_ref[:, other_ref.shape[1] - LANES :] = tile.astype(jnp.bfloat16)
    up_columns(scaled_mlp, w_ref, 1 - up_half(), other_ref)


def up_mine_kernel(scaled_ref, tile_ref, w_ref, mine_ref):
    mine_ref[:, mine_ref.shape[1] - LANES :] = tile_ref[...]
    up_columns(scaled_ref[...], w_ref, up_half(), mine_ref)


def up_pair_kernel(mine_ref, arrived_ref, total_a, sent_a, total_b, sent_b):
    total = mine_ref[...] + arrived_ref[...].astype(jnp.float32)
    start = total_a.shape[1]
    total_a[...] = total[:, :start]
    sent_a[...] = total[:, :start].astype(jnp.bfloat16)
    total_b[...] = total[:, start:]
    sent_b[...] = total[:, start:].astype(jnp.bfloat16)


def up_add_kernel(part_ref, arrived_ref, total_ref, sent_ref):
    total = part_ref[...] + arrived_ref[...].astype(jnp.float32)
    total_ref[...] = total
    sent_ref[...] = total.astype(jnp.bfloat16)


def activate_kernel(part_a, arrived_a, part_b, arrived_b, out_ref):
    start, width = part_a.shape[1], part_b.shape[1] - LANES
    pieces = part_b[:, width:] + arrived_b[:, width:].astype(jnp.float32)
    squares = jnp.sum(pieces, axis=1, keepdims=True)
    inv_mlp = lax.rsqrt(squares / D + NORM_EPS)
    total_a = part_a[...] + arrived_a[...].astype(jnp.float32)
    out_ref[:, :start] = squared_relu(total_a * inv_mlp).astype(jnp.bfloat16)
    total_b = part_b[:, :width] + arrived_b[:, :width].astype(jnp.float32)
    out_ref[:, start:] = squared_relu(total_b * inv_mlp).astype(jnp.bfloat16)


def down_own_kernel(own_ref, w_ref, out_ref):
    out_ref[...] = half_rows(own_ref, w_ref, up_half())


def down_peer_kernel(own_part, peer_ref, w_ref, out_ref):
    out_ref[...] = own_part[...] + half_rows(peer_ref, w_ref, 1 - up_half())


def per_device(
    hidden_in,
    attn_gain,
    mlp_gain,
    query_weight,
    key_weight,
    value_weight,
    out_weight,
    up_weight,
    down_weight,
    key_cache,
    value_cache,
    lengths,
    block_order,
    pad_mask,
):
    n_req, d_here = hidden_in.shape
    kv_here = key_cache.shape[2] // HD
    heads_here = kv_here * (H // KVH)
    n_chips = lax.axis_size("chip")
    core = lax.axis_index("core")
    n_blocks = 2 * n_chips
    half_qkv = (heads_here + 2 * kv_here) * HD // 2
    half_up = up_weight.shape[1] // 2

    row = (1, d_here)
    small = [hidden_in, attn_gain.reshape(row), mlp_gain.reshape(row), pad_mask]
    small += [lengths, block_order, key_cache, value_cache]
    scaled_in, squares, live, x_rows, gain, cache_sent = local_kernel(
        prepare_kernel,
        [
            bf16(*hidden_in.shape),
            f32(n_req, LANES),
            f32(*pad_mask.shape),
            bf16(*hidden_in.shape),
            f32(*row),
            bf16(2, *key_cache.shape[:2], key_cache.shape[2] // 2),
        ],
        small,
        flops=4 * 10**9,
        scratch=[
            pltpu.VMEM(row, jnp.float32),
            pltpu.VMEM(pad_mask.shape, jnp.int32),
            pltpu.SMEM(lengths.shape, jnp.int32),
            pltpu.SMEM(block_order.shape, jnp.int32),
            pltpu.SemaphoreType.DMA((len(small),)),
        ],
        in_hbm=range(len(small)),
    )
    (other,) = local_kernel(
        qkv_other_kernel,
        [f32(n_req, half_qkv + LANES + pad_mask.shape[1])],
        [scaled_in, squares, live, query_weight, key_weight, value_weight],
        flops=4 * 10**9,
        anywhere=(3, 4, 5),
    )
    (mine,) = local_kernel(
        qkv_mine_kernel,
        [f32(n_req, half_qkv + LANES)],
        [scaled_in, squares, query_weight, key_weight, value_weight],
        flops=2 * n_req * d_here * half_qkv,
        anywhere=(2, 3, 4),
    )
    arrived = swap(other, "core")
    width = mine.shape[1]
    (qkv_message,) = local_kernel(
        qkv_message_kernel, [f32(*mine.shape)], [mine, arrived], flops=2 * mine.size
    )
    qkv_message, live_peer, *moved = lax.optimization_barrier(
        (
            qkv_message.astype(jnp.float16),
            arrived[:, width:],
            cache_sent,
            out_weight,
        )
    )
    cache_peer, out_peer = (swap(x, "core") for x in moved)
    sides = [
        [2 * chip + (side + chip_turn(chip)) % 2 for chip in range(n_chips)] for side in range(2)
    ]
    qkv_all = lax.all_to_all(
        jnp.broadcast_to(qkv_message[None], (n_chips,) + qkv_message.shape),
        ("chip", "core"),
        0,
        0,
        axis_index_groups=sides,
    )
    half_heads = heads_here // 2
    (message,) = local_kernel(
        attention_kernel,
        [bf16(n_chips, half_heads, n_req * HD + LANES)],
        [qkv_all.astype(jnp.float32), key_cache, value_cache, cache_peer, live, live_peer],
        anywhere=(1, 2, 3),
        flops=4 * 10**9,
        scratch=[pltpu.VMEM((n_req, half_heads, HD), jnp.float32)] * 3,
    )
    message, out_peer = lax.optimization_barrier((message, out_peer))
    (attended,) = local_kernel(
        combine_kernel,
        [bf16(n_req, half_heads * HD)],
        [lax.all_to_all(message, ("chip", "core"), 0, 0, axis_index_groups=sides)],
        flops=n_chips * n_req * half_heads * HD,
        scratch=[pltpu.VMEM((n_req, half_heads, HD), jnp.float32)],
    )
    attended_peer = swap(attended, "core")
    (head_own,) = local_kernel(
        out_own_kernel,
        [f32(n_req, d_here)],
        [attended, out_peer],
        anywhere=(1,),
        flops=n_req * out_weight.size,
    )
    (head_sent,) = local_kernel(
        out_peer_kernel,
        [f32(n_req, d_here)],
        [head_own, attended_peer, out_peer],
        anywhere=(2,),
        flops=n_req * out_weight.size,
    )
    head_peer = swap_diagonal(head_sent)
    (head_part,) = local_kernel(
        out_both_kernel,
        [f32(n_req, d_here)],
        [attended, attended_peer, out_weight],
        anywhere=(2,),
        flops=2 * n_req * out_weight.size,
    )

    resid_rows, scaled_mlp, tile, up_other = local_kernel(
        up_other_kernel,
        [
            f32(n_req, d_here),
            bf16(n_req, d_here),
            f32(n_req, LANES),
            bf16(n_req, half_up + LANES),
        ],
        [x_rows, head_part, head_peer, gain, up_weight],
        flops=n_req * up_weight.size,
        anywhere=(4,),
    )
    (up_mine,) = local_kernel(
        up_mine_kernel,
        [f32(n_req, half_up + LANES)],
        [scaled_mlp, tile, up_weight],
        flops=n_req * up_weight.size,
        anywhere=(2,),
    )
    width_a = half_up // (2 * LANES) * LANES
    widths = [width_a, half_up + LANES - width_a]
    sums = [[f32(n_req, width), bf16(n_req, width)] for width in widths]
    pair = local_kernel(
        up_pair_kernel,
        sums[0] + sums[1],
        [up_mine, swap(up_other, "core")],
        flops=up_mine.size,
    )
    parts = [pair[:2], pair[2:]]
    orders = [(2, 1, 0), (1, 0, 2)]
    arrived = [swap_chips(part[1], order[0]) for part, order in zip(parts, orders)]
    for step in range(1, chip_bits()):
        for i in range(2):
            parts[i] = local_kernel(
                up_add_kernel, sums[i], [parts[i][0], arrived[i]], flops=n_req * widths[i]
            )
            arrived[i] = swap_chips(parts[i][1], orders[i][step])
    (active_half,) = local_kernel(
        activate_kernel,
        [bf16(n_req, half_up)],
        [parts[0][0], arrived[0], parts[1][0], arrived[1]],
        flops=4 * up_mine.size,
    )
    active_other = swap(active_half, "core")
    (down_own,) = local_kernel(
        down_own_kernel,
        [f32(n_req, d_here)],
        [active_half, down_weight],
        flops=n_req * down_weight.size,
        anywhere=(1,),
    )
    (down_part,) = local_kernel(
        down_peer_kernel,
        [f32(n_req, d_here)],
        [down_own, active_other, down_weight],
        flops=n_req * down_weight.size,
        anywhere=(2,),
    )
    mlp_out = sum_tp(down_part)
    return (resid_rows + mlp_out).astype(jnp.bfloat16)


def solution(mesh):
    n_seq, n_tp = mesh.shape["seq"], mesh.shape["tp"]
    split = Mesh(mesh.devices.reshape(n_seq // 2, 2, n_tp), ("chip", "core", "tp"))
    seq = ("chip", "core")
    chips = n_seq // 2
    whole_tiles = chips == 8 and n_tp == 2
    return jax.shard_map(
        per_device if whole_tiles else per_device_plain,
        mesh=split,
        in_specs=(
            P(None, seq),
            P(seq),
            P(seq),
            P(seq, "tp"),
            P(seq, "tp"),
            P(seq, "tp"),
            P("tp", seq),
            P(seq, "tp"),
            P("tp", seq),
            P(None, seq, "tp"),
            P(None, seq, "tp"),
            P(),
            P(),
            P(None, seq),
        ),
        out_specs=P(None, seq),
        check_vma=False,
    )
```
